32 devices in a mesh: seq: 16 (over z, y, x), ffn: 2 (over core).
Axes of the slice: x: 2, y: 2, z: 4, core: 2. Of those that a mesh axis runs over, the one named last changes fastest.
Arguments:
- tokens: bfloat16 [8192, 2048], P(('seq', 'ffn')), may hold values from -6 to 6
- ln1_gain: float32 [2048], replicated, may hold values from 0.5 to 1.5
- ln1_bias: float32 [2048], replicated, may hold values from -1.5 to 1.5
- w_query: bfloat16 [2048, 2048], P('seq', 'ffn'), may hold values from -0.125 to 0.125
- w_key: bfloat16 [2048, 2048], P('seq', 'ffn'), may hold values from -0.125 to 0.125
- w_value: bfloat16 [2048, 4096], P('seq', 'ffn'), may hold values from -0.125 to 0.125
- w_gate: bfloat16 [2048, 4096], P('seq', 'ffn'), may hold values from -0.125 to 0.125
- w_out: bfloat16 [4096, 2048], P('ffn', 'seq'), may hold values from -0.125 to 0.125
- decay_log: float32 [8192, 8], P('seq', 'ffn'), may hold values from -1 to 0
- ln2_gain: float32 [2048], replicated, may hold values from 0.5 to 1.5
- ln2_bias: float32 [2048], replicated, may hold values from -1.5 to 1.5
- w_up: bfloat16 [2048, 4096], P(None, 'ffn'), may hold values from -0.125 to 0.125
- w_down: bfloat16 [4096, 2048], P('ffn'), may hold values from -0.125 to 0.125
- cotangent: bfloat16 [8192, 2048], P('seq'), may hold values from -6 to 6
Outputs:
- block_out: bfloat16 [8192, 2048], P(('seq', 'ffn'))
- grad_tokens: bfloat16 [8192, 2048], P(('seq', 'ffn'))
- grad_ln1_gain: float32 [2048], replicated
- grad_ln1_bias: float32 [2048], replicated
- grad_w_query: float32 [2048, 2048], P('seq', 'ffn')
- grad_w_key: float32 [2048, 2048], P('seq', 'ffn')
- grad_w_value: float32 [2048, 4096], P('seq', 'ffn')
- grad_w_gate: float32 [2048, 4096], P('seq', 'ffn')
- grad_w_out: float32 [4096, 2048], P('ffn', 'seq')
- grad_ln2_gain: float32 [2048], replicated
- grad_ln2_bias: float32 [2048], replicated
- grad_w_up: float32 [2048, 4096], P('seq', 'ffn')
- grad_w_down: float32 [4096, 2048], P('ffn', 'seq')
The draws below stay inside these ranges and needn't reach their ends.
All inputs are finite; a program needn't handle non-finite values.
Results may differ from the reference program's by a relative error of at most 0.02.
Values may be sent and summed in bfloat16 or wider, within the bound.
A program may use at most 512 MiB of HBM per device.

```python
import jax
import jax.numpy as jnp
from jax import lax

D = 2048
RETENTION_HEADS = 8
KEY_DIM = 256
VALUE_DIM = 512
FF = 4096
STRETCH = 512
SEQUENCE_LENGTH = 8192
TOK_DEV = 512
TOTAL_TOKENS = 8192
QK = 2048
VA = 4096


def draw_decay_log(key, part):
    key = jax.random.fold_in(key, 7)
    key_rows = jax.random.split(key, 7)
    slow_share = 0.5
    slow_heads = jax.random.uniform(key_rows[0], (RETENTION_HEADS,), jnp.float32) < slow_share
    fast_rate = jax.random.uniform(key_rows[1], (RETENTION_HEADS,), jnp.float32, 1.0 / 50.0, 1.0 / 30.0)
    slow_total = jax.random.uniform(key_rows[2], (RETENTION_HEADS,), jnp.float32, 0.1, 0.6)
    base_rate = jnp.where(slow_heads, slow_total / SEQUENCE_LENGTH, fast_rate)
    spans = TOTAL_TOKENS // TOK_DEV
    span_factor = jnp.exp(jax.random.uniform(key_rows[3], (spans, 1, RETENTION_HEADS), jnp.float32, -0.7, 0.7))
    span_factor = jnp.broadcast_to(span_factor, (spans, TOK_DEV, RETENTION_HEADS)).reshape(TOTAL_TOKENS, RETENTION_HEADS)
    place_factor = jax.random.uniform(key_rows[4], (TOTAL_TOKENS, RETENTION_HEADS), jnp.float32, 0.5, 1.5)
    spike_events = jax.random.uniform(key_rows[5], (TOTAL_TOKENS, RETENTION_HEADS), jnp.float32) < 2.0 / SEQUENCE_LENGTH
    spike_decrease = jax.random.uniform(key_rows[6], (TOTAL_TOKENS, RETENTION_HEADS), jnp.float32, 0.22, 0.69)
    decay_rates = base_rate[None, :] * span_factor * place_factor
    return -(decay_rates + jnp.where(spike_events, spike_decrease, 0.0))


def shard_levels(stream_key, extent, shards, least, top_value):
    loudness = 1.0
    for position, parts in shards:
        draws = jax.random.uniform(jax.random.fold_in(jax.random.fold_in(stream_key, 6), position), (parts,), jnp.float32, least / len(shards), top_value / len(shards))
        loudness = loudness * jnp.repeat(jnp.exp(draws), extent[position] // parts).reshape((-1,) + (1,) * (len(extent) - 1 - position))
    return loudness


def scatter_about(key, shape, scale, most, cuts=(), kind=jnp.bfloat16):
    entries = jax.random.normal(key, shape, jnp.float32) * scale
    if len(cuts) > 0:
        entries = shard_levels(key, shape, cuts, -0.22, 0.18) * entries
    return jnp.clip(entries, min=-most, max=most).astype(kind)


def setup_inputs(seed: int = 0) -> dict:
    arg_keys = jax.random.split(jax.random.key(seed), 15)
    tokens = scatter_about(arg_keys[0], (TOTAL_TOKENS, D), 1.0, 6.0, ((0, 32),))
    ln1_gain = jnp.clip(1.0 + 0.1 * jax.random.normal(arg_keys[1], (D,), jnp.float32), 0.5, 1.5)
    ln1_bias = scatter_about(arg_keys[2], (D,), 0.3, 1.5, (), jnp.float32)
    w_query = scatter_about(arg_keys[3], (D, QK), D ** -0.5, 0.125, ((0, 16), (1, 2)))
    w_key = scatter_about(arg_keys[4], (D, QK), D ** -0.5, 0.125, ((0, 16), (1, 2)))
    w_value = scatter_about(arg_keys[5], (D, VA), D ** -0.5, 0.125, ((0, 16), (1, 2)))
    w_gate = scatter_about(arg_keys[6], (D, VA), D ** -0.5, 0.125, ((0, 16), (1, 2)))
    w_out = scatter_about(arg_keys[7], (VA, D), D ** -0.5, 0.125, ((0, 2), (1, 16)))
    decay_log = draw_decay_log(jax.random.fold_in(arg_keys[14], 71), 0)
    ln2_gain = jnp.clip(1.0 + 0.1 * jax.random.normal(arg_keys[9], (D,), jnp.float32), 0.5, 1.5)
    ln2_bias = scatter_about(arg_keys[10], (D,), 0.3, 1.5, (), jnp.float32)
    w_up = scatter_about(arg_keys[11], (D, FF), D ** -0.5, 0.125, ((1, 2),))
    w_down = scatter_about(arg_keys[12], (FF, D), D ** -0.5, 0.125, ((0, 2),))
    cotangent = scatter_about(arg_keys[13], (TOTAL_TOKENS, D), 1.0, 6.0, ((0, 16),))
    return {"tokens": tokens, "ln1_gain": ln1_gain, "ln1_bias": ln1_bias, "w_query": w_query, "w_key": w_key, "w_value": w_value, "w_gate": w_gate, "w_out": w_out, "decay_log": decay_log, "ln2_gain": ln2_gain, "ln2_bias": ln2_bias, "w_up": w_up, "w_down": w_down, "cotangent": cotangent}


@jax.custom_vjp
def low(v):
    return lax.optimization_barrier(v.astype(jnp.bfloat16)).astype(jnp.float32)

@jax.custom_vjp
def low_back(v):
    return v

def low_keep(v):
    return (low(v), None)

def low_pass(kept, grad):
    return (grad,)

def back_keep(v):
    return (v, None)

def back_low(kept, grad):
    return (low(grad),)
low.defvjp(low_keep, low_pass)
low_back.defvjp(back_keep, back_low)

def matmul(left, right):
    return jnp.dot(left, right, precision=lax.Precision.HIGHEST)

def layer_norm(values_in, gain_vec, bias_vec):
    average = lax.optimization_barrier(jnp.mean(values_in, axis=-1, keepdims=True))
    centered = values_in - average
    variance = lax.optimization_barrier(jnp.mean(centered * centered, axis=-1, keepdims=True))
    return centered * lax.rsqrt(variance + 1e-05) * gain_vec + bias_vec

def group_norm(values_in):
    average = lax.optimization_barrier(jnp.mean(values_in, axis=-1, keepdims=True))
    centered = values_in - average
    variance = lax.optimization_barrier(jnp.mean(centered * centered, axis=-1, keepdims=True))
    return centered * lax.rsqrt(variance + 1e-05)

def rotate(values_in, positions):
    half_width = values_in.shape[-1] // 2
    frequency = 10000.0 ** (-jnp.linspace(0.0, 1.0, half_width, dtype=jnp.float32))
    angles = positions.astype(jnp.float32)[:, None] * frequency[None, :]
    cosine = jnp.cos(angles)[:, None, :]
    sine_part = jnp.sin(angles)[:, None, :]
    first_half = values_in[..., :half_width]
    second_half = values_in[..., half_width:]
    return jnp.concatenate([first_half * cosine - second_half * sine_part, second_half * cosine + first_half * sine_part], axis=-1)

def decay_mask(cumulative):
    across = cumulative.T
    gaps = across[:, :, None] - across[:, None, :]
    indices = jnp.arange(cumulative.shape[0])
    lower = indices[:, None] >= indices[None, :]
    return jnp.where(lower[None], jnp.exp(jnp.minimum(gaps, 0.0)), 0.0)

def block_step(state_in, inputs):
    q_block, k_block, v_block, decay_block = inputs
    cumulative = jnp.cumsum(decay_block, axis=0)
    raw_scores = low_back(jnp.einsum('thk,shk->hts', q_block, k_block, precision=lax.Precision.HIGHEST))
    weighted = low(raw_scores * decay_mask(cumulative))
    inside = jnp.einsum('hts,shd->thd', weighted, v_block, precision=lax.Precision.HIGHEST)
    q_decayed = low(q_block * jnp.exp(cumulative)[:, :, None])
    carried = jnp.einsum('thk,hkd->thd', q_decayed, low(state_in), precision=lax.Precision.HIGHEST)
    tail_values = low(v_block * jnp.exp(cumulative[-1:] - cumulative)[:, :, None])
    key_values = low_back(jnp.einsum('shk,shd->hkd', k_block, tail_values, precision=lax.Precision.HIGHEST))
    next_state = jnp.exp(cumulative[-1])[:, None, None] * state_in + key_values
    return (next_state, inside + carried)

def retention(q_rot, k_rot, value_heads, decays):
    block_count = q_rot.shape[0] // STRETCH
    blocks = (q_rot.reshape(block_count, STRETCH, RETENTION_HEADS, KEY_DIM), k_rot.reshape(block_count, STRETCH, RETENTION_HEADS, KEY_DIM), value_heads.reshape(block_count, STRETCH, RETENTION_HEADS, VALUE_DIM), decays.reshape(block_count, STRETCH, RETENTION_HEADS))
    zero_state = jnp.zeros((RETENTION_HEADS, KEY_DIM, VALUE_DIM), jnp.float32)
    final_state, outputs = lax.scan(jax.checkpoint(block_step), zero_state, blocks)
    return outputs.reshape(q_rot.shape[0], RETENTION_HEADS, VALUE_DIM)

def sequence_layer(inputs32, decays, params):
    gain_one, bias_one, query_w, key_w, value_w, gate_w, out_w, gain_two, bias_two, up_w, down_w = params
    xn_first = low(layer_norm(inputs32, gain_one, bias_one))
    query_proj = low_back(matmul(xn_first, query_w))
    key_proj = low_back(matmul(xn_first, key_w))
    value_proj = low_back(low(matmul(xn_first, value_w)))
    gate_proj = low_back(matmul(xn_first, gate_w))
    positions = jnp.arange(SEQUENCE_LENGTH)
    q_rot = low(rotate(query_proj.reshape(SEQUENCE_LENGTH, RETENTION_HEADS, KEY_DIM), positions))
    k_rot = low(rotate(key_proj.reshape(SEQUENCE_LENGTH, RETENTION_HEADS, KEY_DIM), positions))
    retained = low_back(retention(q_rot, k_rot, value_proj.reshape(SEQUENCE_LENGTH, RETENTION_HEADS, VALUE_DIM), decays))
    grouped = group_norm(retained).reshape(SEQUENCE_LENGTH, RETENTION_HEADS * VALUE_DIM)
    gated = low(jax.nn.silu(gate_proj) * grouped)
    residual = inputs32 + low_back(matmul(gated, out_w))
    xn_second = low(layer_norm(residual, gain_two, bias_two))
    upper = low_back(matmul(xn_second, up_w))
    active = low(jax.nn.gelu(upper, approximate=False))
    return residual + low_back(matmul(active, down_w))

def whole_layer(inputs32, decays, params):
    sequences = inputs32.reshape(-1, SEQUENCE_LENGTH, D)
    decay_rows = decays.reshape(-1, SEQUENCE_LENGTH, RETENTION_HEADS)

    def per_sequence(pair):
        return sequence_layer(pair[0], pair[1], params)
    outputs = lax.map(jax.checkpoint(per_sequence), (sequences, decay_rows))
    return outputs.reshape(-1, D)

def reference(tokens, ln1_gain, ln1_bias, w_query, w_key, w_value, w_gate, w_out, decay_log, ln2_gain, ln2_bias, w_up, w_down, cotangent):
    inputs32 = tokens.astype(jnp.float32)
    params = (ln1_gain.astype(jnp.float32), ln1_bias.astype(jnp.float32), w_query.astype(jnp.float32), w_key.astype(jnp.float32), w_value.astype(jnp.float32), w_gate.astype(jnp.float32), w_out.astype(jnp.float32), ln2_gain.astype(jnp.float32), ln2_bias.astype(jnp.float32), w_up.astype(jnp.float32), w_down.astype(jnp.float32))

    def forward(inputs_arg, *param_args):
        return whole_layer(inputs_arg, decay_log.astype(jnp.float32), param_args)
    result, pullback = jax.vjp(forward, inputs32, *params)
    gradients = pullback(cotangent.astype(jnp.float32))
    return (result.astype(jnp.bfloat16), gradients[0].astype(jnp.bfloat16), gradients[1], gradients[2], gradients[3], gradients[4], gradients[5], gradients[6], gradients[7], gradients[8], gradients[9], gradients[10], gradients[11])
```

```python
import functools

import jax
import jax.numpy as jnp
from jax import lax
from jax.experimental import pallas as pl
from jax.experimental.pallas import tpu as pltpu
from jax.sharding import PartitionSpec as P

STRETCH = 512
SEQUENCE_LENGTH = 8192
PLANE = 4
LINE = 4
SPANS = PLANE * LINE
MESH = pl.DeviceIdType.MESH
VMEM_LIMIT = 60 * 1024 * 1024
ANY = pl.BlockSpec(memory_space=pl.ANY)
VM = pl.BlockSpec(memory_space=pltpu.VMEM)
BF16 = jnp.bfloat16
F32 = jnp.float32


class Place:
    def __init__(self):
        s = lax.axis_index("seq")
        self.f = lax.axis_index("ffn")
        lo = s % SPANS
        self.base = s - lo
        self.z = lo // PLANE
        self.p = lo % PLANE

    def plane(self, m):
        return self.at(self.z, self.xor(m), self.f)

    def xor(self, m):
        p = self.p
        low, high = p % 2, p // 2
        if m & 1:
            low = 1 - low
        if m & 2:
            high = 1 - high
        return high * 2 + low

    def at(self, z, p, f):
        return (self.base + z * PLANE + p, f)

    def partner(self):
        return self.at(self.z, self.p, 1 - self.f)

    def up(self):
        return self.at(self.z + 1, self.p, self.f)

    def down(self):
        return self.at(self.z - 1, self.p, self.f)


def greet(peers):
    bar = pltpu.get_barrier_semaphore()
    count = 0
    for device, cond in peers:
        if cond is None:
            pl.semaphore_signal(bar, inc=1, device_id=device, device_id_type=MESH)
            count = count + 1
        else:

            @pl.when(cond)
            def _():
                pl.semaphore_signal(bar, inc=1, device_id=device, device_id_type=MESH)

            count = count + cond.astype(jnp.int32)
    pl.semaphore_wait(bar, count)


def remote(src, dst, send, recv, device):
    return pltpu.make_async_remote_copy(
        src_ref=src, dst_ref=dst, send_sem=send, recv_sem=recv, device_id=device, device_id_type=MESH
    )


def comm_call(kernel, outs, ins, scratch, cid, in_specs=None, out_specs=None):
    return pl.pallas_call(
        kernel,
        out_shape=outs,
        in_specs=in_specs if in_specs is not None else [ANY] * len(ins),
        out_specs=out_specs if out_specs is not None else [ANY] * len(outs),
        scratch_shapes=scratch,
        compiler_params=pltpu.CompilerParams(
            collective_id=cid, has_side_effects=True, vmem_limit_bytes=VMEM_LIMIT
        ),
    )(*ins)


DMA = pltpu.SemaphoreType.DMA


def gather_kernel(widths, rows, *refs):
    count = len(widths)
    xn_ref, dec_ref = refs[:2]
    shards_in = refs[2 : 2 + count]
    xg, decg = refs[2 + count : 4 + count]
    full = refs[4 + count : 4 + 2 * count]
    lsem, psend, precv, usend, dsend, zrecv, xsend, xrecv, csend, crecv, tsend, trecv = refs[4 + 2 * count :]
    me = Place()
    z, p, f = me.z, me.p, me.f
    spot = z * PLANE + p
    chunk = shards_in[0].shape[0]
    deep = chunk * PLANE
    greet(
        [(me.plane(m), None) for m in (1, 2, 3)]
        + [(me.partner(), None), (me.up(), z < LINE - 1), (me.down(), z > 0)]
    )

    def part(i, q):
        w = widths[i]
        if rows[i]:
            return shards_in[i].at[pl.ds(pl.multiple_of(q * w, w), w), :]
        return shards_in[i].at[:, pl.ds(pl.multiple_of(q * w, w), w)]

    def slot(i, ss):
        at = pl.ds(pl.multiple_of(ss * chunk, chunk), chunk)
        return full[i].at[:, at] if rows[i] else full[i].at[at, :]

    def block(i, zz):
        at = pl.ds(pl.multiple_of(zz * deep, deep), deep)
        return full[i].at[:, at] if rows[i] else full[i].at[at, :]

    local, plane = [], []
    for i in range(count):
        own = pltpu.make_async_copy(part(i, p), slot(i, spot), lsem.at[i])
        own.start()
        local.append(own)
        sends = []
        for m in (1, 2, 3):
            c = remote(part(i, me.xor(m)), slot(i, spot), psend.at[i, m], precv.at[i, m], me.plane(m))
            c.start()
            sends.append(c)
        plane.append(sends)
    tiny = []
    for m in (1, 2, 3):
        c = remote(dec_ref, decg.at[p], tsend.at[m], trecv.at[m], me.plane(m))
        c.start()
        tiny.append(c)
    dec_own = pltpu.make_async_copy(dec_ref, decg.at[p], lsem.at[count])
    dec_own.start()

    seat = p * 2 + f
    x_own = pltpu.make_async_copy(xn_ref, xg.at[seat], lsem.at[count + 1])
    x_own.start()
    half = xn_ref.shape[0] // 2
    x1 = remote(xn_ref, xg.at[seat], xsend.at[0], xrecv.at[0], me.plane(1))
    x2 = remote(xn_ref, xg.at[seat], xsend.at[1], xrecv.at[1], me.plane(2))
    xc = remote(xn_ref, xg.at[seat], csend.at[0], crecv.at[0], me.partner())
    x1.start()
    x2.start()
    xc.start()

    def up_copy(i, zz):
        return remote(block(i, zz), block(i, zz), usend.at[i, zz], zrecv.at[i, zz], me.up())

    def down_copy(i, zz):
        return remote(block(i, zz), block(i, zz), dsend.at[i, zz], zrecv.at[i, zz], me.down())

    for i in range(count):
        local[i].wait()
        for c in plane[i]:
            c.wait_recv()

        @pl.when(z < LINE - 1)
        def _():
            up_copy(i, z).start()

        @pl.when(z > 0)
        def _():
            down_copy(i, z).start()

    seat1, seat2, seat3 = (me.xor(m) * 2 + f for m in (1, 2, 3))
    low, high = pl.ds(0, half), pl.ds(half, half)
    x1.wait_recv()
    g1 = remote(xg.at[seat1, low], xg.at[seat1, low], xsend.at[2], xrecv.at[2], me.plane(2))
    g1.start()
    c1 = remote(xg.at[seat1], xg.at[seat1], csend.at[1], crecv.at[1], me.partner())
    c1.start()
    x2.wait_recv()
    g2 = remote(xg.at[seat2, high], xg.at[seat2, high], xsend.at[3], xrecv.at[3], me.plane(1))
    g2.start()
    c2 = remote(xg.at[seat2], xg.at[seat2], csend.at[2], crecv.at[2], me.partner())
    c2.start()
    g1.wait_recv()
    g2.wait_recv()
    c3 = remote(xg.at[seat3], xg.at[seat3], csend.at[3], crecv.at[3], me.partner())
    c3.start()

    for t in range(1, LINE):
        for i in range(count):

            @pl.when(z - t >= 0)
            def _():
                up_copy(i, z - t).wait_recv()

                @pl.when(z < LINE - 1)
                def _():
                    up_copy(i, z - t).start()

            @pl.when(z + t < LINE)
            def _():
                down_copy(i, z + t).wait_recv()

                @pl.when(z > 0)
                def _():
                    down_copy(i, z + t).start()

    for c in (xc, c1, c2, c3):
        c.wait()
    for c in (x1, x2, g1, g2):
        c.wait_send()
    for c in tiny:
        c.wait()
    dec_own.wait()
    x_own.wait()
    for i in range(count):
        for c in plane[i]:
            c.wait_send()
        for zz in range(LINE):

            @pl.when((z < LINE - 1) & (zz <= z))
            def _():
                up_copy(i, zz).wait_send()

            @pl.when((z > 0) & (zz >= z))
            def _():
                down_copy(i, zz).wait_send()


def gather_in(xn, dec, shards_in, rows, cid):
    count = len(shards_in)
    chunk = shards_in[0].shape[0]
    widths, outs = [], []
    for w, r in zip(shards_in, rows):
        if r:
            widths.append(w.shape[0] // PLANE)
            outs.append(jax.ShapeDtypeStruct((w.shape[0] // PLANE, chunk * SPANS), BF16))
        else:
            widths.append(w.shape[1] // PLANE)
            outs.append(jax.ShapeDtypeStruct((chunk * SPANS, w.shape[1] // PLANE), BF16))
    outs = [
        jax.ShapeDtypeStruct((2 * PLANE,) + xn.shape, BF16),
        jax.ShapeDtypeStruct((PLANE,) + dec.shape, F32),
    ] + outs
    scratch = [
        DMA((count + 2,)),
        DMA((count, PLANE)),
        DMA((count, PLANE)),
        DMA((count, LINE)),
        DMA((count, LINE)),
        DMA((count, LINE)),
        DMA((4,)),
        DMA((4,)),
        DMA((4,)),
        DMA((4,)),
        DMA((PLANE,)),
        DMA((PLANE,)),
    ]
    return comm_call(
        functools.partial(gather_kernel, widths, rows), outs, [xn, dec] + shards_in, scratch, cid
    )


def plane_gather_kernel(x_ref, out, lsem, xsend, xrecv, csend, crecv):
    me = Place()
    p, f = me.p, me.f
    greet([(me.plane(1), None), (me.plane(2), None), (me.partner(), None)])
    seat, seat1, seat2, seat3 = (me.xor(m) * 2 + f for m in (0, 1, 2, 3))
    half = x_ref.shape[0] // 2
    low, high = pl.ds(0, half), pl.ds(half, half)
    own = pltpu.make_async_copy(x_ref, out.at[seat], lsem)
    own.start()
    x1 = [
        remote(x_ref.at[h], out.at[seat, h], xsend.at[k], xrecv.at[k], me.plane(1))
        for k, h in ((0, low), (1, high))
    ]
    x2 = [
        remote(x_ref.at[h], out.at[seat, h], xsend.at[k], xrecv.at[k], me.plane(2))
        for k, h in ((2, high), (3, low))
    ]
    for a, b in zip(x1, x2):
        a.start()
        b.start()
    c0 = remote(x_ref, out.at[seat], csend.at[0], crecv.at[0], me.partner())
    c0.start()
    x1[0].wait_recv()
    g1 = remote(out.at[seat1, low], out.at[seat1, low], xsend.at[4], xrecv.at[4], me.plane(2))
    g1.start()
    x2[0].wait_recv()
    g2 = remote(out.at[seat2, high], out.at[seat2, high], xsend.at[5], xrecv.at[5], me.plane(1))
    g2.start()
    x1[1].wait_recv()
    c1 = remote(out.at[seat1], out.at[seat1], csend.at[1], crecv.at[1], me.partner())
    c1.start()
    x2[1].wait_recv()
    c2 = remote(out.at[seat2], out.at[seat2], csend.at[2], crecv.at[2], me.partner())
    c2.start()
    g1.wait_recv()
    c3 = remote(out.at[seat3, low], out.at[seat3, low], csend.at[3], crecv.at[3], me.partner())
    c3.start()
    g2.wait_recv()
    c4 = remote(out.at[seat3, high], out.at[seat3, high], csend.at[4], crecv.at[4], me.partner())
    c4.start()
    for c in (c0, c1, c2, c3, c4):
        c.wait()
    for c in x1 + x2 + [g1, g2]:
        c.wait_send()
    own.wait()


def plane_gather(x, cid):
    return comm_call(
        plane_gather_kernel,
        [jax.ShapeDtypeStruct((2 * PLANE,) + x.shape, x.dtype)],
        [x],
        [DMA, DMA((6,)), DMA((6,)), DMA((5,)), DMA((5,))],
        cid,
    )[0]


def plane_reduce_kernel(x_ref, out, rx0, rx1a, rx1b, rx2a, rx2b, csend, crecv, xsend, xrecv):
    me = Place()
    p, f = me.p, me.f
    greet([(me.plane(1), None), (me.plane(2), None), (me.partner(), None)])
    q = [me.xor(m) for m in range(4)]
    wide = x_ref.shape[-1] // 2
    ca, cb = pl.ds(0, wide), pl.ds(wide, wide)
    order = (3, 1, 2, 0)
    first = []
    for m in order:
        c = remote(x_ref.at[q[m], 1 - f], rx0.at[q[m]], csend.at[m], crecv.at[m], me.partner())
        c.start()
        first.append(c)

    def add(dst, cols, other, others_cols):
        rows = dst.shape[0]

        @pl.loop(0, rows, step=64)
        def _(r):
            at = pl.ds(pl.multiple_of(r, 64), 64)
            dst[at, cols] = (dst[at, cols].astype(F32) + other[at, others_cols].astype(F32)).astype(BF16)

    everything = pl.ds(0, 2 * wide)
    whole = pl.ds(0, wide)
    sends = {}
    for c, m in zip(first, order):
        c.wait_recv()
        add(rx0.at[q[m]], everything, x_ref.at[q[m], f], everything)
        if m & 1:
            k = 0 if m == 3 else 1
            s = remote(rx0.at[q[m], :, ca], rx1a.at[k], xsend.at[k], xrecv.at[k], me.plane(1))
            s.start()
            sends["a", k] = s
        if m & 2:
            k = 0 if m == 3 else 1
            s = remote(rx0.at[q[m], :, cb], rx1b.at[k], xsend.at[2 + k], xrecv.at[2 + k], me.plane(2))
            s.start()
            sends["b", k] = s
    sends["a", 0].wait_recv()
    add(rx1a.at[0], whole, rx0.at[q[2]], ca)
    s2a = remote(rx1a.at[0], rx2a, xsend.at[4], xrecv.at[4], me.plane(2))
    s2a.start()
    sends["b", 0].wait_recv()
    add(rx1b.at[0], whole, rx0.at[q[1]], cb)
    s2b = remote(rx1b.at[0], rx2b, xsend.at[5], xrecv.at[5], me.plane(1))
    s2b.start()
    sends["a", 1].wait_recv()
    sends["b", 1].wait_recv()
    s2a.wait_recv()
    s2b.wait_recv()

    @pl.loop(0, out.shape[0], step=32)
    def _(r):
        at = pl.ds(pl.multiple_of(r, 32), 32)
        out[at, ca] = rx0[q[0], at, ca].astype(F32) + rx1a[1, at, :].astype(F32) + rx2a[at, :].astype(F32)
        out[at, cb] = rx0[q[0], at, cb].astype(F32) + rx1b[1, at, :].astype(F32) + rx2b[at, :].astype(F32)

    for c in first + list(sends.values()) + [s2a, s2b]:
        c.wait_send()


def plane_reduce(x, cid):
    _, _, rows, cols = x.shape
    return comm_call(
        plane_reduce_kernel,
        [jax.ShapeDtypeStruct((rows, cols), F32)],
        [x],
        [
            pltpu.VMEM((PLANE, rows, cols), BF16),
            pltpu.VMEM((2, rows, cols // 2), BF16),
            pltpu.VMEM((2, rows, cols // 2), BF16),
            pltpu.VMEM((rows, cols // 2), BF16),
            pltpu.VMEM((rows, cols // 2), BF16),
            DMA((4,)),
            DMA((4,)),
            DMA((6,)),
            DMA((6,)),
        ],
        cid,
        in_specs=[VM],
        out_specs=[VM],
    )[0]


def pair_gather_kernel(x_ref, out, lsem, csend, crecv):
    me = Place()
    greet([(me.partner(), None)])
    own = pltpu.make_async_copy(x_ref, out.at[me.f], lsem)
    own.start()
    c = remote(x_ref, out.at[me.f], csend, crecv, me.partner())
    c.start()
    own.wait()
    c.wait()


def pair_gather(x, cid):
    return comm_call(
        pair_gather_kernel, [jax.ShapeDtypeStruct((2,) + x.shape, x.dtype)], [x], [DMA, DMA, DMA], cid
    )[0]


def pair_reduce_kernel(x_ref, out, rx, csend, crecv):
    me = Place()
    greet([(me.partner(), None)])
    c = remote(x_ref.at[1 - me.f], rx, csend, crecv, me.partner())
    c.start()
    c.wait_recv()

    @pl.loop(0, out.shape[0], step=32)
    def _(r):
        at = pl.ds(pl.multiple_of(r, 32), 32)
        out[at, :] = x_ref[me.f, at, :].astype(F32) + rx[at, :].astype(F32)

    c.wait_send()


def pair_reduce(x, cid):
    _, rows, cols = x.shape
    return comm_call(
        pair_reduce_kernel,
        [jax.ShapeDtypeStruct((rows, cols), F32)],
        [x],
        [pltpu.VMEM((rows, cols), BF16), DMA, DMA],
        cid,
        in_specs=[VM],
        out_specs=[VM],
    )[0]


def line_states_kernel(backward, x_ref, d_ref, out, dout, lsem, xsend, xrecv, dsend, drecv):
    me = Place()
    z = me.z
    others = [(z + t) % LINE for t in range(1, LINE)]
    greet([(me.at(o, me.p, me.f), None) for o in others])
    own = pltpu.make_async_copy(x_ref, out.at[z], lsem.at[0])
    own.start()
    down = pltpu.make_async_copy(d_ref, dout.at[z], lsem.at[1])
    down.start()

    def pair(step, to, slot):
        sem = step - 1
        device = me.at(to, me.p, me.f)
        return (
            remote(x_ref, out.at[slot], xsend.at[sem], xrecv.at[sem], device),
            remote(d_ref, dout.at[slot], dsend.at[sem], drecv.at[sem], device),
        )

    sign = -1 if backward else 1
    for t in range(1, LINE):
        to, source = z + sign * t, z - sign * t

        @pl.when((to >= 0) & (to < LINE))
        def _():
            for c in pair(t, to, z):
                c.start()

    for t in range(1, LINE):
        to, source = z + sign * t, z - sign * t

        @pl.when((source >= 0) & (source < LINE))
        def _():
            for c in pair(t, source, source):
                c.wait_recv()

        @pl.when((to >= 0) & (to < LINE))
        def _():
            for c in pair(t, to, z):
                c.wait_send()

    own.wait()
    down.wait()


def line_states(x, total, backward, cid):
    sent = jnp.broadcast_to(total, (8, 128))
    got, logs = comm_call(
        functools.partial(line_states_kernel, backward),
        [
            jax.ShapeDtypeStruct((LINE,) + x.shape, x.dtype),
            jax.ShapeDtypeStruct((LINE, 8, 128), F32),
        ],
        [x, sent],
        [DMA((2,)), DMA((3,)), DMA((3,)), DMA((3,)), DMA((3,))],
        cid,
    )
    z = (lax.axis_index("seq") % SPANS) // PLANE
    state = jnp.zeros(x.shape, F32)
    for j in reversed(range(LINE)) if backward else range(LINE):
        used = j > z if backward else j < z
        state = jnp.where(used, jnp.exp(logs[j, 0, 0]) * state + got[j].astype(F32), state)
    return state


def line_scatter_kernel(a_ref, out, up, dn, fin, usend, urecv, dsend, drecv, psend, precv, lsem):
    me = Place()
    z, p = me.z, me.p
    greet(
        [(me.plane(m), None) for m in (1, 2, 3)] + [(me.up(), z < LINE - 1), (me.down(), z > 0)]
    )
    parts = usend.shape[1]
    rows, cols = a_ref.shape[2:]
    wide = cols // parts

    def add(dst, src, at):
        for q in range(PLANE):
            dst[q, :, at] = (dst[q, :, at].astype(F32) + src[q, :, at].astype(F32)).astype(BF16)

    def up_copy(src, zz, c):
        at = pl.ds(c * wide, wide)
        return remote(src.at[zz, :, :, at], up.at[zz, :, :, at], usend.at[zz, c], urecv.at[zz, c], me.up())

    def dn_copy(src, zz, c):
        at = pl.ds(c * wide, wide)
        return remote(src.at[zz, :, :, at], dn.at[zz, :, :, at], dsend.at[zz, c], drecv.at[zz, c], me.down())

    for t in range(LINE - 1):
        zu, zd = LINE - 1 - t, t
        for c in range(parts):
            at = pl.ds(c * wide, wide)

            @pl.when(z == 0)
            def _():
                up_copy(a_ref, zu, c).start()

            @pl.when((z > 0) & (z < zu))
            def _():
                up_copy(up, zu, c).wait_recv()
                add(up.at[zu], a_ref.at[zu], at)
                up_copy(up, zu, c).start()

            @pl.when(z == LINE - 1)
            def _():
                dn_copy(a_ref, zd, c).start()

            @pl.when((z < LINE - 1) & (z > zd))
            def _():
                dn_copy(dn, zd, c).wait_recv()
                add(dn.at[zd], a_ref.at[zd], at)
                dn_copy(dn, zd, c).start()

    plane = []
    for c in range(parts):
        at = pl.ds(c * wide, wide)
        for q in range(PLANE):
            fin[q, :, at] = a_ref[z, q, :, at]

        @pl.when(z > 0)
        def _():
            up_copy(up, z, c).wait_recv()
            add(fin, up.at[z], at)

        @pl.when(z < LINE - 1)
        def _():
            dn_copy(dn, z, c).wait_recv()
            add(fin, dn.at[z], at)

        for m in (1, 2, 3):
            s = remote(fin.at[me.xor(m), :, at], out.at[p, :, at], psend.at[c, m], precv.at[c, m], me.plane(m))
            s.start()
            plane.append(s)
    own = pltpu.make_async_copy(fin.at[p], out.at[p], lsem)
    own.start()
    for s in plane:
        s.wait()
    own.wait()
    for zz in range(LINE):
        for c in range(parts):

            @pl.when((z < LINE - 1) & (zz > z))
            def _():
                up_copy(up, zz, c).wait_send()

            @pl.when((z > 0) & (zz < z))
            def _():
                dn_copy(dn, zz, c).wait_send()


def line_scatter(a, parts, cid):
    _, _, rows, cols = a.shape
    return comm_call(
        line_scatter_kernel,
        [jax.ShapeDtypeStruct((PLANE, rows, cols), BF16)],
        [a],
        [
            pltpu.VMEM((LINE, PLANE, rows, cols), BF16),
            pltpu.VMEM((LINE, PLANE, rows, cols), BF16),
            pltpu.VMEM((PLANE, rows, cols), BF16),
            DMA((LINE, parts)),
            DMA((LINE, parts)),
            DMA((LINE, parts)),
            DMA((LINE, parts)),
            DMA((parts, PLANE)),
            DMA((parts, PLANE)),
            DMA,
        ],
        cid,
        in_specs=[VM],
        out_specs=[VM],
    )[0]


def layer_norm(values_in, gain_vec, bias_vec):
    average = jnp.mean(values_in, axis=-1, keepdims=True)
    centered = values_in - average
    variance = jnp.mean(centered * centered, axis=-1, keepdims=True)
    return centered * lax.rsqrt(variance + 1e-05) * gain_vec + bias_vec


def group_norm(values_in):
    average = jnp.mean(values_in, axis=-1, keepdims=True)
    centered = values_in - average
    variance = jnp.mean(centered * centered, axis=-1, keepdims=True)
    return centered * lax.rsqrt(variance + 1e-05)


def exact_gelu(values_in):
    return jax.nn.gelu(values_in, approximate=False)


def swish_gate(gate_proj, grouped):
    return jax.nn.silu(gate_proj) * grouped


def angles_of(positions, half_width):
    frequency = 10000.0 ** (-jnp.linspace(0.0, 1.0, half_width, dtype=F32))
    angles = positions.astype(F32)[:, None] * frequency[None, :]
    return jnp.cos(angles), jnp.sin(angles)


def rotate(values_in, cosine, sine_part):
    half_width = values_in.shape[-1] // 2
    first_half = values_in[..., :half_width]
    second_half = values_in[..., half_width:]
    return jnp.concatenate(
        [
            first_half * cosine - second_half * sine_part,
            second_half * cosine + first_half * sine_part,
        ],
        axis=-1,
    )


def dot(spec, a, b):
    return jnp.einsum(spec, a, b, preferred_element_type=F32)


def shards(
    tokens,
    ln1_gain,
    ln1_bias,
    w_query,
    w_key,
    w_value,
    w_gate,
    w_out,
    decay_log,
    ln2_gain,
    ln2_bias,
    w_up,
    w_down,
    cotangent,
):
    row_count, width = tokens.shape
    span_rows = cotangent.shape[0]
    heads = decay_log.shape[1]
    repeats = lax.axis_size("seq") // SPANS
    peers = [[lo + SPANS * k for k in range(repeats)] for lo in range(SPANS)]
    narrow = width // (SPANS * repeats)

    def wide_in(w, axis):
        if repeats == 1:
            return w
        return lax.all_gather(w, "seq", axis_index_groups=peers, axis=axis, tiled=True)

    def narrow_out(g, axis):
        if repeats == 1:
            return g
        return lax.psum_scatter(
            g, "seq", scatter_dimension=axis, axis_index_groups=peers, tiled=True
        )

    def features_in(a):
        if repeats == 1:
            return a
        return a.reshape(a.shape[:-1] + (repeats, SPANS, narrow)).swapaxes(-3, -2).reshape(a.shape)

    def features_out(a):
        if repeats == 1:
            return a
        return a.reshape(a.shape[:-1] + (SPANS, repeats, narrow)).swapaxes(-3, -2).reshape(a.shape)

    spot = lax.axis_index("seq") % SPANS
    z, p = spot // PLANE, spot % PLANE
    group_rows = span_rows * PLANE
    blocks = group_rows // STRETCH

    inputs32 = tokens.astype(F32)
    xn_first, norm1_back = jax.vjp(layer_norm, inputs32, ln1_gain, ln1_bias)
    decays = jnp.pad(decay_log.T, ((0, 8 - heads), (0, 0)))
    xg, decay_rows, key_w, value_w, query_w, gate_w, out_w = gather_in(
        features_in(xn_first.astype(BF16)),
        decays,
        [
            wide_in(w_key, 0),
            wide_in(w_value, 0),
            wide_in(w_query, 0),
            wide_in(w_gate, 0),
            wide_in(w_out, 1),
        ],
        (False, False, False, False, True),
        0,
    )
    normed = xg.reshape(group_rows, width)
    key_width, value_width = key_w.shape[1], value_w.shape[1]
    log_decay = lax.dynamic_index_in_dim(decay_rows, p, 1, False).reshape(blocks, STRETCH)
    cumulative = jnp.cumsum(log_decay, axis=1)
    last = cumulative[:, -1]
    total = jnp.sum(last)

    positions = (z * group_rows + jnp.arange(group_rows)) % SEQUENCE_LENGTH
    cosine, sine_part = angles_of(positions, key_width // 2)
    q_rot = rotate(dot("td,dq->tq", normed, query_w), cosine, sine_part).astype(BF16)
    k_rot = rotate(dot("td,dq->tq", normed, key_w), cosine, sine_part).astype(BF16)
    value = dot("td,dv->tv", normed, value_w).astype(BF16)
    gate_proj = dot("td,dv->tv", normed, gate_w)

    q_blocks = q_rot.reshape(blocks, STRETCH, key_width)
    k_blocks = k_rot.reshape(blocks, STRETCH, key_width)
    v_blocks = value.reshape(blocks, STRETCH, value_width)
    tail_scale = jnp.exp(last[:, None] - cumulative)
    tail_values = (v_blocks.astype(F32) * tail_scale[:, :, None]).astype(BF16)
    key_values = dot("csk,csd->ckd", k_blocks, tail_values)
    local = [jnp.zeros((key_width, value_width), F32)]
    for c in range(blocks):
        local.append(jnp.exp(last[c]) * local[-1] + key_values[c])
    incoming = line_states(local[-1].astype(BF16), total, False, 1)
    before = jnp.exp(jnp.cumsum(last) - last)
    prev_states = jnp.stack([local[c] + before[c] * incoming for c in range(blocks)]).astype(BF16)

    gaps = cumulative[:, :, None] - cumulative[:, None, :]
    indices = jnp.arange(STRETCH)
    lower = indices[:, None] >= indices[None, :]
    mask = jnp.where(lower[None], jnp.exp(jnp.minimum(gaps, 0.0)), 0.0)
    weighted = (dot("ctk,csk->cts", q_blocks, k_blocks) * mask).astype(BF16)
    q_decayed = (q_blocks.astype(F32) * jnp.exp(cumulative)[:, :, None]).astype(BF16)
    retained = dot("cts,csd->ctd", weighted, v_blocks) + dot("ctk,ckd->ctd", q_decayed, prev_states)
    retained = retained.reshape(group_rows, value_width)
    grouped, group_back = jax.vjp(group_norm, retained)
    gated, gate_back = jax.vjp(swish_gate, gate_proj, grouped)
    gated_low = gated.astype(BF16)
    attn_share = dot("tv,vd->td", gated_low, out_w).astype(BF16)
    attn_rows = plane_reduce(attn_share.reshape(PLANE, 2, row_count, width), 2)

    residual = inputs32 + features_out(attn_rows)
    xn_second, norm2_back = jax.vjp(layer_norm, residual, ln2_gain, ln2_bias)
    ffn_span = pair_gather(xn_second.astype(BF16), 3).reshape(span_rows, width)
    upper = dot("td,df->tf", ffn_span, w_up)
    active, gelu_back = jax.vjp(exact_gelu, upper)
    active_low = active.astype(BF16)
    grad_down = dot("tf,td->fd", active_low, cotangent).astype(BF16)
    sum_down = lax.psum_scatter(grad_down, "seq", scatter_dimension=1, tiled=True).astype(F32)
    grad_active = dot("td,fd->tf", cotangent, w_down)
    grad_upper = gelu_back(grad_active)[0].astype(BF16)
    grad_up = dot("td,tf->df", ffn_span, grad_upper).astype(BF16)
    sum_up = lax.psum_scatter(grad_up, "seq", scatter_dimension=0, tiled=True).astype(F32)
    ffn_share = dot("tf,fd->td", active_low, w_down).astype(BF16)
    ffn_rows_out = pair_reduce(ffn_share.reshape(2, row_count, width), 4)
    block_out = (residual + ffn_rows_out).astype(BF16)
    own_start = lax.axis_index("ffn") * row_count
    cot_own = lax.dynamic_slice_in_dim(cotangent, own_start, row_count, 0).astype(F32)
    grad_xn2_share = dot("tf,df->td", grad_upper, w_up).astype(BF16)
    grad_xn2 = pair_reduce(grad_xn2_share.reshape(2, row_count, width), 5)
    grad_resid, grad_gain2, grad_bias2 = norm2_back(grad_xn2)
    grad_resid = grad_resid + cot_own

    grad_attn = plane_gather(features_in(grad_resid.astype(BF16)), 6).reshape(group_rows, width)
    grad_gated = dot("td,vd->tv", grad_attn, out_w)
    grad_out_w = dot("td,tv->dv", grad_attn, gated_low).astype(BF16)
    grad_gate, grad_grouped = gate_back(grad_gated)
    grad_gate_low = grad_gate.astype(BF16)
    grad_retained = group_back(grad_grouped)[0].astype(BF16)
    grad_blocks = grad_retained.reshape(blocks, STRETCH, value_width)

    query_out = dot("ctk,ctd->ckd", q_decayed, grad_blocks)
    local_grad = jnp.sum(before[:, None, None] * query_out, axis=0)
    outgoing = line_states(local_grad.astype(BF16), total, True, 7)
    after = [outgoing]
    for c in reversed(range(1, blocks)):
        after.append(jnp.exp(last[c]) * after[-1] + query_out[c])
    grad_kv = jnp.stack(after[::-1]).astype(BF16)

    grad_weighted = dot("ctd,csd->cts", grad_blocks, v_blocks)
    grad_scores = (grad_weighted * mask).astype(BF16)
    grad_q = dot("ctd,ckd->ctk", grad_blocks, prev_states) * jnp.exp(cumulative)[:, :, None]
    grad_q = grad_q + dot("cts,csk->ctk", grad_scores, k_blocks)
    grad_k = dot("csd,ckd->csk", tail_values, grad_kv) + dot("cts,ctk->csk", grad_scores, q_blocks)
    grad_v = dot("csk,ckd->csd", k_blocks, grad_kv) * tail_scale[:, :, None]
    grad_v = grad_v + dot("cts,ctd->csd", weighted, grad_blocks)
    grad_query = rotate(grad_q.reshape(group_rows, key_width), cosine, -sine_part).astype(BF16)
    grad_keys = rotate(grad_k.reshape(group_rows, key_width), cosine, -sine_part).astype(BF16)
    grad_values = grad_v.reshape(group_rows, value_width).astype(BF16)

    grad_heads = jnp.concatenate([grad_query, grad_keys, grad_values, grad_gate_low], axis=1)
    heads_w = jnp.concatenate([query_w, key_w, value_w, gate_w], axis=1)
    grad_xn1_share = dot("tq,dq->td", grad_heads, heads_w).astype(BF16)
    grad_heads_w = dot("td,tq->dq", normed, grad_heads).astype(BF16)
    grad_xn1 = plane_reduce(grad_xn1_share.reshape(PLANE, 2, row_count, width), 8)
    sums = line_scatter(
        jnp.concatenate([grad_heads_w, grad_out_w], axis=1).reshape(
            LINE, PLANE, width // SPANS, 2 * key_width + 3 * value_width
        ),
        4,
        9,
    )
    grad_inputs, grad_gain1, grad_bias1 = norm1_back(features_out(grad_xn1))
    grad_tokens = (grad_resid + grad_inputs).astype(BF16)
    gain_one, bias_one, gain_two, bias_two = lax.psum(
        (grad_gain1, grad_bias1, grad_gain2, grad_bias2), ("seq", "ffn")
    )

    def columns(start, size):
        taken = sums[:, :, start : start + size].astype(F32).swapaxes(0, 1)
        return narrow_out(taken.reshape(taken.shape[0], PLANE * size), 0)

    sum_query = columns(0, key_width)
    sum_key = columns(key_width, key_width)
    sum_value = columns(2 * key_width, value_width)
    sum_gate = columns(2 * key_width + value_width, value_width)
    sum_out = columns(2 * key_width + 2 * value_width, value_width).T
    return (
        block_out,
        grad_tokens,
        gain_one,
        bias_one,
        sum_query,
        sum_key,
        sum_value,
        sum_gate,
        sum_out,
        gain_two,
        bias_two,
        sum_up,
        sum_down,
    )


def solution(mesh):
    return jax.shard_map(
        shards,
        mesh=mesh,
        in_specs=(
            P(("seq", "ffn"), None),
            P(),
            P(),
            P("seq", "ffn"),
            P("seq", "ffn"),
            P("seq", "ffn"),
            P("seq", "ffn"),
            P("ffn", "seq"),
            P("seq", "ffn"),
            P(),
            P(),
            P(None, "ffn"),
            P("ffn", None),
            P("seq", None),
        ),
        out_specs=(
            P(("seq", "ffn"), None),
            P(("seq", "ffn"), None),
            P(),
            P(),
            P("seq", "ffn"),
            P("seq", "ffn"),
            P("seq", "ffn"),
            P("seq", "ffn"),
            P("ffn", "seq"),
            P(),
            P(),
            P("seq", "ffn"),
            P("ffn", "seq"),
        ),
        check_vma=False,
    )
```

```python
import functools

import jax
import jax.numpy as jnp
from jax import lax
from jax.experimental import pallas as pl
from jax.experimental.pallas import tpu as pltpu
from jax.sharding import PartitionSpec as P

STRETCH = 512
SEQUENCE_LENGTH = 8192
PLANE = 4
LINE = 4
SPANS = PLANE * LINE
MESH = pl.DeviceIdType.MESH
VMEM_LIMIT = 60 * 1024 * 1024
ANY = pl.BlockSpec(memory_space=pl.ANY)
VM = pl.BlockSpec(memory_space=pltpu.VMEM)
BF16 = jnp.bfloat16
F32 = jnp.float32


class Place:
    def __init__(self):
        s = lax.axis_index("seq")
        self.f = lax.axis_index("ffn")
        lo = s % SPANS
        self.base = s - lo
        self.z = lo // PLANE
        self.p = lo % PLANE

    def plane(self, m):
        return self.at(self.z, self.xor(m), self.f)

    def xor(self, m):
        p = self.p
        low, high = p % 2, p // 2
        if m & 1:
            low = 1 - low
        if m & 2:
            high = 1 - high
        return high * 2 + low

    def at(self, z, p, f):
        return (self.base + z * PLANE + p, f)

    def partner(self):
        return self.at(self.z, self.p, 1 - self.f)

    def up(self):
        return self.at(self.z + 1, self.p, self.f)

    def down(self):
        return self.at(self.z - 1, self.p, self.f)


def greet(peers):
    bar = pltpu.get_barrier_semaphore()
    count = 0
    for device, cond in peers:
        if cond is None:
            pl.semaphore_signal(bar, inc=1, device_id=device, device_id_type=MESH)
            count = count + 1
        else:

            @pl.when(cond)
            def _():
                pl.semaphore_signal(bar, inc=1, device_id=device, device_id_type=MESH)

            count = count + cond.astype(jnp.int32)
    pl.semaphore_wait(bar, count)


def remote(src, dst, send, recv, device):
    return pltpu.make_async_remote_copy(
        src_ref=src, dst_ref=dst, send_sem=send, recv_sem=recv, device_id=device, device_id_type=MESH
    )


def comm_call(kernel, outs, ins, scratch, cid, in_specs=None, out_specs=None):
    return pl.pallas_call(
        kernel,
        out_shape=outs,
        in_specs=in_specs if in_specs is not None else [ANY] * len(ins),
        out_specs=out_specs if out_specs is not None else [ANY] * len(outs),
        scratch_shapes=scratch,
        compiler_params=pltpu.CompilerParams(
            collective_id=cid, has_side_effects=True, vmem_limit_bytes=VMEM_LIMIT
        ),
    )(*ins)


DMA = pltpu.SemaphoreType.DMA


def gather_kernel(widths, rows, *refs):
    count = len(widths)
    xn_ref, dec_ref = refs[:2]
    shards_in = refs[2 : 2 + count]
    xg, decg = refs[2 + count : 4 + count]
    full = refs[4 + count : 4 + 2 * count]
    hold = refs[4 + 2 * count : 4 + 3 * count]
    lsem, psend, precv, usend, dsend, zrecv, xsend, xrecv, csend, crecv, tsend, trecv = refs[4 + 3 * count :]
    me = Place()
    z, p, f = me.z, me.p, me.f
    spot = z * PLANE + p
    chunk = shards_in[0].shape[0]
    deep = chunk * PLANE
    greet(
        [(me.plane(m), None) for m in (1, 2, 3)]
        + [(me.partner(), None), (me.up(), z < LINE - 1), (me.down(), z > 0)]
    )

    def part(i, q):
        w = widths[i]
        if rows[i]:
            return shards_in[i].at[pl.ds(pl.multiple_of(q * w, w), w), :]
        return shards_in[i].at[:, pl.ds(pl.multiple_of(q * w, w), w)]

    def slot(i, ss):
        at = pl.ds(pl.multiple_of(ss * chunk, chunk), chunk)
        return full[i].at[:, at] if rows[i] else full[i].at[at, :]

    def block(i, zz):
        at = pl.ds(pl.multiple_of(zz * deep, deep), deep)
        return full[i].at[:, at] if rows[i] else full[i].at[at, :]

    local, plane, held = [], [], []
    for i in range(count):
        load = pltpu.make_async_copy(part(i, p), hold[i], lsem.at[i])
        load.start()
        held.append(load)
        local.append(pltpu.make_async_copy(hold[i], slot(i, spot), lsem.at[i]))
        sends = []
        for m in (1, 2, 3):
            c = remote(part(i, me.xor(m)), slot(i, spot), psend.at[i, m], precv.at[i, m], me.plane(m))
            c.start()
            sends.append(c)
        plane.append(sends)
    tiny = []
    for m in (1, 2, 3):
        c = remote(dec_ref, decg.at[p], tsend.at[m], trecv.at[m], me.plane(m))
        c.start()
        tiny.append(c)
    dec_own = pltpu.make_async_copy(dec_ref, decg.at[p], lsem.at[count])
    dec_own.start()

    seat = p * 2 + f
    x_own = pltpu.make_async_copy(xn_ref, xg.at[seat], lsem.at[count + 1])
    x_own.start()
    half = xn_ref.shape[0] // 2
    x1 = remote(xn_ref, xg.at[seat], xsend.at[0], xrecv.at[0], me.plane(1))
    x2 = remote(xn_ref, xg.at[seat], xsend.at[1], xrecv.at[1], me.plane(2))
    xc = remote(xn_ref, xg.at[seat], csend.at[0], crecv.at[0], me.partner())
    x1.start()
    x2.start()
    xc.start()

    def up_copy(i, zz):
        return remote(block(i, zz), block(i, zz), usend.at[i, zz], zrecv.at[i, zz], me.up())

    def down_copy(i, zz):
        return remote(block(i, zz), block(i, zz), dsend.at[i, zz], zrecv.at[i, zz], me.down())

    for i in range(count):
        held[i].wait()
        local[i].start()
    for i in range(count):
        local[i].wait()
        for c in plane[i]:
            c.wait_recv()

        @pl.when(z < LINE - 1)
        def _():
            up_copy(i, z).start()

        @pl.when(z > 0)
        def _():
            down_copy(i, z).start()

    seat1, seat2, seat3 = (me.xor(m) * 2 + f for m in (1, 2, 3))
    low, high = pl.ds(0, half), pl.ds(half, half)
    x1.wait_recv()
    g1 = remote(xg.at[seat1, low], xg.at[seat1, low], xsend.at[2], xrecv.at[2], me.plane(2))
    g1.start()
    c1 = remote(xg.at[seat1], xg.at[seat1], csend.at[1], crecv.at[1], me.partner())
    c1.start()
    x2.wait_recv()
    g2 = remote(xg.at[seat2, high], xg.at[seat2, high], xsend.at[3], xrecv.at[3], me.plane(1))
    g2.start()
    c2 = remote(xg.at[seat2], xg.at[seat2], csend.at[2], crecv.at[2], me.partner())
    c2.start()
    g1.wait_recv()
    g2.wait_recv()
    c3 = remote(xg.at[seat3], xg.at[seat3], csend.at[3], crecv.at[3], me.partner())
    c3.start()

    for t in range(1, LINE):
        for i in range(count):

            @pl.when(z - t >= 0)
            def _():
                up_copy(i, z - t).wait_recv()

                @pl.when(z < LINE - 1)
                def _():
                    up_copy(i, z - t).start()

            @pl.when(z + t < LINE)
            def _():
                down_copy(i, z + t).wait_recv()

                @pl.when(z > 0)
                def _():
                    down_copy(i, z + t).start()

    for c in (xc, c1, c2, c3):
        c.wait()
    for c in (x1, x2, g1, g2):
        c.wait_send()
    for c in tiny:
        c.wait()
    dec_own.wait()
    x_own.wait()
    for i in range(count):
        for c in plane[i]:
            c.wait_send()
        for zz in range(LINE):

            @pl.when((z < LINE - 1) & (zz <= z))
            def _():
                up_copy(i, zz).wait_send()

            @pl.when((z > 0) & (zz >= z))
            def _():
                down_copy(i, zz).wait_send()


def gather_in(xn, dec, shards_in, rows, cid):
    count = len(shards_in)
    chunk = shards_in[0].shape[0]
    widths, outs = [], []
    for w, r in zip(shards_in, rows):
        if r:
            widths.append(w.shape[0] // PLANE)
            outs.append(jax.ShapeDtypeStruct((w.shape[0] // PLANE, chunk * SPANS), BF16))
        else:
            widths.append(w.shape[1] // PLANE)
            outs.append(jax.ShapeDtypeStruct((chunk * SPANS, w.shape[1] // PLANE), BF16))
    outs = [
        jax.ShapeDtypeStruct((2 * PLANE,) + xn.shape, BF16),
        jax.ShapeDtypeStruct((PLANE,) + dec.shape, F32),
    ] + outs
    parts = [
        (w.shape[0] // PLANE, chunk) if r else (chunk, w.shape[1] // PLANE)
        for w, r in zip(shards_in, rows)
    ]
    scratch = [pltpu.VMEM(shape, BF16) for shape in parts] + [
        DMA((count + 2,)),
        DMA((count, PLANE)),
        DMA((count, PLANE)),
        DMA((count, LINE)),
        DMA((count, LINE)),
        DMA((count, LINE)),
        DMA((4,)),
        DMA((4,)),
        DMA((4,)),
        DMA((4,)),
        DMA((PLANE,)),
        DMA((PLANE,)),
    ]
    return comm_call(
        functools.partial(gather_kernel, widths, rows),
        outs,
        [xn, dec] + shards_in,
        scratch,
        cid,
        in_specs=[VM] + [ANY] * (count + 1),
    )


def plane_reduce_kernel(x_ref, out, rx0, rx1a, rx1b, rx2a, rx2b, csend, crecv, xsend, xrecv):
    me = Place()
    p, f = me.p, me.f
    greet([(me.plane(1), None), (me.plane(2), None), (me.partner(), None)])
    q = [me.xor(m) for m in range(4)]
    wide = x_ref.shape[-1] // 2
    ca, cb = pl.ds(0, wide), pl.ds(wide, wide)
    order = (3, 1, 2, 0)
    first = []
    for m in order:
        c = remote(x_ref.at[q[m], 1 - f], rx0.at[q[m]], csend.at[m], crecv.at[m], me.partner())
        c.start()
        first.append(c)

    def add(dst, cols, other, others_cols):
        rows = dst.shape[0]

        @pl.loop(0, rows, step=64)
        def _(r):
            at = pl.ds(pl.multiple_of(r, 64), 64)
            dst[at, cols] = (dst[at, cols].astype(F32) + other[at, others_cols].astype(F32)).astype(BF16)

    everything = pl.ds(0, 2 * wide)
    whole = pl.ds(0, wide)
    sends = {}
    for c, m in zip(first, order):
        c.wait_recv()
        add(rx0.at[q[m]], everything, x_ref.at[q[m], f], everything)
        if m & 1:
            k = 0 if m == 3 else 1
            s = remote(rx0.at[q[m], :, ca], rx1a.at[k], xsend.at[k], xrecv.at[k], me.plane(1))
            s.start()
            sends["a", k] = s
        if m & 2:
            k = 0 if m == 3 else 1
            s = remote(rx0.at[q[m], :, cb], rx1b.at[k], xsend.at[2 + k], xrecv.at[2 + k], me.plane(2))
            s.start()
            sends["b", k] = s
    sends["a", 0].wait_recv()
    add(rx1a.at[0], whole, rx0.at[q[2]], ca)
    s2a = remote(rx1a.at[0], rx2a, xsend.at[4], xrecv.at[4], me.plane(2))
    s2a.start()
    sends["b", 0].wait_recv()
    add(rx1b.at[0], whole, rx0.at[q[1]], cb)
    s2b = remote(rx1b.at[0], rx2b, xsend.at[5], xrecv.at[5], me.plane(1))
    s2b.start()
    sends["a", 1].wait_recv()
    sends["b", 1].wait_recv()
    s2a.wait_recv()
    s2b.wait_recv()

    @pl.loop(0, out.shape[0], step=32)
    def _(r):
        at = pl.ds(pl.multiple_of(r, 32), 32)
        out[at, ca] = rx0[q[0], at, ca].astype(F32) + rx1a[1, at, :].astype(F32) + rx2a[at, :].astype(F32)
        out[at, cb] = rx0[q[0], at, cb].astype(F32) + rx1b[1, at, :].astype(F32) + rx2b[at, :].astype(F32)

    for c in first + list(sends.values()) + [s2a, s2b]:
        c.wait_send()


def plane_reduce(x, cid):
    _, _, rows, cols = x.shape
    return comm_call(
        plane_reduce_kernel,
        [jax.ShapeDtypeStruct((rows, cols), F32)],
        [x],
        [
            pltpu.VMEM((PLANE, rows, cols), BF16),
            pltpu.VMEM((2, rows, cols // 2), BF16),
            pltpu.VMEM((2, rows, cols // 2), BF16),
            pltpu.VMEM((rows, cols // 2), BF16),
            pltpu.VMEM((rows, cols // 2), BF16),
            DMA((4,)),
            DMA((4,)),
            DMA((6,)),
            DMA((6,)),
        ],
        cid,
        in_specs=[VM],
        out_specs=[VM],
    )[0]


def nn(a, b):
    return jnp.dot(a, b, preferred_element_type=F32)


def nt(a, b):
    return lax.dot_general(a, b, (((1,), (1,)), ((), ())), preferred_element_type=F32)


def tn(a, b):
    return lax.dot_general(a, b, (((0,), (0,)), ((), ())), preferred_element_type=F32)


def rows_at(r, size):
    return pl.ds(pl.multiple_of(r, size), size)


def add_into(dst, cols, other, other_cols):
    @pl.loop(0, dst.shape[0], step=64)
    def _(r):
        at = rows_at(r, 64)
        dst[at, cols] = (dst[at, cols].astype(F32) + other[at, other_cols].astype(F32)).astype(BF16)


def start(copy):
    copy.start()
    return copy


def ffn_kernel(
    x_ref, tok_ref, gain_ref, bias_ref, wu_ref, wd_ref, cot_ref,
    block_out, resid_grad, gains, da, fu, fd,
    wu, wd, rx0, rx1a, rx1b, rx2a, rx2b, resid, xn, act, dact, du, part, prx, dab, stage,
    lsem, csend, crecv, xsend, xrecv, psend, precv, gsend, grecv, ssem,
):
    me = Place()
    p, f = me.p, me.f
    greet([(me.plane(1), None), (me.plane(2), None), (me.partner(), None)])
    rows, width = tok_ref.shape
    hidden = wu.shape[1]
    q = [me.xor(m) for m in range(4)]
    wide = width // 2
    ca, cb = pl.ds(0, wide), pl.ds(wide, wide)
    everything, whole = pl.ds(0, width), pl.ds(0, wide)
    load_d = start(pltpu.make_async_copy(wd_ref, wd, lsem.at[0]))
    load_u = start(pltpu.make_async_copy(wu_ref, wu, lsem.at[1]))
    order = (3, 1, 2, 0)
    first = [
        start(remote(x_ref.at[q[m], 1 - f], rx0.at[q[m]], csend.at[m], crecv.at[m], me.partner()))
        for m in order
    ]
    sends = {}
    for c, m in zip(first, order):
        c.wait_recv()
        add_into(rx0.at[q[m]], everything, x_ref.at[q[m], f], everything)
        k = 0 if m == 3 else 1
        if m & 1:
            sends["a", k] = start(
                remote(rx0.at[q[m], :, ca], rx1a.at[k], xsend.at[k], xrecv.at[k], me.plane(1))
            )
        if m & 2:
            sends["b", k] = start(
                remote(rx0.at[q[m], :, cb], rx1b.at[k], xsend.at[2 + k], xrecv.at[2 + k], me.plane(2))
            )

    load_d.wait()

    @pl.loop(0, hidden, step=256)
    def _(c):
        at = rows_at(c, 256)
        dact[:, at] = nt(cot_ref[...], wd[at, :])

    sends["a", 0].wait_recv()
    add_into(rx1a.at[0], whole, rx0.at[q[2]], ca)
    s2a = start(remote(rx1a.at[0], rx2a, xsend.at[4], xrecv.at[4], me.plane(2)))
    sends["b", 0].wait_recv()
    add_into(rx1b.at[0], whole, rx0.at[q[1]], cb)
    s2b = start(remote(rx1b.at[0], rx2b, xsend.at[5], xrecv.at[5], me.plane(1)))
    sends["a", 1].wait_recv()
    sends["b", 1].wait_recv()
    load_u.wait()
    s2a.wait_recv()
    s2b.wait_recv()

    mine = f * rows
    theirs = (1 - f) * rows
    step = 32

    @pl.loop(0, rows, step=step)
    def _(r):
        at = rows_at(r, step)
        left = rx0[q[0], at, ca].astype(F32) + rx1a[1, at, :].astype(F32) + rx2a[at, :].astype(F32)
        right = rx0[q[0], at, cb].astype(F32) + rx1b[1, at, :].astype(F32) + rx2b[at, :].astype(F32)
        v = tok_ref[at, :].astype(F32) + jnp.concatenate([left, right], axis=1)
        resid[at, :] = v
        average = jnp.mean(v, axis=1, keepdims=True)
        centered = v - average
        scale = lax.rsqrt(jnp.mean(centered * centered, axis=1, keepdims=True) + 1e-05)
        xn[pl.ds(pl.multiple_of(mine + r, step), step), :] = (
            centered * scale * gain_ref[...] + bias_ref[...]
        ).astype(BF16)

    own_rows = rows_at(mine, rows)
    their_rows = rows_at(theirs, rows)
    swap_x = start(remote(xn.at[own_rows], xn.at[own_rows], psend.at[0], precv.at[0], me.partner()))

    def hidden_part(at_rows):
        @pl.loop(0, hidden, step=512)
        def _(c):
            at = rows_at(c, 512)
            u = nn(xn[at_rows, :], wu[:, at])
            e = 0.5 * (1.0 + lax.erf(u * 0.7071067811865476))
            act[at_rows, at] = (u * e).astype(BF16)
            slope = e + u * jnp.exp(-0.5 * u * u) * 0.3989422804014327
            du[at_rows, at] = (dact[at_rows, at] * slope).astype(BF16)

    hidden_part(own_rows)
    swap_x.wait_recv()
    hidden_part(their_rows)

    @pl.loop(0, width, step=256)
    def _(c):
        at = rows_at(c, 256)
        part[0, :, at] = nt(du[their_rows, :], wu[at, :]).astype(BF16)

    swap_d = start(remote(part.at[0], prx.at[0], psend.at[1], precv.at[1], me.partner()))
    @pl.loop(0, width, step=256)
    def _(c):
        at = rows_at(c, 256)
        resid_grad[:, at] = nt(du[own_rows, :], wu[at, :])

    swap_d.wait_recv()
    gains[...] = jnp.zeros_like(gains)

    @pl.loop(0, rows, step=step)
    def _(r):
        at = rows_at(r, step)
        dx = resid_grad[at, :] + prx[0, at, :].astype(F32)
        v = resid[at, :]
        average = jnp.mean(v, axis=1, keepdims=True)
        centered = v - average
        scale = lax.rsqrt(jnp.mean(centered * centered, axis=1, keepdims=True) + 1e-05)
        hat = centered * scale
        gains[0:1, :] += jnp.sum(dx * hat, axis=0, keepdims=True)
        gains[1:2, :] += jnp.sum(dx, axis=0, keepdims=True)
        g = dx * gain_ref[...]
        back = scale * (
            g - jnp.mean(g, axis=1, keepdims=True) - hat * jnp.mean(g * hat, axis=1, keepdims=True)
        )
        back = back + cot_ref[pl.ds(pl.multiple_of(mine + r, step), step), :].astype(F32)
        resid_grad[at, :] = back
        dab[at, :] = back.astype(BF16)

    half = rows // 2
    low, high = pl.ds(0, half), pl.ds(half, half)
    seat, seat1, seat2, seat3 = (me.xor(m) * 2 + f for m in (0, 1, 2, 3))
    own = start(pltpu.make_async_copy(dab, da.at[seat], lsem.at[2]))
    x1, x2 = [], []
    for k, (h1, h2) in enumerate(((low, high), (high, low))):
        x1.append(start(remote(dab.at[h1], da.at[seat, h1], gsend.at[k], grecv.at[k], me.plane(1))))
        x2.append(
            start(remote(dab.at[h2], da.at[seat, h2], gsend.at[2 + k], grecv.at[2 + k], me.plane(2)))
        )
    to_core = [start(remote(dab, da.at[seat], gsend.at[6], grecv.at[6], me.partner()))]

    @pl.loop(0, width, step=256)
    def _(c):
        at = rows_at(c, 256)
        part[1, :, at] = nn(act[their_rows, :], wd[:, at]).astype(BF16)

    swap_o = start(remote(part.at[1], prx.at[1], psend.at[2], precv.at[2], me.partner()))
    @pl.loop(0, width, step=256)
    def _(c):
        at = rows_at(c, 256)
        resid[:, at] = resid[:, at] + nn(act[own_rows, :], wd[:, at])

    swap_o.wait_recv()

    @pl.loop(0, rows, step=step)
    def _(r):
        at = rows_at(r, step)
        block_out[at, :] = (resid[at, :] + prx[1, at, :].astype(F32)).astype(BF16)

    x1[0].wait_recv()
    g1 = start(remote(da.at[seat1, low], da.at[seat1, low], gsend.at[4], grecv.at[4], me.plane(2)))
    x2[0].wait_recv()
    g2 = start(remote(da.at[seat2, high], da.at[seat2, high], gsend.at[5], grecv.at[5], me.plane(1)))

    def weights_part(left, right, out, base):
        def spill(slot, i):
            return pltpu.make_async_copy(stage.at[slot], out.at[rows_at(i * 256, 256), :], ssem.at[slot])

        @pl.loop(0, width // 256)
        def _(i):
            slot = i % 2

            @pl.when(i >= 2)
            def _():
                spill(slot, i - 2).wait()

            @pl.loop(0, hidden, step=512)
            def _(c):
                at = rows_at(c, 512)
                stage[slot, :, at] = tn(left[:, rows_at(i * 256, 256)], right[:, at]).astype(BF16)

            spill(slot, i).start()

        for k in (2, 1):
            i = width // 256 - k
            spill(i % 2, i).wait()

    weights_part(xn, du, fu, 0)
    x1[1].wait_recv()
    to_core.append(start(remote(da.at[seat1], da.at[seat1], gsend.at[7], grecv.at[7], me.partner())))
    x2[1].wait_recv()
    to_core.append(start(remote(da.at[seat2], da.at[seat2], gsend.at[8], grecv.at[8], me.partner())))
    weights_part(cot_ref, act, fd, 0)
    g1.wait_recv()
    to_core.append(
        start(remote(da.at[seat3, low], da.at[seat3, low], gsend.at[9], grecv.at[9], me.partner()))
    )
    g2.wait_recv()
    to_core.append(
        start(remote(da.at[seat3, high], da.at[seat3, high], gsend.at[10], grecv.at[10], me.partner()))
    )
    for c in to_core:
        c.wait()
    for c in x1 + x2 + [g1, g2, swap_x, swap_d, swap_o, s2a, s2b] + first + list(sends.values()):
        c.wait_send()
    own.wait()


def ffn_part(share, tokens, gain, bias, w_up, w_down, cotangent, cid):
    _, _, rows, width = share.shape
    span, hidden = 2 * rows, w_up.shape[1]
    return comm_call(
        ffn_kernel,
        [
            jax.ShapeDtypeStruct((rows, width), BF16),
            jax.ShapeDtypeStruct((rows, width), F32),
            jax.ShapeDtypeStruct((8, width), F32),
            jax.ShapeDtypeStruct((2 * PLANE, rows, width), BF16),
            jax.ShapeDtypeStruct((width, hidden), BF16),
            jax.ShapeDtypeStruct((width, hidden), BF16),
        ],
        [share, tokens, gain[None], bias[None], w_up, w_down, cotangent],
        [
            pltpu.VMEM(w_up.shape, BF16),
            pltpu.VMEM(w_down.shape, BF16),
            pltpu.VMEM((PLANE, rows, width), BF16),
            pltpu.VMEM((2, rows, width // 2), BF16),
            pltpu.VMEM((2, rows, width // 2), BF16),
            pltpu.VMEM((rows, width // 2), BF16),
            pltpu.VMEM((rows, width // 2), BF16),
            pltpu.VMEM((rows, width), F32),
            pltpu.VMEM((span, width), BF16),
            pltpu.VMEM((span, hidden), BF16),
            pltpu.VMEM((span, hidden), F32),
            pltpu.VMEM((span, hidden), BF16),
            pltpu.VMEM((2, rows, width), BF16),
            pltpu.VMEM((2, rows, width), BF16),
            pltpu.VMEM((rows, width), BF16),
            pltpu.VMEM((2, 256, hidden), BF16),
            DMA((3,)),
            DMA((4,)),
            DMA((4,)),
            DMA((6,)),
            DMA((6,)),
            DMA((3,)),
            DMA((3,)),
            DMA((11,)),
            DMA((11,)),
            DMA((2,)),
        ],
        cid,
        in_specs=[VM, VM, VM, VM, ANY, ANY, VM],
        out_specs=[VM, VM, VM, ANY, ANY, ANY],
    )


def line_states_kernel(backward, x_ref, d_ref, out, dout, lsem, xsend, xrecv, dsend, drecv):
    me = Place()
    z = me.z
    others = [(z + t) % LINE for t in range(1, LINE)]
    greet([(me.at(o, me.p, me.f), None) for o in others])
    own = pltpu.make_async_copy(x_ref, out.at[z], lsem.at[0])
    own.start()
    down = pltpu.make_async_copy(d_ref, dout.at[z], lsem.at[1])
    down.start()

    def pair(step, to, slot):
        sem = step - 1
        device = me.at(to, me.p, me.f)
        return (
            remote(x_ref, out.at[slot], xsend.at[sem], xrecv.at[sem], device),
            remote(d_ref, dout.at[slot], dsend.at[sem], drecv.at[sem], device),
        )

    sign = -1 if backward else 1
    for t in range(1, LINE):
        to, source = z + sign * t, z - sign * t

        @pl.when((to >= 0) & (to < LINE))
        def _():
            for c in pair(t, to, z):
                c.start()

    for t in range(1, LINE):
        to, source = z + sign * t, z - sign * t

        @pl.when((source >= 0) & (source < LINE))
        def _():
            for c in pair(t, source, source):
                c.wait_recv()

        @pl.when((to >= 0) & (to < LINE))
        def _():
            for c in pair(t, to, z):
                c.wait_send()

    own.wait()
    down.wait()


def line_states(x, total, backward, cid):
    sent = jnp.broadcast_to(total, (8, 128))
    got, logs = comm_call(
        functools.partial(line_states_kernel, backward),
        [
            jax.ShapeDtypeStruct((LINE,) + x.shape, x.dtype),
            jax.ShapeDtypeStruct((LINE, 8, 128), F32),
        ],
        [x, sent],
        [DMA((2,)), DMA((3,)), DMA((3,)), DMA((3,)), DMA((3,))],
        cid,
        in_specs=[VM, VM],
    )
    z = (lax.axis_index("seq") % SPANS) // PLANE
    state = jnp.zeros(x.shape, F32)
    for j in reversed(range(LINE)) if backward else range(LINE):
        used = j > z if backward else j < z
        state = jnp.where(used, jnp.exp(logs[j, 0, 0]) * state + got[j].astype(F32), state)
    return state


def everyone(size):
    return range(0, size, SPANS)


def swap(x, mask):
    n = lax.axis_size("seq")
    return lax.ppermute(x, "seq", [(s, s ^ mask) for s in range(n)])


def take(x, index, axis):
    return lax.dynamic_index_in_dim(x, index, axis, False)


def plus(a, b):
    return (a.astype(F32) + b.astype(F32)).astype(BF16)


def line_sum(x, z):
    n = lax.axis_size("seq")
    up = dn = None
    for t in range(1, LINE):
        up_at = jnp.clip(LINE - t + z, 0, LINE - 1)
        dn_at = jnp.clip(z + t - LINE, 0, LINE - 1)
        ups = [
            (b + k * PLANE + p, b + (k + 1) * PLANE + p)
            for b in everyone(n)
            for k in range(t)
            for p in range(PLANE)
        ]
        dns = [
            (b + (LINE - 1 - k) * PLANE + p, b + (LINE - 2 - k) * PLANE + p)
            for b in everyone(n)
            for k in range(t)
            for p in range(PLANE)
        ]
        send_up, send_dn = take(x, up_at, 0), take(x, dn_at, 0)
        if t > 1:
            send_up, send_dn = plus(send_up, up), plus(send_dn, dn)
        up = lax.ppermute(send_up, "seq", ups)
        dn = lax.ppermute(send_dn, "seq", dns)
    return take(x, z, 0).astype(F32) + up.astype(F32) + dn.astype(F32)


def plane_sum(x, p, first):
    here = (p // 2, p % 2)
    if first == 1:
        kept, sent = take(x, here[1], 2), take(x, 1 - here[1], 2)
        x = plus(kept, swap(sent, 1))
        kept, sent = take(x, here[0], 1), take(x, 1 - here[0], 1)
        return plus(kept, swap(sent, 2))
    kept, sent = take(x, here[0], 1), take(x, 1 - here[0], 1)
    x = plus(kept, swap(sent, 2))
    kept, sent = take(x, here[1], 1), take(x, 1 - here[1], 1)
    return plus(kept, swap(sent, 1))


def plane_deal(x, p):
    got = [take(x, p, 0)]
    for mask in range(1, PLANE):
        got.append(swap(take(x, p ^ mask, 0), mask))
    return jnp.stack([sum_of_choice(got, p, q) for q in range(PLANE)])


def sum_of_choice(got, p, q):
    out = got[0]
    for mask in range(1, PLANE):
        out = jnp.where((p ^ q) == mask, got[mask], out)
    return out


def gains_kernel(x_ref, out, rx, send, recv):
    me = Place()
    rounds = [
        [me.partner()],
        [me.plane(m) for m in (1, 2, 3)],
        [me.at((me.z + t) % LINE, me.p, me.f) for t in (1, 2, 3)],
    ]
    greet([(d, None) for r in rounds for d in r])
    out[...] = x_ref[...]
    k = 0
    for peers in rounds:
        copies = []
        for d in peers:
            c = remote(out, rx.at[k], send.at[k], recv.at[k], d)
            c.start()
            copies.append(c)
            k += 1
        for c in copies:
            c.wait()
        for j in range(k - len(peers), k):
            out[...] += rx[j]


def gains_sum(x, cid):
    return comm_call(
        gains_kernel,
        [jax.ShapeDtypeStruct(x.shape, F32)],
        [x],
        [pltpu.VMEM((7,) + x.shape, F32), DMA((7,)), DMA((7,))],
        cid,
        in_specs=[VM],
        out_specs=[VM],
    )[0]


def layer_norm(values_in, gain_vec, bias_vec):
    average = jnp.mean(values_in, axis=-1, keepdims=True)
    centered = values_in - average
    variance = jnp.mean(centered * centered, axis=-1, keepdims=True)
    return centered * lax.rsqrt(variance + 1e-05) * gain_vec + bias_vec


def group_norm(values_in):
    average = jnp.mean(values_in, axis=-1, keepdims=True)
    centered = values_in - average
    variance = jnp.mean(centered * centered, axis=-1, keepdims=True)
    return centered * lax.rsqrt(variance + 1e-05)


def exact_gelu(values_in):
    return jax.nn.gelu(values_in, approximate=False)


def swish_gate(gate_proj, grouped):
    return jax.nn.silu(gate_proj) * grouped


def angles_of(positions, half_width):
    frequency = 10000.0 ** (-jnp.linspace(0.0, 1.0, half_width, dtype=F32))
    angles = positions.astype(F32)[:, None] * frequency[None, :]
    return jnp.cos(angles), jnp.sin(angles)


def rotate(values_in, cosine, sine_part):
    half_width = values_in.shape[-1] // 2
    first_half = values_in[..., :half_width]
    second_half = values_in[..., half_width:]
    return jnp.concatenate(
        [
            first_half * cosine - second_half * sine_part,
            second_half * cosine + first_half * sine_part,
        ],
        axis=-1,
    )


def dot(spec, a, b):
    return jnp.einsum(spec, a, b, preferred_element_type=F32)


def shards(
    tokens,
    ln1_gain,
    ln1_bias,
    w_query,
    w_key,
    w_value,
    w_gate,
    w_out,
    decay_log,
    ln2_gain,
    ln2_bias,
    w_up,
    w_down,
    cotangent,
):
    row_count, width = tokens.shape
    span_rows = cotangent.shape[0]
    heads = decay_log.shape[1]
    repeats = lax.axis_size("seq") // SPANS
    peers = [[lo + SPANS * k for k in range(repeats)] for lo in range(SPANS)]
    narrow = width // (SPANS * repeats)

    def wide_in(w, axis):
        if repeats == 1:
            return w
        return lax.all_gather(w, "seq", axis_index_groups=peers, axis=axis, tiled=True)

    def narrow_out(g, axis):
        if repeats == 1:
            return g
        return lax.psum_scatter(
            g, "seq", scatter_dimension=axis, axis_index_groups=peers, tiled=True
        )

    def features_in(a):
        if repeats == 1:
            return a
        return a.reshape(a.shape[:-1] + (repeats, SPANS, narrow)).swapaxes(-3, -2).reshape(a.shape)

    def features_out(a):
        if repeats == 1:
            return a
        return a.reshape(a.shape[:-1] + (SPANS, repeats, narrow)).swapaxes(-3, -2).reshape(a.shape)

    spot = lax.axis_index("seq") % SPANS
    z, p = spot // PLANE, spot % PLANE
    group_rows = span_rows * PLANE
    blocks = group_rows // STRETCH

    tokens, cotangent, w_down = features_in(tokens), features_in(cotangent), features_in(w_down)
    w_up = features_in(w_up.T).T if repeats > 1 else w_up
    ln1_gain, ln1_bias = features_in(ln1_gain), features_in(ln1_bias)
    ln2_gain, ln2_bias = features_in(ln2_gain), features_in(ln2_bias)
    inputs32 = tokens.astype(F32)
    xn_first, norm1_back = jax.vjp(layer_norm, inputs32, ln1_gain, ln1_bias)
    decays = jnp.pad(decay_log.T, ((0, 8 - heads), (0, 0)))
    xg, decay_rows, key_w, value_w, query_w, gate_w, out_w = gather_in(
        xn_first.astype(BF16),
        decays,
        [
            wide_in(w_key, 0),
            wide_in(w_value, 0),
            wide_in(w_query, 0),
            wide_in(w_gate, 0),
            wide_in(w_out, 1),
        ],
        (False, False, False, False, True),
        0,
    )
    normed = xg.reshape(group_rows, width)
    key_width, value_width = key_w.shape[1], value_w.shape[1]
    log_decay = lax.dynamic_index_in_dim(decay_rows, p, 1, False).reshape(blocks, STRETCH)
    cumulative = jnp.cumsum(log_decay, axis=1)
    last = cumulative[:, -1]
    total = jnp.sum(last)

    positions = (z * group_rows + jnp.arange(group_rows)) % SEQUENCE_LENGTH
    cosine, sine_part = angles_of(positions, key_width // 2)
    q_rot = rotate(dot("td,dq->tq", normed, query_w), cosine, sine_part).astype(BF16)
    k_rot = rotate(dot("td,dq->tq", normed, key_w), cosine, sine_part).astype(BF16)
    value = dot("td,dv->tv", normed, value_w).astype(BF16)
    gate_proj = dot("td,dv->tv", normed, gate_w)

    q_blocks = q_rot.reshape(blocks, STRETCH, key_width)
    k_blocks = k_rot.reshape(blocks, STRETCH, key_width)
    v_blocks = value.reshape(blocks, STRETCH, value_width)
    tail_scale = jnp.exp(last[:, None] - cumulative)
    tail_values = (v_blocks.astype(F32) * tail_scale[:, :, None]).astype(BF16)
    key_values = dot("csk,csd->ckd", k_blocks, tail_values)
    local = [jnp.zeros((key_width, value_width), F32)]
    for c in range(blocks):
        local.append(jnp.exp(last[c]) * local[-1] + key_values[c])
    incoming = line_states(local[-1].astype(BF16), total, False, 1)
    before = jnp.exp(jnp.cumsum(last) - last)
    prev_states = jnp.stack([local[c] + before[c] * incoming for c in range(blocks)]).astype(BF16)

    gaps = cumulative[:, :, None] - cumulative[:, None, :]
    indices = jnp.arange(STRETCH)
    lower = indices[:, None] >= indices[None, :]
    mask = jnp.where(lower[None], jnp.exp(jnp.minimum(gaps, 0.0)), 0.0)
    weighted = (dot("ctk,csk->cts", q_blocks, k_blocks) * mask).astype(BF16)
    q_decayed = (q_blocks.astype(F32) * jnp.exp(cumulative)[:, :, None]).astype(BF16)
    retained = dot("cts,csd->ctd", weighted, v_blocks) + dot("ctk,ckd->ctd", q_decayed, prev_states)
    retained = retained.reshape(group_rows, value_width)
    grouped, group_back = jax.vjp(group_norm, retained)
    gated, gate_back = jax.vjp(swish_gate, gate_proj, grouped)
    gated_low = gated.astype(BF16)
    attn_share = dot("tv,vd->td", gated_low, out_w).astype(BF16)
    block_out, grad_resid, gains_second, grad_attn, grad_up, grad_down = ffn_part(
        attn_share.reshape(PLANE, 2, row_count, width),
        tokens,
        ln2_gain,
        ln2_bias,
        w_up,
        w_down,
        cotangent,
        2,
    )
    split = (LINE, 2, 2, width // SPANS, w_up.shape[1])
    ffn_sum = line_sum(
        jnp.concatenate(
            [plane_sum(grad_up.reshape(split), p, 1), plane_sum(grad_down.reshape(split), p, 2)], axis=-1
        ),
        z,
    )
    sum_up = narrow_out(ffn_sum[:, : w_up.shape[1]], 0)
    sum_down = narrow_out(ffn_sum[:, w_up.shape[1] :], 0).T

    grad_attn = grad_attn.reshape(group_rows, width)
    grad_gated = dot("td,vd->tv", grad_attn, out_w)
    grad_out_w = dot("td,tv->dv", grad_attn, gated_low).astype(BF16)
    grad_gate, grad_grouped = gate_back(grad_gated)
    grad_gate_low = grad_gate.astype(BF16)
    grad_retained = group_back(grad_grouped)[0].astype(BF16)
    grad_blocks = grad_retained.reshape(blocks, STRETCH, value_width)

    query_out = dot("ctk,ctd->ckd", q_decayed, grad_blocks)
    local_grad = jnp.sum(before[:, None, None] * query_out, axis=0)
    outgoing = line_states(local_grad.astype(BF16), total, True, 7)
    after = [outgoing]
    for c in reversed(range(1, blocks)):
        after.append(jnp.exp(last[c]) * after[-1] + query_out[c])
    grad_kv = jnp.stack(after[::-1]).astype(BF16)

    grad_weighted = dot("ctd,csd->cts", grad_blocks, v_blocks)
    grad_scores = (grad_weighted * mask).astype(BF16)
    grad_q = dot("ctd,ckd->ctk", grad_blocks, prev_states) * jnp.exp(cumulative)[:, :, None]
    grad_q = grad_q + dot("cts,csk->ctk", grad_scores, k_blocks)
    grad_k = dot("csd,ckd->csk", tail_values, grad_kv) + dot("cts,ctk->csk", grad_scores, q_blocks)
    grad_v = dot("csk,ckd->csd", k_blocks, grad_kv) * tail_scale[:, :, None]
    grad_v = grad_v + dot("cts,ctd->csd", weighted, grad_blocks)
    grad_query = rotate(grad_q.reshape(group_rows, key_width), cosine, -sine_part).astype(BF16)
    grad_keys = rotate(grad_k.reshape(group_rows, key_width), cosine, -sine_part).astype(BF16)
    grad_values = grad_v.reshape(group_rows, value_width).astype(BF16)

    grad_heads = jnp.concatenate([grad_query, grad_keys, grad_values, grad_gate_low], axis=1)
    grad_qkv = jnp.concatenate([grad_query, grad_keys, grad_values], axis=1)
    heads_w = jnp.concatenate([query_w, key_w, value_w, gate_w], axis=1)
    grad_xn1_share = dot("tq,dq->td", grad_heads, heads_w).astype(BF16)
    grad_heads_w = dot("td,tq->dq", normed, grad_qkv).astype(BF16)
    grad_gate_w = dot("td,tq->dq", normed, grad_gate_low).astype(BF16)
    grad_xn1 = plane_reduce(grad_xn1_share.reshape(PLANE, 2, row_count, width), 8)
    first = jnp.concatenate([grad_gate_w, grad_out_w], axis=1)
    sums = jnp.concatenate(
        [
            plane_deal(line_sum(g.reshape(LINE, PLANE, width // SPANS, -1), z).astype(BF16), p)
            for g in (grad_heads_w, first)
        ],
        axis=-1,
    )
    grad_inputs, grad_gain1, grad_bias1 = norm1_back(grad_xn1)
    grad_tokens = (grad_resid + grad_inputs).astype(BF16)
    gains = jnp.concatenate([grad_gain1[None], grad_bias1[None], gains_second[:6]])
    gains = gains_sum(gains, 10)
    if repeats > 1:
        gains = lax.psum(gains, "seq", axis_index_groups=peers)
    gains = features_out(gains)
    gain_one, bias_one, gain_two, bias_two = gains[0], gains[1], gains[2], gains[3]

    def columns(start, size):
        taken = sums[:, :, start : start + size].astype(F32).swapaxes(0, 1)
        return narrow_out(taken.reshape(taken.shape[0], PLANE * size), 0)

    sum_query = columns(0, key_width)
    sum_key = columns(key_width, key_width)
    sum_value = columns(2 * key_width, value_width)
    sum_gate = columns(2 * key_width + value_width, value_width)
    sum_out = columns(2 * key_width + 2 * value_width, value_width).T
    return (
        features_out(block_out),
        features_out(grad_tokens),
        gain_one,
        bias_one,
        sum_query,
        sum_key,
        sum_value,
        sum_gate,
        sum_out,
        gain_two,
        bias_two,
        sum_up,
        sum_down,
    )


def solution(mesh):
    return jax.shard_map(
        shards,
        mesh=mesh,
        in_specs=(
            P(("seq", "ffn"), None),
            P(),
            P(),
            P("seq", "ffn"),
            P("seq", "ffn"),
            P("seq", "ffn"),
            P("seq", "ffn"),
            P("ffn", "seq"),
            P("seq", "ffn"),
            P(),
            P(),
            P(None, "ffn"),
            P("ffn", None),
            P("seq", None),
        ),
        out_specs=(
            P(("seq", "ffn"), None),
            P(("seq", "ffn"), None),
            P(),
            P(),
            P("seq", "ffn"),
            P("seq", "ffn"),
            P("seq", "ffn"),
            P("seq", "ffn"),
            P("ffn", "seq"),
            P(),
            P(),
            P("seq", "ffn"),
            P("ffn", "seq"),
        ),
        check_vma=False,
    )
```

```python
import functools

import jax
import jax.numpy as jnp
from jax import lax
from jax.experimental import pallas as pl
from jax.experimental.pallas import tpu as pltpu
from jax.sharding import PartitionSpec as P

STRETCH = 512
SEQUENCE_LENGTH = 8192
PLANE = 4
LINE = 4
SPANS = PLANE * LINE
MESH = pl.DeviceIdType.MESH
VMEM_LIMIT = 60 * 1024 * 1024
ANY = pl.BlockSpec(memory_space=pl.ANY)
VM = pl.BlockSpec(memory_space=pltpu.VMEM)
BF16 = jnp.bfloat16
F32 = jnp.float32


class Place:
    def __init__(self):
        s = lax.axis_index("seq")
        self.f = lax.axis_index("ffn")
        lo = s % SPANS
        self.base = s - lo
        self.z = lo // PLANE
        self.p = lo % PLANE

    def plane(self, m):
        return self.at(self.z, self.xor(m), self.f)

    def xor(self, m):
        p = self.p
        low, high = p % 2, p // 2
        if m & 1:
            low = 1 - low
        if m & 2:
            high = 1 - high
        return high * 2 + low

    def at(self, z, p, f):
        return (self.base + z * PLANE + p, f)

    def partner(self):
        return self.at(self.z, self.p, 1 - self.f)

    def up(self):
        return self.at(self.z + 1, self.p, self.f)

    def down(self):
        return self.at(self.z - 1, self.p, self.f)


def greet(peers):
    bar = pltpu.get_barrier_semaphore()
    count = 0
    for device, cond in peers:
        if cond is None:
            pl.semaphore_signal(bar, inc=1, device_id=device, device_id_type=MESH)
            count = count + 1
        else:

            @pl.when(cond)
            def _():
                pl.semaphore_signal(bar, inc=1, device_id=device, device_id_type=MESH)

            count = count + cond.astype(jnp.int32)
    pl.semaphore_wait(bar, count)


def remote(src, dst, send, recv, device):
    return pltpu.make_async_remote_copy(
        src_ref=src, dst_ref=dst, send_sem=send, recv_sem=recv, device_id=device, device_id_type=MESH
    )


def comm_call(kernel, outs, ins, scratch, cid, in_specs=None, out_specs=None):
    return pl.pallas_call(
        kernel,
        out_shape=outs,
        in_specs=in_specs if in_specs is not None else [ANY] * len(ins),
        out_specs=out_specs if out_specs is not None else [ANY] * len(outs),
        scratch_shapes=scratch,
        compiler_params=pltpu.CompilerParams(
            collective_id=cid, has_side_effects=True, vmem_limit_bytes=VMEM_LIMIT
        ),
    )(*ins)


DMA = pltpu.SemaphoreType.DMA


def gather_kernel(widths, rows, *refs):
    count = len(widths)
    xn_ref, dec_ref = refs[:2]
    shards_in = refs[2 : 2 + count]
    xg, decg = refs[2 + count : 4 + count]
    full = refs[4 + count : 4 + 2 * count]
    hold = refs[4 + 2 * count : 4 + 3 * count]
    lsem, psend, precv, usend, dsend, zrecv, xsend, xrecv, csend, crecv, tsend, trecv = refs[4 + 3 * count :]
    me = Place()
    z, p, f = me.z, me.p, me.f
    spot = z * PLANE + p
    chunk = shards_in[0].shape[0]
    deep = chunk * PLANE
    greet(
        [(me.plane(m), None) for m in (1, 2, 3)]
        + [(me.partner(), None), (me.up(), z < LINE - 1), (me.down(), z > 0)]
    )

    def part(i, q):
        w = widths[i]
        if rows[i]:
            return shards_in[i].at[pl.ds(pl.multiple_of(q * w, w), w), :]
        return shards_in[i].at[:, pl.ds(pl.multiple_of(q * w, w), w)]

    def slot(i, ss):
        at = pl.ds(pl.multiple_of(ss * chunk, chunk), chunk)
        return full[i].at[:, at] if rows[i] else full[i].at[at, :]

    def block(i, zz):
        at = pl.ds(pl.multiple_of(zz * deep, deep), deep)
        return full[i].at[:, at] if rows[i] else full[i].at[at, :]

    local, plane, held = [], [], []
    for i in range(count):
        load = pltpu.make_async_copy(part(i, p), hold[i], lsem.at[i])
        load.start()
        held.append(load)
        local.append(pltpu.make_async_copy(hold[i], slot(i, spot), lsem.at[i]))
        sends = []
        for m in (1, 2, 3):
            c = remote(part(i, me.xor(m)), slot(i, spot), psend.at[i, m], precv.at[i, m], me.plane(m))
            c.start()
            sends.append(c)
        plane.append(sends)
    tiny = []
    for m in (1, 2, 3):
        c = remote(dec_ref, decg.at[p], tsend.at[m], trecv.at[m], me.plane(m))
        c.start()
        tiny.append(c)
    dec_own = pltpu.make_async_copy(dec_ref, decg.at[p], lsem.at[count])
    dec_own.start()

    seat = p * 2 + f
    x_own = pltpu.make_async_copy(xn_ref, xg.at[seat], lsem.at[count + 1])
    x_own.start()
    half = xn_ref.shape[0] // 2
    x1 = remote(xn_ref, xg.at[seat], xsend.at[0], xrecv.at[0], me.plane(1))
    x2 = remote(xn_ref, xg.at[seat], xsend.at[1], xrecv.at[1], me.plane(2))
    xc = remote(xn_ref, xg.at[seat], csend.at[0], crecv.at[0], me.partner())
    x1.start()
    x2.start()
    xc.start()

    def up_copy(i, zz):
        return remote(block(i, zz), block(i, zz), usend.at[i, zz], zrecv.at[i, zz], me.up())

    def down_copy(i, zz):
        return remote(block(i, zz), block(i, zz), dsend.at[i, zz], zrecv.at[i, zz], me.down())

    for i in range(count):
        held[i].wait()
        local[i].start()
    for i in range(count):
        local[i].wait()
        for c in plane[i]:
            c.wait_recv()

        @pl.when(z < LINE - 1)
        def _():
            up_copy(i, z).start()

        @pl.when(z > 0)
        def _():
            down_copy(i, z).start()

    seat1, seat2, seat3 = (me.xor(m) * 2 + f for m in (1, 2, 3))
    low, high = pl.ds(0, half), pl.ds(half, half)
    x1.wait_recv()
    g1 = remote(xg.at[seat1, low], xg.at[seat1, low], xsend.at[2], xrecv.at[2], me.plane(2))
    g1.start()
    c1 = remote(xg.at[seat1], xg.at[seat1], csend.at[1], crecv.at[1], me.partner())
    c1.start()
    x2.wait_recv()
    g2 = remote(xg.at[seat2, high], xg.at[seat2, high], xsend.at[3], xrecv.at[3], me.plane(1))
    g2.start()
    c2 = remote(xg.at[seat2], xg.at[seat2], csend.at[2], crecv.at[2], me.partner())
    c2.start()
    g1.wait_recv()
    g2.wait_recv()
    c3 = remote(xg.at[seat3], xg.at[seat3], csend.at[3], crecv.at[3], me.partner())
    c3.start()

    for t in range(1, LINE):
        for i in range(count):

            @pl.when(z - t >= 0)
            def _():
                up_copy(i, z - t).wait_recv()

                @pl.when(z < LINE - 1)
                def _():
                    up_copy(i, z - t).start()

            @pl.when(z + t < LINE)
            def _():
                down_copy(i, z + t).wait_recv()

                @pl.when(z > 0)
                def _():
                    down_copy(i, z + t).start()

    for c in (xc, c1, c2, c3):
        c.wait()
    for c in (x1, x2, g1, g2):
        c.wait_send()
    for c in tiny:
        c.wait()
    dec_own.wait()
    x_own.wait()
    for i in range(count):
        for c in plane[i]:
            c.wait_send()
        for zz in range(LINE):

            @pl.when((z < LINE - 1) & (zz <= z))
            def _():
                up_copy(i, zz).wait_send()

            @pl.when((z > 0) & (zz >= z))
            def _():
                down_copy(i, zz).wait_send()


def gather_in(xn, dec, shards_in, rows, cid):
    count = len(shards_in)
    chunk = shards_in[0].shape[0]
    widths, outs = [], []
    for w, r in zip(shards_in, rows):
        if r:
            widths.append(w.shape[0] // PLANE)
            outs.append(jax.ShapeDtypeStruct((w.shape[0] // PLANE, chunk * SPANS), BF16))
        else:
            widths.append(w.shape[1] // PLANE)
            outs.append(jax.ShapeDtypeStruct((chunk * SPANS, w.shape[1] // PLANE), BF16))
    outs = [
        jax.ShapeDtypeStruct((2 * PLANE,) + xn.shape, BF16),
        jax.ShapeDtypeStruct((PLANE,) + dec.shape, F32),
    ] + outs
    parts = [
        (w.shape[0] // PLANE, chunk) if r else (chunk, w.shape[1] // PLANE)
        for w, r in zip(shards_in, rows)
    ]
    scratch = [pltpu.VMEM(shape, BF16) for shape in parts] + [
        DMA((count + 2,)),
        DMA((count, PLANE)),
        DMA((count, PLANE)),
        DMA((count, LINE)),
        DMA((count, LINE)),
        DMA((count, LINE)),
        DMA((4,)),
        DMA((4,)),
        DMA((4,)),
        DMA((4,)),
        DMA((PLANE,)),
        DMA((PLANE,)),
    ]
    return comm_call(
        functools.partial(gather_kernel, widths, rows),
        outs,
        [xn, dec] + shards_in,
        scratch,
        cid,
        in_specs=[VM] + [ANY] * (count + 1),
    )


def nn(a, b):
    return jnp.dot(a, b, preferred_element_type=F32)


def nt(a, b):
    return lax.dot_general(a, b, (((1,), (1,)), ((), ())), preferred_element_type=F32)


def tn(a, b):
    return lax.dot_general(a, b, (((0,), (0,)), ((), ())), preferred_element_type=F32)


def rows_at(r, size):
    return pl.ds(pl.multiple_of(r, size), size)


def add_into(dst, cols, other, other_cols):
    @pl.loop(0, dst.shape[0], step=64)
    def _(r):
        at = rows_at(r, 64)
        dst[at, cols] = (dst[at, cols].astype(F32) + other[at, other_cols].astype(F32)).astype(BF16)


def start(copy):
    copy.start()
    return copy


def ffn_kernel(
    x_ref, tok_ref, gain_ref, bias_ref, wu_ref, wd_ref, cot_ref,
    block_out, resid_grad, gains, da, fu, fd,
    wu, wd, rx0, rx1a, rx1b, rx2a, rx2b, resid, xn, act, dact, du, part, prx, dab, stage,
    lsem, csend, crecv, xsend, xrecv, psend, precv, gsend, grecv, ssem,
):
    me = Place()
    p, f = me.p, me.f
    greet([(me.plane(1), None), (me.plane(2), None), (me.partner(), None)])
    rows, width = tok_ref.shape
    hidden = wu.shape[1]
    q = [me.xor(m) for m in range(4)]
    wide = width // 2
    ca, cb = pl.ds(0, wide), pl.ds(wide, wide)
    everything, whole = pl.ds(0, width), pl.ds(0, wide)
    load_d = start(pltpu.make_async_copy(wd_ref, wd, lsem.at[0]))
    load_u = start(pltpu.make_async_copy(wu_ref, wu, lsem.at[1]))
    order = (3, 1, 2, 0)
    first = [
        start(remote(x_ref.at[q[m], 1 - f], rx0.at[q[m]], csend.at[m], crecv.at[m], me.partner()))
        for m in order
    ]
    sends = {}
    for c, m in zip(first, order):
        c.wait_recv()
        add_into(rx0.at[q[m]], everything, x_ref.at[q[m], f], everything)
        k = 0 if m == 3 else 1
        if m & 1:
            sends["a", k] = start(
                remote(rx0.at[q[m], :, ca], rx1a.at[k], xsend.at[k], xrecv.at[k], me.plane(1))
            )
        if m & 2:
            sends["b", k] = start(
                remote(rx0.at[q[m], :, cb], rx1b.at[k], xsend.at[2 + k], xrecv.at[2 + k], me.plane(2))
            )

    load_d.wait()

    @pl.loop(0, hidden, step=256)
    def _(c):
        at = rows_at(c, 256)
        dact[:, at] = nt(cot_ref[...], wd[at, :])

    sends["a", 0].wait_recv()
    add_into(rx1a.at[0], whole, rx0.at[q[2]], ca)
    s2a = start(remote(rx1a.at[0], rx2a, xsend.at[4], xrecv.at[4], me.plane(2)))
    sends["b", 0].wait_recv()
    add_into(rx1b.at[0], whole, rx0.at[q[1]], cb)
    s2b = start(remote(rx1b.at[0], rx2b, xsend.at[5], xrecv.at[5], me.plane(1)))
    sends["a", 1].wait_recv()
    sends["b", 1].wait_recv()
    load_u.wait()
    s2a.wait_recv()
    s2b.wait_recv()

    mine = f * rows
    theirs = (1 - f) * rows
    step = 32

    @pl.loop(0, rows, step=step)
    def _(r):
        at = rows_at(r, step)
        left = rx0[q[0], at, ca].astype(F32) + rx1a[1, at, :].astype(F32) + rx2a[at, :].astype(F32)
        right = rx0[q[0], at, cb].astype(F32) + rx1b[1, at, :].astype(F32) + rx2b[at, :].astype(F32)
        v = tok_ref[at, :].astype(F32) + jnp.concatenate([left, right], axis=1)
        resid[at, :] = v
        average = jnp.mean(v, axis=1, keepdims=True)
        centered = v - average
        scale = lax.rsqrt(jnp.mean(centered * centered, axis=1, keepdims=True) + 1e-05)
        xn[pl.ds(pl.multiple_of(mine + r, step), step), :] = (
            centered * scale * gain_ref[...] + bias_ref[...]
        ).astype(BF16)

    own_rows = rows_at(mine, rows)
    their_rows = rows_at(theirs, rows)
    swap_x = start(remote(xn.at[own_rows], xn.at[own_rows], psend.at[0], precv.at[0], me.partner()))

    def hidden_part(at_rows):
        @pl.loop(0, hidden, step=512)
        def _(c):
            at = rows_at(c, 512)
            u = nn(xn[at_rows, :], wu[:, at])
            e = 0.5 * (1.0 + lax.erf(u * 0.7071067811865476))
            act[at_rows, at] = (u * e).astype(BF16)
            slope = e + u * jnp.exp(-0.5 * u * u) * 0.3989422804014327
            du[at_rows, at] = (dact[at_rows, at] * slope).astype(BF16)

    hidden_part(own_rows)
    swap_x.wait_recv()
    hidden_part(their_rows)

    @pl.loop(0, width, step=256)
    def _(c):
        at = rows_at(c, 256)
        part[0, :, at] = nt(du[their_rows, :], wu[at, :]).astype(BF16)

    swap_d = start(remote(part.at[0], prx.at[0], psend.at[1], precv.at[1], me.partner()))
    @pl.loop(0, width, step=256)
    def _(c):
        at = rows_at(c, 256)
        resid_grad[:, at] = nt(du[own_rows, :], wu[at, :])

    swap_d.wait_recv()
    gains[...] = jnp.zeros_like(gains)

    @pl.loop(0, rows, step=step)
    def _(r):
        at = rows_at(r, step)
        dx = resid_grad[at, :] + prx[0, at, :].astype(F32)
        v = resid[at, :]
        average = jnp.mean(v, axis=1, keepdims=True)
        centered = v - average
        scale = lax.rsqrt(jnp.mean(centered * centered, axis=1, keepdims=True) + 1e-05)
        hat = centered * scale
        gains[0:1, :] += jnp.sum(dx * hat, axis=0, keepdims=True)
        gains[1:2, :] += jnp.sum(dx, axis=0, keepdims=True)
        g = dx * gain_ref[...]
        back = scale * (
            g - jnp.mean(g, axis=1, keepdims=True) - hat * jnp.mean(g * hat, axis=1, keepdims=True)
        )
        back = back + cot_ref[pl.ds(pl.multiple_of(mine + r, step), step), :].astype(F32)
        resid_grad[at, :] = back
        dab[at, :] = back.astype(BF16)

    half = rows // 2
    low, high = pl.ds(0, half), pl.ds(half, half)
    seat, seat1, seat2, seat3 = (me.xor(m) * 2 + f for m in (0, 1, 2, 3))
    own = start(pltpu.make_async_copy(dab, da.at[seat], lsem.at[2]))
    x1, x2 = [], []
    for k, (h1, h2) in enumerate(((low, high), (high, low))):
        x1.append(start(remote(dab.at[h1], da.at[seat, h1], gsend.at[k], grecv.at[k], me.plane(1))))
        x2.append(
            start(remote(dab.at[h2], da.at[seat, h2], gsend.at[2 + k], grecv.at[2 + k], me.plane(2)))
        )
    to_core = [start(remote(dab, da.at[seat], gsend.at[6], grecv.at[6], me.partner()))]

    @pl.loop(0, width, step=256)
    def _(c):
        at = rows_at(c, 256)
        part[1, :, at] = nn(act[their_rows, :], wd[:, at]).astype(BF16)

    swap_o = start(remote(part.at[1], prx.at[1], psend.at[2], precv.at[2], me.partner()))
    @pl.loop(0, width, step=256)
    def _(c):
        at = rows_at(c, 256)
        resid[:, at] = resid[:, at] + nn(act[own_rows, :], wd[:, at])

    swap_o.wait_recv()

    @pl.loop(0, rows, step=step)
    def _(r):
        at = rows_at(r, step)
        block_out[at, :] = (resid[at, :] + prx[1, at, :].astype(F32)).astype(BF16)

    x1[0].wait_recv()
    g1 = start(remote(da.at[seat1, low], da.at[seat1, low], gsend.at[4], grecv.at[4], me.plane(2)))
    x2[0].wait_recv()
    g2 = start(remote(da.at[seat2, high], da.at[seat2, high], gsend.at[5], grecv.at[5], me.plane(1)))

    def weights_part(left, right, out, base):
        def spill(slot, i):
            return pltpu.make_async_copy(stage.at[slot], out.at[rows_at(i * 256, 256), :], ssem.at[slot])

        @pl.loop(0, width // 256)
        def _(i):
            slot = i % 2

            @pl.when(i >= 2)
            def _():
                spill(slot, i - 2).wait()

            @pl.loop(0, hidden, step=512)
            def _(c):
                at = rows_at(c, 512)
                stage[slot, :, at] = tn(left[:, rows_at(i * 256, 256)], right[:, at]).astype(BF16)

            spill(slot, i).start()

        for k in (2, 1):
            i = width // 256 - k
            spill(i % 2, i).wait()

    weights_part(xn, du, fu, 0)
    x1[1].wait_recv()
    to_core.append(start(remote(da.at[seat1], da.at[seat1], gsend.at[7], grecv.at[7], me.partner())))
    x2[1].wait_recv()
    to_core.append(start(remote(da.at[seat2], da.at[seat2], gsend.at[8], grecv.at[8], me.partner())))
    weights_part(cot_ref, act, fd, 0)
    g1.wait_recv()
    to_core.append(
        start(remote(da.at[seat3, low], da.at[seat3, low], gsend.at[9], grecv.at[9], me.partner()))
    )
    g2.wait_recv()
    to_core.append(
        start(remote(da.at[seat3, high], da.at[seat3, high], gsend.at[10], grecv.at[10], me.partner()))
    )
    for c in to_core:
        c.wait()
    for c in x1 + x2 + [g1, g2, swap_x, swap_d, swap_o, s2a, s2b] + first + list(sends.values()):
        c.wait_send()
    own.wait()


def ffn_part(share, tokens, gain, bias, w_up, w_down, cotangent, cid):
    _, _, rows, width = share.shape
    span, hidden = 2 * rows, w_up.shape[1]
    return comm_call(
        ffn_kernel,
        [
            jax.ShapeDtypeStruct((rows, width), BF16),
            jax.ShapeDtypeStruct((rows, width), F32),
            jax.ShapeDtypeStruct((8, width), F32),
            jax.ShapeDtypeStruct((2 * PLANE, rows, width), BF16),
            jax.ShapeDtypeStruct((width, hidden), BF16),
            jax.ShapeDtypeStruct((width, hidden), BF16),
        ],
        [share, tokens, gain[None], bias[None], w_up, w_down, cotangent],
        [
            pltpu.VMEM(w_up.shape, BF16),
            pltpu.VMEM(w_down.shape, BF16),
            pltpu.VMEM((PLANE, rows, width), BF16),
            pltpu.VMEM((2, rows, width // 2), BF16),
            pltpu.VMEM((2, rows, width // 2), BF16),
            pltpu.VMEM((rows, width // 2), BF16),
            pltpu.VMEM((rows, width // 2), BF16),
            pltpu.VMEM((rows, width), F32),
            pltpu.VMEM((span, width), BF16),
            pltpu.VMEM((span, hidden), BF16),
            pltpu.VMEM((span, hidden), F32),
            pltpu.VMEM((span, hidden), BF16),
            pltpu.VMEM((2, rows, width), BF16),
            pltpu.VMEM((2, rows, width), BF16),
            pltpu.VMEM((rows, width), BF16),
            pltpu.VMEM((2, 256, hidden), BF16),
            DMA((3,)),
            DMA((4,)),
            DMA((4,)),
            DMA((6,)),
            DMA((6,)),
            DMA((3,)),
            DMA((3,)),
            DMA((11,)),
            DMA((11,)),
            DMA((2,)),
        ],
        cid,
        in_specs=[VM, VM, VM, VM, ANY, ANY, VM],
        out_specs=[VM, VM, VM, ANY, ANY, ANY],
    )


def line_states_kernel(backward, x_ref, d_ref, out, dout, lsem, xsend, xrecv, dsend, drecv):
    me = Place()
    z = me.z
    others = [(z + t) % LINE for t in range(1, LINE)]
    greet([(me.at(o, me.p, me.f), None) for o in others])
    own = pltpu.make_async_copy(x_ref, out.at[z], lsem.at[0])
    own.start()
    down = pltpu.make_async_copy(d_ref, dout.at[z], lsem.at[1])
    down.start()

    def pair(step, to, slot):
        sem = step - 1
        device = me.at(to, me.p, me.f)
        return (
            remote(x_ref, out.at[slot], xsend.at[sem], xrecv.at[sem], device),
            remote(d_ref, dout.at[slot], dsend.at[sem], drecv.at[sem], device),
        )

    sign = -1 if backward else 1
    for t in range(1, LINE):
        to, source = z + sign * t, z - sign * t

        @pl.when((to >= 0) & (to < LINE))
        def _():
            for c in pair(t, to, z):
                c.start()

    for t in range(1, LINE):
        to, source = z + sign * t, z - sign * t

        @pl.when((source >= 0) & (source < LINE))
        def _():
            for c in pair(t, source, source):
                c.wait_recv()

        @pl.when((to >= 0) & (to < LINE))
        def _():
            for c in pair(t, to, z):
                c.wait_send()

    own.wait()
    down.wait()


def line_states(x, total, backward, cid):
    sent = jnp.broadcast_to(total, (8, 128))
    got, logs = comm_call(
        functools.partial(line_states_kernel, backward),
        [
            jax.ShapeDtypeStruct((LINE,) + x.shape, x.dtype),
            jax.ShapeDtypeStruct((LINE, 8, 128), F32),
        ],
        [x, sent],
        [DMA((2,)), DMA((3,)), DMA((3,)), DMA((3,)), DMA((3,))],
        cid,
        in_specs=[VM, VM],
    )
    z = (lax.axis_index("seq") % SPANS) // PLANE
    state = jnp.zeros(x.shape, F32)
    for j in reversed(range(LINE)) if backward else range(LINE):
        used = j > z if backward else j < z
        state = jnp.where(used, jnp.exp(logs[j, 0, 0]) * state + got[j].astype(F32), state)
    return state


class LineSum:
    def __init__(self, me, own, rx, usend, urecv, dsend, drecv, add):
        self.me, self.own, self.rx, self.add = me, own, rx, add
        self.sems = usend, urecv, dsend, drecv

    def up(self, src, zz):
        return remote(src, self.rx.at[zz], self.sems[0].at[zz], self.sems[1].at[zz], self.me.up())

    def down(self, src, zz):
        slot = jnp.where(zz == self.me.z - 1, LINE, zz)
        return remote(src, self.rx.at[slot], self.sems[2].at[zz], self.sems[3].at[zz], self.me.down())

    def begin(self):
        for zz in reversed(range(1, LINE)):

            @pl.when(self.me.z == 0)
            def _():
                self.up(self.own(zz), zz).start()

            @pl.when(self.me.z == LINE - 1)
            def _():
                self.down(self.own(LINE - 1 - zz), LINE - 1 - zz).start()

    def step(self, t):
        z = self.me.z
        zu, zd = LINE - 1 - t, t

        @pl.when((z > 0) & (z < zu))
        def _():
            self.up(self.own(zu), zu).wait_recv()
            self.add(self.rx.at[zu], self.own(zu))
            self.up(self.rx.at[zu], zu).start()

        @pl.when((z < LINE - 1) & (z > zd))
        def _():
            self.down(self.own(zd), zd).wait_recv()
            self.add(self.rx.at[zd], self.own(zd))
            self.down(self.rx.at[zd], zd).start()

    def arrive(self):
        z = self.me.z

        @pl.when(z > 0)
        def _():
            self.up(self.own(z), z).wait_recv()

        @pl.when(z < LINE - 1)
        def _():
            self.down(self.own(z), z).wait_recv()

    def finish(self):
        z = self.me.z
        for zz in range(LINE):

            @pl.when((z < LINE - 1) & (zz > z))
            def _():
                self.up(self.own(zz), zz).wait_send()

            @pl.when((z > 0) & (zz < z))
            def _():
                self.down(self.own(zz), zz).wait_send()


def add_rows(dst, src):
    rows = dst.shape[0]
    step = 32 if dst.shape[1] > 512 else 128

    @pl.loop(0, rows, step=step)
    def _(r):
        at = rows_at(r, step)
        dst[at, :] = (dst[at, :].astype(F32) + src[at, :].astype(F32)).astype(BF16)


def total_rows(z, dst, own, rx):
    rows = dst.shape[0]
    step = 32 if dst.shape[1] > 512 else 128

    @pl.loop(0, rows, step=step)
    def _(r):
        at = rows_at(r, step)
        v = own[at, :].astype(F32)
        v = v + jnp.where(z > 0, rx[z, at, :].astype(F32), 0.0)
        v = v + jnp.where(z < LINE - 1, rx[LINE, at, :].astype(F32), 0.0)
        dst[at, :] = v.astype(dst.dtype)


def line_sems():
    return [DMA((LINE,)) for _ in range(4)]


def retention_back_kernel(
    da_ref, wo_ref, gated_ref, gate_ref, ret_ref, q_ref, k_ref, v_ref, s_ref, cos_ref, sin_ref,
    ccol_ref, crow_ref, scal_ref, xg_ref, fu_ref, fd_ref,
    dh, sums, f1,
    da, wo, gated, gr, q, k, v, st, cos, sin, dr, xt, ao, ag, rxo, rxg, fin, qo, gb, lg, got, logs, rxf, fo, pbuf, gbuf,
    lsem, gsem, xsem, fsend, frecv, osem, fosem, ssend, srecv, lsend, lrecv, psend, precv, *line,
):
    me = Place()
    z, p = me.z, me.p
    greet(
        [(me.plane(m), None) for m in (1, 2, 3)]
        + [(me.at((z + t) % LINE, p, me.f), None) for t in range(1, LINE)]
    )
    width = da.shape[1]
    tokens = da.shape[0]
    keys, values = q.shape[1], v.shape[1]
    blocks = tokens // STRETCH
    half = keys // 2
    pq = [me.xor(m) for m in range(4)]
    chunk = fu_ref.shape[0] // SPANS

    def f_block(h, zp, place):
        return (fu_ref, fd_ref)[h].at[pl.ds(pl.multiple_of((zp * PLANE + place) * chunk, chunk), chunk), :]

    away = ((1, 3), (2, 3))
    kept = ((0, 2), (0, 1))
    nbr = (1, 2)

    def f_copy(h, zp, j):
        return remote(
            f_block(h, zp, pq[away[h][j]]), rxf.at[h, zp, j], fsend.at[h, zp, j], frecv.at[h, zp, j], me.plane(nbr[h])
        )

    loads = [
        start(pltpu.make_async_copy(a, b, lsem.at[i]))
        for i, (a, b) in enumerate(
            [(da_ref, da), (gated_ref, gated), (wo_ref, wo), (q_ref, q), (k_ref, k), (v_ref, v), (s_ref, st),
             (cos_ref, cos), (sin_ref, sin)]
        )
    ]
    for zp in range(LINE):
        for h in range(2):
            for j in range(2):
                f_copy(h, zp, j).start()

    def f_own(u):
        h, zp = u % 2, u // 2
        return [
            pltpu.make_async_copy(f_block(h, zp, pq[kept[h][j]]), fo.at[u % 2, j], fosem.at[u % 2, j])
            for j in range(2)
        ]

    def f_out(u):
        h, zp = u % 2, u // 2
        return pltpu.make_async_copy(rxf.at[h, zp], f1.at[h, zp], osem.at[u])

    for u in range(2):
        for c in f_own(u):
            c.start()

    def f_unit(u):
        h, zp = u % 2, u // 2
        for j, c in enumerate(f_own(u)):
            c.wait()
            f_copy(h, zp, j).wait_recv()
            add_rows(rxf.at[h, zp, j], fo.at[u % 2, j])
        f_out(u).start()
        if u + 2 < 2 * LINE:
            for c in f_own(u + 2):
                c.start()

    def tile_rows(i):
        return rows_at(i * 256, 256)

    def gate_loads(i):
        at = tile_rows(i)
        slot = i % 2
        return (
            pltpu.make_async_copy(gate_ref.at[at, :], gr.at[slot, 0], gsem.at[slot, 0]),
            pltpu.make_async_copy(ret_ref.at[at, :], gr.at[slot, 1], gsem.at[slot, 1]),
        )

    for c in gate_loads(0):
        c.start()

    out_sum = LineSum(me, lambda zz: ao.at[rows_at(zz * (width // LINE), width // LINE), :], rxo, *line[:4], add_rows)
    gate_sum = LineSum(me, lambda zz: ag.at[rows_at(zz * (width // LINE), width // LINE), :], rxg, *line[4:], add_rows)

    loads[0].wait()
    loads[1].wait()

    @pl.loop(0, width, step=256)
    def _(i):
        at = rows_at(i, 256)
        ao[at, :] = tn(da[:, at], gated[...]).astype(BF16)

    out_sum.begin()
    for c in loads[2:]:
        c.wait()

    tiles = tokens // 256

    @pl.loop(0, tiles)
    def _(i):
        @pl.when(i + 1 < tiles)
        def _():
            for c in gate_loads(i + 1):
                c.start()

        for c in gate_loads(i):
            c.wait()
        at = tile_rows(i)
        slot = i % 2
        dgated = nt(da[at, :], wo[...])
        gate = gr[slot, 0]
        ret = gr[slot, 1]
        centered = ret - jnp.mean(ret, axis=1, keepdims=True)
        scale = lax.rsqrt(jnp.mean(centered * centered, axis=1, keepdims=True) + 1e-05)
        grouped = centered * scale
        sig = 1.0 / (1.0 + jnp.exp(-gate))
        silu = gate * sig
        dh[at, 2 * keys + values :] = (dgated * grouped * (sig * (1.0 + gate * (1.0 - sig)))).astype(BF16)
        dg = dgated * silu
        dr[at, :] = (
            scale * (dg - jnp.mean(dg, axis=1, keepdims=True) - grouped * jnp.mean(dg * grouped, axis=1, keepdims=True))
        ).astype(BF16)

    lg[...] = jnp.zeros_like(lg)

    @pl.loop(0, blocks)
    def _(c):
        at = rows_at(c * STRETCH, STRETCH)
        decayed = (q[at, :].astype(F32) * jnp.exp(ccol_ref[at, :])).astype(BF16)
        got_q = tn(decayed, dr[at, :])
        qo[c] = got_q
        lg[...] += scal_ref[blocks + c, 0:1, 0:1] * got_q

    gb[0] = lg[...].astype(BF16)

    def state_copies(t, to, slot):
        device = me.at(to, p, me.f)
        return (
            remote(gb.at[0], got.at[slot], ssend.at[t - 1], srecv.at[t - 1], device),
            remote(scal_ref.at[2 * blocks], logs.at[slot], lsend.at[t - 1], lrecv.at[t - 1], device),
        )

    for t in range(1, LINE):

        @pl.when(z - t >= 0)
        def _():
            for c in state_copies(t, z - t, z):
                c.start()

    def x_tile(i):
        return pltpu.make_async_copy(xg_ref.at[:, rows_at(i * 256, 256)], xt.at[i % 2], xsem.at[i % 2])

    x_tile(0).start()

    @pl.loop(0, width // 256)
    def _(i):
        @pl.when(i + 1 < width // 256)
        def _():
            x_tile(i + 1).start()

        x_tile(i).wait()
        ag[rows_at(i * 256, 256), :] = tn(xt[i % 2], dh[:, 2 * keys + values :]).astype(BF16)

    gate_sum.begin()
    out_sum.step(0)
    f_unit(0)
    f_unit(1)
    out_sum.step(1)

    for t in range(1, LINE):

        @pl.when(z + t < LINE)
        def _():
            for c in state_copies(t, z + t, z + t):
                c.wait_recv()

        @pl.when(z - t >= 0)
        def _():
            for c in state_copies(t, z - t, z):
                c.wait_send()

    lg[...] = jnp.zeros_like(lg)
    for j in reversed(range(1, LINE)):

        @pl.when(z < j)
        def _():
            lg[...] = lg[...] * jnp.exp(logs[j, 0:1, 0:1]) + got[j].astype(F32)

    for c in reversed(range(blocks)):
        gb[c] = lg[...].astype(BF16)
        if c:
            lg[...] = lg[...] * scal_ref[c, 0:1, 0:1] + qo[c]

    t_size = 256

    @pl.loop(0, blocks)
    def _(c):
        blk = rows_at(c * STRETCH, STRETCH)
        row = crow_ref[c, 0:1, :]
        end = crow_ref[c, 0:1, STRETCH - 1 : STRETCH]
        for r in range(0, STRETCH, t_size):
            at = rows_at(c * STRETCH + r, t_size)
            col = ccol_ref[at, :]
            t_index = lax.broadcasted_iota(jnp.int32, (t_size, STRETCH), 0) + r
            s_index = lax.broadcasted_iota(jnp.int32, (t_size, STRETCH), 1)
            mask = jnp.where(t_index >= s_index, jnp.exp(jnp.minimum(col - row, 0.0)), 0.0)
            pbuf[r : r + t_size, :] = (nt(q[at, :], k[blk, :]) * mask).astype(BF16)
            g = (nt(dr[at, :], v[blk, :]) * mask).astype(BF16)
            gbuf[r : r + t_size, :] = g
            dq = nt(dr[at, :], st[c]) * jnp.exp(col) + nn(g, k[blk, :])
            a, b = dq[:, :half], dq[:, half:]
            dh[at, :half] = (a * cos[at, :] + b * sin[at, :]).astype(BF16)
            dh[at, half:keys] = (b * cos[at, :] - a * sin[at, :]).astype(BF16)
        for r in range(0, STRETCH, t_size):
            at = rows_at(c * STRETCH + r, t_size)
            tail = jnp.exp(end - ccol_ref[at, :])
            w = (v[at, :].astype(F32) * tail).astype(BF16)
            dk = nt(w, gb[c]) + tn(gbuf[:, r : r + t_size], q[blk, :])
            a, b = dk[:, :half], dk[:, half:]
            dh[at, keys : keys + half] = (a * cos[at, :] + b * sin[at, :]).astype(BF16)
            dh[at, keys + half : 2 * keys] = (b * cos[at, :] - a * sin[at, :]).astype(BF16)
            dv = nn(k[at, :], gb[c]) * tail + tn(pbuf[:, r : r + t_size], dr[blk, :])
            dh[at, 2 * keys : 2 * keys + values] = dv.astype(BF16)

    plane = []

    def deal(i, chain, a):
        chain.arrive()
        total_rows(z, fin.at[i], a.at[rows_at(z * (width // LINE), width // LINE), :], chain.rx)
        cols = pl.ds(i * values, values)
        for m in (1, 2, 3):
            plane.append(
                start(
                    remote(
                        fin.at[i, rows_at(pq[m] * chunk, chunk), :], sums.at[p, :, cols],
                        psend.at[i, m], precv.at[i, m], me.plane(m),
                    )
                )
            )
        plane.append(
            start(
                pltpu.make_async_copy(
                    fin.at[i, rows_at(p * chunk, chunk), :], sums.at[p, :, cols], psend.at[i, 0]
                )
            )
        )

    out_sum.step(2)
    for u in range(2, 4):
        f_unit(u)
    gate_sum.step(0)
    deal(0, out_sum, ao)
    gate_sum.step(1)
    for u in range(4, 6):
        f_unit(u)
    gate_sum.step(2)
    deal(1, gate_sum, ag)
    for u in range(6, 2 * LINE):
        f_unit(u)
    for c in plane:
        c.wait()
    out_sum.finish()
    gate_sum.finish()
    for u in range(2 * LINE):
        f_out(u).wait()
    for zp in range(LINE):
        for h in range(2):
            for j in range(2):
                f_copy(h, zp, j).wait_send()


def retention_back(da, wo, gated, gate, ret, q, k, v, states, cos, sin, ccol, crow, scal, xg, fu, fd, cid):
    tokens, width = da.shape
    keys, values = q.shape[1], v.shape[1]
    chunk = width // SPANS
    blocks = tokens // STRETCH
    hidden = fu.shape[1]
    deep = width // LINE
    return comm_call(
        retention_back_kernel,
        [
            jax.ShapeDtypeStruct((tokens, 2 * keys + 2 * values), BF16),
            jax.ShapeDtypeStruct((PLANE, chunk, 2 * values), BF16),
            jax.ShapeDtypeStruct((2, LINE, 2, chunk, hidden), BF16),
        ],
        [da, wo, gated, gate, ret, q, k, v, states, cos, sin, ccol, crow, scal, xg, fu, fd],
        [
            pltpu.VMEM((tokens, width), BF16),
            pltpu.VMEM(wo.shape, BF16),
            pltpu.VMEM(gated.shape, BF16),
            pltpu.VMEM((2, 2, 256, values), F32),
            pltpu.VMEM(q.shape, BF16),
            pltpu.VMEM(k.shape, BF16),
            pltpu.VMEM(v.shape, BF16),
            pltpu.VMEM(states.shape, BF16),
            pltpu.VMEM(cos.shape, F32),
            pltpu.VMEM(sin.shape, F32),
            pltpu.VMEM((tokens, values), BF16),
            pltpu.VMEM((2, tokens, 256), BF16),
            pltpu.VMEM((width, values), BF16),
            pltpu.VMEM((width, values), BF16),
            pltpu.VMEM((LINE + 1, deep, values), BF16),
            pltpu.VMEM((LINE + 1, deep, values), BF16),
            pltpu.VMEM((2, deep, values), BF16),
            pltpu.VMEM((blocks, keys, values), F32),
            pltpu.VMEM((blocks, keys, values), BF16),
            pltpu.VMEM((keys, values), F32),
            pltpu.VMEM((LINE, keys, values), BF16),
            pltpu.VMEM((LINE, 8, 128), F32),
            pltpu.VMEM((2, LINE, 2, chunk, hidden), BF16),
            pltpu.VMEM((2, 2, chunk, hidden), BF16),
            pltpu.VMEM((STRETCH, STRETCH), BF16),
            pltpu.VMEM((STRETCH, STRETCH), BF16),
            DMA((9,)),
            DMA((2, 2)),
            DMA((2,)),
            DMA((2, LINE, 2)),
            DMA((2, LINE, 2)),
            DMA((2 * LINE,)),
            DMA((2, 2)),
            DMA((LINE - 1,)),
            DMA((LINE - 1,)),
            DMA((LINE - 1,)),
            DMA((LINE - 1,)),
            DMA((2, PLANE)),
            DMA((2, PLANE)),
        ]
        + line_sems()
        + line_sems(),
        cid,
        in_specs=[ANY] * 11 + [VM] * 3 + [ANY] * 3,
        out_specs=[VM, ANY, ANY],
    )


class LineSum:
    def __init__(self, me, own, rx, usend, urecv, dsend, drecv, add):
        self.me, self.own, self.rx, self.add = me, own, rx, add
        self.sems = usend, urecv, dsend, drecv

    def up(self, src, zz):
        return remote(src, self.rx.at[zz], self.sems[0].at[zz], self.sems[1].at[zz], self.me.up())

    def down(self, src, zz):
        slot = jnp.where(zz == self.me.z - 1, LINE, zz)
        return remote(src, self.rx.at[slot], self.sems[2].at[zz], self.sems[3].at[zz], self.me.down())

    def begin(self):
        for zz in reversed(range(1, LINE)):

            @pl.when(self.me.z == 0)
            def _():
                self.up(self.own(zz), zz).start()

            @pl.when(self.me.z == LINE - 1)
            def _():
                self.down(self.own(LINE - 1 - zz), LINE - 1 - zz).start()

    def step(self, t):
        z = self.me.z
        zu, zd = LINE - 1 - t, t

        @pl.when((z > 0) & (z < zu))
        def _():
            self.up(self.own(zu), zu).wait_recv()
            self.add(self.rx.at[zu], self.own(zu))
            self.up(self.rx.at[zu], zu).start()

        @pl.when((z < LINE - 1) & (z > zd))
        def _():
            self.down(self.own(zd), zd).wait_recv()
            self.add(self.rx.at[zd], self.own(zd))
            self.down(self.rx.at[zd], zd).start()

    def arrive(self):
        z = self.me.z

        @pl.when(z > 0)
        def _():
            self.up(self.own(z), z).wait_recv()

        @pl.when(z < LINE - 1)
        def _():
            self.down(self.own(z), z).wait_recv()

    def finish(self):
        z = self.me.z
        for zz in range(LINE):

            @pl.when((z < LINE - 1) & (zz > z))
            def _():
                self.up(self.own(zz), zz).wait_send()

            @pl.when((z > 0) & (zz < z))
            def _():
                self.down(self.own(zz), zz).wait_send()


def add_rows(dst, src):
    rows = dst.shape[0]
    step = 32 if dst.shape[1] > 512 else 128

    @pl.loop(0, rows, step=step)
    def _(r):
        at = rows_at(r, step)
        dst[at, :] = (dst[at, :].astype(F32) + src[at, :].astype(F32)).astype(BF16)


def total_rows(z, dst, own, rx):
    rows = dst.shape[0]
    step = 32 if dst.shape[1] > 512 else 128

    @pl.loop(0, rows, step=step)
    def _(r):
        at = rows_at(r, step)
        v = own[at, :].astype(F32)
        v = v + jnp.where(z > 0, rx[z, at, :].astype(F32), 0.0)
        v = v + jnp.where(z < LINE - 1, rx[LINE, at, :].astype(F32), 0.0)
        dst[at, :] = v.astype(dst.dtype)


def line_sems():
    return [DMA((LINE,)) for _ in range(4)]


def retention_back_kernel(
    da_ref, wo_ref, gated_ref, gate_ref, ret_ref, q_ref, k_ref, v_ref, s_ref, cos_ref, sin_ref,
    ccol_ref, crow_ref, scal_ref, xg_ref, fu_ref, fd_ref,
    dh, sums, f1,
    da, wo, gated, gr, q, k, v, st, cos, sin, dr, xt, ao, ag, rxo, rxg, fin, qo, gb, lg, got, logs, rxf, fo, pbuf, gbuf,
    lsem, gsem, xsem, fsend, frecv, osem, fosem, ssend, srecv, lsend, lrecv, psend, precv, *line,
):
    me = Place()
    z, p = me.z, me.p
    greet(
        [(me.plane(m), None) for m in (1, 2, 3)]
        + [(me.at((z + t) % LINE, p, me.f), None) for t in range(1, LINE)]
    )
    width = da.shape[1]
    tokens = da.shape[0]
    keys, values = q.shape[1], v.shape[1]
    blocks = tokens // STRETCH
    half = keys // 2
    pq = [me.xor(m) for m in range(4)]
    chunk = fu_ref.shape[0] // SPANS

    def f_block(h, zp, place):
        return (fu_ref, fd_ref)[h].at[pl.ds(pl.multiple_of((zp * PLANE + place) * chunk, chunk), chunk), :]

    away = ((1, 3), (2, 3))
    kept = ((0, 2), (0, 1))
    nbr = (1, 2)

    def f_copy(h, zp, j):
        return remote(
            f_block(h, zp, pq[away[h][j]]), rxf.at[h, zp, j], fsend.at[h, zp, j], frecv.at[h, zp, j], me.plane(nbr[h])
        )

    loads = [
        start(pltpu.make_async_copy(a, b, lsem.at[i]))
        for i, (a, b) in enumerate(
            [(da_ref, da), (gated_ref, gated), (wo_ref, wo), (q_ref, q), (k_ref, k), (v_ref, v), (s_ref, st),
             (cos_ref, cos), (sin_ref, sin)]
        )
    ]
    for zp in range(LINE):
        for h in range(2):
            for j in range(2):
                f_copy(h, zp, j).start()

    def f_own(u):
        h, zp = u % 2, u // 2
        return [
            pltpu.make_async_copy(f_block(h, zp, pq[kept[h][j]]), fo.at[u % 2, j], fosem.at[u % 2, j])
            for j in range(2)
        ]

    def f_out(u):
        h, zp = u % 2, u // 2
        return pltpu.make_async_copy(rxf.at[h, zp], f1.at[h, zp], osem.at[u])

    for u in range(2):
        for c in f_own(u):
            c.start()

    def f_unit(u):
        h, zp = u % 2, u // 2
        for j, c in enumerate(f_own(u)):
            c.wait()
            f_copy(h, zp, j).wait_recv()
            add_rows(rxf.at[h, zp, j], fo.at[u % 2, j])
        f_out(u).start()
        if u + 2 < 2 * LINE:
            for c in f_own(u + 2):
                c.start()

    def tile_rows(i):
        return rows_at(i * 256, 256)

    def gate_loads(i):
        at = tile_rows(i)
        slot = i % 2
        return (
            pltpu.make_async_copy(gate_ref.at[at, :], gr.at[slot, 0], gsem.at[slot, 0]),
            pltpu.make_async_copy(ret_ref.at[at, :], gr.at[slot, 1], gsem.at[slot, 1]),
        )

    for c in gate_loads(0):
        c.start()

    out_sum = LineSum(me, lambda zz: ao.at[rows_at(zz * (width // LINE), width // LINE), :], rxo, *line[:4], add_rows)
    gate_sum = LineSum(me, lambda zz: ag.at[rows_at(zz * (width // LINE), width // LINE), :], rxg, *line[4:], add_rows)

    loads[0].wait()
    loads[1].wait()

    @pl.loop(0, width, step=256)
    def _(i):
        at = rows_at(i, 256)
        ao[at, :] = tn(da[:, at], gated[...]).astype(BF16)

    out_sum.begin()
    for c in loads[2:]:
        c.wait()

    tiles = tokens // 256

    @pl.loop(0, tiles)
    def _(i):
        @pl.when(i + 1 < tiles)
        def _():
            for c in gate_loads(i + 1):
                c.start()

        for c in gate_loads(i):
            c.wait()
        at = tile_rows(i)
        slot = i % 2
        dgated = nt(da[at, :], wo[...])
        gate = gr[slot, 0]
        ret = gr[slot, 1]
        centered = ret - jnp.mean(ret, axis=1, keepdims=True)
        scale = lax.rsqrt(jnp.mean(centered * centered, axis=1, keepdims=True) + 1e-05)
        grouped = centered * scale
        sig = 1.0 / (1.0 + jnp.exp(-gate))
        silu = gate * sig
        dh[at, 2 * keys + values :] = (dgated * grouped * (sig * (1.0 + gate * (1.0 - sig)))).astype(BF16)
        dg = dgated * silu
        dr[at, :] = (
            scale * (dg - jnp.mean(dg, axis=1, keepdims=True) - grouped * jnp.mean(dg * grouped, axis=1, keepdims=True))
        ).astype(BF16)

    lg[...] = jnp.zeros_like(lg)

    @pl.loop(0, blocks)
    def _(c):
        at = rows_at(c * STRETCH, STRETCH)
        decayed = (q[at, :].astype(F32) * jnp.exp(ccol_ref[at, :])).astype(BF16)
        got_q = tn(decayed, dr[at, :])
        qo[c] = got_q
        lg[...] += scal_ref[blocks + c, 0:1, 0:1] * got_q

    gb[0] = lg[...].astype(BF16)

    def state_copies(t, to, slot):
        device = me.at(to, p, me.f)
        return (
            remote(gb.at[0], got.at[slot], ssend.at[t - 1], srecv.at[t - 1], device),
            remote(scal_ref.at[2 * blocks], logs.at[slot], lsend.at[t - 1], lrecv.at[t - 1], device),
        )

    for t in range(1, LINE):

        @pl.when(z - t >= 0)
        def _():
            for c in state_copies(t, z - t, z):
                c.start()

    def x_tile(i):
        return pltpu.make_async_copy(xg_ref.at[:, rows_at(i * 256, 256)], xt.at[i % 2], xsem.at[i % 2])

    x_tile(0).start()

    @pl.loop(0, width // 256)
    def _(i):
        @pl.when(i + 1 < width // 256)
        def _():
            x_tile(i + 1).start()

        x_tile(i).wait()
        ag[rows_at(i * 256, 256), :] = tn(xt[i % 2], dh[:, 2 * keys + values :]).astype(BF16)

    gate_sum.begin()
    out_sum.step(0)
    f_unit(0)
    f_unit(1)
    out_sum.step(1)

    for t in range(1, LINE):

        @pl.when(z + t < LINE)
        def _():
            for c in state_copies(t, z + t, z + t):
                c.wait_recv()

        @pl.when(z - t >= 0)
        def _():
            for c in state_copies(t, z - t, z):
                c.wait_send()

    lg[...] = jnp.zeros_like(lg)
    for j in reversed(range(1, LINE)):

        @pl.when(z < j)
        def _():
            lg[...] = lg[...] * jnp.exp(logs[j, 0:1, 0:1]) + got[j].astype(F32)

    for c in reversed(range(blocks)):
        gb[c] = lg[...].astype(BF16)
        if c:
            lg[...] = lg[...] * scal_ref[c, 0:1, 0:1] + qo[c]

    t_size = 256

    @pl.loop(0, blocks)
    def _(c):
        blk = rows_at(c * STRETCH, STRETCH)
        row = crow_ref[c, 0:1, :]
        end = crow_ref[c, 0:1, STRETCH - 1 : STRETCH]
        for r in range(0, STRETCH, t_size):
            at = rows_at(c * STRETCH + r, t_size)
            col = ccol_ref[at, :]
            t_index = lax.broadcasted_iota(jnp.int32, (t_size, STRETCH), 0) + r
            s_index = lax.broadcasted_iota(jnp.int32, (t_size, STRETCH), 1)
            mask = jnp.where(t_index >= s_index, jnp.exp(jnp.minimum(col - row, 0.0)), 0.0)
            pbuf[r : r + t_size, :] = (nt(q[at, :], k[blk, :]) * mask).astype(BF16)
            g = (nt(dr[at, :], v[blk, :]) * mask).astype(BF16)
            gbuf[r : r + t_size, :] = g
            dq = nt(dr[at, :], st[c]) * jnp.exp(col) + nn(g, k[blk, :])
            a, b = dq[:, :half], dq[:, half:]
            dh[at, :half] = (a * cos[at, :] + b * sin[at, :]).astype(BF16)
            dh[at, half:keys] = (b * cos[at, :] - a * sin[at, :]).astype(BF16)
        for r in range(0, STRETCH, t_size):
            at = rows_at(c * STRETCH + r, t_size)
            tail = jnp.exp(end - ccol_ref[at, :])
            w = (v[at, :].astype(F32) * tail).astype(BF16)
            dk = nt(w, gb[c]) + tn(gbuf[:, r : r + t_size], q[blk, :])
            a, b = dk[:, :half], dk[:, half:]
            dh[at, keys : keys + half] = (a * cos[at, :] + b * sin[at, :]).astype(BF16)
            dh[at, keys + half : 2 * keys] = (b * cos[at, :] - a * sin[at, :]).astype(BF16)
            dv = nn(k[at, :], gb[c]) * tail + tn(pbuf[:, r : r + t_size], dr[blk, :])
            dh[at, 2 * keys : 2 * keys + values] = dv.astype(BF16)

    plane = []

    def deal(i, chain, a):
        chain.arrive()
        total_rows(z, fin.at[i], a.at[rows_at(z * (width // LINE), width // LINE), :], chain.rx)
        cols = pl.ds(i * values, values)
        for m in (1, 2, 3):
            plane.append(
                start(
                    remote(
                        fin.at[i, rows_at(pq[m] * chunk, chunk), :], sums.at[p, :, cols],
                        psend.at[i, m], precv.at[i, m], me.plane(m),
                    )
                )
            )
        plane.append(
            start(
                pltpu.make_async_copy(
                    fin.at[i, rows_at(p * chunk, chunk), :], sums.at[p, :, cols], psend.at[i, 0]
                )
            )
        )

    out_sum.step(2)
    for u in range(2, 4):
        f_unit(u)
    gate_sum.step(0)
    deal(0, out_sum, ao)
    gate_sum.step(1)
    for u in range(4, 6):
        f_unit(u)
    gate_sum.step(2)
    deal(1, gate_sum, ag)
    for u in range(6, 2 * LINE):
        f_unit(u)
    for c in plane:
        c.wait()
    out_sum.finish()
    gate_sum.finish()
    for u in range(2 * LINE):
        f_out(u).wait()
    for zp in range(LINE):
        for h in range(2):
            for j in range(2):
                f_copy(h, zp, j).wait_send()


def retention_back(da, wo, gated, gate, ret, q, k, v, states, cos, sin, ccol, crow, scal, xg, fu, fd, cid):
    tokens, width = da.shape
    keys, values = q.shape[1], v.shape[1]
    chunk = width // SPANS
    blocks = tokens // STRETCH
    hidden = fu.shape[1]
    deep = width // LINE
    return comm_call(
        retention_back_kernel,
        [
            jax.ShapeDtypeStruct((tokens, 2 * keys + 2 * values), BF16),
            jax.ShapeDtypeStruct((PLANE, chunk, 2 * values), BF16),
            jax.ShapeDtypeStruct((2, LINE, 2, chunk, hidden), BF16),
        ],
        [da, wo, gated, gate, ret, q, k, v, states, cos, sin, ccol, crow, scal, xg, fu, fd],
        [
            pltpu.VMEM((tokens, width), BF16),
            pltpu.VMEM(wo.shape, BF16),
            pltpu.VMEM(gated.shape, BF16),
            pltpu.VMEM((2, 2, 256, values), F32),
            pltpu.VMEM(q.shape, BF16),
            pltpu.VMEM(k.shape, BF16),
            pltpu.VMEM(v.shape, BF16),
            pltpu.VMEM(states.shape, BF16),
            pltpu.VMEM(cos.shape, F32),
            pltpu.VMEM(sin.shape, F32),
            pltpu.VMEM((tokens, values), BF16),
            pltpu.VMEM((2, tokens, 256), BF16),
            pltpu.VMEM((width, values), BF16),
            pltpu.VMEM((width, values), BF16),
            pltpu.VMEM((LINE + 1, deep, values), BF16),
            pltpu.VMEM((LINE + 1, deep, values), BF16),
            pltpu.VMEM((2, deep, values), BF16),
            pltpu.VMEM((blocks, keys, values), F32),
            pltpu.VMEM((blocks, keys, values), BF16),
            pltpu.VMEM((keys, values), F32),
            pltpu.VMEM((LINE, keys, values), BF16),
            pltpu.VMEM((LINE, 8, 128), F32),
            pltpu.VMEM((2, LINE, 2, chunk, hidden), BF16),
            pltpu.VMEM((2, 2, chunk, hidden), BF16),
            pltpu.VMEM((STRETCH, STRETCH), BF16),
            pltpu.VMEM((STRETCH, STRETCH), BF16),
            DMA((9,)),
            DMA((2, 2)),
            DMA((2,)),
            DMA((2, LINE, 2)),
            DMA((2, LINE, 2)),
            DMA((2 * LINE,)),
            DMA((2, 2)),
            DMA((LINE - 1,)),
            DMA((LINE - 1,)),
            DMA((LINE - 1,)),
            DMA((LINE - 1,)),
            DMA((2, PLANE)),
            DMA((2, PLANE)),
        ]
        + line_sems()
        + line_sems(),
        cid,
        in_specs=[ANY] * 11 + [VM] * 3 + [ANY] * 3,
        out_specs=[VM, ANY, ANY],
    )


def everyone(size):
    return range(0, size, SPANS)


def swap(x, mask):
    n = lax.axis_size("seq")
    return lax.ppermute(x, "seq", [(s, s ^ mask) for s in range(n)])


def take(x, index, axis):
    return lax.dynamic_index_in_dim(x, index, axis, False)


def plus(a, b):
    return (a.astype(F32) + b.astype(F32)).astype(BF16)


def line_sum(x, z):
    n = lax.axis_size("seq")
    up = dn = None
    for t in range(1, LINE):
        up_at = jnp.clip(LINE - t + z, 0, LINE - 1)
        dn_at = jnp.clip(z + t - LINE, 0, LINE - 1)
        ups = [
            (b + k * PLANE + p, b + (k + 1) * PLANE + p)
            for b in everyone(n)
            for k in range(t)
            for p in range(PLANE)
        ]
        dns = [
            (b + (LINE - 1 - k) * PLANE + p, b + (LINE - 2 - k) * PLANE + p)
            for b in everyone(n)
            for k in range(t)
            for p in range(PLANE)
        ]
        send_up, send_dn = take(x, up_at, 0), take(x, dn_at, 0)
        if t > 1:
            send_up, send_dn = plus(send_up, up), plus(send_dn, dn)
        up = lax.ppermute(send_up, "seq", ups)
        dn = lax.ppermute(send_dn, "seq", dns)
    return take(x, z, 0).astype(F32) + up.astype(F32) + dn.astype(F32)


def plane_deal(x, p):
    got = [take(x, p, 0)]
    for mask in range(1, PLANE):
        got.append(swap(take(x, p ^ mask, 0), mask))
    return jnp.stack([sum_of_choice(got, p, q) for q in range(PLANE)])


def sum_of_choice(got, p, q):
    out = got[0]
    for mask in range(1, PLANE):
        out = jnp.where((p ^ q) == mask, got[mask], out)
    return out


def gains_kernel(x_ref, out, rx, send, recv):
    me = Place()
    rounds = [
        [me.partner()],
        [me.plane(m) for m in (1, 2, 3)],
        [me.at((me.z + t) % LINE, me.p, me.f) for t in (1, 2, 3)],
    ]
    greet([(d, None) for r in rounds for d in r])
    out[...] = x_ref[...]
    k = 0
    for peers in rounds:
        copies = []
        for d in peers:
            c = remote(out, rx.at[k], send.at[k], recv.at[k], d)
            c.start()
            copies.append(c)
            k += 1
        for c in copies:
            c.wait()
        for j in range(k - len(peers), k):
            out[...] += rx[j]


def gains_sum(x, cid):
    return comm_call(
        gains_kernel,
        [jax.ShapeDtypeStruct(x.shape, F32)],
        [x],
        [pltpu.VMEM((7,) + x.shape, F32), DMA((7,)), DMA((7,))],
        cid,
        in_specs=[VM],
        out_specs=[VM],
    )[0]


def last_kernel(
    dh_ref, xg_ref, wq_ref, wk_ref, wv_ref, wg_ref, f1_ref, tok_ref, gain_ref, resid_ref, second_ref,
    grad_tokens, gains, fout, sums,
    dh, xt, wh, share, rx0, rx1a, rx1b, rx2a, rx2b, av, aq, rxv, rxq, fin, rf2, kf, rxfa, rxfb, grx,
    lsem, xsem, fsend, frecv, csend, crecv, xsend, xrecv, gsend, grecv, psend, precv, *line,
):
    me = Place()
    z, p, f = me.z, me.p, me.f
    rounds = [
        [me.partner()],
        [me.plane(m) for m in (1, 2, 3)],
        [me.at((z + t) % LINE, p, f) for t in range(1, LINE)],
    ]
    greet([(d, None) for r in rounds for d in r])
    width, keys2, values = xg_ref.shape[1], aq.shape[1], av.shape[1]
    rows = tok_ref.shape[0]
    pq = [me.xor(m) for m in range(4)]
    chunk = width // SPANS
    deep = width // LINE

    def f_copy(h, zp):
        return remote(f1_ref.at[h, zp, 1], rf2.at[h, zp], fsend.at[h, zp], frecv.at[h, zp], me.plane(2 - h))

    def x_tile(i):
        return pltpu.make_async_copy(xg_ref.at[:, rows_at(i * 256, 256)], xt.at[i % 2], xsem.at[i % 2])

    load = start(pltpu.make_async_copy(dh_ref, dh, lsem.at[0]))
    x_tile(0).start()
    for zp in (3, 0, 2, 1):
        for h in range(2):
            f_copy(h, zp).start()
    loads, at = [], 0
    for i, w in enumerate((wq_ref, wk_ref, wv_ref, wg_ref)):
        size = w.shape[1]
        loads.append(start(pltpu.make_async_copy(w, wh.at[:, at : at + size], lsem.at[1 + i])))
        at += size
    keeps = [start(pltpu.make_async_copy(f1_ref.at[h, :, 0], kf.at[h], lsem.at[5 + h])) for h in range(2)]

    def block_of(a, size):
        return lambda zz: a.at[rows_at(zz * size, size), :]

    v_sum = LineSum(me, block_of(av, deep), rxv, *line[:4], add_rows)
    q_sum = LineSum(me, block_of(aq, deep), rxq, *line[4:8], add_rows)
    fa_sum = LineSum(me, lambda zz: kf.at[0, zz], rxfa, *line[8:12], add_rows)
    fb_sum = LineSum(me, lambda zz: kf.at[1, zz], rxfb, *line[12:16], add_rows)
    load.wait()
    tiles = width // 256
    for out, cols, chain in ((av, pl.ds(keys2, values), v_sum), (aq, pl.ds(0, keys2), q_sum)):
        if chain is q_sum:
            x_tile(0).start()

        @pl.loop(0, tiles)
        def _(i):
            @pl.when(i + 1 < tiles)
            def _():
                x_tile(i + 1).start()

            x_tile(i).wait()
            out[rows_at(i * 256, 256), :] = tn(xt[i % 2], dh[:, cols]).astype(BF16)

        chain.begin()
    for c in loads:
        c.wait()

    own_rows, their_rows = rows_at(f * rows, rows), rows_at((1 - f) * rows, rows)
    wide = width // 2
    ca, cb = pl.ds(0, wide), pl.ds(wide, wide)
    everything, whole = pl.ds(0, width), pl.ds(0, wide)
    first, sends = {}, {}

    def share_part(m):
        at_rows = rows_at(pq[m] * 2 * rows, 2 * rows)

        @pl.loop(0, width, step=256)
        def _(c):
            at = rows_at(c, 256)
            share[m, :, at] = nt(dh[at_rows, :], wh[at, :]).astype(BF16)

        first[m] = start(
            remote(share.at[m, their_rows], rx0.at[m], csend.at[m], crecv.at[m], me.partner())
        )

    def pass_on(m):
        first[m].wait_recv()
        add_into(rx0.at[m], everything, share.at[m, own_rows], everything)
        k = 0 if m == 3 else 1
        if m & 1:
            sends["a", k] = start(
                remote(rx0.at[m, :, ca], rx1a.at[k], xsend.at[k], xrecv.at[k], me.plane(1))
            )
        if m & 2:
            sends["b", k] = start(
                remote(rx0.at[m, :, cb], rx1b.at[k], xsend.at[2 + k], xrecv.at[2 + k], me.plane(2))
            )

    share_part(3)
    share_part(1)
    pass_on(3)
    share_part(2)
    pass_on(1)
    share_part(0)
    pass_on(2)
    pass_on(0)
    v_sum.step(0)
    sends["a", 0].wait_recv()
    add_into(rx1a.at[0], whole, rx0.at[2], ca)
    s2a = start(remote(rx1a.at[0], rx2a, xsend.at[4], xrecv.at[4], me.plane(2)))
    sends["b", 0].wait_recv()
    add_into(rx1b.at[0], whole, rx0.at[1], cb)
    s2b = start(remote(rx1b.at[0], rx2b, xsend.at[5], xrecv.at[5], me.plane(1)))
    v_sum.step(1)
    for c in keeps:
        c.wait()
    for zp in (3, 0, 2, 1):
        for h in range(2):
            f_copy(h, zp).wait_recv()
            add_rows(kf.at[h, zp], rf2.at[h, zp])
    fa_sum.begin()
    fb_sum.begin()
    v_sum.step(2)
    q_sum.step(0)
    sends["a", 1].wait_recv()
    sends["b", 1].wait_recv()
    s2a.wait_recv()
    s2b.wait_recv()
    gains[...] = jnp.zeros_like(gains)
    gains[2:4, :] = second_ref[0:2, :]
    step = 32

    @pl.loop(0, rows, step=step)
    def _(r):
        at = rows_at(r, step)
        left = rx0[0, at, ca].astype(F32) + rx1a[1, at, :].astype(F32) + rx2a[at, :].astype(F32)
        right = rx0[0, at, cb].astype(F32) + rx1b[1, at, :].astype(F32) + rx2b[at, :].astype(F32)
        dx = jnp.concatenate([left, right], axis=1)
        v = tok_ref[at, :].astype(F32)
        centered = v - jnp.mean(v, axis=1, keepdims=True)
        scale = lax.rsqrt(jnp.mean(centered * centered, axis=1, keepdims=True) + 1e-05)
        hat = centered * scale
        gains[0:1, :] += jnp.sum(dx * hat, axis=0, keepdims=True)
        gains[1:2, :] += jnp.sum(dx, axis=0, keepdims=True)
        g = dx * gain_ref[...]
        back = scale * (
            g - jnp.mean(g, axis=1, keepdims=True) - hat * jnp.mean(g * hat, axis=1, keepdims=True)
        )
        grad_tokens[at, :] = (back + resid_ref[at, :]).astype(BF16)

    def gain_copies(r):
        base = (0, 1, 4)[r]
        return [
            remote(gains, grx.at[base + i], gsend.at[base + i], grecv.at[base + i], d)
            for i, d in enumerate(rounds[r])
        ]

    def gain_begin(r):
        for c in gain_copies(r):
            c.start()

    def gain_end(r):
        for c in gain_copies(r):
            c.wait()
        for i in range(len(rounds[r])):
            gains[...] += grx[(0, 1, 4)[r] + i]

    plane = []

    def deal(i, chain, a):
        chain.arrive()
        total_rows(z, fin.at[i], a.at[rows_at(z * deep, deep), :], chain.rx)
        cols = pl.ds(i * values, values)
        for m in (1, 2, 3):
            plane.append(
                start(
                    remote(
                        fin.at[i, rows_at(pq[m] * chunk, chunk), :], sums.at[p, :, cols],
                        psend.at[i, m], precv.at[i, m], me.plane(m),
                    )
                )
            )
        plane.append(
            start(
                pltpu.make_async_copy(
                    fin.at[i, rows_at(p * chunk, chunk), :], sums.at[p, :, cols], psend.at[i, 0]
                )
            )
        )

    gain_begin(0)
    q_sum.step(1)
    gain_end(0)
    gain_begin(1)
    deal(0, v_sum, av)
    gain_end(1)
    gain_begin(2)
    q_sum.step(2)
    fa_sum.step(0)
    gain_end(2)
    fb_sum.step(0)
    deal(1, q_sum, aq)
    fa_sum.step(1)
    fb_sum.step(1)
    fa_sum.step(2)
    fb_sum.step(2)
    fa_sum.arrive()
    total_rows(z, fout.at[0], kf.at[0, z], rxfa)
    fb_sum.arrive()
    total_rows(z, fout.at[1], kf.at[1, z], rxfb)
    for c in plane:
        c.wait()
    for chain in (v_sum, q_sum, fa_sum, fb_sum):
        chain.finish()
    for c in list(first.values()) + list(sends.values()) + [s2a, s2b]:
        c.wait_send()
    for zp in range(LINE):
        for h in range(2):
            f_copy(h, zp).wait_send()


def last_sums(dh, xg, wq, wk, wv, wg, f1, tokens, gain, resid, second, cid):
    group, width = xg.shape
    rows = tokens.shape[0]
    keys, values = wq.shape[1], wv.shape[1]
    assert 2 * keys == values
    chunk, deep = width // SPANS, width // LINE
    hidden = f1.shape[-1]
    return comm_call(
        last_kernel,
        [
            jax.ShapeDtypeStruct((rows, width), BF16),
            jax.ShapeDtypeStruct((8, width), F32),
            jax.ShapeDtypeStruct((2, chunk, hidden), F32),
            jax.ShapeDtypeStruct((PLANE, chunk, 2 * values), BF16),
        ],
        [dh, xg, wq, wk, wv, wg, f1, tokens, gain[None], resid, second],
        [
            pltpu.VMEM(dh.shape, BF16),
            pltpu.VMEM((2, group, 256), BF16),
            pltpu.VMEM((width, dh.shape[1]), BF16),
            pltpu.VMEM((PLANE, 2 * rows, width), BF16),
            pltpu.VMEM((PLANE, rows, width), BF16),
            pltpu.VMEM((2, rows, width // 2), BF16),
            pltpu.VMEM((2, rows, width // 2), BF16),
            pltpu.VMEM((rows, width // 2), BF16),
            pltpu.VMEM((rows, width // 2), BF16),
            pltpu.VMEM((width, values), BF16),
            pltpu.VMEM((width, 2 * keys), BF16),
            pltpu.VMEM((LINE + 1, deep, values), BF16),
            pltpu.VMEM((LINE + 1, deep, 2 * keys), BF16),
            pltpu.VMEM((2, deep, values), BF16),
            pltpu.VMEM((2, LINE, chunk, hidden), BF16),
            pltpu.VMEM((2, LINE, chunk, hidden), BF16),
            pltpu.VMEM((LINE + 1, chunk, hidden), BF16),
            pltpu.VMEM((LINE + 1, chunk, hidden), BF16),
            pltpu.VMEM((7, 8, width), F32),
            DMA((7,)),
            DMA((2,)),
            DMA((2, LINE)),
            DMA((2, LINE)),
            DMA((4,)),
            DMA((4,)),
            DMA((6,)),
            DMA((6,)),
            DMA((7,)),
            DMA((7,)),
            DMA((2, PLANE)),
            DMA((2, PLANE)),
        ]
        + line_sems()
        + line_sems()
        + line_sems()
        + line_sems(),
        cid,
        in_specs=[ANY] * 7 + [VM] * 4,
        out_specs=[VM, VM, VM, ANY],
    )


def layer_norm(values_in, gain_vec, bias_vec):
    average = jnp.mean(values_in, axis=-1, keepdims=True)
    centered = values_in - average
    variance = jnp.mean(centered * centered, axis=-1, keepdims=True)
    return centered * lax.rsqrt(variance + 1e-05) * gain_vec + bias_vec


def group_norm(values_in):
    average = jnp.mean(values_in, axis=-1, keepdims=True)
    centered = values_in - average
    variance = jnp.mean(centered * centered, axis=-1, keepdims=True)
    return centered * lax.rsqrt(variance + 1e-05)


def exact_gelu(values_in):
    return jax.nn.gelu(values_in, approximate=False)


def swish_gate(gate_proj, grouped):
    return jax.nn.silu(gate_proj) * grouped


def angles_of(positions, half_width):
    frequency = 10000.0 ** (-jnp.linspace(0.0, 1.0, half_width, dtype=F32))
    angles = positions.astype(F32)[:, None] * frequency[None, :]
    return jnp.cos(angles), jnp.sin(angles)


def rotate(values_in, cosine, sine_part):
    half_width = values_in.shape[-1] // 2
    first_half = values_in[..., :half_width]
    second_half = values_in[..., half_width:]
    return jnp.concatenate(
        [
            first_half * cosine - second_half * sine_part,
            second_half * cosine + first_half * sine_part,
        ],
        axis=-1,
    )


def dot(spec, a, b):
    return jnp.einsum(spec, a, b, preferred_element_type=F32)


def shards(
    tokens,
    ln1_gain,
    ln1_bias,
    w_query,
    w_key,
    w_value,
    w_gate,
    w_out,
    decay_log,
    ln2_gain,
    ln2_bias,
    w_up,
    w_down,
    cotangent,
):
    row_count, width = tokens.shape
    span_rows = cotangent.shape[0]
    heads = decay_log.shape[1]
    repeats = lax.axis_size("seq") // SPANS
    peers = [[lo + SPANS * k for k in range(repeats)] for lo in range(SPANS)]
    narrow = width // (SPANS * repeats)

    def wide_in(w, axis):
        if repeats == 1:
            return w
        return lax.all_gather(w, "seq", axis_index_groups=peers, axis=axis, tiled=True)

    def narrow_out(g, axis):
        if repeats == 1:
            return g
        return lax.psum_scatter(
            g, "seq", scatter_dimension=axis, axis_index_groups=peers, tiled=True
        )

    def features_in(a):
        if repeats == 1:
            return a
        return a.reshape(a.shape[:-1] + (repeats, SPANS, narrow)).swapaxes(-3, -2).reshape(a.shape)

    def features_out(a):
        if repeats == 1:
            return a
        return a.reshape(a.shape[:-1] + (SPANS, repeats, narrow)).swapaxes(-3, -2).reshape(a.shape)

    spot = lax.axis_index("seq") % SPANS
    z, p = spot // PLANE, spot % PLANE
    group_rows = span_rows * PLANE
    blocks = group_rows // STRETCH

    tokens, cotangent, w_down = features_in(tokens), features_in(cotangent), features_in(w_down)
    w_up = features_in(w_up.T).T if repeats > 1 else w_up
    ln1_gain, ln1_bias = features_in(ln1_gain), features_in(ln1_bias)
    ln2_gain, ln2_bias = features_in(ln2_gain), features_in(ln2_bias)
    inputs32 = tokens.astype(F32)
    xn_first = layer_norm(inputs32, ln1_gain, ln1_bias)
    decays = jnp.pad(decay_log.T, ((0, 8 - heads), (0, 0)))
    xg, decay_rows, key_w, value_w, query_w, gate_w, out_w = gather_in(
        xn_first.astype(BF16),
        decays,
        [
            wide_in(w_key, 0),
            wide_in(w_value, 0),
            wide_in(w_query, 0),
            wide_in(w_gate, 0),
            wide_in(w_out, 1),
        ],
        (False, False, False, False, True),
        0,
    )
    normed = xg.reshape(group_rows, width)
    key_width, value_width = key_w.shape[1], value_w.shape[1]
    log_decay = lax.dynamic_index_in_dim(decay_rows, p, 1, False).reshape(blocks, STRETCH)
    cumulative = jnp.cumsum(log_decay, axis=1)
    last = cumulative[:, -1]
    total = jnp.sum(last)

    positions = (z * group_rows + jnp.arange(group_rows)) % SEQUENCE_LENGTH
    cosine, sine_part = angles_of(positions, key_width // 2)
    q_rot = rotate(dot("td,dq->tq", normed, query_w), cosine, sine_part).astype(BF16)
    k_rot = rotate(dot("td,dq->tq", normed, key_w), cosine, sine_part).astype(BF16)
    value = dot("td,dv->tv", normed, value_w).astype(BF16)
    gate_proj = dot("td,dv->tv", normed, gate_w)

    q_blocks = q_rot.reshape(blocks, STRETCH, key_width)
    k_blocks = k_rot.reshape(blocks, STRETCH, key_width)
    v_blocks = value.reshape(blocks, STRETCH, value_width)
    tail_scale = jnp.exp(last[:, None] - cumulative)
    tail_values = (v_blocks.astype(F32) * tail_scale[:, :, None]).astype(BF16)
    key_values = dot("csk,csd->ckd", k_blocks, tail_values)
    local = [jnp.zeros((key_width, value_width), F32)]
    for c in range(blocks):
        local.append(jnp.exp(last[c]) * local[-1] + key_values[c])
    incoming = line_states(local[-1].astype(BF16), total, False, 1)
    before = jnp.exp(jnp.cumsum(last) - last)
    prev_states = jnp.stack([local[c] + before[c] * incoming for c in range(blocks)]).astype(BF16)

    gaps = cumulative[:, :, None] - cumulative[:, None, :]
    indices = jnp.arange(STRETCH)
    lower = indices[:, None] >= indices[None, :]
    mask = jnp.where(lower[None], jnp.exp(jnp.minimum(gaps, 0.0)), 0.0)
    weighted = (dot("ctk,csk->cts", q_blocks, k_blocks) * mask).astype(BF16)
    q_decayed = (q_blocks.astype(F32) * jnp.exp(cumulative)[:, :, None]).astype(BF16)
    retained = dot("cts,csd->ctd", weighted, v_blocks) + dot("ctk,ckd->ctd", q_decayed, prev_states)
    retained = retained.reshape(group_rows, value_width)
    gated_low = swish_gate(gate_proj, group_norm(retained)).astype(BF16)
    attn_share = dot("tv,vd->td", gated_low, out_w).astype(BF16)
    block_out, grad_resid, gains_second, grad_attn, grad_up, grad_down = ffn_part(
        attn_share.reshape(PLANE, 2, row_count, width),
        tokens,
        ln2_gain,
        ln2_bias,
        w_up,
        w_down,
        cotangent,
        2,
    )
    grad_attn = grad_attn.reshape(group_rows, width)
    crow = jnp.broadcast_to(cumulative[:, None, :], (blocks, 8, STRETCH))
    scalars = jnp.concatenate([jnp.exp(last), before, total[None]])
    scalars = jnp.broadcast_to(scalars[:, None, None], (2 * blocks + 1, 8, 128))
    grad_heads, sums_first, ffn_first = retention_back(
        grad_attn,
        out_w,
        gated_low,
        gate_proj,
        retained,
        q_rot,
        k_rot,
        value,
        prev_states,
        cosine,
        sine_part,
        cumulative.reshape(group_rows, 1),
        crow,
        scalars,
        normed,
        grad_up,
        grad_down,
        7,
    )
    grad_tokens, gains, ffn_sum, sums_last = last_sums(
        grad_heads,
        normed,
        query_w,
        key_w,
        value_w,
        gate_w,
        ffn_first,
        tokens,
        ln1_gain,
        grad_resid,
        gains_second,
        8,
    )
    sum_up = narrow_out(ffn_sum[0], 0)
    sum_down = narrow_out(ffn_sum[1], 0).T
    if repeats > 1:
        gains = lax.psum(gains, "seq", axis_index_groups=peers)
    gains = features_out(gains)
    gain_one, bias_one, gain_two, bias_two = gains[0], gains[1], gains[2], gains[3]

    def columns(sums, start, size):
        taken = sums[:, :, start : start + size].astype(F32).swapaxes(0, 1)
        return narrow_out(taken.reshape(taken.shape[0], PLANE * size), 0)

    sum_value = columns(sums_last, 0, value_width)
    sum_query = columns(sums_last, value_width, key_width)
    sum_key = columns(sums_last, value_width + key_width, key_width)
    sum_out = columns(sums_first, 0, value_width).T
    sum_gate = columns(sums_first, value_width, value_width)
    return (
        features_out(block_out),
        features_out(grad_tokens),
        gain_one,
        bias_one,
        sum_query,
        sum_key,
        sum_value,
        sum_gate,
        sum_out,
        gain_two,
        bias_two,
        sum_up,
        sum_down,
    )


def solution(mesh):
    return jax.shard_map(
        shards,
        mesh=mesh,
        in_specs=(
            P(("seq", "ffn"), None),
            P(),
            P(),
            P("seq", "ffn"),
            P("seq", "ffn"),
            P("seq", "ffn"),
            P("seq", "ffn"),
            P("ffn", "seq"),
            P("seq", "ffn"),
            P(),
            P(),
            P(None, "ffn"),
            P("ffn", None),
            P("seq", None),
        ),
        out_specs=(
            P(("seq", "ffn"), None),
            P(("seq", "ffn"), None),
            P(),
            P(),
            P("seq", "ffn"),
            P("seq", "ffn"),
            P("seq", "ffn"),
            P("seq", "ffn"),
            P("ffn", "seq"),
            P(),
            P(),
            P("seq", "ffn"),
            P("ffn", "seq"),
        ),
        check_vma=False,
    )
```

```python
import functools

import jax
import jax.numpy as jnp
from jax import lax
from jax.experimental import pallas as pl
from jax.experimental.pallas import tpu as pltpu
from jax.sharding import PartitionSpec as P

STRETCH = 512
SEQUENCE_LENGTH = 8192
PLANE = 4
LINE = 4
SPANS = PLANE * LINE
MESH = pl.DeviceIdType.MESH
VMEM_LIMIT = 60 * 1024 * 1024
ANY = pl.BlockSpec(memory_space=pl.ANY)
VM = pl.BlockSpec(memory_space=pltpu.VMEM)
BF16 = jnp.bfloat16
F32 = jnp.float32


class Place:
    def __init__(self):
        s = lax.axis_index("seq")
        self.f = lax.axis_index("ffn")
        lo = s % SPANS
        self.base = s - lo
        self.z = lo // PLANE
        self.p = lo % PLANE

    def plane(self, m):
        return self.at(self.z, self.xor(m), self.f)

    def xor(self, m):
        p = self.p
        low, high = p % 2, p // 2
        if m & 1:
            low = 1 - low
        if m & 2:
            high = 1 - high
        return high * 2 + low

    def at(self, z, p, f):
        return (self.base + z * PLANE + p, f)

    def partner(self):
        return self.at(self.z, self.p, 1 - self.f)

    def up(self):
        return self.at(self.z + 1, self.p, self.f)

    def down(self):
        return self.at(self.z - 1, self.p, self.f)


def greet(peers):
    bar = pltpu.get_barrier_semaphore()
    count = 0
    for device, cond in peers:
        if cond is None:
            pl.semaphore_signal(bar, inc=1, device_id=device, device_id_type=MESH)
            count = count + 1
        else:

            @pl.when(cond)
            def _():
                pl.semaphore_signal(bar, inc=1, device_id=device, device_id_type=MESH)

            count = count + cond.astype(jnp.int32)
    pl.semaphore_wait(bar, count)


def remote(src, dst, send, recv, device):
    return pltpu.make_async_remote_copy(
        src_ref=src, dst_ref=dst, send_sem=send, recv_sem=recv, device_id=device, device_id_type=MESH
    )


def comm_call(kernel, outs, ins, scratch, cid, in_specs=None, out_specs=None):
    return pl.pallas_call(
        kernel,
        out_shape=outs,
        in_specs=in_specs if in_specs is not None else [ANY] * len(ins),
        out_specs=out_specs if out_specs is not None else [ANY] * len(outs),
        scratch_shapes=scratch,
        compiler_params=pltpu.CompilerParams(
            collective_id=cid, has_side_effects=True, vmem_limit_bytes=VMEM_LIMIT
        ),
    )(*ins)


DMA = pltpu.SemaphoreType.DMA


def nn(a, b):
    return jnp.dot(a, b, preferred_element_type=F32)


def nt(a, b):
    return lax.dot_general(a, b, (((1,), (1,)), ((), ())), preferred_element_type=F32)


def tn(a, b):
    return lax.dot_general(a, b, (((0,), (0,)), ((), ())), preferred_element_type=F32)


def rows_at(r, size):
    return pl.ds(pl.multiple_of(r, size), size)


def add_into(dst, cols, other, other_cols):
    @pl.loop(0, dst.shape[0], step=64)
    def _(r):
        at = rows_at(r, 64)
        dst[at, cols] = (dst[at, cols].astype(F32) + other[at, other_cols].astype(F32)).astype(BF16)


def start(copy):
    copy.start()
    return copy


def ffn_kernel(
    x_ref, tok_ref, gain_ref, bias_ref, wu_ref, wd_ref, cot_ref,
    block_out, resid_grad, gains, da, fu, fd,
    wu, wd, rx0, rx1a, rx1b, rx2a, rx2b, resid, xn, act, dact, du, part, prx, dab, stage,
    lsem, csend, crecv, xsend, xrecv, psend, precv, gsend, grecv, ssem,
):
    me = Place()
    p, f = me.p, me.f
    greet([(me.plane(1), None), (me.plane(2), None), (me.partner(), None)])
    rows, width = tok_ref.shape
    hidden = wu.shape[1]
    q = [me.xor(m) for m in range(4)]
    wide = width // 2
    ca, cb = pl.ds(0, wide), pl.ds(wide, wide)
    everything, whole = pl.ds(0, width), pl.ds(0, wide)
    load_d = start(pltpu.make_async_copy(wd_ref, wd, lsem.at[0]))
    load_u = start(pltpu.make_async_copy(wu_ref, wu, lsem.at[1]))
    order = (3, 1, 2, 0)
    first = [
        start(remote(x_ref.at[q[m], 1 - f], rx0.at[q[m]], csend.at[m], crecv.at[m], me.partner()))
        for m in order
    ]
    sends = {}
    for c, m in zip(first, order):
        c.wait_recv()
        add_into(rx0.at[q[m]], everything, x_ref.at[q[m], f], everything)
        k = 0 if m == 3 else 1
        if m & 1:
            sends["a", k] = start(
                remote(rx0.at[q[m], :, ca], rx1a.at[k], xsend.at[k], xrecv.at[k], me.plane(1))
            )
        if m & 2:
            sends["b", k] = start(
                remote(rx0.at[q[m], :, cb], rx1b.at[k], xsend.at[2 + k], xrecv.at[2 + k], me.plane(2))
            )

    load_d.wait()

    @pl.loop(0, hidden, step=256)
    def _(c):
        at = rows_at(c, 256)
        dact[:, at] = nt(cot_ref[...], wd[at, :])

    sends["a", 0].wait_recv()
    add_into(rx1a.at[0], whole, rx0.at[q[2]], ca)
    s2a = start(remote(rx1a.at[0], rx2a, xsend.at[4], xrecv.at[4], me.plane(2)))
    sends["b", 0].wait_recv()
    add_into(rx1b.at[0], whole, rx0.at[q[1]], cb)
    s2b = start(remote(rx1b.at[0], rx2b, xsend.at[5], xrecv.at[5], me.plane(1)))
    sends["a", 1].wait_recv()
    sends["b", 1].wait_recv()
    load_u.wait()
    s2a.wait_recv()
    s2b.wait_recv()

    mine = f * rows
    theirs = (1 - f) * rows
    step = 32

    @pl.loop(0, rows, step=step)
    def _(r):
        at = rows_at(r, step)
        left = rx0[q[0], at, ca].astype(F32) + rx1a[1, at, :].astype(F32) + rx2a[at, :].astype(F32)
        right = rx0[q[0], at, cb].astype(F32) + rx1b[1, at, :].astype(F32) + rx2b[at, :].astype(F32)
        v = tok_ref[at, :].astype(F32) + jnp.concatenate([left, right], axis=1)
        resid[at, :] = v
        average = jnp.mean(v, axis=1, keepdims=True)
        centered = v - average
        scale = lax.rsqrt(jnp.mean(centered * centered, axis=1, keepdims=True) + 1e-05)
        xn[pl.ds(pl.multiple_of(mine + r, step), step), :] = (
            centered * scale * gain_ref[...] + bias_ref[...]
        ).astype(BF16)

    own_rows = rows_at(mine, rows)
    their_rows = rows_at(theirs, rows)
    swap_x = start(remote(xn.at[own_rows], xn.at[own_rows], psend.at[0], precv.at[0], me.partner()))

    def hidden_part(at_rows):
        @pl.loop(0, hidden, step=512)
        def _(c):
            at = rows_at(c, 512)
            u = nn(xn[at_rows, :], wu[:, at])
            e = 0.5 * (1.0 + lax.erf(u * 0.7071067811865476))
            act[at_rows, at] = (u * e).astype(BF16)
            slope = e + u * jnp.exp(-0.5 * u * u) * 0.3989422804014327
            du[at_rows, at] = (dact[at_rows, at] * slope).astype(BF16)

    hidden_part(own_rows)
    swap_x.wait_recv()
    hidden_part(their_rows)

    @pl.loop(0, width, step=256)
    def _(c):
        at = rows_at(c, 256)
        part[0, :, at] = nt(du[their_rows, :], wu[at, :]).astype(BF16)

    swap_d = start(remote(part.at[0], prx.at[0], psend.at[1], precv.at[1], me.partner()))
    @pl.loop(0, width, step=256)
    def _(c):
        at = rows_at(c, 256)
        resid_grad[:, at] = nt(du[own_rows, :], wu[at, :])

    swap_d.wait_recv()
    gains[...] = jnp.zeros_like(gains)

    @pl.loop(0, rows, step=step)
    def _(r):
        at = rows_at(r, step)
        dx = resid_grad[at, :] + prx[0, at, :].astype(F32)
        v = resid[at, :]
        average = jnp.mean(v, axis=1, keepdims=True)
        centered = v - average
        scale = lax.rsqrt(jnp.mean(centered * centered, axis=1, keepdims=True) + 1e-05)
        hat = centered * scale
        gains[0:1, :] += jnp.sum(dx * hat, axis=0, keepdims=True)
        gains[1:2, :] += jnp.sum(dx, axis=0, keepdims=True)
        g = dx * gain_ref[...]
        back = scale * (
            g - jnp.mean(g, axis=1, keepdims=True) - hat * jnp.mean(g * hat, axis=1, keepdims=True)
        )
        back = back + cot_ref[pl.ds(pl.multiple_of(mine + r, step), step), :].astype(F32)
        resid_grad[at, :] = back
        dab[at, :] = back.astype(BF16)

    half = rows // 2
    low, high = pl.ds(0, half), pl.ds(half, half)
    seat, seat1, seat2, seat3 = (me.xor(m) * 2 + f for m in (0, 1, 2, 3))
    own = start(pltpu.make_async_copy(dab, da.at[seat], lsem.at[2]))
    x1, x2 = [], []
    for k, (h1, h2) in enumerate(((low, high), (high, low))):
        x1.append(start(remote(dab.at[h1], da.at[seat, h1], gsend.at[k], grecv.at[k], me.plane(1))))
        x2.append(
            start(remote(dab.at[h2], da.at[seat, h2], gsend.at[2 + k], grecv.at[2 + k], me.plane(2)))
        )
    to_core = [start(remote(dab, da.at[seat], gsend.at[6], grecv.at[6], me.partner()))]

    @pl.loop(0, width, step=256)
    def _(c):
        at = rows_at(c, 256)
        part[1, :, at] = nn(act[their_rows, :], wd[:, at]).astype(BF16)

    swap_o = start(remote(part.at[1], prx.at[1], psend.at[2], precv.at[2], me.partner()))
    @pl.loop(0, width, step=256)
    def _(c):
        at = rows_at(c, 256)
        resid[:, at] = resid[:, at] + nn(act[own_rows, :], wd[:, at])

    swap_o.wait_recv()

    @pl.loop(0, rows, step=step)
    def _(r):
        at = rows_at(r, step)
        block_out[at, :] = (resid[at, :] + prx[1, at, :].astype(F32)).astype(BF16)

    x1[0].wait_recv()
    g1 = start(remote(da.at[seat1, low], da.at[seat1, low], gsend.at[4], grecv.at[4], me.plane(2)))
    x2[0].wait_recv()
    g2 = start(remote(da.at[seat2, high], da.at[seat2, high], gsend.at[5], grecv.at[5], me.plane(1)))

    def weights_part(left, right, out, base):
        def spill(slot, i):
            return pltpu.make_async_copy(stage.at[slot], out.at[rows_at(i * 256, 256), :], ssem.at[slot])

        @pl.loop(0, width // 256)
        def _(i):
            slot = i % 2

            @pl.when(i >= 2)
            def _():
                spill(slot, i - 2).wait()

            @pl.loop(0, hidden, step=512)
            def _(c):
                at = rows_at(c, 512)
                stage[slot, :, at] = tn(left[:, rows_at(i * 256, 256)], right[:, at]).astype(BF16)

            spill(slot, i).start()

        for k in (2, 1):
            i = width // 256 - k
            spill(i % 2, i).wait()

    weights_part(xn, du, fu, 0)
    x1[1].wait_recv()
    to_core.append(start(remote(da.at[seat1], da.at[seat1], gsend.at[7], grecv.at[7], me.partner())))
    x2[1].wait_recv()
    to_core.append(start(remote(da.at[seat2], da.at[seat2], gsend.at[8], grecv.at[8], me.partner())))
    weights_part(cot_ref, act, fd, 0)
    g1.wait_recv()
    to_core.append(
        start(remote(da.at[seat3, low], da.at[seat3, low], gsend.at[9], grecv.at[9], me.partner()))
    )
    g2.wait_recv()
    to_core.append(
        start(remote(da.at[seat3, high], da.at[seat3, high], gsend.at[10], grecv.at[10], me.partner()))
    )
    for c in to_core:
        c.wait()
    for c in x1 + x2 + [g1, g2, swap_x, swap_d, swap_o, s2a, s2b] + first + list(sends.values()):
        c.wait_send()
    own.wait()


def ffn_part(share, tokens, gain, bias, w_up, w_down, cotangent, cid):
    _, _, rows, width = share.shape
    span, hidden = 2 * rows, w_up.shape[1]
    return comm_call(
        ffn_kernel,
        [
            jax.ShapeDtypeStruct((rows, width), BF16),
            jax.ShapeDtypeStruct((rows, width), F32),
            jax.ShapeDtypeStruct((8, width), F32),
            jax.ShapeDtypeStruct((2 * PLANE, rows, width), BF16),
            jax.ShapeDtypeStruct((width, hidden), BF16),
            jax.ShapeDtypeStruct((width, hidden), BF16),
        ],
        [share, tokens, gain[None], bias[None], w_up, w_down, cotangent],
        [
            pltpu.VMEM(w_up.shape, BF16),
            pltpu.VMEM(w_down.shape, BF16),
            pltpu.VMEM((PLANE, rows, width), BF16),
            pltpu.VMEM((2, rows, width // 2), BF16),
            pltpu.VMEM((2, rows, width // 2), BF16),
            pltpu.VMEM((rows, width // 2), BF16),
            pltpu.VMEM((rows, width // 2), BF16),
            pltpu.VMEM((rows, width), F32),
            pltpu.VMEM((span, width), BF16),
            pltpu.VMEM((span, hidden), BF16),
            pltpu.VMEM((span, hidden), F32),
            pltpu.VMEM((span, hidden), BF16),
            pltpu.VMEM((2, rows, width), BF16),
            pltpu.VMEM((2, rows, width), BF16),
            pltpu.VMEM((rows, width), BF16),
            pltpu.VMEM((2, 256, hidden), BF16),
            DMA((3,)),
            DMA((4,)),
            DMA((4,)),
            DMA((6,)),
            DMA((6,)),
            DMA((3,)),
            DMA((3,)),
            DMA((11,)),
            DMA((11,)),
            DMA((2,)),
        ],
        cid,
        in_specs=[VM, VM, VM, VM, ANY, ANY, VM],
        out_specs=[VM, VM, VM, ANY, ANY, ANY],
    )


def attention_kernel(
    widths, by_rows,
    tok_ref, gain_ref, bias_ref, dec_ref, cbase, sbase, coff, soff, *refs,
):
    count = len(widths)
    shards_in, refs = refs[:count], refs[count:]
    (xg, q_out, k_out, v_out, gate_out, ret_out, gated_out, states_out, share_out, cos_out, sin_out, ccol, crow, scal), refs = (
        refs[:14], refs[14:],
    )
    full, refs = refs[:count], refs[count:]
    hold, refs = refs[:count], refs[count:]
    wl, refs = refs[:count], refs[count:]
    (xn, xv, q, k, v, gate, ret, gated, share, cos, sin, kv, st, sloc, sgot, decg, pbuf,
     lsem, psend, precv, usend, dsend, zrecv, xsend, xrecv, csend, crecv, tsend, trecv, ssend, srecv, osem, wsem) = refs
    me = Place()
    z, p, f = me.z, me.p, me.f
    spot = z * PLANE + p
    chunk = hold[0].shape[0]
    deep = chunk * PLANE
    tokens, width = xv.shape
    rows = tok_ref.shape[0]
    keys, values = q.shape[1], v.shape[1]
    half = keys // 2
    blocks = tokens // STRETCH
    greet(
        [(me.plane(m), None) for m in (1, 2, 3)]
        + [(me.partner(), None), (me.up(), z < LINE - 1), (me.down(), z > 0)]
    )

    def part(i, at):
        w = widths[i]
        if by_rows[i]:
            return shards_in[i].at[pl.ds(pl.multiple_of(at * w, w), w), :]
        return shards_in[i].at[:, pl.ds(pl.multiple_of(at * w, w), w)]

    def slot(i, ss):
        at = pl.ds(pl.multiple_of(ss * chunk, chunk), chunk)
        return full[i].at[:, at] if by_rows[i] else full[i].at[at, :]

    def block(i, zz):
        at = pl.ds(pl.multiple_of(zz * deep, deep), deep)
        return full[i].at[:, at] if by_rows[i] else full[i].at[at, :]

    local, plane, held = [], [], []
    for i in range(count):
        held.append(start(pltpu.make_async_copy(part(i, p), hold[i], lsem.at[i])))
        local.append(pltpu.make_async_copy(hold[i], slot(i, spot), lsem.at[i]))
        plane.append(
            [
                start(remote(part(i, me.xor(m)), slot(i, spot), psend.at[i, m], precv.at[i, m], me.plane(m)))
                for m in (1, 2, 3)
            ]
        )
    tiny = [start(remote(dec_ref, decg.at[p], tsend.at[m], trecv.at[m], me.plane(m))) for m in (1, 2, 3)]
    tiny_own = start(pltpu.make_async_copy(dec_ref, decg.at[p], tsend.at[0]))
    step = 32

    @pl.loop(0, rows, step=step)
    def _(r):
        at = rows_at(r, step)
        t = tok_ref[at, :].astype(F32)
        centered = t - jnp.mean(t, axis=1, keepdims=True)
        scale = lax.rsqrt(jnp.mean(centered * centered, axis=1, keepdims=True) + 1e-05)
        xn[at, :] = (centered * scale * gain_ref[...] + bias_ref[...]).astype(BF16)

    def seat(m, h=None):
        base = (me.xor(m) * 2 + f) * rows
        if h is None:
            return xv.at[rows_at(base, rows)]
        return xv.at[pl.ds(pl.multiple_of(base + h * (rows // 2), rows // 2), rows // 2)]

    x_own = start(pltpu.make_async_copy(xn, seat(0), lsem.at[count]))
    x1 = start(remote(xn, seat(0), xsend.at[0], xrecv.at[0], me.plane(1)))
    x2 = start(remote(xn, seat(0), xsend.at[1], xrecv.at[1], me.plane(2)))
    xc = start(remote(xn, seat(0), csend.at[0], crecv.at[0], me.partner()))
    for i in range(count):
        held[i].wait()
        local[i].start()

    def up_copy(i, zz):
        return remote(block(i, zz), block(i, zz), usend.at[i, zz], zrecv.at[i, zz], me.up())

    def down_copy(i, zz):
        return remote(block(i, zz), block(i, zz), dsend.at[i, zz], zrecv.at[i, zz], me.down())

    def own(i):
        local[i].wait()
        for c in plane[i]:
            c.wait_recv()

        @pl.when(z < LINE - 1)
        def _():
            up_copy(i, z).start()

        @pl.when(z > 0)
        def _():
            down_copy(i, z).start()

    def forward(i, t):
        @pl.when(z - t >= 0)
        def _():
            up_copy(i, z - t).wait_recv()

            @pl.when(z < LINE - 1)
            def _():
                up_copy(i, z - t).start()

        @pl.when(z + t < LINE)
        def _():
            down_copy(i, z + t).wait_recv()

            @pl.when(z > 0)
            def _():
                down_copy(i, z + t).start()

    def fetch(i):
        forward(i, LINE - 1)
        return start(pltpu.make_async_copy(full[i], wl[i], wsem.at[i]))

    K, V, Q, G, O = range(count)
    own(K)
    own(V)
    forward(K, 1)
    forward(K, 2)
    own(Q)

    for c in tiny:
        c.wait()
    tiny_own.wait()
    heads = lax.broadcasted_iota(jnp.int32, decg.shape[1:], 0)
    lines = [jnp.sum(jnp.where(heads == p, decg[j], 0.0), axis=0, keepdims=True) for j in range(blocks)]
    lines = jnp.concatenate(lines + [jnp.zeros_like(lines[0])] * (8 - blocks), axis=0)
    i0 = lax.broadcasted_iota(jnp.int32, (STRETCH, STRETCH), 0)
    i1 = lax.broadcasted_iota(jnp.int32, (STRETCH, STRETCH), 1)
    row_sums = jnp.dot(
        lines, jnp.where(i0 <= i1, 1.0, 0.0), preferred_element_type=F32, precision=lax.Precision.HIGHEST
    )
    col_sums = lax.dot_general(
        jnp.where(i1 <= i0, 1.0, 0.0), lines, (((1,), (1,)), ((), ())),
        preferred_element_type=F32, precision=lax.Precision.HIGHEST,
    )
    total = jnp.zeros((1, 1), F32)
    for c in range(blocks):
        end = row_sums[c : c + 1, STRETCH - 1 : STRETCH]
        crow[c] = jnp.broadcast_to(row_sums[c : c + 1, :], (8, STRETCH))
        ccol[c * STRETCH : (c + 1) * STRETCH, :] = col_sums[:, c : c + 1]
        scal[c] = jnp.broadcast_to(jnp.exp(end), (8, 128))
        scal[blocks + c] = jnp.broadcast_to(jnp.exp(total), (8, 128))
        total = total + end
    scal[2 * blocks] = jnp.broadcast_to(total, (8, 128))

    fine = coff.shape[0]

    @pl.loop(0, tokens // fine)
    def _(a):
        at = rows_at(a * fine, fine)
        ca, sa = cbase[a, 0:1, :], sbase[a, 0:1, :]
        cos[at, :] = ca * coff[...] - sa * soff[...]
        sin[at, :] = sa * coff[...] + ca * soff[...]

    forward(V, 1)
    x1.wait_recv()
    g1 = start(remote(seat(1, 0), seat(1, 0), xsend.at[2], xrecv.at[2], me.plane(2)))
    c1 = start(remote(seat(1), seat(1), csend.at[1], crecv.at[1], me.partner()))
    x2.wait_recv()
    g2 = start(remote(seat(2, 1), seat(2, 1), xsend.at[3], xrecv.at[3], me.plane(1)))
    c2 = start(remote(seat(2), seat(2), csend.at[2], crecv.at[2], me.partner()))
    forward(V, 2)
    forward(Q, 1)
    own(G)
    forward(Q, 2)
    own(O)
    load_k = fetch(K)
    g1.wait_recv()
    g2.wait_recv()
    c3 = start(remote(seat(3), seat(3), csend.at[3], crecv.at[3], me.partner()))
    x_own.wait()
    for c in (xc, c1, c2, c3):
        c.wait_recv()
    outs = []

    def put(src, dst):
        outs.append(start(pltpu.make_async_copy(src, dst, osem.at[len(outs)])))

    put(xv, xg)
    put(cos, cos_out)
    put(sin, sin_out)
    load_k.wait()

    def turned(at, w, dst):
        y = nn(xv[at, :], w[...])
        a, b = y[:, :half], y[:, half:]
        dst[at, :half] = (a * cos[at, :] - b * sin[at, :]).astype(BF16)
        dst[at, half:] = (b * cos[at, :] + a * sin[at, :]).astype(BF16)

    @pl.loop(0, blocks)
    def _(c):
        turned(rows_at(c * STRETCH, STRETCH), wl[K], k)

    fetch(V).wait()

    @pl.loop(0, blocks)
    def _(c):
        at = rows_at(c * STRETCH, STRETCH)
        val = nn(xv[at, :], wl[V][...]).astype(BF16)
        v[at, :] = val
        end = crow[c, 0:1, STRETCH - 1 : STRETCH]
        kv[c] = tn(k[at, :], (val.astype(F32) * jnp.exp(end - ccol[at, :])).astype(BF16))

    put(k, k_out)
    put(v, v_out)
    sloc[...] = kv[0]
    kv[0] = jnp.zeros_like(sloc)
    for c in range(1, blocks):
        nxt = sloc[...] * scal[c, 0:1, 0:1] + kv[c]
        kv[c] = sloc[...]
        sloc[...] = nxt

    def state_copy(zz):
        return remote(st.at[0], sgot, ssend.at[zz], srecv.at[zz], me.up())

    def send_state():
        st[0] = sloc[...].astype(BF16)
        state_copy(0).start()

    @pl.when(z == 0)
    def _():
        send_state()

    def pass_state(zz):
        @pl.when(z == zz)
        def _():
            state_copy(0).wait_recv()
            if zz < LINE - 1:
                sloc[...] = sloc[...] + sgot[...].astype(F32) * jnp.exp(scal[2 * blocks, 0:1, 0:1])
                send_state()

    pass_state(1)
    forward(G, 1)
    forward(O, 1)
    fetch(Q).wait()
    t_size = 256

    @pl.loop(0, blocks)
    def _(c):
        blk = rows_at(c * STRETCH, STRETCH)
        turned(blk, wl[Q], q)
        row = crow[c, 0:1, :]
        for r in range(0, STRETCH, t_size):
            at = rows_at(c * STRETCH + r, t_size)
            col = ccol[at, :]
            t_index = lax.broadcasted_iota(jnp.int32, (t_size, STRETCH), 0) + r
            s_index = lax.broadcasted_iota(jnp.int32, (t_size, STRETCH), 1)
            mask = jnp.where(t_index >= s_index, jnp.exp(jnp.minimum(col - row, 0.0)), 0.0)
            scores = (nt(q[at, :], k[blk, :]) * mask).astype(BF16)
            ret[at, :] = nn(scores, v[blk, :])

    put(q, q_out)
    pass_state(2)
    forward(G, 2)
    forward(O, 2)
    pass_state(3)

    @pl.when((z > 0) & (z < LINE - 1))
    def _():
        state_copy(0).wait_send()

    @pl.when(z == 0)
    def _():
        state_copy(0).wait_send()
        sgot[...] = jnp.zeros_like(sgot)

    for c in range(blocks):
        st[c] = (kv[c] + sgot[...].astype(F32) * scal[blocks + c, 0:1, 0:1]).astype(BF16)

    @pl.loop(0, blocks)
    def _(c):
        at = rows_at(c * STRETCH, STRETCH)
        decayed = (q[at, :].astype(F32) * jnp.exp(ccol[at, :])).astype(BF16)
        ret[at, :] += nn(decayed, st[c])

    put(ret, ret_out)
    put(st, states_out)
    fetch(G).wait()

    @pl.loop(0, tokens, step=256)
    def _(r):
        at = rows_at(r, 256)
        g = nn(xv[at, :], wl[G][...])
        gate[at, :] = g
        t = ret[at, :]
        centered = t - jnp.mean(t, axis=1, keepdims=True)
        scale = lax.rsqrt(jnp.mean(centered * centered, axis=1, keepdims=True) + 1e-05)
        gated[at, :] = (g / (1.0 + jnp.exp(-g)) * centered * scale).astype(BF16)

    put(gate, gate_out)
    put(gated, gated_out)
    fetch(O).wait()
    for c in range(blocks):
        at = pl.ds(c * STRETCH, STRETCH)

        @pl.loop(0, width, step=512)
        def _(d):
            cols = rows_at(d, 512)
            share[at, cols] = nn(gated[at, :], wl[O][:, cols]).astype(BF16)

        put(share.at[at], share_out.at[at])

    for c in (xc, c1, c2, c3, x1, x2, g1, g2):
        c.wait_send()
    for i in range(count):
        for c in plane[i]:
            c.wait_send()
        for zz in range(LINE):

            @pl.when((z < LINE - 1) & (zz <= z))
            def _():
                up_copy(i, zz).wait_send()

            @pl.when((z > 0) & (zz >= z))
            def _():
                down_copy(i, zz).wait_send()

    for c in outs:
        c.wait()


def attention(tokens, gain, bias, decays, tables, shards_in, by_rows, cid):
    rows, width = tokens.shape
    count = len(shards_in)
    chunk = shards_in[0].shape[0]
    group = 2 * PLANE * rows
    blocks = group // STRETCH
    parts = [
        (w.shape[0] // PLANE, chunk) if r else (chunk, w.shape[1] // PLANE) for w, r in zip(shards_in, by_rows)
    ]
    widths = [s[0] if r else s[1] for s, r in zip(parts, by_rows)]
    wholes = [(s[0], width) if r else (width, s[1]) for s, r in zip(parts, by_rows)]
    values, keys = widths[1], widths[0]
    half = keys // 2
    sd = jax.ShapeDtypeStruct
    outs = [
        sd((group, width), BF16),
        sd((group, keys), BF16),
        sd((group, keys), BF16),
        sd((group, values), BF16),
        sd((group, values), F32),
        sd((group, values), F32),
        sd((group, values), BF16),
        sd((blocks, keys, values), BF16),
        sd((group, width), BF16),
        sd((group, half), F32),
        sd((group, half), F32),
        sd((group, 1), F32),
        sd((blocks, 8, STRETCH), F32),
        sd((2 * blocks + 1, 8, 128), F32),
    ] + [sd(s, BF16) for s in wholes]
    scratch = (
        [pltpu.VMEM(s, BF16) for s in parts]
        + [pltpu.VMEM(s, BF16) for s in wholes]
        + [
            pltpu.VMEM((rows, width), BF16),
            pltpu.VMEM((group, width), BF16),
            pltpu.VMEM((group, keys), BF16),
            pltpu.VMEM((group, keys), BF16),
            pltpu.VMEM((group, values), BF16),
            pltpu.VMEM((group, values), F32),
            pltpu.VMEM((group, values), F32),
            pltpu.VMEM((group, values), BF16),
            pltpu.VMEM((group, width), BF16),
            pltpu.VMEM((group, half), F32),
            pltpu.VMEM((group, half), F32),
            pltpu.VMEM((blocks, keys, values), F32),
            pltpu.VMEM((blocks, keys, values), BF16),
            pltpu.VMEM((keys, values), F32),
            pltpu.VMEM((keys, values), BF16),
            pltpu.VMEM((PLANE,) + decays.shape, F32),
            pltpu.VMEM((8, 128), BF16),
            DMA((count + 1,)),
            DMA((count, PLANE)),
            DMA((count, PLANE)),
            DMA((count, LINE)),
            DMA((count, LINE)),
            DMA((count, LINE)),
            DMA((4,)),
            DMA((4,)),
            DMA((4,)),
            DMA((4,)),
            DMA((PLANE,)),
            DMA((PLANE,)),
            DMA((1,)),
            DMA((1,)),
            DMA((16,)),
            DMA((count,)),
        ]
    )
    return comm_call(
        functools.partial(attention_kernel, widths, by_rows),
        outs,
        [tokens, gain[None], bias[None], decays] + list(tables) + list(shards_in),
        scratch,
        cid,
        in_specs=[VM] * 8 + [ANY] * count,
        out_specs=[ANY] * 11 + [VM] * 3 + [ANY] * count,
    )


class LineSum:
    def __init__(self, me, own, rx, usend, urecv, dsend, drecv, add):
        self.me, self.own, self.rx, self.add = me, own, rx, add
        self.sems = usend, urecv, dsend, drecv

    def up(self, src, zz):
        return remote(src, self.rx.at[zz], self.sems[0].at[zz], self.sems[1].at[zz], self.me.up())

    def down(self, src, zz):
        slot = jnp.where(zz == self.me.z - 1, LINE, zz)
        return remote(src, self.rx.at[slot], self.sems[2].at[zz], self.sems[3].at[zz], self.me.down())

    def begin(self, order=(3, 2, 1)):
        for zz in order:

            @pl.when(self.me.z == 0)
            def _():
                self.up(self.own(zz), zz).start()

            @pl.when(self.me.z == LINE - 1)
            def _():
                self.down(self.own(LINE - 1 - zz), LINE - 1 - zz).start()

    def pass_up(self, zz):
        self.up(self.own(zz), zz).wait_recv()
        self.add(self.rx.at[zz], self.own(zz))
        self.up(self.rx.at[zz], zz).start()

    def pass_down(self, zz):
        self.down(self.own(zz), zz).wait_recv()
        self.add(self.rx.at[zz], self.own(zz))
        self.down(self.rx.at[zz], zz).start()

    def near(self, k):
        @pl.when(self.me.z == 1)
        def _():
            self.pass_up(LINE - 1 - k)

        @pl.when(self.me.z == 2)
        def _():
            self.pass_down(k)

    def far(self):
        @pl.when(self.me.z == 1)
        def _():
            self.pass_down(0)

        @pl.when(self.me.z == 2)
        def _():
            self.pass_up(LINE - 1)

    def arrive(self):
        z = self.me.z

        @pl.when(z > 0)
        def _():
            self.up(self.own(z), z).wait_recv()

        @pl.when(z < LINE - 1)
        def _():
            self.down(self.own(z), z).wait_recv()

    def finish(self):
        z = self.me.z
        for zz in range(LINE):

            @pl.when((z < LINE - 1) & (zz > z))
            def _():
                self.up(self.own(zz), zz).wait_send()

            @pl.when((z > 0) & (zz < z))
            def _():
                self.down(self.own(zz), zz).wait_send()


def add_rows(dst, src):
    rows = dst.shape[0]
    step = 32 if dst.shape[1] > 512 else 128

    @pl.loop(0, rows, step=step)
    def _(r):
        at = rows_at(r, step)
        dst[at, :] = (dst[at, :].astype(F32) + src[at, :].astype(F32)).astype(BF16)


def total_rows(z, dst, own, rx):
    rows = dst.shape[0]
    step = 32 if dst.shape[1] > 512 else 128

    @pl.loop(0, rows, step=step)
    def _(r):
        at = rows_at(r, step)
        v = own[at, :].astype(F32)
        v = v + jnp.where(z > 0, rx[z, at, :].astype(F32), 0.0)
        v = v + jnp.where(z < LINE - 1, rx[LINE, at, :].astype(F32), 0.0)
        dst[at, :] = v.astype(dst.dtype)


def line_sems():
    return [DMA((LINE,)) for _ in range(4)]


def retention_back_kernel(
    da_ref, wo_ref, gated_ref, gate_ref, ret_ref, q_ref, k_ref, v_ref, s_ref, cos_ref, sin_ref,
    ccol_ref, crow_ref, scal_ref, xg_ref, fu_ref, fd_ref,
    dh, sums, f1,
    da, wo, gated, gr, q, k, v, st, cos, sin, dr, xt, ao, ag, rxo, rxg, fin, qo, gb, lg, got, logs, rxf, fo, pbuf, gbuf,
    lsem, gsem, xsem, fsend, frecv, osem, fosem, ssend, srecv, lsend, lrecv, psend, precv, *line,
):
    me = Place()
    z, p = me.z, me.p
    greet(
        [(me.plane(m), None) for m in (1, 2, 3)]
        + [(me.at((z + t) % LINE, p, me.f), None) for t in range(1, LINE)]
    )
    width = da.shape[1]
    tokens = da.shape[0]
    keys, values = q.shape[1], v.shape[1]
    blocks = tokens // STRETCH
    half = keys // 2
    pq = [me.xor(m) for m in range(4)]
    chunk = fu_ref.shape[0] // SPANS

    def f_block(h, zp, place):
        return (fu_ref, fd_ref)[h].at[pl.ds(pl.multiple_of((zp * PLANE + place) * chunk, chunk), chunk), :]

    away = ((1, 3), (2, 3))
    kept = ((0, 2), (0, 1))
    nbr = (1, 2)

    def f_copy(h, zp, j):
        return remote(
            f_block(h, zp, pq[away[h][j]]), rxf.at[h, zp, j], fsend.at[h, zp, j], frecv.at[h, zp, j], me.plane(nbr[h])
        )

    loads = [
        start(pltpu.make_async_copy(a, b, lsem.at[i]))
        for i, (a, b) in enumerate(
            [(da_ref, da), (gated_ref, gated), (wo_ref, wo), (q_ref, q), (k_ref, k), (v_ref, v), (s_ref, st),
             (cos_ref, cos), (sin_ref, sin)]
        )
    ]
    for zp in range(LINE):
        for h in range(2):
            for j in range(2):
                f_copy(h, zp, j).start()

    def f_own(u):
        h, zp = u % 2, u // 2
        return [
            pltpu.make_async_copy(f_block(h, zp, pq[kept[h][j]]), fo.at[u % 2, j], fosem.at[u % 2, j])
            for j in range(2)
        ]

    def f_out(u):
        h, zp = u % 2, u // 2
        return pltpu.make_async_copy(rxf.at[h, zp], f1.at[h, zp], osem.at[u])

    for u in range(2):
        for c in f_own(u):
            c.start()

    def f_unit(u):
        h, zp = u % 2, u // 2
        for j, c in enumerate(f_own(u)):
            c.wait()
            f_copy(h, zp, j).wait_recv()
            add_rows(rxf.at[h, zp, j], fo.at[u % 2, j])
        f_out(u).start()
        if u + 2 < 2 * LINE:
            for c in f_own(u + 2):
                c.start()

    def tile_rows(i):
        return rows_at(i * 256, 256)

    def gate_loads(i):
        at = tile_rows(i)
        slot = i % 2
        return (
            pltpu.make_async_copy(gate_ref.at[at, :], gr.at[slot, 0], gsem.at[slot, 0]),
            pltpu.make_async_copy(ret_ref.at[at, :], gr.at[slot, 1], gsem.at[slot, 1]),
        )

    for c in gate_loads(0):
        c.start()

    out_sum = LineSum(me, lambda zz: ao.at[rows_at(zz * (width // LINE), width // LINE), :], rxo, *line[:4], add_rows)
    gate_sum = LineSum(me, lambda zz: ag.at[rows_at(zz * (width // LINE), width // LINE), :], rxg, *line[4:], add_rows)

    loads[0].wait()
    loads[1].wait()

    @pl.loop(0, width, step=256)
    def _(i):
        at = rows_at(i, 256)
        ao[at, :] = tn(da[:, at], gated[...]).astype(BF16)

    out_sum.begin((3, 2))
    for c in loads[2:]:
        c.wait()

    tiles = tokens // 256

    @pl.loop(0, tiles)
    def _(i):
        @pl.when(i + 1 < tiles)
        def _():
            for c in gate_loads(i + 1):
                c.start()

        for c in gate_loads(i):
            c.wait()
        at = tile_rows(i)
        slot = i % 2
        dgated = nt(da[at, :], wo[...])
        gate = gr[slot, 0]
        ret = gr[slot, 1]
        centered = ret - jnp.mean(ret, axis=1, keepdims=True)
        scale = lax.rsqrt(jnp.mean(centered * centered, axis=1, keepdims=True) + 1e-05)
        grouped = centered * scale
        sig = 1.0 / (1.0 + jnp.exp(-gate))
        silu = gate * sig
        dh[at, 2 * keys + values :] = (dgated * grouped * (sig * (1.0 + gate * (1.0 - sig)))).astype(BF16)
        dg = dgated * silu
        dr[at, :] = (
            scale * (dg - jnp.mean(dg, axis=1, keepdims=True) - grouped * jnp.mean(dg * grouped, axis=1, keepdims=True))
        ).astype(BF16)

    lg[...] = jnp.zeros_like(lg)

    @pl.loop(0, blocks)
    def _(c):
        at = rows_at(c * STRETCH, STRETCH)
        decayed = (q[at, :].astype(F32) * jnp.exp(ccol_ref[at, :])).astype(BF16)
        got_q = tn(decayed, dr[at, :])
        qo[c] = got_q
        lg[...] += scal_ref[blocks + c, 0:1, 0:1] * got_q

    gb[0] = lg[...].astype(BF16)

    def state_copies(t, to, slot):
        device = me.at(to, p, me.f)
        return (
            remote(gb.at[0], got.at[slot], ssend.at[t - 1], srecv.at[t - 1], device),
            remote(scal_ref.at[2 * blocks], logs.at[slot], lsend.at[t - 1], lrecv.at[t - 1], device),
        )

    for t in range(1, LINE):

        @pl.when(z - t >= 0)
        def _():
            for c in state_copies(t, z - t, z):
                c.start()

    out_sum.begin((1,))
    out_sum.near(0)
    def x_tile(i):
        return pltpu.make_async_copy(xg_ref.at[:, rows_at(i * 256, 256)], xt.at[i % 2], xsem.at[i % 2])

    x_tile(0).start()

    @pl.loop(0, width // 256)
    def _(i):
        @pl.when(i + 1 < width // 256)
        def _():
            x_tile(i + 1).start()

        x_tile(i).wait()
        ag[rows_at(i * 256, 256), :] = tn(xt[i % 2], dh[:, 2 * keys + values :]).astype(BF16)

    gate_sum.begin()
    out_sum.near(1)
    out_sum.far()
    f_unit(0)
    f_unit(1)

    for t in range(1, LINE):

        @pl.when(z + t < LINE)
        def _():
            for c in state_copies(t, z + t, z + t):
                c.wait_recv()

        @pl.when(z - t >= 0)
        def _():
            for c in state_copies(t, z - t, z):
                c.wait_send()

    lg[...] = jnp.zeros_like(lg)
    for j in reversed(range(1, LINE)):

        @pl.when(z < j)
        def _():
            lg[...] = lg[...] * jnp.exp(logs[j, 0:1, 0:1]) + got[j].astype(F32)

    for c in reversed(range(blocks)):
        gb[c] = lg[...].astype(BF16)
        if c:
            lg[...] = lg[...] * scal_ref[c, 0:1, 0:1] + qo[c]

    t_size = 256

    @pl.loop(0, blocks)
    def _(c):
        blk = rows_at(c * STRETCH, STRETCH)
        row = crow_ref[c, 0:1, :]
        end = crow_ref[c, 0:1, STRETCH - 1 : STRETCH]
        for r in range(0, STRETCH, t_size):
            at = rows_at(c * STRETCH + r, t_size)
            col = ccol_ref[at, :]
            t_index = lax.broadcasted_iota(jnp.int32, (t_size, STRETCH), 0) + r
            s_index = lax.broadcasted_iota(jnp.int32, (t_size, STRETCH), 1)
            mask = jnp.where(t_index >= s_index, jnp.exp(jnp.minimum(col - row, 0.0)), 0.0)
            pbuf[r : r + t_size, :] = (nt(q[at, :], k[blk, :]) * mask).astype(BF16)
            g = (nt(dr[at, :], v[blk, :]) * mask).astype(BF16)
            gbuf[r : r + t_size, :] = g
            dq = nt(dr[at, :], st[c]) * jnp.exp(col) + nn(g, k[blk, :])
            a, b = dq[:, :half], dq[:, half:]
            dh[at, :half] = (a * cos[at, :] + b * sin[at, :]).astype(BF16)
            dh[at, half:keys] = (b * cos[at, :] - a * sin[at, :]).astype(BF16)
        for r in range(0, STRETCH, t_size):
            at = rows_at(c * STRETCH + r, t_size)
            tail = jnp.exp(end - ccol_ref[at, :])
            w = (v[at, :].astype(F32) * tail).astype(BF16)
            dk = nt(w, gb[c]) + tn(gbuf[:, r : r + t_size], q[blk, :])
            a, b = dk[:, :half], dk[:, half:]
            dh[at, keys : keys + half] = (a * cos[at, :] + b * sin[at, :]).astype(BF16)
            dh[at, keys + half : 2 * keys] = (b * cos[at, :] - a * sin[at, :]).astype(BF16)
            dv = nn(k[at, :], gb[c]) * tail + tn(pbuf[:, r : r + t_size], dr[blk, :])
            dh[at, 2 * keys : 2 * keys + values] = dv.astype(BF16)

    plane = []

    def deal(i, chain, a):
        chain.arrive()
        total_rows(z, fin.at[i], a.at[rows_at(z * (width // LINE), width // LINE), :], chain.rx)
        cols = pl.ds(i * values, values)
        for m in (1, 2, 3):
            plane.append(
                start(
                    remote(
                        fin.at[i, rows_at(pq[m] * chunk, chunk), :], sums.at[p, :, cols],
                        psend.at[i, m], precv.at[i, m], me.plane(m),
                    )
                )
            )
        plane.append(
            start(
                pltpu.make_async_copy(
                    fin.at[i, rows_at(p * chunk, chunk), :], sums.at[p, :, cols], psend.at[i, 0]
                )
            )
        )

    gate_sum.near(0)
    gate_sum.near(1)
    for u in range(2, 4):
        f_unit(u)
    gate_sum.far()
    deal(0, out_sum, ao)
    for u in range(4, 6):
        f_unit(u)
    deal(1, gate_sum, ag)
    for u in range(6, 2 * LINE):
        f_unit(u)
    for c in plane:
        c.wait()
    out_sum.finish()
    gate_sum.finish()
    for u in range(2 * LINE):
        f_out(u).wait()
    for zp in range(LINE):
        for h in range(2):
            for j in range(2):
                f_copy(h, zp, j).wait_send()


def retention_back(da, wo, gated, gate, ret, q, k, v, states, cos, sin, ccol, crow, scal, xg, fu, fd, cid):
    tokens, width = da.shape
    keys, values = q.shape[1], v.shape[1]
    chunk = width // SPANS
    blocks = tokens // STRETCH
    hidden = fu.shape[1]
    deep = width // LINE
    return comm_call(
        retention_back_kernel,
        [
            jax.ShapeDtypeStruct((tokens, 2 * keys + 2 * values), BF16),
            jax.ShapeDtypeStruct((PLANE, chunk, 2 * values), BF16),
            jax.ShapeDtypeStruct((2, LINE, 2, chunk, hidden), BF16),
        ],
        [da, wo, gated, gate, ret, q, k, v, states, cos, sin, ccol, crow, scal, xg, fu, fd],
        [
            pltpu.VMEM((tokens, width), BF16),
            pltpu.VMEM(wo.shape, BF16),
            pltpu.VMEM(gated.shape, BF16),
            pltpu.VMEM((2, 2, 256, values), F32),
            pltpu.VMEM(q.shape, BF16),
            pltpu.VMEM(k.shape, BF16),
            pltpu.VMEM(v.shape, BF16),
            pltpu.VMEM(states.shape, BF16),
            pltpu.VMEM(cos.shape, F32),
            pltpu.VMEM(sin.shape, F32),
            pltpu.VMEM((tokens, values), BF16),
            pltpu.VMEM((2, tokens, 256), BF16),
            pltpu.VMEM((width, values), BF16),
            pltpu.VMEM((width, values), BF16),
            pltpu.VMEM((LINE + 1, deep, values), BF16),
            pltpu.VMEM((LINE + 1, deep, values), BF16),
            pltpu.VMEM((2, deep, values), BF16),
            pltpu.VMEM((blocks, keys, values), F32),
            pltpu.VMEM((blocks, keys, values), BF16),
            pltpu.VMEM((keys, values), F32),
            pltpu.VMEM((LINE, keys, values), BF16),
            pltpu.VMEM((LINE, 8, 128), F32),
            pltpu.VMEM((2, LINE, 2, chunk, hidden), BF16),
            pltpu.VMEM((2, 2, chunk, hidden), BF16),
            pltpu.VMEM((STRETCH, STRETCH), BF16),
            pltpu.VMEM((STRETCH, STRETCH), BF16),
            DMA((9,)),
            DMA((2, 2)),
            DMA((2,)),
            DMA((2, LINE, 2)),
            DMA((2, LINE, 2)),
            DMA((2 * LINE,)),
            DMA((2, 2)),
            DMA((LINE - 1,)),
            DMA((LINE - 1,)),
            DMA((LINE - 1,)),
            DMA((LINE - 1,)),
            DMA((2, PLANE)),
            DMA((2, PLANE)),
        ]
        + line_sems()
        + line_sems(),
        cid,
        in_specs=[ANY] * 11 + [VM] * 3 + [ANY] * 3,
        out_specs=[VM, ANY, ANY],
    )


def last_kernel(
    dh_ref, xg_ref, wq_ref, wk_ref, wv_ref, wg_ref, f1_ref, tok_ref, gain_ref, resid_ref, second_ref,
    grad_tokens, gains, fout, sums,
    dh, xt, wh, share, rx0, rx1a, rx1b, rx2a, rx2b, av, aq, rxv, rxq, fin, rf2, kf, rxfa, rxfb, grx,
    lsem, xsem, fsend, frecv, csend, crecv, xsend, xrecv, gsend, grecv, psend, precv, *line,
):
    me = Place()
    z, p, f = me.z, me.p, me.f
    rounds = [
        [me.partner()],
        [me.plane(m) for m in (1, 2, 3)],
        [me.at((z + t) % LINE, p, f) for t in range(1, LINE)],
    ]
    greet([(d, None) for r in rounds for d in r])
    width, keys2, values = xg_ref.shape[1], aq.shape[1], av.shape[1]
    rows = tok_ref.shape[0]
    pq = [me.xor(m) for m in range(4)]
    chunk = width // SPANS
    deep = width // LINE

    def f_copy(h, zp):
        return remote(f1_ref.at[h, zp, 1], rf2.at[h, zp], fsend.at[h, zp], frecv.at[h, zp], me.plane(2 - h))

    def x_tile(i):
        return pltpu.make_async_copy(xg_ref.at[:, rows_at(i * 256, 256)], xt.at[i % 2], xsem.at[i % 2])

    load = start(pltpu.make_async_copy(dh_ref, dh, lsem.at[0]))
    x_tile(0).start()
    for zp in (3, 0, 2, 1):
        for h in range(2):
            f_copy(h, zp).start()
    loads, at = [], 0
    for i, w in enumerate((wq_ref, wk_ref, wv_ref, wg_ref)):
        size = w.shape[1]
        loads.append(start(pltpu.make_async_copy(w, wh.at[:, at : at + size], lsem.at[1 + i])))
        at += size
    keeps = [start(pltpu.make_async_copy(f1_ref.at[h, :, 0], kf.at[h], lsem.at[5 + h])) for h in range(2)]

    def block_of(a, size):
        return lambda zz: a.at[rows_at(zz * size, size), :]

    v_sum = LineSum(me, block_of(av, deep), rxv, *line[:4], add_rows)
    q_sum = LineSum(me, block_of(aq, deep), rxq, *line[4:8], add_rows)
    fa_sum = LineSum(me, lambda zz: kf.at[0, zz], rxfa, *line[8:12], add_rows)
    fb_sum = LineSum(me, lambda zz: kf.at[1, zz], rxfb, *line[12:16], add_rows)
    load.wait()
    tiles = width // 256
    for out, cols, chain in ((av, pl.ds(keys2, values), v_sum), (aq, pl.ds(0, keys2), q_sum)):
        if chain is q_sum:
            x_tile(0).start()

        @pl.loop(0, tiles)
        def _(i):
            @pl.when(i + 1 < tiles)
            def _():
                x_tile(i + 1).start()

            x_tile(i).wait()
            out[rows_at(i * 256, 256), :] = tn(xt[i % 2], dh[:, cols]).astype(BF16)

        chain.begin()
    for c in loads:
        c.wait()

    own_rows, their_rows = rows_at(f * rows, rows), rows_at((1 - f) * rows, rows)
    wide = width // 2
    ca, cb = pl.ds(0, wide), pl.ds(wide, wide)
    everything, whole = pl.ds(0, width), pl.ds(0, wide)
    first, sends = {}, {}

    def share_part(m):
        at_rows = rows_at(pq[m] * 2 * rows, 2 * rows)

        @pl.loop(0, width, step=256)
        def _(c):
            at = rows_at(c, 256)
            share[m, :, at] = nt(dh[at_rows, :], wh[at, :]).astype(BF16)

        first[m] = start(
            remote(share.at[m, their_rows], rx0.at[m], csend.at[m], crecv.at[m], me.partner())
        )

    def pass_on(m):
        first[m].wait_recv()
        add_into(rx0.at[m], everything, share.at[m, own_rows], everything)
        k = 0 if m == 3 else 1
        if m & 1:
            sends["a", k] = start(
                remote(rx0.at[m, :, ca], rx1a.at[k], xsend.at[k], xrecv.at[k], me.plane(1))
            )
        if m & 2:
            sends["b", k] = start(
                remote(rx0.at[m, :, cb], rx1b.at[k], xsend.at[2 + k], xrecv.at[2 + k], me.plane(2))
            )

    share_part(3)
    share_part(1)
    pass_on(3)
    v_sum.near(0)
    share_part(2)
    pass_on(1)
    share_part(0)
    v_sum.near(1)
    pass_on(2)
    pass_on(0)
    v_sum.far()
    for c in keeps:
        c.wait()
    for zp in (3, 0, 2, 1):
        for h in range(2):
            f_copy(h, zp).wait_recv()
            add_rows(kf.at[h, zp], rf2.at[h, zp])
    for zz in (3, 2, 1):
        fa_sum.begin((zz,))
        fb_sum.begin((zz,))
    q_sum.near(0)
    sends["a", 0].wait_recv()
    add_into(rx1a.at[0], whole, rx0.at[2], ca)
    s2a = start(remote(rx1a.at[0], rx2a, xsend.at[4], xrecv.at[4], me.plane(2)))
    sends["b", 0].wait_recv()
    add_into(rx1b.at[0], whole, rx0.at[1], cb)
    s2b = start(remote(rx1b.at[0], rx2b, xsend.at[5], xrecv.at[5], me.plane(1)))
    q_sum.near(1)
    q_sum.far()
    sends["a", 1].wait_recv()
    sends["b", 1].wait_recv()
    s2a.wait_recv()
    s2b.wait_recv()
    gains[...] = jnp.zeros_like(gains)
    gains[2:4, :] = second_ref[0:2, :]
    step = 32

    @pl.loop(0, rows, step=step)
    def _(r):
        at = rows_at(r, step)
        left = rx0[0, at, ca].astype(F32) + rx1a[1, at, :].astype(F32) + rx2a[at, :].astype(F32)
        right = rx0[0, at, cb].astype(F32) + rx1b[1, at, :].astype(F32) + rx2b[at, :].astype(F32)
        dx = jnp.concatenate([left, right], axis=1)
        v = tok_ref[at, :].astype(F32)
        centered = v - jnp.mean(v, axis=1, keepdims=True)
        scale = lax.rsqrt(jnp.mean(centered * centered, axis=1, keepdims=True) + 1e-05)
        hat = centered * scale
        gains[0:1, :] += jnp.sum(dx * hat, axis=0, keepdims=True)
        gains[1:2, :] += jnp.sum(dx, axis=0, keepdims=True)
        g = dx * gain_ref[...]
        back = scale * (
            g - jnp.mean(g, axis=1, keepdims=True) - hat * jnp.mean(g * hat, axis=1, keepdims=True)
        )
        grad_tokens[at, :] = (back + resid_ref[at, :]).astype(BF16)

    def gain_copies(r):
        base = (0, 1, 4)[r]
        return [
            remote(gains, grx.at[base + i], gsend.at[base + i], grecv.at[base + i], d)
            for i, d in enumerate(rounds[r])
        ]

    def gain_begin(r):
        for c in gain_copies(r):
            c.start()

    def gain_end(r):
        for c in gain_copies(r):
            c.wait()
        for i in range(len(rounds[r])):
            gains[...] += grx[(0, 1, 4)[r] + i]

    plane = []

    def deal(i, chain, a):
        chain.arrive()
        total_rows(z, fin.at[i], a.at[rows_at(z * deep, deep), :], chain.rx)
        cols = pl.ds(i * values, values)
        for m in (1, 2, 3):
            plane.append(
                start(
                    remote(
                        fin.at[i, rows_at(pq[m] * chunk, chunk), :], sums.at[p, :, cols],
                        psend.at[i, m], precv.at[i, m], me.plane(m),
                    )
                )
            )
        plane.append(
            start(
                pltpu.make_async_copy(
                    fin.at[i, rows_at(p * chunk, chunk), :], sums.at[p, :, cols], psend.at[i, 0]
                )
            )
        )

    gain_begin(0)
    deal(0, v_sum, av)
    gain_end(0)
    gain_begin(1)
    deal(1, q_sum, aq)
    gain_end(1)
    gain_begin(2)
    fa_sum.near(0)
    fb_sum.near(0)
    fa_sum.near(1)
    fa_sum.far()
    fb_sum.near(1)
    fb_sum.far()
    fa_sum.arrive()
    total_rows(z, fout.at[0], kf.at[0, z], rxfa)
    fb_sum.arrive()
    total_rows(z, fout.at[1], kf.at[1, z], rxfb)
    gain_end(2)
    for c in plane:
        c.wait()
    for chain in (v_sum, q_sum, fa_sum, fb_sum):
        chain.finish()
    for c in list(first.values()) + list(sends.values()) + [s2a, s2b]:
        c.wait_send()
    for zp in range(LINE):
        for h in range(2):
            f_copy(h, zp).wait_send()


def last_sums(dh, xg, wq, wk, wv, wg, f1, tokens, gain, resid, second, cid):
    group, width = xg.shape
    rows = tokens.shape[0]
    keys, values = wq.shape[1], wv.shape[1]
    assert 2 * keys == values
    chunk, deep = width // SPANS, width // LINE
    hidden = f1.shape[-1]
    return comm_call(
        last_kernel,
        [
            jax.ShapeDtypeStruct((rows, width), BF16),
            jax.ShapeDtypeStruct((8, width), F32),
            jax.ShapeDtypeStruct((2, chunk, hidden), F32),
            jax.ShapeDtypeStruct((PLANE, chunk, 2 * values), BF16),
        ],
        [dh, xg, wq, wk, wv, wg, f1, tokens, gain[None], resid, second],
        [
            pltpu.VMEM(dh.shape, BF16),
            pltpu.VMEM((2, group, 256), BF16),
            pltpu.VMEM((width, dh.shape[1]), BF16),
            pltpu.VMEM((PLANE, 2 * rows, width), BF16),
            pltpu.VMEM((PLANE, rows, width), BF16),
            pltpu.VMEM((2, rows, width // 2), BF16),
            pltpu.VMEM((2, rows, width // 2), BF16),
            pltpu.VMEM((rows, width // 2), BF16),
            pltpu.VMEM((rows, width // 2), BF16),
            pltpu.VMEM((width, values), BF16),
            pltpu.VMEM((width, 2 * keys), BF16),
            pltpu.VMEM((LINE + 1, deep, values), BF16),
            pltpu.VMEM((LINE + 1, deep, 2 * keys), BF16),
            pltpu.VMEM((2, deep, values), BF16),
            pltpu.VMEM((2, LINE, chunk, hidden), BF16),
            pltpu.VMEM((2, LINE, chunk, hidden), BF16),
            pltpu.VMEM((LINE + 1, chunk, hidden), BF16),
            pltpu.VMEM((LINE + 1, chunk, hidden), BF16),
            pltpu.VMEM((7, 8, width), F32),
            DMA((7,)),
            DMA((2,)),
            DMA((2, LINE)),
            DMA((2, LINE)),
            DMA((4,)),
            DMA((4,)),
            DMA((6,)),
            DMA((6,)),
            DMA((7,)),
            DMA((7,)),
            DMA((2, PLANE)),
            DMA((2, PLANE)),
        ]
        + line_sems()
        + line_sems()
        + line_sems()
        + line_sems(),
        cid,
        in_specs=[ANY] * 7 + [VM] * 4,
        out_specs=[VM, VM, VM, ANY],
    )


def angle_tables(first, count, fine, half_width):
    frequency = 10000.0 ** (-jnp.linspace(0.0, 1.0, half_width, dtype=F32))
    coarse = ((first + fine * jnp.arange(count)) % SEQUENCE_LENGTH).astype(F32)[:, None] * frequency[None, :]
    near = jnp.arange(fine).astype(F32)[:, None] * frequency[None, :]
    wide = (count, 8, half_width)
    return [
        jnp.broadcast_to(jnp.cos(coarse)[:, None], wide),
        jnp.broadcast_to(jnp.sin(coarse)[:, None], wide),
        jnp.cos(near),
        jnp.sin(near),
    ]


def shards(
    tokens,
    ln1_gain,
    ln1_bias,
    w_query,
    w_key,
    w_value,
    w_gate,
    w_out,
    decay_log,
    ln2_gain,
    ln2_bias,
    w_up,
    w_down,
    cotangent,
):
    row_count, width = tokens.shape
    span_rows = cotangent.shape[0]
    heads = decay_log.shape[1]
    repeats = lax.axis_size("seq") // SPANS
    peers = [[lo + SPANS * k for k in range(repeats)] for lo in range(SPANS)]
    narrow = width // (SPANS * repeats)

    def wide_in(w, axis):
        if repeats == 1:
            return w
        return lax.all_gather(w, "seq", axis_index_groups=peers, axis=axis, tiled=True)

    def narrow_out(g, axis):
        if repeats == 1:
            return g
        return lax.psum_scatter(
            g, "seq", scatter_dimension=axis, axis_index_groups=peers, tiled=True
        )

    def features_in(a):
        if repeats == 1:
            return a
        return a.reshape(a.shape[:-1] + (repeats, SPANS, narrow)).swapaxes(-3, -2).reshape(a.shape)

    def features_out(a):
        if repeats == 1:
            return a
        return a.reshape(a.shape[:-1] + (SPANS, repeats, narrow)).swapaxes(-3, -2).reshape(a.shape)

    spot = lax.axis_index("seq") % SPANS
    z, p = spot // PLANE, spot % PLANE
    group_rows = span_rows * PLANE
    blocks = group_rows // STRETCH

    tokens, cotangent, w_down = features_in(tokens), features_in(cotangent), features_in(w_down)
    w_up = features_in(w_up.T).T if repeats > 1 else w_up
    ln1_gain, ln1_bias = features_in(ln1_gain), features_in(ln1_bias)
    ln2_gain, ln2_bias = features_in(ln2_gain), features_in(ln2_bias)
    decays = jnp.pad(decay_log.T, ((0, 8 - heads), (0, 0)))
    fine = 64
    (
        normed, q_rot, k_rot, value, gate_proj, retained, gated_low, prev_states, attn_share,
        cosine, sine_part, ccol, crow, scalars, key_w, value_w, query_w, gate_w, out_w,
    ) = attention(
        tokens,
        ln1_gain,
        ln1_bias,
        decays,
        angle_tables(z * group_rows, group_rows // fine, fine, w_key.shape[1] // heads // 2),
        [
            wide_in(w_key, 0),
            wide_in(w_value, 0),
            wide_in(w_query, 0),
            wide_in(w_gate, 0),
            wide_in(w_out, 1),
        ],
        (False, False, False, False, True),
        0,
    )
    key_width, value_width = key_w.shape[1], value_w.shape[1]
    block_out, grad_resid, gains_second, grad_attn, grad_up, grad_down = ffn_part(
        attn_share.reshape(PLANE, 2, row_count, width),
        tokens,
        ln2_gain,
        ln2_bias,
        w_up,
        w_down,
        cotangent,
        2,
    )
    grad_attn = grad_attn.reshape(group_rows, width)
    grad_heads, sums_first, ffn_first = retention_back(
        grad_attn,
        out_w,
        gated_low,
        gate_proj,
        retained,
        q_rot,
        k_rot,
        value,
        prev_states,
        cosine,
        sine_part,
        ccol,
        crow,
        scalars,
        normed,
        grad_up,
        grad_down,
        7,
    )
    grad_tokens, gains, ffn_sum, sums_last = last_sums(
        grad_heads,
        normed,
        query_w,
        key_w,
        value_w,
        gate_w,
        ffn_first,
        tokens,
        ln1_gain,
        grad_resid,
        gains_second,
        8,
    )
    sum_up = narrow_out(ffn_sum[0], 0)
    sum_down = narrow_out(ffn_sum[1], 0).T
    if repeats > 1:
        gains = lax.psum(gains, "seq", axis_index_groups=peers)
    gains = features_out(gains)
    gain_one, bias_one, gain_two, bias_two = gains[0], gains[1], gains[2], gains[3]

    def columns(sums, start, size):
        taken = sums[:, :, start : start + size].astype(F32).swapaxes(0, 1)
        return narrow_out(taken.reshape(taken.shape[0], PLANE * size), 0)

    sum_value = columns(sums_last, 0, value_width)
    sum_query = columns(sums_last, value_width, key_width)
    sum_key = columns(sums_last, value_width + key_width, key_width)
    sum_out = columns(sums_first, 0, value_width).T
    sum_gate = columns(sums_first, value_width, value_width)
    return (
        features_out(block_out),
        features_out(grad_tokens),
        gain_one,
        bias_one,
        sum_query,
        sum_key,
        sum_value,
        sum_gate,
        sum_out,
        gain_two,
        bias_two,
        sum_up,
        sum_down,
    )


def solution(mesh):
    return jax.shard_map(
        shards,
        mesh=mesh,
        in_specs=(
            P(("seq", "ffn"), None),
            P(),
            P(),
            P("seq", "ffn"),
            P("seq", "ffn"),
            P("seq", "ffn"),
            P("seq", "ffn"),
            P("ffn", "seq"),
            P("seq", "ffn"),
            P(),
            P(),
            P(None, "ffn"),
            P("ffn", None),
            P("seq", None),
        ),
        out_specs=(
            P(("seq", "ffn"), None),
            P(("seq", "ffn"), None),
            P(),
            P(),
            P("seq", "ffn"),
            P("seq", "ffn"),
            P("seq", "ffn"),
            P("seq", "ffn"),
            P("ffn", "seq"),
            P(),
            P(),
            P("seq", "ffn"),
            P("ffn", "seq"),
        ),
        check_vma=False,
    )
```

```python
import functools

import jax
import jax.numpy as jnp
from jax import lax
from jax.experimental import pallas as pl
from jax.experimental.pallas import tpu as pltpu
from jax.sharding import PartitionSpec as P

STRETCH = 512
SEQUENCE_LENGTH = 8192
PLANE = 4
LINE = 4
SPANS = PLANE * LINE
MESH = pl.DeviceIdType.MESH
VMEM_LIMIT = 60 * 1024 * 1024
ANY = pl.BlockSpec(memory_space=pl.ANY)
VM = pl.BlockSpec(memory_space=pltpu.VMEM)
BF16 = jnp.bfloat16
F32 = jnp.float32


class Place:
    def __init__(self):
        s = lax.axis_index("seq")
        self.f = lax.axis_index("ffn")
        lo = s % SPANS
        self.base = s - lo
        self.z = lo // PLANE
        self.p = lo % PLANE

    def plane(self, m):
        return self.at(self.z, self.xor(m), self.f)

    def xor(self, m):
        p = self.p
        low, high = p % 2, p // 2
        if m & 1:
            low = 1 - low
        if m & 2:
            high = 1 - high
        return high * 2 + low

    def at(self, z, p, f):
        return (self.base + z * PLANE + p, f)

    def partner(self):
        return self.at(self.z, self.p, 1 - self.f)

    def up(self):
        return self.at(self.z + 1, self.p, self.f)

    def down(self):
        return self.at(self.z - 1, self.p, self.f)


def greet(peers):
    bar = pltpu.get_barrier_semaphore()
    count = 0
    for device, cond in peers:
        if cond is None:
            pl.semaphore_signal(bar, inc=1, device_id=device, device_id_type=MESH)
            count = count + 1
        else:

            @pl.when(cond)
            def _():
                pl.semaphore_signal(bar, inc=1, device_id=device, device_id_type=MESH)

            count = count + cond.astype(jnp.int32)
    pl.semaphore_wait(bar, count)


def remote(src, dst, send, recv, device):
    return pltpu.make_async_remote_copy(
        src_ref=src, dst_ref=dst, send_sem=send, recv_sem=recv, device_id=device, device_id_type=MESH
    )


def comm_call(kernel, outs, ins, scratch, cid, in_specs=None, out_specs=None):
    return pl.pallas_call(
        kernel,
        out_shape=outs,
        in_specs=in_specs if in_specs is not None else [ANY] * len(ins),
        out_specs=out_specs if out_specs is not None else [ANY] * len(outs),
        scratch_shapes=scratch,
        compiler_params=pltpu.CompilerParams(
            collective_id=cid, has_side_effects=True, vmem_limit_bytes=VMEM_LIMIT
        ),
    )(*ins)


DMA = pltpu.SemaphoreType.DMA


def nn(a, b):
    return jnp.dot(a, b, preferred_element_type=F32)


def nt(a, b):
    return lax.dot_general(a, b, (((1,), (1,)), ((), ())), preferred_element_type=F32)


def tn(a, b):
    return lax.dot_general(a, b, (((0,), (0,)), ((), ())), preferred_element_type=F32)


def rows_at(r, size):
    return pl.ds(pl.multiple_of(r, size), size)


def add_into(dst, cols, other, other_cols):
    @pl.loop(0, dst.shape[0], step=64)
    def _(r):
        at = rows_at(r, 64)
        dst[at, cols] = (dst[at, cols].astype(F32) + other[at, other_cols].astype(F32)).astype(BF16)


def start(copy):
    copy.start()
    return copy


def ffn_kernel(
    gated_ref, wo_ref, tok_ref, gain_ref, bias_ref, wu_ref, wd_ref, cot_ref,
    block_out, resid_grad, gains, da, fu, fd,
    share, wu, wd, rx0, rx1a, rx1b, rx2a, rx2b, resid, xn, act, dact, du, cot, dab, stage, tmp,
    lsem, gload, csend, crecv, xsend, xrecv, psend, precv, gsend, grecv, ksend, krecv, ssem,
):
    me = Place()
    p, f = me.p, me.f
    greet([(me.plane(1), None), (me.plane(2), None), (me.partner(), None)])
    rows, width = tok_ref.shape
    hidden = wu.shape[1]
    q = [me.xor(m) for m in range(4)]
    wide = width // 2
    hr = rows // 2
    span = 2 * rows
    ca, cb = pl.ds(0, wide), pl.ds(wide, wide)
    everything, whole = pl.ds(0, width), pl.ds(0, wide)
    own_half = [pl.ds(h * hr, hr) for h in range(2)]
    mine = [rows_at(h * rows + f * hr, hr) for h in range(2)]
    theirs = [rows_at(h * rows + (1 - f) * hr, hr) for h in range(2)]
    both = [pl.ds(h * rows, rows) for h in range(2)]

    order = (3, 1, 2, 0)
    part_width = gated_ref.shape[1]
    load_o = start(pltpu.make_async_copy(wo_ref, act, lsem.at[0]))
    load_g = {
        m: start(
            pltpu.make_async_copy(
                gated_ref.at[rows_at(q[m] * span, span), :],
                xn.at[:, m * part_width : (m + 1) * part_width],
                gload.at[m],
            )
        )
        for m in order
    }
    load_d = start(pltpu.make_async_copy(wd_ref, wd, lsem.at[1]))
    load_c = [
        start(
            pltpu.make_async_copy(
                cot_ref.at[pl.ds(c * rows + h * hr, hr), :], cot.at[pl.ds(h * rows + c * hr, hr), :], lsem.at[3 + 2 * h + c]
            )
        )
        for h in range(2)
        for c in range(2)
    ]
    load_u = start(pltpu.make_async_copy(wu_ref, wu, lsem.at[2]))
    load_o.wait()
    first, sends = {}, {}

    def to_partner(m, h):
        first[m, h] = start(
            remote(
                share.at[m, rows_at((1 - f) * rows + h * hr, hr)], rx0.at[m, own_half[h]],
                csend.at[m, h], crecv.at[m, h], me.partner(),
            )
        )

    for m in order:
        load_g[m].wait()

        @pl.loop(0, width, step=512)
        def _(c):
            at = rows_at(c, 512)
            share[m, :, at] = nn(xn[:, m * part_width : (m + 1) * part_width], act[:, at]).astype(BF16)

        to_partner(m, 0)
    for m in order:
        to_partner(m, 1)

    def pass_on(m, h):
        first[m, h].wait_recv()
        at = own_half[h]
        add_into(rx0.at[m, at], everything, share.at[m, rows_at(f * rows + h * hr, hr)], everything)
        k = 0 if m == 3 else 1
        if m & 1:
            sends["a", k, h] = start(
                remote(rx0.at[m, at, ca], rx1a.at[k, at], xsend.at[k, h], xrecv.at[k, h], me.plane(1))
            )
        if m & 2:
            sends["b", k, h] = start(
                remote(rx0.at[m, at, cb], rx1b.at[k, at], xsend.at[2 + k, h], xrecv.at[2 + k, h], me.plane(2))
            )

    def second(h):
        at = own_half[h]
        sends["a", 0, h].wait_recv()
        add_into(rx1a.at[0, at], whole, rx0.at[2, at], ca)
        sends["a", 2, h] = start(
            remote(rx1a.at[0, at], rx2a.at[at], xsend.at[4, h], xrecv.at[4, h], me.plane(2))
        )
        sends["b", 0, h].wait_recv()
        add_into(rx1b.at[0, at], whole, rx0.at[1, at], cb)
        sends["b", 2, h] = start(
            remote(rx1b.at[0, at], rx2b.at[at], xsend.at[5, h], xrecv.at[5, h], me.plane(1))
        )

    for m in order:
        pass_on(m, 0)

    load_d.wait()
    for c in load_c:
        c.wait()

    @pl.loop(0, hidden, step=256)
    def _(c):
        at = rows_at(c, 256)
        dact[:, at] = nt(cot[...], wd[at, :])

    second(0)
    for m in order:
        pass_on(m, 1)
    load_u.wait()
    step = 32

    def norm(h):
        for key in (("a", 1, h), ("b", 1, h), ("a", 2, h), ("b", 2, h)):
            sends[key].wait_recv()

        @pl.loop(0, hr, step=step)
        def _(r):
            at = pl.ds(pl.multiple_of(h * hr + r, step), step)
            left = rx0[0, at, ca].astype(F32) + rx1a[1, at, :].astype(F32) + rx2a[at, :].astype(F32)
            right = rx0[0, at, cb].astype(F32) + rx1b[1, at, :].astype(F32) + rx2b[at, :].astype(F32)
            v = tok_ref[at, :].astype(F32) + jnp.concatenate([left, right], axis=1)
            resid[at, :] = v
            centered = v - jnp.mean(v, axis=1, keepdims=True)
            scale = lax.rsqrt(jnp.mean(centered * centered, axis=1, keepdims=True) + 1e-05)
            xn[pl.ds(pl.multiple_of(h * rows + f * hr + r, step), step), :] = (
                centered * scale * gain_ref[...] + bias_ref[...]
            ).astype(BF16)

        return start(remote(xn.at[mine[h]], xn.at[mine[h]], psend.at[0, h], precv.at[0, h], me.partner()))

    def hidden_part(h):
        @pl.loop(0, hidden, step=512)
        def _(c):
            at = rows_at(c, 512)
            u = nn(xn[both[h], :], wu[:, at])
            e = 0.5 * (1.0 + lax.erf(u * 0.7071067811865476))
            act[both[h], at] = (u * e).astype(BF16)
            slope = e + u * jnp.exp(-0.5 * u * u) * 0.3989422804014327
            du[both[h], at] = (dact[both[h], at] * slope).astype(BF16)

    def back_part(h):
        @pl.loop(0, width, step=512)
        def _(c):
            at = rows_at(c, 512)
            tmp[:rows, :] = nt(du[both[h], :], wu[at, :])
            resid_grad[own_half[h], at] = tmp[rows_at(f * hr, hr), :]
            share[0, own_half[h], at] = tmp[rows_at((1 - f) * hr, hr), :].astype(BF16)

        return start(
            remote(share.at[0, own_half[h]], share.at[1, own_half[h]], psend.at[1, h], precv.at[1, h], me.partner())
        )

    def norm_back(h):
        @pl.loop(0, hr, step=step)
        def _(r):
            at = pl.ds(pl.multiple_of(h * hr + r, step), step)
            dx = resid_grad[at, :] + share[1, at, :].astype(F32)
            v = resid[at, :]
            centered = v - jnp.mean(v, axis=1, keepdims=True)
            scale = lax.rsqrt(jnp.mean(centered * centered, axis=1, keepdims=True) + 1e-05)
            hat = centered * scale
            gains[0:1, :] += jnp.sum(dx * hat, axis=0, keepdims=True)
            gains[1:2, :] += jnp.sum(dx, axis=0, keepdims=True)
            g = dx * gain_ref[...]
            back = scale * (
                g - jnp.mean(g, axis=1, keepdims=True) - hat * jnp.mean(g * hat, axis=1, keepdims=True)
            )
            back = back + cot[pl.ds(pl.multiple_of(h * rows + f * hr + r, step), step), :].astype(F32)
            resid_grad[at, :] = back
            dab[at, :] = back.astype(BF16)

    quarter = hr // 2

    def seat(m, h, k=None):
        base = (q[m] * 2 + f) * rows + h * hr
        if k is None:
            return da.at[pl.ds(pl.multiple_of(base, hr), hr), :]
        return da.at[pl.ds(pl.multiple_of(base + k * quarter, quarter), quarter), :]

    spread = {}

    def spread_begin(h):
        spread["own", h] = start(pltpu.make_async_copy(dab.at[own_half[h]], seat(0, h), gload.at[h]))
        for i in range(2):
            for to, k in ((1, i), (2, 1 - i)):
                sem = (to - 1) * 2 + i
                spread[to, i, h] = start(
                    remote(
                        dab.at[pl.ds(h * hr + k * quarter, quarter)], seat(0, h, k),
                        gsend.at[sem, h], grecv.at[sem, h], me.plane(to),
                    )
                )
        spread["core", 0, h] = start(
            remote(dab.at[own_half[h]], seat(0, h), ksend.at[0, h], krecv.at[0, h], me.partner())
        )

    def spread_on(h):
        spread[1, 0, h].wait_recv()
        spread["g1", h] = start(
            remote(seat(1, h, 0), seat(1, h, 0), gsend.at[4, h], grecv.at[4, h], me.plane(2))
        )
        spread[2, 0, h].wait_recv()
        spread["g2", h] = start(
            remote(seat(2, h, 1), seat(2, h, 1), gsend.at[5, h], grecv.at[5, h], me.plane(1))
        )

    def spread_end(h):
        for m in (1, 2):
            spread[m, 1, h].wait_recv()
            spread["core", m, h] = start(
                remote(seat(m, h), seat(m, h), ksend.at[m, h], krecv.at[m, h], me.partner())
            )
        spread["g1", h].wait_recv()
        spread["g2", h].wait_recv()
        spread["core", 3, h] = start(
            remote(seat(3, h), seat(3, h), ksend.at[3, h], krecv.at[3, h], me.partner())
        )

    gains[...] = jnp.zeros_like(gains)
    for c in first.values():
        c.wait_send()
    swaps = [norm(0)]
    swaps[0].wait_recv()
    hidden_part(0)
    second(1)
    swaps.append(back_part(0))
    swaps[1].wait_recv()
    norm_back(0)
    spread_begin(0)
    swaps.append(norm(1))
    swaps[2].wait_recv()
    hidden_part(1)
    spread_on(0)
    swaps.append(back_part(1))
    swaps[3].wait_recv()
    norm_back(1)
    spread_begin(1)

    @pl.loop(0, width, step=512)
    def _(c):
        at = rows_at(c, 512)
        tmp[...] = nn(act[...], wd[:, at])
        for h in range(2):
            resid[own_half[h], at] = resid[own_half[h], at] + tmp[mine[h], :]
            share[2, own_half[h], at] = tmp[theirs[h], :].astype(BF16)

    swaps.append(
        start(remote(share.at[2, pl.ds(0, rows)], share.at[3, pl.ds(0, rows)], psend.at[2, 0], precv.at[2, 0], me.partner()))
    )
    spread_on(1)

    def weights_part(left, right, out):
        def spill(slot, i):
            return pltpu.make_async_copy(stage.at[slot], out.at[rows_at(i * 256, 256), :], ssem.at[slot])

        @pl.loop(0, width // 256)
        def _(i):
            slot = i % 2

            @pl.when(i >= 2)
            def _():
                spill(slot, i - 2).wait()

            stage[slot] = tn(left[:, rows_at(i * 256, 256)], right[...]).astype(BF16)
            spill(slot, i).start()

        for k in (2, 1):
            i = width // 256 - k
            spill(i % 2, i).wait()

    weights_part(xn, du, fu)
    spread_end(0)
    swaps[4].wait_recv()

    @pl.loop(0, rows, step=step)
    def _(r):
        at = rows_at(r, step)
        block_out[at, :] = (resid[at, :] + share[3, at, :].astype(F32)).astype(BF16)

    weights_part(cot, act, fd)
    spread_end(1)
    for h in range(2):
        spread["own", h].wait()
        for m in range(4):
            spread["core", m, h].wait()
        for key in ((1, 0, h), (1, 1, h), (2, 0, h), (2, 1, h), ("g1", h), ("g2", h)):
            spread[key].wait_send()
    for c in swaps + list(sends.values()):
        c.wait_send()


def ffn_part(gated, w_out, tokens, gain, bias, w_up, w_down, cotangent, cid):
    rows, width = tokens.shape
    assert PLANE * gated.shape[1] == width and w_out.shape == (2 * rows, w_up.shape[1])
    span, hidden = 2 * rows, w_up.shape[1]
    sd = jax.ShapeDtypeStruct
    return comm_call(
        ffn_kernel,
        [
            sd((rows, width), BF16),
            sd((rows, width), F32),
            sd((8, width), F32),
            sd((2 * PLANE * rows, width), BF16),
            sd((width, hidden), BF16),
            sd((width, hidden), BF16),
        ],
        [gated, w_out, tokens, gain[None], bias[None], w_up, w_down, cotangent],
        [
            pltpu.VMEM((PLANE, span, width), BF16),
            pltpu.VMEM(w_up.shape, BF16),
            pltpu.VMEM(w_down.shape, BF16),
            pltpu.VMEM((PLANE, rows, width), BF16),
            pltpu.VMEM((2, rows, width // 2), BF16),
            pltpu.VMEM((2, rows, width // 2), BF16),
            pltpu.VMEM((rows, width // 2), BF16),
            pltpu.VMEM((rows, width // 2), BF16),
            pltpu.VMEM((rows, width), F32),
            pltpu.VMEM((span, width), BF16),
            pltpu.VMEM((span, hidden), BF16),
            pltpu.VMEM((span, hidden), F32),
            pltpu.VMEM((span, hidden), BF16),
            pltpu.VMEM((span, width), BF16),
            pltpu.VMEM((rows, width), BF16),
            pltpu.VMEM((2, 256, hidden), BF16),
            pltpu.VMEM((span, 512), F32),
            DMA((7,)),
            DMA((PLANE,)),
            DMA((PLANE, 2)),
            DMA((PLANE, 2)),
            DMA((6, 2)),
            DMA((6, 2)),
            DMA((3, 2)),
            DMA((3, 2)),
            DMA((6, 2)),
            DMA((6, 2)),
            DMA((4, 2)),
            DMA((4, 2)),
            DMA((2,)),
        ],
        cid,
        in_specs=[ANY, ANY, VM, VM, VM, ANY, ANY, ANY],
        out_specs=[VM, VM, VM, ANY, ANY, ANY],
    )


def attention_kernel(
    widths, by_rows,
    tok_ref, gain_ref, bias_ref, dec_ref, cbase, sbase, coff, soff, *refs,
):
    count = len(widths)
    shards_in, refs = refs[:count], refs[count:]
    (xg, q_out, k_out, v_out, gate_out, ret_out, gated_out, states_out, cos_out, sin_out, ccol, crow, scal), refs = (
        refs[:13], refs[13:],
    )
    full, refs = refs[:count], refs[count:]
    hold, refs = refs[:count], refs[count:]
    wl, refs = refs[: count - 1], refs[count - 1 :]
    (xn, xv, q, k, v, gate, ret, gated, cos, sin, kv, st, sloc, sgot, decg,
     lsem, psend, precv, usend, dsend, zrecv, xsend, xrecv, csend, crecv, tsend, trecv, ssend, srecv, osem, wsem) = refs
    me = Place()
    z, p, f = me.z, me.p, me.f
    spot = z * PLANE + p
    chunk = hold[0].shape[0]
    deep = chunk * PLANE
    tokens, width = xv.shape
    rows = tok_ref.shape[0]
    keys, values = q.shape[1], v.shape[1]
    half = keys // 2
    blocks = tokens // STRETCH
    greet(
        [(me.plane(m), None) for m in (1, 2, 3)]
        + [(me.partner(), None), (me.up(), z < LINE - 1), (me.down(), z > 0)]
    )

    def part(i, at):
        w = widths[i]
        if by_rows[i]:
            return shards_in[i].at[pl.ds(pl.multiple_of(at * w, w), w), :]
        return shards_in[i].at[:, pl.ds(pl.multiple_of(at * w, w), w)]

    def slot(i, ss):
        at = pl.ds(pl.multiple_of(ss * chunk, chunk), chunk)
        return full[i].at[:, at] if by_rows[i] else full[i].at[at, :]

    def block(i, zz):
        at = pl.ds(pl.multiple_of(zz * deep, deep), deep)
        return full[i].at[:, at] if by_rows[i] else full[i].at[at, :]

    local, plane, held = [], [], []
    for i in range(count):
        held.append(start(pltpu.make_async_copy(part(i, p), hold[i], lsem.at[i])))
        local.append(pltpu.make_async_copy(hold[i], slot(i, spot), lsem.at[i]))
        plane.append(
            [
                start(remote(part(i, me.xor(m)), slot(i, spot), psend.at[i, m], precv.at[i, m], me.plane(m)))
                for m in (1, 2, 3)
            ]
        )
    tiny = [start(remote(dec_ref, decg.at[p], tsend.at[m], trecv.at[m], me.plane(m))) for m in (1, 2, 3)]
    tiny_own = start(pltpu.make_async_copy(dec_ref, decg.at[p], tsend.at[0]))
    step = 32

    @pl.loop(0, rows, step=step)
    def _(r):
        at = rows_at(r, step)
        t = tok_ref[at, :].astype(F32)
        centered = t - jnp.mean(t, axis=1, keepdims=True)
        scale = lax.rsqrt(jnp.mean(centered * centered, axis=1, keepdims=True) + 1e-05)
        xn[at, :] = (centered * scale * gain_ref[...] + bias_ref[...]).astype(BF16)

    def seat(m, h=None):
        base = (me.xor(m) * 2 + f) * rows
        if h is None:
            return xv.at[rows_at(base, rows)]
        return xv.at[pl.ds(pl.multiple_of(base + h * (rows // 2), rows // 2), rows // 2)]

    x_own = start(pltpu.make_async_copy(xn, seat(0), lsem.at[count]))
    x1 = start(remote(xn, seat(0), xsend.at[0], xrecv.at[0], me.plane(1)))
    x2 = start(remote(xn, seat(0), xsend.at[1], xrecv.at[1], me.plane(2)))
    xc = start(remote(xn, seat(0), csend.at[0], crecv.at[0], me.partner()))
    for i in range(count):
        held[i].wait()
        local[i].start()

    def up_copy(i, zz):
        return remote(block(i, zz), block(i, zz), usend.at[i, zz], zrecv.at[i, zz], me.up())

    def down_copy(i, zz):
        return remote(block(i, zz), block(i, zz), dsend.at[i, zz], zrecv.at[i, zz], me.down())

    def own(i):
        local[i].wait()
        for c in plane[i]:
            c.wait_recv()

        @pl.when(z < LINE - 1)
        def _():
            up_copy(i, z).start()

        @pl.when(z > 0)
        def _():
            down_copy(i, z).start()

    def forward(i, t):
        @pl.when(z - t >= 0)
        def _():
            up_copy(i, z - t).wait_recv()

            @pl.when(z < LINE - 1)
            def _():
                up_copy(i, z - t).start()

        @pl.when(z + t < LINE)
        def _():
            down_copy(i, z + t).wait_recv()

            @pl.when(z > 0)
            def _():
                down_copy(i, z + t).start()

    def fetch(i):
        forward(i, LINE - 1)
        return start(pltpu.make_async_copy(full[i], wl[i], wsem.at[i]))

    K, V, Q, G, O = range(count)
    own(K)
    own(V)
    forward(K, 1)
    forward(K, 2)
    own(Q)

    for c in tiny:
        c.wait()
    tiny_own.wait()
    heads = lax.broadcasted_iota(jnp.int32, decg.shape[1:], 0)
    lines = [jnp.sum(jnp.where(heads == p, decg[j], 0.0), axis=0, keepdims=True) for j in range(blocks)]
    lines = jnp.concatenate(lines + [jnp.zeros_like(lines[0])] * (8 - blocks), axis=0)
    i0 = lax.broadcasted_iota(jnp.int32, (STRETCH, STRETCH), 0)
    i1 = lax.broadcasted_iota(jnp.int32, (STRETCH, STRETCH), 1)
    row_sums = jnp.dot(
        lines, jnp.where(i0 <= i1, 1.0, 0.0), preferred_element_type=F32, precision=lax.Precision.HIGHEST
    )
    col_sums = lax.dot_general(
        jnp.where(i1 <= i0, 1.0, 0.0), lines, (((1,), (1,)), ((), ())),
        preferred_element_type=F32, precision=lax.Precision.HIGHEST,
    )
    total = jnp.zeros((1, 1), F32)
    for c in range(blocks):
        end = row_sums[c : c + 1, STRETCH - 1 : STRETCH]
        crow[c] = jnp.broadcast_to(row_sums[c : c + 1, :], (8, STRETCH))
        ccol[c * STRETCH : (c + 1) * STRETCH, :] = col_sums[:, c : c + 1]
        scal[c] = jnp.broadcast_to(jnp.exp(end), (8, 128))
        scal[blocks + c] = jnp.broadcast_to(jnp.exp(total), (8, 128))
        total = total + end
    scal[2 * blocks] = jnp.broadcast_to(total, (8, 128))

    fine = coff.shape[0]

    @pl.loop(0, tokens // fine)
    def _(a):
        at = rows_at(a * fine, fine)
        ca, sa = cbase[a, 0:1, :], sbase[a, 0:1, :]
        cos[at, :] = ca * coff[...] - sa * soff[...]
        sin[at, :] = sa * coff[...] + ca * soff[...]

    forward(V, 1)
    x1.wait_recv()
    g1 = start(remote(seat(1, 0), seat(1, 0), xsend.at[2], xrecv.at[2], me.plane(2)))
    c1 = start(remote(seat(1), seat(1), csend.at[1], crecv.at[1], me.partner()))
    x2.wait_recv()
    g2 = start(remote(seat(2, 1), seat(2, 1), xsend.at[3], xrecv.at[3], me.plane(1)))
    c2 = start(remote(seat(2), seat(2), csend.at[2], crecv.at[2], me.partner()))
    forward(V, 2)
    forward(Q, 1)
    own(G)
    forward(Q, 2)
    own(O)
    load_k = fetch(K)
    g1.wait_recv()
    g2.wait_recv()
    c3 = start(remote(seat(3), seat(3), csend.at[3], crecv.at[3], me.partner()))
    x_own.wait()
    for c in (xc, c1, c2, c3):
        c.wait_recv()
    outs = []

    def put(src, dst):
        outs.append(start(pltpu.make_async_copy(src, dst, osem.at[len(outs)])))

    put(xv, xg)
    put(cos, cos_out)
    put(sin, sin_out)
    load_k.wait()

    def turned(at, w, dst):
        y = nn(xv[at, :], w[...])
        a, b = y[:, :half], y[:, half:]
        dst[at, :half] = (a * cos[at, :] - b * sin[at, :]).astype(BF16)
        dst[at, half:] = (b * cos[at, :] + a * sin[at, :]).astype(BF16)

    @pl.loop(0, blocks)
    def _(c):
        turned(rows_at(c * STRETCH, STRETCH), wl[K], k)

    fetch(V).wait()

    @pl.loop(0, blocks)
    def _(c):
        at = rows_at(c * STRETCH, STRETCH)
        val = nn(xv[at, :], wl[V][...]).astype(BF16)
        v[at, :] = val
        end = crow[c, 0:1, STRETCH - 1 : STRETCH]
        kv[c] = tn(k[at, :], (val.astype(F32) * jnp.exp(end - ccol[at, :])).astype(BF16))

    put(k, k_out)
    put(v, v_out)
    sloc[...] = kv[0]
    kv[0] = jnp.zeros_like(sloc)
    for c in range(1, blocks):
        nxt = sloc[...] * scal[c, 0:1, 0:1] + kv[c]
        kv[c] = sloc[...]
        sloc[...] = nxt

    def state_copy(zz):
        return remote(st.at[0], sgot, ssend.at[zz], srecv.at[zz], me.up())

    def send_state():
        st[0] = sloc[...].astype(BF16)
        state_copy(0).start()

    @pl.when(z == 0)
    def _():
        send_state()

    def pass_state(zz):
        @pl.when(z == zz)
        def _():
            state_copy(0).wait_recv()
            if zz < LINE - 1:
                sloc[...] = sloc[...] + sgot[...].astype(F32) * jnp.exp(scal[2 * blocks, 0:1, 0:1])
                send_state()

    pass_state(1)
    forward(G, 1)
    forward(O, 1)
    fetch(Q).wait()
    t_size = 256

    @pl.loop(0, blocks)
    def _(c):
        blk = rows_at(c * STRETCH, STRETCH)
        turned(blk, wl[Q], q)
        row = crow[c, 0:1, :]
        for r in range(0, STRETCH, t_size):
            at = rows_at(c * STRETCH + r, t_size)
            col = ccol[at, :]
            t_index = lax.broadcasted_iota(jnp.int32, (t_size, STRETCH), 0) + r
            s_index = lax.broadcasted_iota(jnp.int32, (t_size, STRETCH), 1)
            mask = jnp.where(t_index >= s_index, jnp.exp(jnp.minimum(col - row, 0.0)), 0.0)
            scores = (nt(q[at, :], k[blk, :]) * mask).astype(BF16)
            ret[at, :] = nn(scores, v[blk, :])

    put(q, q_out)
    pass_state(2)
    forward(G, 2)
    forward(O, 2)
    pass_state(3)

    @pl.when((z > 0) & (z < LINE - 1))
    def _():
        state_copy(0).wait_send()

    @pl.when(z == 0)
    def _():
        state_copy(0).wait_send()
        sgot[...] = jnp.zeros_like(sgot)

    for c in range(blocks):
        st[c] = (kv[c] + sgot[...].astype(F32) * scal[blocks + c, 0:1, 0:1]).astype(BF16)

    @pl.loop(0, blocks)
    def _(c):
        at = rows_at(c * STRETCH, STRETCH)
        decayed = (q[at, :].astype(F32) * jnp.exp(ccol[at, :])).astype(BF16)
        ret[at, :] += nn(decayed, st[c])

    put(ret, ret_out)
    put(st, states_out)
    fetch(G).wait()

    @pl.loop(0, tokens, step=256)
    def _(r):
        at = rows_at(r, 256)
        g = nn(xv[at, :], wl[G][...])
        gate[at, :] = g
        t = ret[at, :]
        centered = t - jnp.mean(t, axis=1, keepdims=True)
        scale = lax.rsqrt(jnp.mean(centered * centered, axis=1, keepdims=True) + 1e-05)
        gated[at, :] = (g / (1.0 + jnp.exp(-g)) * centered * scale).astype(BF16)

    put(gate, gate_out)
    put(gated, gated_out)
    forward(O, LINE - 1)
    for c in (xc, c1, c2, c3, x1, x2, g1, g2):
        c.wait_send()
    for i in range(count):
        for c in plane[i]:
            c.wait_send()
        for zz in range(LINE):

            @pl.when((z < LINE - 1) & (zz <= z))
            def _():
                up_copy(i, zz).wait_send()

            @pl.when((z > 0) & (zz >= z))
            def _():
                down_copy(i, zz).wait_send()

    for c in outs:
        c.wait()


def attention(tokens, gain, bias, decays, tables, shards_in, by_rows, cid):
    rows, width = tokens.shape
    count = len(shards_in)
    chunk = shards_in[0].shape[0]
    group = 2 * PLANE * rows
    blocks = group // STRETCH
    parts = [
        (w.shape[0] // PLANE, chunk) if r else (chunk, w.shape[1] // PLANE) for w, r in zip(shards_in, by_rows)
    ]
    widths = [s[0] if r else s[1] for s, r in zip(parts, by_rows)]
    wholes = [(s[0], width) if r else (width, s[1]) for s, r in zip(parts, by_rows)]
    values, keys = widths[1], widths[0]
    half = keys // 2
    sd = jax.ShapeDtypeStruct
    outs = [
        sd((group, width), BF16),
        sd((group, keys), BF16),
        sd((group, keys), BF16),
        sd((group, values), BF16),
        sd((group, values), F32),
        sd((group, values), F32),
        sd((group, values), BF16),
        sd((blocks, keys, values), BF16),
        sd((group, half), F32),
        sd((group, half), F32),
        sd((group, 1), F32),
        sd((blocks, 8, STRETCH), F32),
        sd((2 * blocks + 1, 8, 128), F32),
    ] + [sd(s, BF16) for s in wholes]
    scratch = (
        [pltpu.VMEM(s, BF16) for s in parts]
        + [pltpu.VMEM(s, BF16) for s in wholes[:-1]]
        + [
            pltpu.VMEM((rows, width), BF16),
            pltpu.VMEM((group, width), BF16),
            pltpu.VMEM((group, keys), BF16),
            pltpu.VMEM((group, keys), BF16),
            pltpu.VMEM((group, values), BF16),
            pltpu.VMEM((group, values), F32),
            pltpu.VMEM((group, values), F32),
            pltpu.VMEM((group, values), BF16),
            pltpu.VMEM((group, half), F32),
            pltpu.VMEM((group, half), F32),
            pltpu.VMEM((blocks, keys, values), F32),
            pltpu.VMEM((blocks, keys, values), BF16),
            pltpu.VMEM((keys, values), F32),
            pltpu.VMEM((keys, values), BF16),
            pltpu.VMEM((PLANE,) + decays.shape, F32),
            DMA((count + 1,)),
            DMA((count, PLANE)),
            DMA((count, PLANE)),
            DMA((count, LINE)),
            DMA((count, LINE)),
            DMA((count, LINE)),
            DMA((4,)),
            DMA((4,)),
            DMA((4,)),
            DMA((4,)),
            DMA((PLANE,)),
            DMA((PLANE,)),
            DMA((1,)),
            DMA((1,)),
            DMA((16,)),
            DMA((count,)),
        ]
    )
    return comm_call(
        functools.partial(attention_kernel, widths, by_rows),
        outs,
        [tokens, gain[None], bias[None], decays] + list(tables) + list(shards_in),
        scratch,
        cid,
        in_specs=[VM] * 8 + [ANY] * count,
        out_specs=[ANY] * 10 + [VM] * 3 + [ANY] * count,
    )


class LineSum:
    def __init__(self, me, own, rx, usend, urecv, dsend, drecv, add):
        self.me, self.own, self.rx, self.add = me, own, rx, add
        self.sems = usend, urecv, dsend, drecv

    def up(self, src, zz):
        return remote(src, self.rx.at[zz], self.sems[0].at[zz], self.sems[1].at[zz], self.me.up())

    def down(self, src, zz):
        slot = jnp.where(zz == self.me.z - 1, LINE, zz)
        return remote(src, self.rx.at[slot], self.sems[2].at[zz], self.sems[3].at[zz], self.me.down())

    def begin(self, order=(3, 2, 1), src=None):
        src = src or self.own
        for zz in order:

            @pl.when(self.me.z == 0)
            def _():
                self.up(src(zz), zz).start()

            @pl.when(self.me.z == LINE - 1)
            def _():
                self.down(src(LINE - 1 - zz), LINE - 1 - zz).start()

    def pass_up(self, zz):
        self.up(self.own(zz), zz).wait_recv()
        self.add(self.rx.at[zz], self.own(zz))
        self.up(self.rx.at[zz], zz).start()

    def pass_down(self, zz):
        self.down(self.own(zz), zz).wait_recv()
        self.add(self.rx.at[zz], self.own(zz))
        self.down(self.rx.at[zz], zz).start()

    def near(self, k):
        @pl.when(self.me.z == 1)
        def _():
            self.pass_up(LINE - 1 - k)

        @pl.when(self.me.z == 2)
        def _():
            self.pass_down(k)

    def far(self):
        @pl.when(self.me.z == 1)
        def _():
            self.pass_down(0)

        @pl.when(self.me.z == 2)
        def _():
            self.pass_up(LINE - 1)

    def arrive(self):
        z = self.me.z

        @pl.when(z > 0)
        def _():
            self.up(self.own(z), z).wait_recv()

        @pl.when(z < LINE - 1)
        def _():
            self.down(self.own(z), z).wait_recv()

    def finish(self):
        z = self.me.z
        for zz in range(LINE):

            @pl.when((z < LINE - 1) & (zz > z))
            def _():
                self.up(self.own(zz), zz).wait_send()

            @pl.when((z > 0) & (zz < z))
            def _():
                self.down(self.own(zz), zz).wait_send()


def add_rows(dst, src):
    rows = dst.shape[0]
    step = 32 if dst.shape[1] > 512 else 128

    @pl.loop(0, rows, step=step)
    def _(r):
        at = rows_at(r, step)
        dst[at, :] = (dst[at, :].astype(F32) + src[at, :].astype(F32)).astype(BF16)


def total_rows(z, dst, own, rx):
    rows = dst.shape[0]
    step = 32 if dst.shape[1] > 512 else 128

    @pl.loop(0, rows, step=step)
    def _(r):
        at = rows_at(r, step)
        v = own[at, :].astype(F32)
        v = v + jnp.where(z > 0, rx[z, at, :].astype(F32), 0.0)
        v = v + jnp.where(z < LINE - 1, rx[LINE, at, :].astype(F32), 0.0)
        dst[at, :] = v.astype(dst.dtype)


def line_sems():
    return [DMA((LINE,)) for _ in range(4)]


def retention_back_kernel(
    da_ref, wo_ref, gated_ref, gate_ref, ret_ref, q_ref, k_ref, v_ref, s_ref, cos_ref, sin_ref,
    ccol_ref, crow_ref, scal_ref, xg_ref, fu_ref, fd_ref,
    dh, sums, f1, av_out, aq_out,
    da, wo, gated, gr, q, k, v, st, cos, sin, dr, xt, ao, ag, rxo, rxg, fin, qo, gb, lg, got, rxf, fo, pbuf, gbuf,
    lsem, gsem, xsem, fsend, frecv, osem, fosem, ssend, srecv, psend, precv, *line,
):
    me = Place()
    z, p = me.z, me.p
    greet(
        [(me.plane(m), None) for m in (1, 2, 3)]
        + [(me.up(), z < LINE - 1), (me.down(), z > 0)]
    )
    width = da.shape[1]
    tokens = da.shape[0]
    keys, values = q.shape[1], v.shape[1]
    blocks = tokens // STRETCH
    half = keys // 2
    pq = [me.xor(m) for m in range(4)]
    chunk = fu_ref.shape[0] // SPANS

    def f_block(h, zp, place):
        return (fu_ref, fd_ref)[h].at[pl.ds(pl.multiple_of((zp * PLANE + place) * chunk, chunk), chunk), :]

    away = ((1, 3), (2, 3))
    kept = ((0, 2), (0, 1))
    nbr = (1, 2)

    def f_copy(h, zp, j):
        return remote(
            f_block(h, zp, pq[away[h][j]]), rxf.at[h, zp, j], fsend.at[h, zp, j], frecv.at[h, zp, j], me.plane(nbr[h])
        )

    loads = [
        start(pltpu.make_async_copy(a, b, lsem.at[i]))
        for i, (a, b) in enumerate(
            [(da_ref, da), (gated_ref, gated), (wo_ref, wo), (q_ref, q), (k_ref, k), (v_ref, v), (s_ref, st),
             (cos_ref, cos), (sin_ref, sin)]
        )
    ]
    for zp in range(LINE):
        for h in range(2):
            for j in range(2):
                f_copy(h, zp, j).start()

    def f_own(u):
        h, zp = u % 2, u // 2
        return [
            pltpu.make_async_copy(f_block(h, zp, pq[kept[h][j]]), fo.at[u % 2, j], fosem.at[u % 2, j])
            for j in range(2)
        ]

    def f_out(u):
        h, zp = u % 2, u // 2
        return pltpu.make_async_copy(rxf.at[h, zp], f1.at[h, zp], osem.at[u])

    for u in range(2):
        for c in f_own(u):
            c.start()

    def f_unit(u):
        h, zp = u % 2, u // 2
        for j, c in enumerate(f_own(u)):
            c.wait()
            f_copy(h, zp, j).wait_recv()
            add_rows(rxf.at[h, zp, j], fo.at[u % 2, j])
        f_out(u).start()
        if u + 2 < 2 * LINE:
            for c in f_own(u + 2):
                c.start()

    def tile_rows(i):
        return rows_at(i * 256, 256)

    def gate_loads(i):
        at = tile_rows(i)
        slot = i % 2
        return (
            pltpu.make_async_copy(gate_ref.at[at, :], gr.at[slot, 0], gsem.at[slot, 0]),
            pltpu.make_async_copy(ret_ref.at[at, :], gr.at[slot, 1], gsem.at[slot, 1]),
        )

    for c in gate_loads(0):
        c.start()

    out_sum = LineSum(me, lambda zz: ao.at[rows_at(zz * (width // LINE), width // LINE), :], rxo, *line[:4], add_rows)
    gate_sum = LineSum(me, lambda zz: ag.at[rows_at(zz * (width // LINE), width // LINE), :], rxg, *line[4:], add_rows)

    loads[0].wait()
    loads[1].wait()

    @pl.loop(0, width, step=256)
    def _(i):
        at = rows_at(i, 256)
        ao[at, :] = tn(da[:, at], gated[...]).astype(BF16)

    out_sum.begin((3, 2))
    for c in loads[2:]:
        c.wait()

    tiles = tokens // 256

    @pl.loop(0, tiles)
    def _(i):
        @pl.when(i + 1 < tiles)
        def _():
            for c in gate_loads(i + 1):
                c.start()

        for c in gate_loads(i):
            c.wait()
        at = tile_rows(i)
        slot = i % 2
        dgated = nt(da[at, :], wo[...])
        gate = gr[slot, 0]
        ret = gr[slot, 1]
        centered = ret - jnp.mean(ret, axis=1, keepdims=True)
        scale = lax.rsqrt(jnp.mean(centered * centered, axis=1, keepdims=True) + 1e-05)
        grouped = centered * scale
        sig = 1.0 / (1.0 + jnp.exp(-gate))
        silu = gate * sig
        dh[at, 2 * keys + values :] = (dgated * grouped * (sig * (1.0 + gate * (1.0 - sig)))).astype(BF16)
        dg = dgated * silu
        dr[at, :] = (
            scale * (dg - jnp.mean(dg, axis=1, keepdims=True) - grouped * jnp.mean(dg * grouped, axis=1, keepdims=True))
        ).astype(BF16)

    lg[...] = jnp.zeros_like(lg)

    @pl.loop(0, blocks)
    def _(c):
        at = rows_at(c * STRETCH, STRETCH)
        decayed = (q[at, :].astype(F32) * jnp.exp(ccol_ref[at, :])).astype(BF16)
        got_q = tn(decayed, dr[at, :])
        qo[c] = got_q
        lg[...] += scal_ref[blocks + c, 0:1, 0:1] * got_q

    state_copy = remote(gb.at[0], got, ssend.at[0], srecv.at[0], me.down())

    def pass_state(zz):
        @pl.when(z == zz)
        def _():
            if zz < LINE - 1:
                state_copy.wait_recv()
            if zz > 0:
                add = lg[...]
                if zz < LINE - 1:
                    add = add + got[...].astype(F32) * jnp.exp(scal_ref[2 * blocks, 0:1, 0:1])
                gb[0] = add.astype(BF16)
                state_copy.start()

    pass_state(LINE - 1)
    out_sum.begin((1,))
    out_sum.near(0)
    def x_tile(i):
        return pltpu.make_async_copy(xg_ref.at[:, rows_at(i * 256, 256)], xt.at[i % 2], xsem.at[i % 2])

    x_tile(0).start()

    @pl.loop(0, width // 256)
    def _(i):
        @pl.when(i + 1 < width // 256)
        def _():
            x_tile(i + 1).start()

        x_tile(i).wait()
        ag[rows_at(i * 256, 256), :] = tn(xt[i % 2], dh[:, 2 * keys + values :]).astype(BF16)

    gate_sum.begin()
    out_sum.near(1)
    pass_state(2)
    f_unit(0)
    f_unit(1)
    out_sum.far()

    pass_state(1)
    pass_state(0)

    @pl.when(z > 0)
    def _():
        state_copy.wait_send()

    @pl.when(z < LINE - 1)
    def _():
        lg[...] = got[...].astype(F32)

    @pl.when(z == LINE - 1)
    def _():
        lg[...] = jnp.zeros_like(lg)

    for c in reversed(range(blocks)):
        gb[c] = lg[...].astype(BF16)
        if c:
            lg[...] = lg[...] * scal_ref[c, 0:1, 0:1] + qo[c]

    t_size = 256

    @pl.loop(0, blocks)
    def _(c):
        blk = rows_at(c * STRETCH, STRETCH)
        row = crow_ref[c, 0:1, :]
        end = crow_ref[c, 0:1, STRETCH - 1 : STRETCH]
        for r in range(0, STRETCH, t_size):
            at = rows_at(c * STRETCH + r, t_size)
            col = ccol_ref[at, :]
            t_index = lax.broadcasted_iota(jnp.int32, (t_size, STRETCH), 0) + r
            s_index = lax.broadcasted_iota(jnp.int32, (t_size, STRETCH), 1)
            mask = jnp.where(t_index >= s_index, jnp.exp(jnp.minimum(col - row, 0.0)), 0.0)
            pbuf[r : r + t_size, :] = (nt(q[at, :], k[blk, :]) * mask).astype(BF16)
            g = (nt(dr[at, :], v[blk, :]) * mask).astype(BF16)
            gbuf[r : r + t_size, :] = g
            dq = nt(dr[at, :], st[c]) * jnp.exp(col) + nn(g, k[blk, :])
            a, b = dq[:, :half], dq[:, half:]
            dh[at, :half] = (a * cos[at, :] + b * sin[at, :]).astype(BF16)
            dh[at, half:keys] = (b * cos[at, :] - a * sin[at, :]).astype(BF16)
        for r in range(0, STRETCH, t_size):
            at = rows_at(c * STRETCH + r, t_size)
            tail = jnp.exp(end - ccol_ref[at, :])
            w = (v[at, :].astype(F32) * tail).astype(BF16)
            dk = nt(w, gb[c]) + tn(gbuf[:, r : r + t_size], q[blk, :])
            a, b = dk[:, :half], dk[:, half:]
            dh[at, keys : keys + half] = (a * cos[at, :] + b * sin[at, :]).astype(BF16)
            dh[at, keys + half : 2 * keys] = (b * cos[at, :] - a * sin[at, :]).astype(BF16)
            dv = nn(k[at, :], gb[c]) * tail + tn(pbuf[:, r : r + t_size], dr[blk, :])
            dh[at, 2 * keys : 2 * keys + values] = dv.astype(BF16)

    plane = []

    def deal(i, chain, a):
        chain.arrive()
        total_rows(z, fin.at[i], a.at[rows_at(z * (width // LINE), width // LINE), :], chain.rx)
        cols = pl.ds(i * values, values)
        for m in (1, 2, 3):
            plane.append(
                start(
                    remote(
                        fin.at[i, rows_at(pq[m] * chunk, chunk), :], sums.at[p, :, cols],
                        psend.at[i, m], precv.at[i, m], me.plane(m),
                    )
                )
            )
        plane.append(
            start(
                pltpu.make_async_copy(
                    fin.at[i, rows_at(p * chunk, chunk), :], sums.at[p, :, cols], psend.at[i, 0]
                )
            )
        )

    gate_sum.near(0)
    for u in range(2, 4):
        f_unit(u)
    deal(0, out_sum, ao)
    x_tile(0).start()
    wide = 2 * keys + values

    @pl.loop(0, width // 256)
    def _(i):
        @pl.when(i + 1 < width // 256)
        def _():
            x_tile(i + 1).start()

        x_tile(i).wait()
        da[rows_at(i * 256, 256), :wide] = tn(xt[i % 2], dh[:, :wide]).astype(BF16)

    to_last = [
        start(pltpu.make_async_copy(da.at[:, : 2 * keys], aq_out, lsem.at[0])),
        start(pltpu.make_async_copy(da.at[:, 2 * keys : wide], av_out, lsem.at[1])),
    ]
    gate_sum.near(1)
    gate_sum.far()
    for u in range(4, 6):
        f_unit(u)
    deal(1, gate_sum, ag)
    for u in range(6, 2 * LINE):
        f_unit(u)
    for c in plane + to_last:
        c.wait()
    out_sum.finish()
    gate_sum.finish()
    for u in range(2 * LINE):
        f_out(u).wait()
    for zp in range(LINE):
        for h in range(2):
            for j in range(2):
                f_copy(h, zp, j).wait_send()


def retention_back(da, wo, gated, gate, ret, q, k, v, states, cos, sin, ccol, crow, scal, xg, fu, fd, cid):
    tokens, width = da.shape
    keys, values = q.shape[1], v.shape[1]
    chunk = width // SPANS
    blocks = tokens // STRETCH
    hidden = fu.shape[1]
    deep = width // LINE
    return comm_call(
        retention_back_kernel,
        [
            jax.ShapeDtypeStruct((tokens, 2 * keys + 2 * values), BF16),
            jax.ShapeDtypeStruct((PLANE, chunk, 2 * values), BF16),
            jax.ShapeDtypeStruct((2, LINE, 2, chunk, hidden), BF16),
            jax.ShapeDtypeStruct((width, values), BF16),
            jax.ShapeDtypeStruct((width, 2 * keys), BF16),
        ],
        [da, wo, gated, gate, ret, q, k, v, states, cos, sin, ccol, crow, scal, xg, fu, fd],
        [
            pltpu.VMEM((tokens, width), BF16),
            pltpu.VMEM(wo.shape, BF16),
            pltpu.VMEM(gated.shape, BF16),
            pltpu.VMEM((2, 2, 256, values), F32),
            pltpu.VMEM(q.shape, BF16),
            pltpu.VMEM(k.shape, BF16),
            pltpu.VMEM(v.shape, BF16),
            pltpu.VMEM(states.shape, BF16),
            pltpu.VMEM(cos.shape, F32),
            pltpu.VMEM(sin.shape, F32),
            pltpu.VMEM((tokens, values), BF16),
            pltpu.VMEM((2, tokens, 256), BF16),
            pltpu.VMEM((width, values), BF16),
            pltpu.VMEM((width, values), BF16),
            pltpu.VMEM((LINE + 1, deep, values), BF16),
            pltpu.VMEM((LINE + 1, deep, values), BF16),
            pltpu.VMEM((2, deep, values), BF16),
            pltpu.VMEM((blocks, keys, values), F32),
            pltpu.VMEM((blocks, keys, values), BF16),
            pltpu.VMEM((keys, values), F32),
            pltpu.VMEM((keys, values), BF16),
            pltpu.VMEM((2, LINE, 2, chunk, hidden), BF16),
            pltpu.VMEM((2, 2, chunk, hidden), BF16),
            pltpu.VMEM((STRETCH, STRETCH), BF16),
            pltpu.VMEM((STRETCH, STRETCH), BF16),
            DMA((9,)),
            DMA((2, 2)),
            DMA((2,)),
            DMA((2, LINE, 2)),
            DMA((2, LINE, 2)),
            DMA((2 * LINE,)),
            DMA((2, 2)),
            DMA((1,)),
            DMA((1,)),
            DMA((2, PLANE)),
            DMA((2, PLANE)),
        ]
        + line_sems()
        + line_sems(),
        cid,
        in_specs=[ANY] * 11 + [VM] * 3 + [ANY] * 3,
        out_specs=[VM, ANY, ANY, ANY, ANY],
    )


def last_kernel(
    dh_ref, av_ref, aq_ref, wq_ref, wk_ref, wv_ref, wg_ref, f1_ref, tok_ref, gain_ref, resid_ref, second_ref,
    grad_tokens, gains, fout, sums,
    dh, wh, share, rx0, rx1a, rx1b, rx2a, rx2b, av, aq, rxv, rxq, fin, rf2, kf, rxfa, rxfb, grx,
    lsem, fsend, frecv, csend, crecv, xsend, xrecv, gsend, grecv, psend, precv, *line,
):
    me = Place()
    z, p, f = me.z, me.p, me.f
    rounds = [
        [me.partner()],
        [me.plane(m) for m in (1, 2, 3)],
        [me.at((z + t) % LINE, p, f) for t in range(1, LINE)],
    ]
    greet([(d, None) for r in rounds for d in r])
    width, keys2, values = av.shape[0], aq.shape[1], av.shape[1]
    rows = tok_ref.shape[0]
    pq = [me.xor(m) for m in range(4)]
    chunk = width // SPANS
    deep = width // LINE

    def f_copy(h, zp):
        return remote(f1_ref.at[h, zp, 1], rf2.at[h, zp], fsend.at[h, zp], frecv.at[h, zp], me.plane(2 - h))

    def block_of(a, size):
        return lambda zz: a.at[rows_at(zz * size, size), :]

    v_sum = LineSum(me, block_of(av, deep), rxv, *line[:4], add_rows)
    q_sum = LineSum(me, block_of(aq, deep), rxq, *line[4:8], add_rows)
    fa_sum = LineSum(me, lambda zz: kf.at[0, zz], rxfa, *line[8:12], add_rows)
    fb_sum = LineSum(me, lambda zz: kf.at[1, zz], rxfb, *line[12:16], add_rows)
    v_sum.begin(src=block_of(av_ref, deep))
    q_sum.begin(src=block_of(aq_ref, deep))
    for zp in (3, 0, 2, 1):
        for h in range(2):
            f_copy(h, zp).start()
    load = start(pltpu.make_async_copy(dh_ref, dh, lsem.at[0]))
    owns = [
        start(pltpu.make_async_copy(av_ref, av, lsem.at[7])),
        start(pltpu.make_async_copy(aq_ref, aq, lsem.at[8])),
    ]
    loads, at = [], 0
    for i, w in enumerate((wq_ref, wk_ref, wv_ref, wg_ref)):
        size = w.shape[1]
        loads.append(start(pltpu.make_async_copy(w, wh.at[:, at : at + size], lsem.at[1 + i])))
        at += size
    keeps = [start(pltpu.make_async_copy(f1_ref.at[h, :, 0], kf.at[h], lsem.at[5 + h])) for h in range(2)]

    load.wait()
    for c in loads + owns:
        c.wait()

    own_rows, their_rows = rows_at(f * rows, rows), rows_at((1 - f) * rows, rows)
    wide = width // 2
    ca, cb = pl.ds(0, wide), pl.ds(wide, wide)
    everything, whole = pl.ds(0, width), pl.ds(0, wide)
    first, sends = {}, {}

    def share_part(m):
        at_rows = rows_at(pq[m] * 2 * rows, 2 * rows)

        @pl.loop(0, width, step=256)
        def _(c):
            at = rows_at(c, 256)
            share[m, :, at] = nt(dh[at_rows, :], wh[at, :]).astype(BF16)

        first[m] = start(
            remote(share.at[m, their_rows], rx0.at[m], csend.at[m], crecv.at[m], me.partner())
        )

    def pass_on(m):
        first[m].wait_recv()
        add_into(rx0.at[m], everything, share.at[m, own_rows], everything)
        k = 0 if m == 3 else 1
        if m & 1:
            sends["a", k] = start(
                remote(rx0.at[m, :, ca], rx1a.at[k], xsend.at[k], xrecv.at[k], me.plane(1))
            )
        if m & 2:
            sends["b", k] = start(
                remote(rx0.at[m, :, cb], rx1b.at[k], xsend.at[2 + k], xrecv.at[2 + k], me.plane(2))
            )

    share_part(3)
    share_part(1)
    pass_on(3)
    v_sum.near(0)
    share_part(2)
    pass_on(1)
    share_part(0)
    v_sum.near(1)
    pass_on(2)
    pass_on(0)
    v_sum.far()
    for c in keeps:
        c.wait()
    for zp in (3, 0, 2, 1):
        for h in range(2):
            f_copy(h, zp).wait_recv()
            add_rows(kf.at[h, zp], rf2.at[h, zp])
    for zz in (3, 2, 1):
        fa_sum.begin((zz,))
        fb_sum.begin((zz,))
    q_sum.near(0)
    sends["a", 0].wait_recv()
    add_into(rx1a.at[0], whole, rx0.at[2], ca)
    s2a = start(remote(rx1a.at[0], rx2a, xsend.at[4], xrecv.at[4], me.plane(2)))
    sends["b", 0].wait_recv()
    add_into(rx1b.at[0], whole, rx0.at[1], cb)
    s2b = start(remote(rx1b.at[0], rx2b, xsend.at[5], xrecv.at[5], me.plane(1)))
    q_sum.near(1)
    q_sum.far()
    sends["a", 1].wait_recv()
    sends["b", 1].wait_recv()
    s2a.wait_recv()
    s2b.wait_recv()
    gains[...] = jnp.zeros_like(gains)
    gains[2:4, :] = second_ref[0:2, :]
    step = 32

    @pl.loop(0, rows, step=step)
    def _(r):
        at = rows_at(r, step)
        left = rx0[0, at, ca].astype(F32) + rx1a[1, at, :].astype(F32) + rx2a[at, :].astype(F32)
        right = rx0[0, at, cb].astype(F32) + rx1b[1, at, :].astype(F32) + rx2b[at, :].astype(F32)
        dx = jnp.concatenate([left, right], axis=1)
        v = tok_ref[at, :].astype(F32)
        centered = v - jnp.mean(v, axis=1, keepdims=True)
        scale = lax.rsqrt(jnp.mean(centered * centered, axis=1, keepdims=True) + 1e-05)
        hat = centered * scale
        gains[0:1, :] += jnp.sum(dx * hat, axis=0, keepdims=True)
        gains[1:2, :] += jnp.sum(dx, axis=0, keepdims=True)
        g = dx * gain_ref[...]
        back = scale * (
            g - jnp.mean(g, axis=1, keepdims=True) - hat * jnp.mean(g * hat, axis=1, keepdims=True)
        )
        grad_tokens[at, :] = (back + resid_ref[at, :]).astype(BF16)

    def gain_copies(r):
        base = (0, 1, 4)[r]
        return [
            remote(gains, grx.at[base + i], gsend.at[base + i], grecv.at[base + i], d)
            for i, d in enumerate(rounds[r])
        ]

    def gain_begin(r):
        for c in gain_copies(r):
            c.start()

    def gain_end(r):
        for c in gain_copies(r):
            c.wait()
        for i in range(len(rounds[r])):
            gains[...] += grx[(0, 1, 4)[r] + i]

    plane = []

    def deal(i, chain, a):
        chain.arrive()
        total_rows(z, fin.at[i], a.at[rows_at(z * deep, deep), :], chain.rx)
        cols = pl.ds(i * values, values)
        for m in (1, 2, 3):
            plane.append(
                start(
                    remote(
                        fin.at[i, rows_at(pq[m] * chunk, chunk), :], sums.at[p, :, cols],
                        psend.at[i, m], precv.at[i, m], me.plane(m),
                    )
                )
            )
        plane.append(
            start(
                pltpu.make_async_copy(
                    fin.at[i, rows_at(p * chunk, chunk), :], sums.at[p, :, cols], psend.at[i, 0]
                )
            )
        )

    gain_begin(0)
    deal(0, v_sum, av)
    gain_end(0)
    gain_begin(1)
    deal(1, q_sum, aq)
    gain_end(1)
    gain_begin(2)
    fa_sum.near(0)
    fb_sum.near(0)
    fa_sum.near(1)
    fa_sum.far()
    fb_sum.near(1)
    fb_sum.far()
    fa_sum.arrive()
    total_rows(z, fout.at[0], kf.at[0, z], rxfa)
    fb_sum.arrive()
    total_rows(z, fout.at[1], kf.at[1, z], rxfb)
    gain_end(2)
    for c in plane:
        c.wait()
    for chain in (v_sum, q_sum, fa_sum, fb_sum):
        chain.finish()
    for c in list(first.values()) + list(sends.values()) + [s2a, s2b]:
        c.wait_send()
    for zp in range(LINE):
        for h in range(2):
            f_copy(h, zp).wait_send()


def last_sums(dh, av, aq, wq, wk, wv, wg, f1, tokens, gain, resid, second, cid):
    width = av.shape[0]
    rows = tokens.shape[0]
    keys, values = wq.shape[1], wv.shape[1]
    assert 2 * keys == values
    chunk, deep = width // SPANS, width // LINE
    hidden = f1.shape[-1]
    return comm_call(
        last_kernel,
        [
            jax.ShapeDtypeStruct((rows, width), BF16),
            jax.ShapeDtypeStruct((8, width), F32),
            jax.ShapeDtypeStruct((2, chunk, hidden), F32),
            jax.ShapeDtypeStruct((PLANE, chunk, 2 * values), BF16),
        ],
        [dh, av, aq, wq, wk, wv, wg, f1, tokens, gain[None], resid, second],
        [
            pltpu.VMEM(dh.shape, BF16),
            pltpu.VMEM((width, dh.shape[1]), BF16),
            pltpu.VMEM((PLANE, 2 * rows, width), BF16),
            pltpu.VMEM((PLANE, rows, width), BF16),
            pltpu.VMEM((2, rows, width // 2), BF16),
            pltpu.VMEM((2, rows, width // 2), BF16),
            pltpu.VMEM((rows, width // 2), BF16),
            pltpu.VMEM((rows, width // 2), BF16),
            pltpu.VMEM((width, values), BF16),
            pltpu.VMEM((width, 2 * keys), BF16),
            pltpu.VMEM((LINE + 1, deep, values), BF16),
            pltpu.VMEM((LINE + 1, deep, 2 * keys), BF16),
            pltpu.VMEM((2, deep, values), BF16),
            pltpu.VMEM((2, LINE, chunk, hidden), BF16),
            pltpu.VMEM((2, LINE, chunk, hidden), BF16),
            pltpu.VMEM((LINE + 1, chunk, hidden), BF16),
            pltpu.VMEM((LINE + 1, chunk, hidden), BF16),
            pltpu.VMEM((7, 8, width), F32),
            DMA((9,)),
            DMA((2, LINE)),
            DMA((2, LINE)),
            DMA((4,)),
            DMA((4,)),
            DMA((6,)),
            DMA((6,)),
            DMA((7,)),
            DMA((7,)),
            DMA((2, PLANE)),
            DMA((2, PLANE)),
        ]
        + line_sems()
        + line_sems()
        + line_sems()
        + line_sems(),
        cid,
        in_specs=[ANY] * 8 + [VM] * 4,
        out_specs=[VM, VM, VM, ANY],
    )


def outputs_kernel(last, first, ffn, low_out, low_grad, q, k, v, gate, out, up, down, block_out, grad_tokens):
    values = v.shape[1]
    keys = q.shape[1]
    v[...] = last[0, :, :values].astype(F32)
    q[...] = last[0, :, values : values + keys].astype(F32)
    k[...] = last[0, :, values + keys :].astype(F32)
    out[...] = first[0, :, :values].astype(F32).T
    gate[...] = first[0, :, values:].astype(F32)
    up[...] = ffn[0]
    down[...] = ffn[1].T
    block_out[...] = low_out[...]
    grad_tokens[...] = low_grad[...]


def outputs(last, first, ffn, low_out, low_grad, keys):
    heads, chunk, both = last.shape
    values, hidden = both // 2, ffn.shape[-1]
    rows, width = low_out.shape
    piece, slab = hidden // heads, rows // heads
    sd = jax.ShapeDtypeStruct
    by_column = [pl.BlockSpec((chunk, size), lambda i: (0, i)) for size in (keys, keys, values, values)]
    by_row = pl.BlockSpec((values, chunk), lambda i: (i, 0))
    low = pl.BlockSpec((slab, width), lambda i: (i, 0))
    sums = pl.BlockSpec((1, chunk, both), lambda i: (i, 0, 0))
    return pl.pallas_call(
        outputs_kernel,
        grid=(heads,),
        in_specs=[sums, sums, pl.BlockSpec((2, chunk, piece), lambda i: (0, 0, i)), low, low],
        out_specs=by_column
        + [
            by_row,
            pl.BlockSpec((chunk, piece), lambda i: (0, i)),
            pl.BlockSpec((piece, chunk), lambda i: (i, 0)),
            low,
            low,
        ],
        out_shape=[
            sd((chunk, heads * keys), F32),
            sd((chunk, heads * keys), F32),
            sd((chunk, heads * values), F32),
            sd((chunk, heads * values), F32),
            sd((heads * values, chunk), F32),
            sd((chunk, hidden), F32),
            sd((hidden, chunk), F32),
            sd((rows, width), BF16),
            sd((rows, width), BF16),
        ],
    )(last, first, ffn, low_out, low_grad)


def angle_tables(first, count, fine, half_width):
    frequency = 10000.0 ** (-jnp.linspace(0.0, 1.0, half_width, dtype=F32))
    coarse = ((first + fine * jnp.arange(count)) % SEQUENCE_LENGTH).astype(F32)[:, None] * frequency[None, :]
    near = jnp.arange(fine).astype(F32)[:, None] * frequency[None, :]
    wide = (count, 8, half_width)
    return [
        jnp.broadcast_to(jnp.cos(coarse)[:, None], wide),
        jnp.broadcast_to(jnp.sin(coarse)[:, None], wide),
        jnp.cos(near),
        jnp.sin(near),
    ]


def shards(
    tokens,
    ln1_gain,
    ln1_bias,
    w_query,
    w_key,
    w_value,
    w_gate,
    w_out,
    decay_log,
    ln2_gain,
    ln2_bias,
    w_up,
    w_down,
    cotangent,
):
    row_count, width = tokens.shape
    span_rows = cotangent.shape[0]
    heads = decay_log.shape[1]
    repeats = lax.axis_size("seq") // SPANS
    peers = [[lo + SPANS * k for k in range(repeats)] for lo in range(SPANS)]
    narrow = width // (SPANS * repeats)

    def wide_in(w, axis):
        if repeats == 1:
            return w
        return lax.all_gather(w, "seq", axis_index_groups=peers, axis=axis, tiled=True)

    def narrow_out(g, axis):
        if repeats == 1:
            return g
        return lax.psum_scatter(
            g, "seq", scatter_dimension=axis, axis_index_groups=peers, tiled=True
        )

    def features_in(a):
        if repeats == 1:
            return a
        return a.reshape(a.shape[:-1] + (repeats, SPANS, narrow)).swapaxes(-3, -2).reshape(a.shape)

    def features_out(a):
        if repeats == 1:
            return a
        return a.reshape(a.shape[:-1] + (SPANS, repeats, narrow)).swapaxes(-3, -2).reshape(a.shape)

    spot = lax.axis_index("seq") % SPANS
    z, p = spot // PLANE, spot % PLANE
    group_rows = span_rows * PLANE
    blocks = group_rows // STRETCH

    tokens, cotangent, w_down = features_in(tokens), features_in(cotangent), features_in(w_down)
    w_up = features_in(w_up.T).T if repeats > 1 else w_up
    ln1_gain, ln1_bias = features_in(ln1_gain), features_in(ln1_bias)
    ln2_gain, ln2_bias = features_in(ln2_gain), features_in(ln2_bias)
    decays = jnp.pad(decay_log.T, ((0, 8 - heads), (0, 0)))
    fine = 64
    (
        normed, q_rot, k_rot, value, gate_proj, retained, gated_low, prev_states,
        cosine, sine_part, ccol, crow, scalars, key_w, value_w, query_w, gate_w, out_w,
    ) = attention(
        tokens,
        ln1_gain,
        ln1_bias,
        decays,
        angle_tables(z * group_rows, group_rows // fine, fine, w_key.shape[1] // heads // 2),
        [
            wide_in(w_key, 0),
            wide_in(w_value, 0),
            wide_in(w_query, 0),
            wide_in(w_gate, 0),
            wide_in(w_out, 1),
        ],
        (False, False, False, False, True),
        0,
    )
    block_out, grad_resid, gains_second, grad_attn, grad_up, grad_down = ffn_part(
        gated_low,
        out_w,
        tokens,
        ln2_gain,
        ln2_bias,
        w_up,
        w_down,
        cotangent,
        2,
    )
    grad_heads, sums_first, ffn_first, grad_value_w, grad_qk_w = retention_back(
        grad_attn,
        out_w,
        gated_low,
        gate_proj,
        retained,
        q_rot,
        k_rot,
        value,
        prev_states,
        cosine,
        sine_part,
        ccol,
        crow,
        scalars,
        normed,
        grad_up,
        grad_down,
        7,
    )
    grad_tokens, gains, ffn_sum, sums_last = last_sums(
        grad_heads,
        grad_value_w,
        grad_qk_w,
        query_w,
        key_w,
        value_w,
        gate_w,
        ffn_first,
        tokens,
        ln1_gain,
        grad_resid,
        gains_second,
        8,
    )
    if repeats > 1:
        gains = lax.psum(gains, "seq", axis_index_groups=peers)
    gains = features_out(gains)
    gain_one, bias_one, gain_two, bias_two = gains[0], gains[1], gains[2], gains[3]

    *sums, block_out, grad_tokens = outputs(
        sums_last, sums_first, ffn_sum, block_out, grad_tokens, key_w.shape[1]
    )
    sum_query, sum_key, sum_value, sum_gate, sum_out, sum_up, sum_down = (
        narrow_out(g, axis) for g, axis in zip(sums, (0, 0, 0, 0, 1, 0, 1))
    )
    return (
        features_out(block_out),
        features_out(grad_tokens),
        gain_one,
        bias_one,
        sum_query,
        sum_key,
        sum_value,
        sum_gate,
        sum_out,
        gain_two,
        bias_two,
        sum_up,
        sum_down,
    )


def solution(mesh):
    return jax.shard_map(
        shards,
        mesh=mesh,
        in_specs=(
            P(("seq", "ffn"), None),
            P(),
            P(),
            P("seq", "ffn"),
            P("seq", "ffn"),
            P("seq", "ffn"),
            P("seq", "ffn"),
            P("ffn", "seq"),
            P("seq", "ffn"),
            P(),
            P(),
            P(None, "ffn"),
            P("ffn", None),
            P("seq", None),
        ),
        out_specs=(
            P(("seq", "ffn"), None),
            P(("seq", "ffn"), None),
            P(),
            P(),
            P("seq", "ffn"),
            P("seq", "ffn"),
            P("seq", "ffn"),
            P("seq", "ffn"),
            P("ffn", "seq"),
            P(),
            P(),
            P("seq", "ffn"),
            P("ffn", "seq"),
        ),
        check_vma=False,
    )
```

```python
import functools

import jax
import jax.numpy as jnp
from jax import lax
from jax.experimental import pallas as pl
from jax.experimental.pallas import tpu as pltpu
from jax.sharding import PartitionSpec as P

STRETCH = 512
SEQUENCE_LENGTH = 8192
PLANE = 4
LINE = 4
SPANS = PLANE * LINE
MESH = pl.DeviceIdType.MESH
VMEM_LIMIT = 63 * 1024 * 1024
ANY = pl.BlockSpec(memory_space=pl.ANY)
VM = pl.BlockSpec(memory_space=pltpu.VMEM)
BF16 = jnp.bfloat16
F32 = jnp.float32


class Place:
    def __init__(self):
        s = lax.axis_index("seq")
        self.f = lax.axis_index("ffn")
        lo = s % SPANS
        self.base = s - lo
        self.z = lo // PLANE
        self.p = lo % PLANE

    def plane(self, m):
        return self.at(self.z, self.xor(m), self.f)

    def xor(self, m):
        p = self.p
        low, high = p % 2, p // 2
        if m & 1:
            low = 1 - low
        if m & 2:
            high = 1 - high
        return high * 2 + low

    def at(self, z, p, f):
        return (self.base + z * PLANE + p, f)

    def partner(self):
        return self.at(self.z, self.p, 1 - self.f)

    def up(self):
        return self.at(self.z + 1, self.p, self.f)

    def down(self):
        return self.at(self.z - 1, self.p, self.f)


def greet(peers):
    bar = pltpu.get_barrier_semaphore()
    count = 0
    for device, cond in peers:
        if cond is None:
            pl.semaphore_signal(bar, inc=1, device_id=device, device_id_type=MESH)
            count = count + 1
        else:

            @pl.when(cond)
            def _():
                pl.semaphore_signal(bar, inc=1, device_id=device, device_id_type=MESH)

            count = count + cond.astype(jnp.int32)
    pl.semaphore_wait(bar, count)


def remote(src, dst, send, recv, device):
    return pltpu.make_async_remote_copy(
        src_ref=src, dst_ref=dst, send_sem=send, recv_sem=recv, device_id=device, device_id_type=MESH
    )


def comm_call(kernel, outs, ins, scratch, cid, in_specs=None, out_specs=None):
    return pl.pallas_call(
        kernel,
        out_shape=outs,
        in_specs=in_specs if in_specs is not None else [ANY] * len(ins),
        out_specs=out_specs if out_specs is not None else [ANY] * len(outs),
        scratch_shapes=scratch,
        compiler_params=pltpu.CompilerParams(
            collective_id=cid, has_side_effects=True, vmem_limit_bytes=VMEM_LIMIT
        ),
    )(*ins)


DMA = pltpu.SemaphoreType.DMA


def nn(a, b):
    return jnp.dot(a, b, preferred_element_type=F32)


def nt(a, b):
    return lax.dot_general(a, b, (((1,), (1,)), ((), ())), preferred_element_type=F32)


def tn(a, b):
    return lax.dot_general(a, b, (((0,), (0,)), ((), ())), preferred_element_type=F32)


def rows_at(r, size):
    return pl.ds(pl.multiple_of(r, size), size)


def add_into(dst, cols, other, other_cols):
    @pl.loop(0, dst.shape[0], step=64)
    def _(r):
        at = rows_at(r, 64)
        dst[at, cols] = (dst[at, cols].astype(F32) + other[at, other_cols].astype(F32)).astype(BF16)


def start(copy):
    copy.start()
    return copy


def ffn_kernel(
    gated_ref, wo_ref, tok_ref, gain_ref, bias_ref, wu_ref, wd_ref, cot_ref,
    block_out, resid_out, gains, da, fu, fd,
    tok, resid_grad, share, wu, wd, rx0, rx1a, rx1b, rx2a, rx2b, resid, xn, act, dact, du, cot, dab, stage, tmp,
    lsem, gload, csend, crecv, xsend, xrecv, psend, precv, gsend, grecv, ksend, krecv, ssem,
):
    me = Place()
    p, f = me.p, me.f
    greet([(me.plane(1), None), (me.plane(2), None), (me.partner(), None)])
    rows, width = tok_ref.shape
    hidden = wu.shape[1]
    q = [me.xor(m) for m in range(4)]
    wide = width // 2
    hr = rows // 2
    span = 2 * rows
    ca, cb = pl.ds(0, wide), pl.ds(wide, wide)
    everything, whole = pl.ds(0, width), pl.ds(0, wide)
    own_half = [pl.ds(h * hr, hr) for h in range(2)]
    mine = [rows_at(h * rows + f * hr, hr) for h in range(2)]
    theirs = [rows_at(h * rows + (1 - f) * hr, hr) for h in range(2)]
    both = [pl.ds(h * rows, rows) for h in range(2)]

    order = (3, 1, 2, 0)
    part_width = gated_ref.shape[1]
    load_o = start(pltpu.make_async_copy(wo_ref, act, lsem.at[0]))
    load_t = pltpu.make_async_copy(tok_ref, tok, lsem.at[7])
    load_g = {
        m: start(
            pltpu.make_async_copy(
                gated_ref.at[rows_at(q[m] * span, span), :],
                xn.at[:, m * part_width : (m + 1) * part_width],
                gload.at[m],
            )
        )
        for m in order
    }
    load_t.start()
    load_d = start(pltpu.make_async_copy(wd_ref, wd, lsem.at[1]))
    load_c = [
        start(
            pltpu.make_async_copy(
                cot_ref.at[pl.ds(c * rows + h * hr, hr), :], cot.at[pl.ds(h * rows + c * hr, hr), :], lsem.at[3 + 2 * h + c]
            )
        )
        for h in range(2)
        for c in range(2)
    ]
    load_u = start(pltpu.make_async_copy(wu_ref, wu, lsem.at[2]))
    load_o.wait()
    first, sends = {}, {}

    def to_partner(m, h):
        first[m, h] = start(
            remote(
                share.at[m, rows_at((1 - f) * rows + h * hr, hr)], rx0.at[m, own_half[h]],
                csend.at[m, h], crecv.at[m, h], me.partner(),
            )
        )

    for m in order:
        load_g[m].wait()

        @pl.loop(0, width, step=512)
        def _(c):
            at = rows_at(c, 512)
            share[m, :, at] = nn(xn[:, m * part_width : (m + 1) * part_width], act[:, at]).astype(BF16)

        to_partner(m, 0)
    for m in order:
        to_partner(m, 1)

    def pass_on(m, h):
        first[m, h].wait_recv()
        at = own_half[h]
        add_into(rx0.at[m, at], everything, share.at[m, rows_at(f * rows + h * hr, hr)], everything)
        k = 0 if m == 3 else 1
        if m & 1:
            sends["a", k, h] = start(
                remote(rx0.at[m, at, ca], rx1a.at[k, at], xsend.at[k, h], xrecv.at[k, h], me.plane(1))
            )
        if m & 2:
            sends["b", k, h] = start(
                remote(rx0.at[m, at, cb], rx1b.at[k, at], xsend.at[2 + k, h], xrecv.at[2 + k, h], me.plane(2))
            )

    def second(h):
        at = own_half[h]
        sends["a", 0, h].wait_recv()
        add_into(rx1a.at[0, at], whole, rx0.at[2, at], ca)
        sends["a", 2, h] = start(
            remote(rx1a.at[0, at], rx2a.at[at], xsend.at[4, h], xrecv.at[4, h], me.plane(2))
        )
        sends["b", 0, h].wait_recv()
        add_into(rx1b.at[0, at], whole, rx0.at[1, at], cb)
        sends["b", 2, h] = start(
            remote(rx1b.at[0, at], rx2b.at[at], xsend.at[5, h], xrecv.at[5, h], me.plane(1))
        )

    for m in order:
        pass_on(m, 0)

    load_d.wait()
    for c in load_c:
        c.wait()

    @pl.loop(0, hidden, step=256)
    def _(c):
        at = rows_at(c, 256)
        dact[:, at] = nt(cot[...], wd[at, :])

    second(0)
    for m in order:
        pass_on(m, 1)
    load_u.wait()
    step = 32

    def norm(h):
        for key in (("a", 1, h), ("b", 1, h), ("a", 2, h), ("b", 2, h)):
            sends[key].wait_recv()

        @pl.loop(0, hr, step=step)
        def _(r):
            at = pl.ds(pl.multiple_of(h * hr + r, step), step)
            left = rx0[0, at, ca].astype(F32) + rx1a[1, at, :].astype(F32) + rx2a[at, :].astype(F32)
            right = rx0[0, at, cb].astype(F32) + rx1b[1, at, :].astype(F32) + rx2b[at, :].astype(F32)
            v = tok[at, :].astype(F32) + jnp.concatenate([left, right], axis=1)
            resid[at, :] = v
            centered = v - jnp.mean(v, axis=1, keepdims=True)
            scale = lax.rsqrt(jnp.mean(centered * centered, axis=1, keepdims=True) + 1e-05)
            xn[pl.ds(pl.multiple_of(h * rows + f * hr + r, step), step), :] = (
                centered * scale * gain_ref[...] + bias_ref[...]
            ).astype(BF16)

        return start(remote(xn.at[mine[h]], xn.at[mine[h]], psend.at[0, h], precv.at[0, h], me.partner()))

    def hidden_part(h):
        @pl.loop(0, hidden, step=512)
        def _(c):
            at = rows_at(c, 512)
            u = nn(xn[both[h], :], wu[:, at])
            e = 0.5 * (1.0 + lax.erf(u * 0.7071067811865476))
            act[both[h], at] = (u * e).astype(BF16)
            slope = e + u * jnp.exp(-0.5 * u * u) * 0.3989422804014327
            du[both[h], at] = (dact[both[h], at] * slope).astype(BF16)

    def back_part(h):
        @pl.loop(0, width, step=512)
        def _(c):
            at = rows_at(c, 512)
            tmp[...] = nt(du[both[h], :], wu[at, :])
            resid_grad[own_half[h], at] = tmp[rows_at(f * hr, hr), :]
            share[0, own_half[h], at] = tmp[rows_at((1 - f) * hr, hr), :].astype(BF16)

        return start(
            remote(share.at[0, own_half[h]], share.at[1, own_half[h]], psend.at[1, h], precv.at[1, h], me.partner())
        )

    def norm_back(h):
        @pl.loop(0, hr, step=step)
        def _(r):
            at = pl.ds(pl.multiple_of(h * hr + r, step), step)
            dx = resid_grad[at, :] + share[1, at, :].astype(F32)
            v = resid[at, :]
            centered = v - jnp.mean(v, axis=1, keepdims=True)
            scale = lax.rsqrt(jnp.mean(centered * centered, axis=1, keepdims=True) + 1e-05)
            hat = centered * scale
            gains[0:1, :] += jnp.sum(dx * hat, axis=0, keepdims=True)
            gains[1:2, :] += jnp.sum(dx, axis=0, keepdims=True)
            g = dx * gain_ref[...]
            back = scale * (
                g - jnp.mean(g, axis=1, keepdims=True) - hat * jnp.mean(g * hat, axis=1, keepdims=True)
            )
            back = back + cot[pl.ds(pl.multiple_of(h * rows + f * hr + r, step), step), :].astype(F32)
            resid_grad[at, :] = back
            dab[at, :] = back.astype(BF16)

    def out_part(h):
        @pl.loop(0, width, step=512)
        def _(c):
            at = rows_at(c, 512)
            tmp[...] = nn(act[both[h], :], wd[:, at])
            dact[pl.ds(h * rows, hr), at] = tmp[rows_at(f * hr, hr), :]
            share[2, own_half[h], at] = tmp[rows_at((1 - f) * hr, hr), :].astype(BF16)

        return start(
            remote(share.at[2, own_half[h]], share.at[3, own_half[h]], psend.at[2, h], precv.at[2, h], me.partner())
        )

    quarter = hr // 2

    def seat(m, h, k=None):
        base = (q[m] * 2 + f) * rows + h * hr
        if k is None:
            return da.at[pl.ds(pl.multiple_of(base, hr), hr), :]
        return da.at[pl.ds(pl.multiple_of(base + k * quarter, quarter), quarter), :]

    spread = {}

    def spread_begin(h):
        spread["own", h] = start(pltpu.make_async_copy(dab.at[own_half[h]], seat(0, h), gload.at[h]))
        for i in range(2):
            for to, k in ((1, i), (2, 1 - i)):
                sem = (to - 1) * 2 + i
                spread[to, i, h] = start(
                    remote(
                        dab.at[pl.ds(h * hr + k * quarter, quarter)], seat(0, h, k),
                        gsend.at[sem, h], grecv.at[sem, h], me.plane(to),
                    )
                )
        spread["core", 0, h] = start(
            remote(dab.at[own_half[h]], seat(0, h), ksend.at[0, h], krecv.at[0, h], me.partner())
        )

    def spread_on(h):
        spread[1, 0, h].wait_recv()
        spread["g1", h] = start(
            remote(seat(1, h, 0), seat(1, h, 0), gsend.at[4, h], grecv.at[4, h], me.plane(2))
        )
        spread[2, 0, h].wait_recv()
        spread["g2", h] = start(
            remote(seat(2, h, 1), seat(2, h, 1), gsend.at[5, h], grecv.at[5, h], me.plane(1))
        )

    def spread_end(h):
        for m in (1, 2):
            spread[m, 1, h].wait_recv()
            spread["core", m, h] = start(
                remote(seat(m, h), seat(m, h), ksend.at[m, h], krecv.at[m, h], me.partner())
            )
        spread["g1", h].wait_recv()
        spread["g2", h].wait_recv()
        spread["core", 3, h] = start(
            remote(seat(3, h), seat(3, h), ksend.at[3, h], krecv.at[3, h], me.partner())
        )

    gains[...] = jnp.zeros_like(gains)
    for c in first.values():
        c.wait_send()
    load_t.wait()
    swaps = [norm(0)]
    swaps[0].wait_recv()
    hidden_part(0)
    second(1)
    swaps.append(back_part(0))
    out_swaps = [out_part(0)]
    swaps[1].wait_recv()
    norm_back(0)
    spread_begin(0)
    swaps.append(norm(1))
    swaps[2].wait_recv()
    hidden_part(1)
    spread_on(0)
    swaps.append(back_part(1))
    out_swaps.append(out_part(1))
    swaps[3].wait_recv()
    norm_back(1)
    spread_begin(1)
    resid_copy = start(pltpu.make_async_copy(resid_grad, resid_out, lsem.at[0]))

    def weights_part(left, right, out):
        def spill(slot, i):
            return pltpu.make_async_copy(stage.at[slot], out.at[rows_at(i * 256, 256), :], ssem.at[slot])

        @pl.loop(0, width // 256)
        def _(i):
            slot = i % 3

            @pl.when(i >= 3)
            def _():
                spill(slot, i - 3).wait()

            stage[slot] = tn(left[:, rows_at(i * 256, 256)], right[...]).astype(BF16)
            spill(slot, i).start()

        for k in (3, 2, 1):
            i = width // 256 - k
            spill(i % 3, i).wait()

    weights_part(cot, act, fd)
    spread_on(1)
    spread_end(0)
    for h in range(2):
        out_swaps[h].wait_recv()

        @pl.loop(0, hr, step=step)
        def _(r):
            at = pl.ds(pl.multiple_of(h * hr + r, step), step)
            own = dact[pl.ds(pl.multiple_of(h * rows + r, step), step), :]
            tok[at, :] = (resid[at, :] + own + share[3, at, :].astype(F32)).astype(BF16)

    out_copy = start(pltpu.make_async_copy(tok, block_out, lsem.at[1]))
    weights_part(xn, du, fu)
    spread_end(1)
    resid_copy.wait()
    out_copy.wait()
    for h in range(2):
        spread["own", h].wait()
        for m in range(4):
            spread["core", m, h].wait()
        for key in ((1, 0, h), (1, 1, h), (2, 0, h), (2, 1, h), ("g1", h), ("g2", h)):
            spread[key].wait_send()
    for c in swaps + out_swaps + list(sends.values()):
        c.wait_send()


def ffn_part(gated, w_out, tokens, gain, bias, w_up, w_down, cotangent, cid):
    rows, width = tokens.shape
    assert PLANE * gated.shape[1] == width and w_out.shape == (2 * rows, w_up.shape[1])
    span, hidden = 2 * rows, w_up.shape[1]
    sd = jax.ShapeDtypeStruct
    return comm_call(
        ffn_kernel,
        [
            sd((rows, width), BF16),
            sd((rows, width), F32),
            sd((8, width), F32),
            sd((2 * PLANE * rows, width), BF16),
            sd((width, hidden), BF16),
            sd((width, hidden), BF16),
        ],
        [gated, w_out, tokens, gain[None], bias[None], w_up, w_down, cotangent],
        [
            pltpu.VMEM((rows, width), BF16),
            pltpu.VMEM((rows, width), F32),
            pltpu.VMEM((PLANE, span, width), BF16),
            pltpu.VMEM(w_up.shape, BF16),
            pltpu.VMEM(w_down.shape, BF16),
            pltpu.VMEM((PLANE, rows, width), BF16),
            pltpu.VMEM((2, rows, width // 2), BF16),
            pltpu.VMEM((2, rows, width // 2), BF16),
            pltpu.VMEM((rows, width // 2), BF16),
            pltpu.VMEM((rows, width // 2), BF16),
            pltpu.VMEM((rows, width), F32),
            pltpu.VMEM((span, width), BF16),
            pltpu.VMEM((span, hidden), BF16),
            pltpu.VMEM((span, hidden), F32),
            pltpu.VMEM((span, hidden), BF16),
            pltpu.VMEM((span, width), BF16),
            pltpu.VMEM((rows, width), BF16),
            pltpu.VMEM((3, 256, hidden), BF16),
            pltpu.VMEM((rows, 512), F32),
            DMA((8,)),
            DMA((PLANE,)),
            DMA((PLANE, 2)),
            DMA((PLANE, 2)),
            DMA((6, 2)),
            DMA((6, 2)),
            DMA((3, 2)),
            DMA((3, 2)),
            DMA((6, 2)),
            DMA((6, 2)),
            DMA((4, 2)),
            DMA((4, 2)),
            DMA((3,)),
        ],
        cid,
        in_specs=[ANY, ANY, ANY, VM, VM, ANY, ANY, ANY],
        out_specs=[ANY, ANY, VM, ANY, ANY, ANY],
    )


def attention_kernel(
    widths, by_rows,
    tok_ref, gain_ref, bias_ref, dec_ref, cbase, sbase, coff, soff, *refs,
):
    count = len(widths)
    shards_in, refs = refs[:count], refs[count:]
    (xg, q_out, k_out, v_out, gate_out, ret_out, gated_out, states_out, cos_out, sin_out, ccol, crow, scal), refs = (
        refs[:13], refs[13:],
    )
    full, refs = refs[:count], refs[count:]
    hold, refs = refs[:count], refs[count:]
    wl, refs = refs[: count - 1], refs[count - 1 :]
    (xn, xv, q, k, v, gate, ret, gated, cos, sin, kv, st, sloc, sgot, decg,
     lsem, psend, precv, usend, dsend, zrecv, xsend, xrecv, csend, crecv, tsend, trecv, ssend, srecv, osem, wsem) = refs
    me = Place()
    z, p, f = me.z, me.p, me.f
    spot = z * PLANE + p
    chunk = hold[0].shape[0]
    deep = chunk * PLANE
    tokens, width = xv.shape
    rows = tok_ref.shape[0]
    keys, values = q.shape[1], v.shape[1]
    half = keys // 2
    blocks = tokens // STRETCH
    greet(
        [(me.plane(m), None) for m in (1, 2, 3)]
        + [(me.partner(), None), (me.up(), z < LINE - 1), (me.down(), z > 0)]
    )

    def part(i, at):
        w = widths[i]
        if by_rows[i]:
            return shards_in[i].at[pl.ds(pl.multiple_of(at * w, w), w), :]
        return shards_in[i].at[:, pl.ds(pl.multiple_of(at * w, w), w)]

    def slot(i, ss):
        at = pl.ds(pl.multiple_of(ss * chunk, chunk), chunk)
        return full[i].at[:, at] if by_rows[i] else full[i].at[at, :]

    def block(i, zz):
        at = pl.ds(pl.multiple_of(zz * deep, deep), deep)
        return full[i].at[:, at] if by_rows[i] else full[i].at[at, :]

    local, plane, held = [], [], []
    for i in range(count):
        held.append(start(pltpu.make_async_copy(part(i, p), hold[i], lsem.at[i])))
        local.append(pltpu.make_async_copy(hold[i], slot(i, spot), lsem.at[i]))
        plane.append(
            [
                start(remote(part(i, me.xor(m)), slot(i, spot), psend.at[i, m], precv.at[i, m], me.plane(m)))
                for m in (1, 2, 3)
            ]
        )
    tiny = [start(remote(dec_ref, decg.at[p], tsend.at[m], trecv.at[m], me.plane(m))) for m in (1, 2, 3)]
    tiny_own = start(pltpu.make_async_copy(dec_ref, decg.at[p], tsend.at[0]))
    step = 32

    @pl.loop(0, rows, step=step)
    def _(r):
        at = rows_at(r, step)
        t = tok_ref[at, :].astype(F32)
        centered = t - jnp.mean(t, axis=1, keepdims=True)
        scale = lax.rsqrt(jnp.mean(centered * centered, axis=1, keepdims=True) + 1e-05)
        xn[at, :] = (centered * scale * gain_ref[...] + bias_ref[...]).astype(BF16)

    def seat(m, h=None):
        base = (me.xor(m) * 2 + f) * rows
        if h is None:
            return xv.at[rows_at(base, rows)]
        return xv.at[pl.ds(pl.multiple_of(base + h * (rows // 2), rows // 2), rows // 2)]

    x_own = start(pltpu.make_async_copy(xn, seat(0), lsem.at[count]))
    x1 = start(remote(xn, seat(0), xsend.at[0], xrecv.at[0], me.plane(1)))
    x2 = start(remote(xn, seat(0), xsend.at[1], xrecv.at[1], me.plane(2)))
    xc = start(remote(xn, seat(0), csend.at[0], crecv.at[0], me.partner()))
    for i in range(count):
        held[i].wait()
        local[i].start()

    def up_copy(i, zz):
        return remote(block(i, zz), block(i, zz), usend.at[i, zz], zrecv.at[i, zz], me.up())

    def down_copy(i, zz):
        return remote(block(i, zz), block(i, zz), dsend.at[i, zz], zrecv.at[i, zz], me.down())

    def own(i):
        local[i].wait()
        for c in plane[i]:
            c.wait_recv()

        @pl.when(z < LINE - 1)
        def _():
            up_copy(i, z).start()

        @pl.when(z > 0)
        def _():
            down_copy(i, z).start()

    def forward(i, t):
        @pl.when(z - t >= 0)
        def _():
            up_copy(i, z - t).wait_recv()

            @pl.when(z < LINE - 1)
            def _():
                up_copy(i, z - t).start()

        @pl.when(z + t < LINE)
        def _():
            down_copy(i, z + t).wait_recv()

            @pl.when(z > 0)
            def _():
                down_copy(i, z + t).start()

    def fetch(i):
        forward(i, LINE - 1)
        return start(pltpu.make_async_copy(full[i], wl[i], wsem.at[i]))

    K, V, Q, G, O = range(count)
    own(K)
    own(V)
    forward(K, 1)
    forward(K, 2)
    own(Q)

    for c in tiny:
        c.wait()
    tiny_own.wait()
    heads = lax.broadcasted_iota(jnp.int32, decg.shape[1:], 0)
    lines = [jnp.sum(jnp.where(heads == p, decg[j], 0.0), axis=0, keepdims=True) for j in range(blocks)]
    lines = jnp.concatenate(lines + [jnp.zeros_like(lines[0])] * (8 - blocks), axis=0)
    i0 = lax.broadcasted_iota(jnp.int32, (STRETCH, STRETCH), 0)
    i1 = lax.broadcasted_iota(jnp.int32, (STRETCH, STRETCH), 1)
    row_sums = jnp.dot(
        lines, jnp.where(i0 <= i1, 1.0, 0.0), preferred_element_type=F32, precision=lax.Precision.HIGHEST
    )
    col_sums = lax.dot_general(
        jnp.where(i1 <= i0, 1.0, 0.0), lines, (((1,), (1,)), ((), ())),
        preferred_element_type=F32, precision=lax.Precision.HIGHEST,
    )
    total = jnp.zeros((1, 1), F32)
    for c in range(blocks):
        end = row_sums[c : c + 1, STRETCH - 1 : STRETCH]
        crow[c] = jnp.broadcast_to(row_sums[c : c + 1, :], (8, STRETCH))
        ccol[c * STRETCH : (c + 1) * STRETCH, :] = col_sums[:, c : c + 1]
        scal[c] = jnp.broadcast_to(jnp.exp(end), (8, 128))
        scal[blocks + c] = jnp.broadcast_to(jnp.exp(total), (8, 128))
        total = total + end
    scal[2 * blocks] = jnp.broadcast_to(total, (8, 128))

    fine = coff.shape[0]

    @pl.loop(0, tokens // fine)
    def _(a):
        at = rows_at(a * fine, fine)
        ca, sa = cbase[a, 0:1, :], sbase[a, 0:1, :]
        cos[at, :] = ca * coff[...] - sa * soff[...]
        sin[at, :] = sa * coff[...] + ca * soff[...]

    forward(V, 1)
    x1.wait_recv()
    g1 = start(remote(seat(1, 0), seat(1, 0), xsend.at[2], xrecv.at[2], me.plane(2)))
    c1 = start(remote(seat(1), seat(1), csend.at[1], crecv.at[1], me.partner()))
    x2.wait_recv()
    g2 = start(remote(seat(2, 1), seat(2, 1), xsend.at[3], xrecv.at[3], me.plane(1)))
    c2 = start(remote(seat(2), seat(2), csend.at[2], crecv.at[2], me.partner()))
    forward(V, 2)
    forward(Q, 1)
    own(G)
    forward(Q, 2)
    own(O)
    load_k = fetch(K)
    g1.wait_recv()
    g2.wait_recv()
    c3 = start(remote(seat(3), seat(3), csend.at[3], crecv.at[3], me.partner()))
    x_own.wait()
    for c in (xc, c1, c2, c3):
        c.wait_recv()
    outs = []

    def put(src, dst):
        outs.append(start(pltpu.make_async_copy(src, dst, osem.at[len(outs)])))

    put(xv, xg)
    put(cos, cos_out)
    put(sin, sin_out)
    load_k.wait()

    def turned(at, w, dst):
        y = nn(xv[at, :], w[...])
        a, b = y[:, :half], y[:, half:]
        dst[at, :half] = (a * cos[at, :] - b * sin[at, :]).astype(BF16)
        dst[at, half:] = (b * cos[at, :] + a * sin[at, :]).astype(BF16)

    @pl.loop(0, blocks)
    def _(c):
        turned(rows_at(c * STRETCH, STRETCH), wl[K], k)

    fetch(V).wait()

    @pl.loop(0, blocks)
    def _(c):
        at = rows_at(c * STRETCH, STRETCH)
        val = nn(xv[at, :], wl[V][...]).astype(BF16)
        v[at, :] = val
        end = crow[c, 0:1, STRETCH - 1 : STRETCH]
        kv[c] = tn(k[at, :], (val.astype(F32) * jnp.exp(end - ccol[at, :])).astype(BF16))

    put(k, k_out)
    put(v, v_out)
    sloc[...] = kv[0]
    kv[0] = jnp.zeros_like(sloc)
    for c in range(1, blocks):
        nxt = sloc[...] * scal[c, 0:1, 0:1] + kv[c]
        kv[c] = sloc[...]
        sloc[...] = nxt

    def state_copy(zz):
        return remote(st.at[0], sgot, ssend.at[zz], srecv.at[zz], me.up())

    def send_state():
        st[0] = sloc[...].astype(BF16)
        state_copy(0).start()

    @pl.when(z == 0)
    def _():
        send_state()

    def pass_state(zz):
        @pl.when(z == zz)
        def _():
            state_copy(0).wait_recv()
            if zz < LINE - 1:
                sloc[...] = sloc[...] + sgot[...].astype(F32) * jnp.exp(scal[2 * blocks, 0:1, 0:1])
                send_state()

    pass_state(1)
    forward(G, 1)
    forward(O, 1)
    fetch(Q).wait()
    t_size = 256

    @pl.loop(0, blocks)
    def _(c):
        blk = rows_at(c * STRETCH, STRETCH)
        turned(blk, wl[Q], q)
        row = crow[c, 0:1, :]
        for r in range(0, STRETCH, t_size):
            at = rows_at(c * STRETCH + r, t_size)
            col = ccol[at, :]
            t_index = lax.broadcasted_iota(jnp.int32, (t_size, STRETCH), 0) + r
            s_index = lax.broadcasted_iota(jnp.int32, (t_size, STRETCH), 1)
            mask = jnp.where(t_index >= s_index, jnp.exp(jnp.minimum(col - row, 0.0)), 0.0)
            scores = (nt(q[at, :], k[blk, :]) * mask).astype(BF16)
            ret[at, :] = nn(scores, v[blk, :])

    put(q, q_out)
    pass_state(2)
    forward(G, 2)
    forward(O, 2)
    pass_state(3)

    @pl.when((z > 0) & (z < LINE - 1))
    def _():
        state_copy(0).wait_send()

    @pl.when(z == 0)
    def _():
        state_copy(0).wait_send()
        sgot[...] = jnp.zeros_like(sgot)

    for c in range(blocks):
        st[c] = (kv[c] + sgot[...].astype(F32) * scal[blocks + c, 0:1, 0:1]).astype(BF16)

    @pl.loop(0, blocks)
    def _(c):
        at = rows_at(c * STRETCH, STRETCH)
        decayed = (q[at, :].astype(F32) * jnp.exp(ccol[at, :])).astype(BF16)
        ret[at, :] += nn(decayed, st[c])

    put(ret, ret_out)
    put(st, states_out)
    fetch(G).wait()

    @pl.loop(0, tokens, step=256)
    def _(r):
        at = rows_at(r, 256)
        g = nn(xv[at, :], wl[G][...])
        gate[at, :] = g
        t = ret[at, :]
        centered = t - jnp.mean(t, axis=1, keepdims=True)
        scale = lax.rsqrt(jnp.mean(centered * centered, axis=1, keepdims=True) + 1e-05)
        gated[at, :] = (g / (1.0 + jnp.exp(-g)) * centered * scale).astype(BF16)

    put(gate, gate_out)
    put(gated, gated_out)
    forward(O, LINE - 1)
    for c in (xc, c1, c2, c3, x1, x2, g1, g2):
        c.wait_send()
    for i in range(count):
        for c in plane[i]:
            c.wait_send()
        for zz in range(LINE):

            @pl.when((z < LINE - 1) & (zz <= z))
            def _():
                up_copy(i, zz).wait_send()

            @pl.when((z > 0) & (zz >= z))
            def _():
                down_copy(i, zz).wait_send()

    for c in outs:
        c.wait()


def attention(tokens, gain, bias, decays, tables, shards_in, by_rows, cid):
    rows, width = tokens.shape
    count = len(shards_in)
    chunk = shards_in[0].shape[0]
    group = 2 * PLANE * rows
    blocks = group // STRETCH
    parts = [
        (w.shape[0] // PLANE, chunk) if r else (chunk, w.shape[1] // PLANE) for w, r in zip(shards_in, by_rows)
    ]
    widths = [s[0] if r else s[1] for s, r in zip(parts, by_rows)]
    wholes = [(s[0], width) if r else (width, s[1]) for s, r in zip(parts, by_rows)]
    values, keys = widths[1], widths[0]
    half = keys // 2
    sd = jax.ShapeDtypeStruct
    outs = [
        sd((group, width), BF16),
        sd((group, keys), BF16),
        sd((group, keys), BF16),
        sd((group, values), BF16),
        sd((group, values), F32),
        sd((group, values), F32),
        sd((group, values), BF16),
        sd((blocks, keys, values), BF16),
        sd((group, half), F32),
        sd((group, half), F32),
        sd((group, 1), F32),
        sd((blocks, 8, STRETCH), F32),
        sd((2 * blocks + 1, 8, 128), F32),
    ] + [sd(s, BF16) for s in wholes]
    scratch = (
        [pltpu.VMEM(s, BF16) for s in parts]
        + [pltpu.VMEM(s, BF16) for s in wholes[:-1]]
        + [
            pltpu.VMEM((rows, width), BF16),
            pltpu.VMEM((group, width), BF16),
            pltpu.VMEM((group, keys), BF16),
            pltpu.VMEM((group, keys), BF16),
            pltpu.VMEM((group, values), BF16),
            pltpu.VMEM((group, values), F32),
            pltpu.VMEM((group, values), F32),
            pltpu.VMEM((group, values), BF16),
            pltpu.VMEM((group, half), F32),
            pltpu.VMEM((group, half), F32),
            pltpu.VMEM((blocks, keys, values), F32),
            pltpu.VMEM((blocks, keys, values), BF16),
            pltpu.VMEM((keys, values), F32),
            pltpu.VMEM((keys, values), BF16),
            pltpu.VMEM((PLANE,) + decays.shape, F32),
            DMA((count + 1,)),
            DMA((count, PLANE)),
            DMA((count, PLANE)),
            DMA((count, LINE)),
            DMA((count, LINE)),
            DMA((count, LINE)),
            DMA((4,)),
            DMA((4,)),
            DMA((4,)),
            DMA((4,)),
            DMA((PLANE,)),
            DMA((PLANE,)),
            DMA((1,)),
            DMA((1,)),
            DMA((16,)),
            DMA((count,)),
        ]
    )
    return comm_call(
        functools.partial(attention_kernel, widths, by_rows),
        outs,
        [tokens, gain[None], bias[None], decays] + list(tables) + list(shards_in),
        scratch,
        cid,
        in_specs=[VM] * 8 + [ANY] * count,
        out_specs=[ANY] * 10 + [VM] * 3 + [ANY] * count,
    )


class LineSum:
    def __init__(self, me, own, rx, usend, urecv, dsend, drecv, add):
        self.me, self.own, self.rx, self.add = me, own, rx, add
        self.sems = usend, urecv, dsend, drecv

    def up(self, src, zz):
        return remote(src, self.rx.at[zz], self.sems[0].at[zz], self.sems[1].at[zz], self.me.up())

    def down(self, src, zz):
        slot = jnp.where(zz == self.me.z - 1, LINE, zz)
        return remote(src, self.rx.at[slot], self.sems[2].at[zz], self.sems[3].at[zz], self.me.down())

    def begin(self, order=(3, 2, 1), src=None):
        src = src or self.own
        for zz in order:

            @pl.when(self.me.z == 0)
            def _():
                self.up(src(zz), zz).start()

            @pl.when(self.me.z == LINE - 1)
            def _():
                self.down(src(LINE - 1 - zz), LINE - 1 - zz).start()

    def pass_up(self, zz):
        self.up(self.own(zz), zz).wait_recv()
        self.add(self.rx.at[zz], self.own(zz))
        self.up(self.rx.at[zz], zz).start()

    def pass_down(self, zz):
        self.down(self.own(zz), zz).wait_recv()
        self.add(self.rx.at[zz], self.own(zz))
        self.down(self.rx.at[zz], zz).start()

    def near(self, k):
        @pl.when(self.me.z == 1)
        def _():
            self.pass_up(LINE - 1 - k)

        @pl.when(self.me.z == 2)
        def _():
            self.pass_down(k)

    def far(self):
        @pl.when(self.me.z == 1)
        def _():
            self.pass_down(0)

        @pl.when(self.me.z == 2)
        def _():
            self.pass_up(LINE - 1)

    def arrive(self):
        z = self.me.z

        @pl.when(z > 0)
        def _():
            self.up(self.own(z), z).wait_recv()

        @pl.when(z < LINE - 1)
        def _():
            self.down(self.own(z), z).wait_recv()

    def finish(self):
        z = self.me.z
        for zz in range(LINE):

            @pl.when((z < LINE - 1) & (zz > z))
            def _():
                self.up(self.own(zz), zz).wait_send()

            @pl.when((z > 0) & (zz < z))
            def _():
                self.down(self.own(zz), zz).wait_send()


def add_rows(dst, src):
    rows = dst.shape[0]
    step = 32 if dst.shape[1] > 512 else 128

    @pl.loop(0, rows, step=step)
    def _(r):
        at = rows_at(r, step)
        dst[at, :] = (dst[at, :].astype(F32) + src[at, :].astype(F32)).astype(BF16)


def total_rows(z, dst, own, rx):
    rows = dst.shape[0]
    step = 32 if dst.shape[1] > 512 else 128

    @pl.loop(0, rows, step=step)
    def _(r):
        at = rows_at(r, step)
        v = own[at, :].astype(F32)
        v = v + jnp.where(z > 0, rx[z, at, :].astype(F32), 0.0)
        v = v + jnp.where(z < LINE - 1, rx[LINE, at, :].astype(F32), 0.0)
        dst[at, :] = v.astype(dst.dtype)


def line_sems():
    return [DMA((LINE,)) for _ in range(4)]


def retention_back_kernel(
    da_ref, wo_ref, gated_ref, gate_ref, ret_ref, q_ref, k_ref, v_ref, s_ref, cos_ref, sin_ref,
    ccol_ref, crow_ref, scal_ref, xg_ref, fu_ref, fd_ref,
    dh_out, sums, f1, av_out, aq_out,
    dh, da, wo, gated, gr, q, k, v, st, cos, sin, dr, xt, ao, ag, rxo, rxg, fin, qo, gb, lg, got, rxf, fo, pbuf, gbuf,
    lsem, gsem, xsem, fsend, frecv, osem, fosem, ssend, srecv, psend, precv, *line,
):
    me = Place()
    z, p = me.z, me.p
    greet(
        [(me.plane(m), None) for m in (1, 2, 3)]
        + [(me.up(), z < LINE - 1), (me.down(), z > 0)]
    )
    width = da.shape[1]
    tokens = da.shape[0]
    keys, values = q.shape[1], v.shape[1]
    blocks = tokens // STRETCH
    half = keys // 2
    pq = [me.xor(m) for m in range(4)]
    chunk = fu_ref.shape[0] // SPANS

    def f_block(h, zp, place):
        return (fu_ref, fd_ref)[h].at[pl.ds(pl.multiple_of((zp * PLANE + place) * chunk, chunk), chunk), :]

    early = (3, 0, 2)
    units = 2 * len(early)
    away = ((1, 3), (2, 3))
    kept = ((0, 2), (0, 1))
    nbr = (1, 2)

    def f_copy(h, zp, j):
        return remote(
            f_block(h, zp, pq[away[h][j]]), rxf.at[h, early.index(zp), j], fsend.at[h, zp, j], frecv.at[h, zp, j], me.plane(nbr[h])
        )

    loads = [
        start(pltpu.make_async_copy(a, b, lsem.at[i]))
        for i, (a, b) in enumerate(
            [(da_ref, da), (gated_ref, gated), (wo_ref, wo), (q_ref, q), (k_ref, k), (v_ref, v), (s_ref, st),
             (cos_ref, cos), (sin_ref, sin)]
        )
    ]
    for zp in early:
        for h in range(2):
            for j in range(2):
                f_copy(h, zp, j).start()

    def f_own(u):
        h, zp = u % 2, early[u // 2]
        return [
            pltpu.make_async_copy(f_block(h, zp, pq[kept[h][j]]), fo.at[u % 2, j], fosem.at[u % 2, j])
            for j in range(2)
        ]

    def f_out(u):
        h, zp = u % 2, early[u // 2]
        return pltpu.make_async_copy(rxf.at[h, u // 2], f1.at[h, zp], osem.at[u])

    for u in range(2):
        for c in f_own(u):
            c.start()

    def f_unit(u):
        h, zp = u % 2, early[u // 2]
        for j, c in enumerate(f_own(u)):
            c.wait()
            f_copy(h, zp, j).wait_recv()
            add_rows(rxf.at[h, u // 2, j], fo.at[u % 2, j])
        f_out(u).start()
        if u + 2 < units:
            for c in f_own(u + 2):
                c.start()

    def tile_rows(i):
        return rows_at(i * 256, 256)

    def gate_loads(i):
        at = tile_rows(i)
        slot = i % 3
        return (
            pltpu.make_async_copy(gate_ref.at[at, :], gr.at[slot, 0], gsem.at[slot, 0]),
            pltpu.make_async_copy(ret_ref.at[at, :], gr.at[slot, 1], gsem.at[slot, 1]),
        )

    for c in gate_loads(0) + gate_loads(1):
        c.start()

    out_sum = LineSum(me, lambda zz: ao.at[rows_at(zz * (width // LINE), width // LINE), :], rxo, *line[:4], add_rows)
    gate_sum = LineSum(me, lambda zz: ag.at[rows_at(zz * (width // LINE), width // LINE), :], rxg, *line[4:], add_rows)

    loads[0].wait()
    loads[1].wait()

    for ends, turn in (((3, 0), 3), ((2, 1), 2)):
        for zz in ends:

            @pl.loop(0, width // LINE, step=256)
            def _(i):
                at = rows_at(zz * (width // LINE) + i, 256)
                ao[at, :] = tn(da[:, at], gated[...]).astype(BF16)

        out_sum.begin((turn,))
    for c in loads[2:]:
        c.wait()

    tiles = tokens // 256

    @pl.loop(0, tiles)
    def _(i):
        @pl.when(i + 2 < tiles)
        def _():
            for c in gate_loads(i + 2):
                c.start()

        for c in gate_loads(i):
            c.wait()
        at = tile_rows(i)
        slot = i % 3
        dgated = nt(da[at, :], wo[...])
        gate = gr[slot, 0]
        ret = gr[slot, 1]
        centered = ret - jnp.mean(ret, axis=1, keepdims=True)
        scale = lax.rsqrt(jnp.mean(centered * centered, axis=1, keepdims=True) + 1e-05)
        grouped = centered * scale
        sig = 1.0 / (1.0 + jnp.exp(-gate))
        silu = gate * sig
        dh[at, 2 * keys + values :] = (dgated * grouped * (sig * (1.0 + gate * (1.0 - sig)))).astype(BF16)
        dg = dgated * silu
        dr[at, :] = (
            scale * (dg - jnp.mean(dg, axis=1, keepdims=True) - grouped * jnp.mean(dg * grouped, axis=1, keepdims=True))
        ).astype(BF16)

    lg[...] = jnp.zeros_like(lg)

    @pl.loop(0, blocks)
    def _(c):
        at = rows_at(c * STRETCH, STRETCH)
        decayed = (q[at, :].astype(F32) * jnp.exp(ccol_ref[at, :])).astype(BF16)
        got_q = tn(decayed, dr[at, :])
        qo[c] = got_q
        lg[...] += scal_ref[blocks + c, 0:1, 0:1] * got_q

    state_copy = remote(gb.at[0], got, ssend.at[0], srecv.at[0], me.down())

    def pass_state(zz):
        @pl.when(z == zz)
        def _():
            if zz < LINE - 1:
                state_copy.wait_recv()
            if zz > 0:
                add = lg[...]
                if zz < LINE - 1:
                    add = add + got[...].astype(F32) * jnp.exp(scal_ref[2 * blocks, 0:1, 0:1])
                gb[0] = add.astype(BF16)
                state_copy.start()

    pass_state(LINE - 1)
    out_sum.begin((1,))
    out_sum.near(0)
    def x_tile(i):
        return pltpu.make_async_copy(xg_ref.at[:, rows_at(i * 256, 256)], xt.at[i % 3], xsem.at[i % 3])

    x_tile(0).start()
    x_tile(1).start()

    @pl.loop(0, width // 256)
    def _(i):
        @pl.when(i + 2 < width // 256)
        def _():
            x_tile(i + 2).start()

        x_tile(i).wait()
        ag[rows_at(i * 256, 256), :] = tn(xt[i % 3], dh[:, 2 * keys + values :]).astype(BF16)

    gate_sum.begin()
    out_sum.near(1)
    pass_state(2)
    f_unit(0)
    f_unit(1)
    out_sum.far()

    pass_state(1)
    pass_state(0)

    @pl.when(z > 0)
    def _():
        state_copy.wait_send()

    @pl.when(z < LINE - 1)
    def _():
        lg[...] = got[...].astype(F32)

    @pl.when(z == LINE - 1)
    def _():
        lg[...] = jnp.zeros_like(lg)

    for c in reversed(range(blocks)):
        gb[c] = lg[...].astype(BF16)
        if c:
            lg[...] = lg[...] * scal_ref[c, 0:1, 0:1] + qo[c]

    t_size = 256

    @pl.loop(0, blocks)
    def _(c):
        blk = rows_at(c * STRETCH, STRETCH)
        row = crow_ref[c, 0:1, :]
        end = crow_ref[c, 0:1, STRETCH - 1 : STRETCH]
        for r in range(0, STRETCH, t_size):
            at = rows_at(c * STRETCH + r, t_size)
            col = ccol_ref[at, :]
            t_index = lax.broadcasted_iota(jnp.int32, (t_size, STRETCH), 0) + r
            s_index = lax.broadcasted_iota(jnp.int32, (t_size, STRETCH), 1)
            mask = jnp.where(t_index >= s_index, jnp.exp(jnp.minimum(col - row, 0.0)), 0.0)
            pbuf[r : r + t_size, :] = (nt(q[at, :], k[blk, :]) * mask).astype(BF16)
            g = (nt(dr[at, :], v[blk, :]) * mask).astype(BF16)
            gbuf[r : r + t_size, :] = g
            dq = nt(dr[at, :], st[c]) * jnp.exp(col) + nn(g, k[blk, :])
            a, b = dq[:, :half], dq[:, half:]
            dh[at, :half] = (a * cos[at, :] + b * sin[at, :]).astype(BF16)
            dh[at, half:keys] = (b * cos[at, :] - a * sin[at, :]).astype(BF16)
        for r in range(0, STRETCH, t_size):
            at = rows_at(c * STRETCH + r, t_size)
            tail = jnp.exp(end - ccol_ref[at, :])
            w = (v[at, :].astype(F32) * tail).astype(BF16)
            dk = nt(w, gb[c]) + tn(gbuf[:, r : r + t_size], q[blk, :])
            a, b = dk[:, :half], dk[:, half:]
            dh[at, keys : keys + half] = (a * cos[at, :] + b * sin[at, :]).astype(BF16)
            dh[at, keys + half : 2 * keys] = (b * cos[at, :] - a * sin[at, :]).astype(BF16)
            dv = nn(k[at, :], gb[c]) * tail + tn(pbuf[:, r : r + t_size], dr[blk, :])
            dh[at, 2 * keys : 2 * keys + values] = dv.astype(BF16)

    dh_copy = start(pltpu.make_async_copy(dh, dh_out, lsem.at[2]))
    plane = []

    def deal(i, chain, a):
        chain.arrive()
        total_rows(z, fin.at[i], a.at[rows_at(z * (width // LINE), width // LINE), :], chain.rx)
        cols = pl.ds(i * values, values)
        for m in (1, 2, 3):
            plane.append(
                start(
                    remote(
                        fin.at[i, rows_at(pq[m] * chunk, chunk), :], sums.at[p, :, cols],
                        psend.at[i, m], precv.at[i, m], me.plane(m),
                    )
                )
            )
        plane.append(
            start(
                pltpu.make_async_copy(
                    fin.at[i, rows_at(p * chunk, chunk), :], sums.at[p, :, cols], psend.at[i, 0]
                )
            )
        )

    gate_sum.near(0)
    for u in range(2, 4):
        f_unit(u)
    deal(0, out_sum, ao)
    x_tile(0).start()
    x_tile(1).start()
    wide = 2 * keys + values

    @pl.loop(0, width // 256)
    def _(i):
        @pl.when(i + 2 < width // 256)
        def _():
            x_tile(i + 2).start()

        x_tile(i).wait()
        da[rows_at(i * 256, 256), :wide] = tn(xt[i % 3], dh[:, :wide]).astype(BF16)

    to_last = [
        start(pltpu.make_async_copy(da.at[:, : 2 * keys], aq_out, lsem.at[0])),
        start(pltpu.make_async_copy(da.at[:, 2 * keys : wide], av_out, lsem.at[1])),
    ]
    gate_sum.near(1)
    gate_sum.far()
    for u in range(4, 6):
        f_unit(u)
    deal(1, gate_sum, ag)
    for c in plane + to_last + [dh_copy]:
        c.wait()
    out_sum.finish()
    gate_sum.finish()
    for u in range(units):
        f_out(u).wait()
    for zp in early:
        for h in range(2):
            for j in range(2):
                f_copy(h, zp, j).wait_send()


def retention_back(da, wo, gated, gate, ret, q, k, v, states, cos, sin, ccol, crow, scal, xg, fu, fd, cid):
    tokens, width = da.shape
    keys, values = q.shape[1], v.shape[1]
    chunk = width // SPANS
    blocks = tokens // STRETCH
    hidden = fu.shape[1]
    deep = width // LINE
    return comm_call(
        retention_back_kernel,
        [
            jax.ShapeDtypeStruct((tokens, 2 * keys + 2 * values), BF16),
            jax.ShapeDtypeStruct((PLANE, chunk, 2 * values), BF16),
            jax.ShapeDtypeStruct((2, LINE, 2, chunk, hidden), BF16),
            jax.ShapeDtypeStruct((width, values), BF16),
            jax.ShapeDtypeStruct((width, 2 * keys), BF16),
        ],
        [da, wo, gated, gate, ret, q, k, v, states, cos, sin, ccol, crow, scal, xg, fu, fd],
        [
            pltpu.VMEM((tokens, 2 * keys + 2 * values), BF16),
            pltpu.VMEM((tokens, width), BF16),
            pltpu.VMEM(wo.shape, BF16),
            pltpu.VMEM(gated.shape, BF16),
            pltpu.VMEM((3, 2, 256, values), F32),
            pltpu.VMEM(q.shape, BF16),
            pltpu.VMEM(k.shape, BF16),
            pltpu.VMEM(v.shape, BF16),
            pltpu.VMEM(states.shape, BF16),
            pltpu.VMEM(cos.shape, F32),
            pltpu.VMEM(sin.shape, F32),
            pltpu.VMEM((tokens, values), BF16),
            pltpu.VMEM((3, tokens, 256), BF16),
            pltpu.VMEM((width, values), BF16),
            pltpu.VMEM((width, values), BF16),
            pltpu.VMEM((LINE + 1, deep, values), BF16),
            pltpu.VMEM((LINE + 1, deep, values), BF16),
            pltpu.VMEM((2, deep, values), BF16),
            pltpu.VMEM((blocks, keys, values), F32),
            pltpu.VMEM((blocks, keys, values), BF16),
            pltpu.VMEM((keys, values), F32),
            pltpu.VMEM((keys, values), BF16),
            pltpu.VMEM((2, LINE - 1, 2, chunk, hidden), BF16),
            pltpu.VMEM((2, 2, chunk, hidden), BF16),
            pltpu.VMEM((STRETCH, STRETCH), BF16),
            pltpu.VMEM((STRETCH, STRETCH), BF16),
            DMA((9,)),
            DMA((3, 2)),
            DMA((3,)),
            DMA((2, LINE, 2)),
            DMA((2, LINE, 2)),
            DMA((2 * LINE,)),
            DMA((2, 2)),
            DMA((1,)),
            DMA((1,)),
            DMA((2, PLANE)),
            DMA((2, PLANE)),
        ]
        + line_sems()
        + line_sems(),
        cid,
        in_specs=[ANY] * 11 + [VM] * 3 + [ANY] * 3,
        out_specs=[ANY] * 5,
    )


def last_kernel(
    dh_ref, av_ref, aq_ref, wq_ref, wk_ref, wv_ref, wg_ref, f1_ref, fu_ref, fd_ref, tok_ref, gain_ref, resid_ref, second_ref,
    grad_out, gains, fout, sums,
    tok, resid, rxl, flow, dh, wh, share, rx0, rx1a, rx1b, rx2a, rx2b, av, aq, rxv, rxq, fin, rf2, kf, rxfa, rxfb, grx,
    lsem, ksem, lsend, lrecv, fsend, frecv, csend, crecv, xsend, xrecv, gsend, grecv, psend, precv, *line,
):
    me = Place()
    z, p, f = me.z, me.p, me.f
    rounds = [
        [me.partner()],
        [me.plane(m) for m in (1, 2, 3)],
        [me.at((z + t) % LINE, p, f) for t in range(1, LINE)],
    ]
    greet([(d, None) for r in rounds for d in r])
    width, keys2, values = av.shape[0], aq.shape[1], av.shape[1]
    rows = tok_ref.shape[0]
    pq = [me.xor(m) for m in range(4)]
    chunk = width // SPANS
    deep = width // LINE

    late = 1

    def f_copy(h, zp):
        src = flow.at[h] if zp == late else f1_ref.at[h, zp, 1]
        return remote(src, rf2.at[h, zp], fsend.at[h, zp], frecv.at[h, zp], me.plane(2 - h))

    def f_block(h, place):
        return (fu_ref, fd_ref)[h].at[rows_at((late * PLANE + place) * chunk, chunk), :]

    def late_copy(h, j):
        place = pq[((1, 3), (2, 3))[h][j]]
        return remote(f_block(h, place), rxl.at[h, j], lsend.at[h, j], lrecv.at[h, j], me.plane(1 + h))

    def block_of(a, size):
        return lambda zz: a.at[rows_at(zz * size, size), :]

    v_sum = LineSum(me, block_of(av, deep), rxv, *line[:4], add_rows)
    q_sum = LineSum(me, block_of(aq, deep), rxq, *line[4:8], add_rows)
    fa_sum = LineSum(me, lambda zz: kf.at[0, zz], rxfa, *line[8:12], add_rows)
    fb_sum = LineSum(me, lambda zz: kf.at[1, zz], rxfb, *line[12:16], add_rows)
    v_sum.begin(src=block_of(av_ref, deep))
    q_sum.begin(src=block_of(aq_ref, deep))
    for j in (1, 0):
        for h in range(2):
            late_copy(h, j).start()
    for zp in (3, 0, 2):
        for h in range(2):
            f_copy(h, zp).start()
    load = start(pltpu.make_async_copy(dh_ref, dh, lsem.at[0]))
    owns = [
        start(pltpu.make_async_copy(av_ref, av, lsem.at[7])),
        start(pltpu.make_async_copy(aq_ref, aq, lsem.at[8])),
    ]
    loads, at = [], 0
    for i, w in enumerate((wq_ref, wk_ref, wv_ref, wg_ref)):
        size = w.shape[1]
        loads.append(start(pltpu.make_async_copy(w, wh.at[:, at : at + size], lsem.at[1 + i])))
        at += size
    keeps = []
    for h in range(2):
        for i, zp in enumerate((3, 0, 2)):
            keeps.append(start(pltpu.make_async_copy(f1_ref.at[h, zp, 0], kf.at[h, zp], ksem.at[h, i])))
        for j, dst in ((0, kf.at[h, late]), (1, flow.at[h])):
            place = pq[((0, 2), (0, 1))[h][j]]
            keeps.append(start(pltpu.make_async_copy(f_block(h, place), dst, ksem.at[h, 3 + j])))
    rest = [
        start(pltpu.make_async_copy(tok_ref, tok, lsem.at[5])),
        start(pltpu.make_async_copy(resid_ref, resid, lsem.at[6])),
    ]

    load.wait()
    for c in loads + owns:
        c.wait()

    own_rows, their_rows = rows_at(f * rows, rows), rows_at((1 - f) * rows, rows)
    wide = width // 2
    ca, cb = pl.ds(0, wide), pl.ds(wide, wide)
    everything, whole = pl.ds(0, width), pl.ds(0, wide)
    first, sends = {}, {}

    def share_part(m):
        at_rows = rows_at(pq[m] * 2 * rows, 2 * rows)

        @pl.loop(0, width, step=256)
        def _(c):
            at = rows_at(c, 256)
            share[m, :, at] = nt(dh[at_rows, :], wh[at, :]).astype(BF16)

        first[m] = start(
            remote(share.at[m, their_rows], rx0.at[m], csend.at[m], crecv.at[m], me.partner())
        )

    def pass_on(m):
        first[m].wait_recv()
        add_into(rx0.at[m], everything, share.at[m, own_rows], everything)
        k = 0 if m == 3 else 1
        if m & 1:
            sends["a", k] = start(
                remote(rx0.at[m, :, ca], rx1a.at[k], xsend.at[k], xrecv.at[k], me.plane(1))
            )
        if m & 2:
            sends["b", k] = start(
                remote(rx0.at[m, :, cb], rx1b.at[k], xsend.at[2 + k], xrecv.at[2 + k], me.plane(2))
            )

    plane = []

    def deal(i, chain, a):
        chain.arrive()
        total_rows(z, fin.at[i], a.at[rows_at(z * deep, deep), :], chain.rx)
        cols = pl.ds(i * values, values)
        for m in (1, 2, 3):
            plane.append(
                start(
                    remote(
                        fin.at[i, rows_at(pq[m] * chunk, chunk), :], sums.at[p, :, cols],
                        psend.at[i, m], precv.at[i, m], me.plane(m),
                    )
                )
            )
        plane.append(
            start(
                pltpu.make_async_copy(
                    fin.at[i, rows_at(p * chunk, chunk), :], sums.at[p, :, cols], psend.at[i, 0]
                )
            )
        )

    share_part(3)
    share_part(1)
    v_sum.near(0)
    share_part(2)
    for c in keeps:
        c.wait()
    for h in range(2):
        late_copy(h, 1).wait_recv()
        add_rows(flow.at[h], rxl.at[h, 1])
        f_copy(h, late).start()
    pass_on(3)
    pass_on(1)
    share_part(0)
    v_sum.near(1)
    pass_on(2)
    pass_on(0)
    for h in range(2):
        late_copy(h, 0).wait_recv()
        add_rows(kf.at[h, late], rxl.at[h, 0])
    v_sum.far()
    q_sum.near(0)
    for zp in (3, 0, 2, 1):
        for h in range(2):
            f_copy(h, zp).wait_recv()
            add_rows(kf.at[h, zp], rf2.at[h, zp])
    for zz in (3, 2, 1):
        fa_sum.begin((zz,))
        fb_sum.begin((zz,))
    q_sum.near(1)
    q_sum.far()
    deal(0, v_sum, av)
    sends["a", 0].wait_recv()
    add_into(rx1a.at[0], whole, rx0.at[2], ca)
    s2a = start(remote(rx1a.at[0], rx2a, xsend.at[4], xrecv.at[4], me.plane(2)))
    sends["b", 0].wait_recv()
    add_into(rx1b.at[0], whole, rx0.at[1], cb)
    s2b = start(remote(rx1b.at[0], rx2b, xsend.at[5], xrecv.at[5], me.plane(1)))
    fa_sum.near(0)
    sends["a", 1].wait_recv()
    sends["b", 1].wait_recv()
    deal(1, q_sum, aq)
    fb_sum.near(0)
    s2a.wait_recv()
    s2b.wait_recv()
    for c in rest:
        c.wait()
    gains[...] = jnp.zeros_like(gains)
    gains[2:4, :] = second_ref[0:2, :]
    step = 32

    @pl.loop(0, rows, step=step)
    def _(r):
        at = rows_at(r, step)
        left = rx0[0, at, ca].astype(F32) + rx1a[1, at, :].astype(F32) + rx2a[at, :].astype(F32)
        right = rx0[0, at, cb].astype(F32) + rx1b[1, at, :].astype(F32) + rx2b[at, :].astype(F32)
        dx = jnp.concatenate([left, right], axis=1)
        v = tok[at, :].astype(F32)
        centered = v - jnp.mean(v, axis=1, keepdims=True)
        scale = lax.rsqrt(jnp.mean(centered * centered, axis=1, keepdims=True) + 1e-05)
        hat = centered * scale
        gains[0:1, :] += jnp.sum(dx * hat, axis=0, keepdims=True)
        gains[1:2, :] += jnp.sum(dx, axis=0, keepdims=True)
        g = dx * gain_ref[...]
        back = scale * (
            g - jnp.mean(g, axis=1, keepdims=True) - hat * jnp.mean(g * hat, axis=1, keepdims=True)
        )
        tok[at, :] = (back + resid[at, :]).astype(BF16)

    out_copy = start(pltpu.make_async_copy(tok, grad_out, lsem.at[0]))

    def gain_copies(r):
        base = (0, 1, 4)[r]
        return [
            remote(gains, grx.at[base + i], gsend.at[base + i], grecv.at[base + i], d)
            for i, d in enumerate(rounds[r])
        ]

    def gain_begin(r):
        for c in gain_copies(r):
            c.start()

    def gain_end(r):
        for c in gain_copies(r):
            c.wait()
        for i in range(len(rounds[r])):
            gains[...] += grx[(0, 1, 4)[r] + i]

    gain_begin(0)
    fa_sum.near(1)
    fa_sum.far()
    gain_end(0)
    gain_begin(1)
    fb_sum.near(1)
    gain_end(1)
    gain_begin(2)
    fb_sum.far()
    fa_sum.arrive()
    total_rows(z, fout.at[0], kf.at[0, z], rxfa)
    fb_sum.arrive()
    total_rows(z, fout.at[1], kf.at[1, z], rxfb)
    gain_end(2)
    for c in plane + [out_copy]:
        c.wait()
    for h in range(2):
        for j in range(2):
            late_copy(h, j).wait_send()
    for chain in (v_sum, q_sum, fa_sum, fb_sum):
        chain.finish()
    for c in list(first.values()) + list(sends.values()) + [s2a, s2b]:
        c.wait_send()
    for zp in range(LINE):
        for h in range(2):
            f_copy(h, zp).wait_send()


def last_sums(dh, av, aq, wq, wk, wv, wg, f1, fu, fd, tokens, gain, resid, second, cid):
    width = av.shape[0]
    rows = tokens.shape[0]
    keys, values = wq.shape[1], wv.shape[1]
    assert 2 * keys == values
    chunk, deep = width // SPANS, width // LINE
    hidden = f1.shape[-1]
    return comm_call(
        last_kernel,
        [
            jax.ShapeDtypeStruct((rows, width), BF16),
            jax.ShapeDtypeStruct((8, width), F32),
            jax.ShapeDtypeStruct((2, chunk, hidden), F32),
            jax.ShapeDtypeStruct((PLANE, chunk, 2 * values), BF16),
        ],
        [dh, av, aq, wq, wk, wv, wg, f1, fu, fd, tokens, gain[None], resid, second],
        [
            pltpu.VMEM((rows, width), BF16),
            pltpu.VMEM((rows, width), F32),
            pltpu.VMEM((2, 2, chunk, hidden), BF16),
            pltpu.VMEM((2, chunk, hidden), BF16),
            pltpu.VMEM(dh.shape, BF16),
            pltpu.VMEM((width, dh.shape[1]), BF16),
            pltpu.VMEM((PLANE, 2 * rows, width), BF16),
            pltpu.VMEM((PLANE, rows, width), BF16),
            pltpu.VMEM((2, rows, width // 2), BF16),
            pltpu.VMEM((2, rows, width // 2), BF16),
            pltpu.VMEM((rows, width // 2), BF16),
            pltpu.VMEM((rows, width // 2), BF16),
            pltpu.VMEM((width, values), BF16),
            pltpu.VMEM((width, 2 * keys), BF16),
            pltpu.VMEM((LINE + 1, deep, values), BF16),
            pltpu.VMEM((LINE + 1, deep, 2 * keys), BF16),
            pltpu.VMEM((2, deep, values), BF16),
            pltpu.VMEM((2, LINE, chunk, hidden), BF16),
            pltpu.VMEM((2, LINE, chunk, hidden), BF16),
            pltpu.VMEM((LINE + 1, chunk, hidden), BF16),
            pltpu.VMEM((LINE + 1, chunk, hidden), BF16),
            pltpu.VMEM((7, 8, width), F32),
            DMA((9,)),
            DMA((2, 5)),
            DMA((2, 2)),
            DMA((2, 2)),
            DMA((2, LINE)),
            DMA((2, LINE)),
            DMA((4,)),
            DMA((4,)),
            DMA((6,)),
            DMA((6,)),
            DMA((7,)),
            DMA((7,)),
            DMA((2, PLANE)),
            DMA((2, PLANE)),
        ]
        + line_sems()
        + line_sems()
        + line_sems()
        + line_sems(),
        cid,
        in_specs=[ANY] * 11 + [VM, ANY, VM],
        out_specs=[ANY, VM, VM, ANY],
    )


def outputs_kernel(last, first, ffn, low_out, low_grad, q, k, v, gate, out, up, down, block_out, grad_tokens):
    values = v.shape[1]
    keys = q.shape[1]
    v[...] = last[0, :, :values].astype(F32)
    q[...] = last[0, :, values : values + keys].astype(F32)
    k[...] = last[0, :, values + keys :].astype(F32)
    out[...] = first[0, :, :values].astype(F32).T
    gate[...] = first[0, :, values:].astype(F32)
    up[...] = ffn[0]
    down[...] = ffn[1].T
    block_out[...] = low_out[...]
    grad_tokens[...] = low_grad[...]


def outputs(last, first, ffn, low_out, low_grad, keys):
    heads, chunk, both = last.shape
    values, hidden = both // 2, ffn.shape[-1]
    rows, width = low_out.shape
    piece, slab = hidden // heads, rows // heads
    sd = jax.ShapeDtypeStruct
    by_column = [pl.BlockSpec((chunk, size), lambda i: (0, i)) for size in (keys, keys, values, values)]
    by_row = pl.BlockSpec((values, chunk), lambda i: (i, 0))
    low = pl.BlockSpec((slab, width), lambda i: (i, 0))
    sums = pl.BlockSpec((1, chunk, both), lambda i: (i, 0, 0))
    return pl.pallas_call(
        outputs_kernel,
        grid=(heads,),
        in_specs=[sums, sums, pl.BlockSpec((2, chunk, piece), lambda i: (0, 0, i)), low, low],
        out_specs=by_column
        + [
            by_row,
            pl.BlockSpec((chunk, piece), lambda i: (0, i)),
            pl.BlockSpec((piece, chunk), lambda i: (i, 0)),
            low,
            low,
        ],
        out_shape=[
            sd((chunk, heads * keys), F32),
            sd((chunk, heads * keys), F32),
            sd((chunk, heads * values), F32),
            sd((chunk, heads * values), F32),
            sd((heads * values, chunk), F32),
            sd((chunk, hidden), F32),
            sd((hidden, chunk), F32),
            sd((rows, width), BF16),
            sd((rows, width), BF16),
        ],
    )(last, first, ffn, low_out, low_grad)


def angle_tables(first, count, fine, half_width):
    frequency = 10000.0 ** (-jnp.linspace(0.0, 1.0, half_width, dtype=F32))
    coarse = ((first + fine * jnp.arange(count)) % SEQUENCE_LENGTH).astype(F32)[:, None] * frequency[None, :]
    near = jnp.arange(fine).astype(F32)[:, None] * frequency[None, :]
    wide = (count, 8, half_width)
    return [
        jnp.broadcast_to(jnp.cos(coarse)[:, None], wide),
        jnp.broadcast_to(jnp.sin(coarse)[:, None], wide),
        jnp.cos(near),
        jnp.sin(near),
    ]


def shards(
    tokens,
    ln1_gain,
    ln1_bias,
    w_query,
    w_key,
    w_value,
    w_gate,
    w_out,
    decay_log,
    ln2_gain,
    ln2_bias,
    w_up,
    w_down,
    cotangent,
):
    row_count, width = tokens.shape
    span_rows = cotangent.shape[0]
    heads = decay_log.shape[1]
    repeats = lax.axis_size("seq") // SPANS
    peers = [[lo + SPANS * k for k in range(repeats)] for lo in range(SPANS)]
    narrow = width // (SPANS * repeats)

    def wide_in(w, axis):
        if repeats == 1:
            return w
        return lax.all_gather(w, "seq", axis_index_groups=peers, axis=axis, tiled=True)

    def narrow_out(g, axis):
        if repeats == 1:
            return g
        return lax.psum_scatter(
            g, "seq", scatter_dimension=axis, axis_index_groups=peers, tiled=True
        )

    def features_in(a):
        if repeats == 1:
            return a
        return a.reshape(a.shape[:-1] + (repeats, SPANS, narrow)).swapaxes(-3, -2).reshape(a.shape)

    def features_out(a):
        if repeats == 1:
            return a
        return a.reshape(a.shape[:-1] + (SPANS, repeats, narrow)).swapaxes(-3, -2).reshape(a.shape)

    spot = lax.axis_index("seq") % SPANS
    z, p = spot // PLANE, spot % PLANE
    group_rows = span_rows * PLANE
    blocks = group_rows // STRETCH

    tokens, cotangent, w_down = features_in(tokens), features_in(cotangent), features_in(w_down)
    w_up = features_in(w_up.T).T if repeats > 1 else w_up
    ln1_gain, ln1_bias = features_in(ln1_gain), features_in(ln1_bias)
    ln2_gain, ln2_bias = features_in(ln2_gain), features_in(ln2_bias)
    decays = jnp.pad(decay_log.T, ((0, 8 - heads), (0, 0)))
    fine = 64
    (
        normed, q_rot, k_rot, value, gate_proj, retained, gated_low, prev_states,
        cosine, sine_part, ccol, crow, scalars, key_w, value_w, query_w, gate_w, out_w,
    ) = attention(
        tokens,
        ln1_gain,
        ln1_bias,
        decays,
        angle_tables(z * group_rows, group_rows // fine, fine, w_key.shape[1] // heads // 2),
        [
            wide_in(w_key, 0),
            wide_in(w_value, 0),
            wide_in(w_query, 0),
            wide_in(w_gate, 0),
            wide_in(w_out, 1),
        ],
        (False, False, False, False, True),
        0,
    )
    block_out, grad_resid, gains_second, grad_attn, grad_up, grad_down = ffn_part(
        gated_low,
        out_w,
        tokens,
        ln2_gain,
        ln2_bias,
        w_up,
        w_down,
        cotangent,
        2,
    )
    grad_heads, sums_first, ffn_first, grad_value_w, grad_qk_w = retention_back(
        grad_attn,
        out_w,
        gated_low,
        gate_proj,
        retained,
        q_rot,
        k_rot,
        value,
        prev_states,
        cosine,
        sine_part,
        ccol,
        crow,
        scalars,
        normed,
        grad_up,
        grad_down,
        7,
    )
    grad_tokens, gains, ffn_sum, sums_last = last_sums(
        grad_heads,
        grad_value_w,
        grad_qk_w,
        query_w,
        key_w,
        value_w,
        gate_w,
        ffn_first,
        grad_up,
        grad_down,
        tokens,
        ln1_gain,
        grad_resid,
        gains_second,
        8,
    )
    if repeats > 1:
        gains = lax.psum(gains, "seq", axis_index_groups=peers)
    gains = features_out(gains)
    gain_one, bias_one, gain_two, bias_two = gains[0], gains[1], gains[2], gains[3]

    *sums, block_out, grad_tokens = outputs(
        sums_last, sums_first, ffn_sum, block_out, grad_tokens, key_w.shape[1]
    )
    sum_query, sum_key, sum_value, sum_gate, sum_out, sum_up, sum_down = (
        narrow_out(g, axis) for g, axis in zip(sums, (0, 0, 0, 0, 1, 0, 1))
    )
    return (
        features_out(block_out),
        features_out(grad_tokens),
        gain_one,
        bias_one,
        sum_query,
        sum_key,
        sum_value,
        sum_gate,
        sum_out,
        gain_two,
        bias_two,
        sum_up,
        sum_down,
    )


def solution(mesh):
    return jax.shard_map(
        shards,
        mesh=mesh,
        in_specs=(
            P(("seq", "ffn"), None),
            P(),
            P(),
            P("seq", "ffn"),
            P("seq", "ffn"),
            P("seq", "ffn"),
            P("seq", "ffn"),
            P("ffn", "seq"),
            P("seq", "ffn"),
            P(),
            P(),
            P(None, "ffn"),
            P("ffn", None),
            P("seq", None),
        ),
        out_specs=(
            P(("seq", "ffn"), None),
            P(("seq", "ffn"), None),
            P(),
            P(),
            P("seq", "ffn"),
            P("seq", "ffn"),
            P("seq", "ffn"),
            P("seq", "ffn"),
            P("ffn", "seq"),
            P(),
            P(),
            P("seq", "ffn"),
            P("ffn", "seq"),
        ),
        check_vma=False,
    )
```

```python
import functools

import jax
import jax.numpy as jnp
import numpy as np
from jax import lax
from jax.experimental import pallas as pl
from jax.experimental.pallas import tpu as pltpu
from jax.sharding import PartitionSpec as P

STRETCH = 512
SEQUENCE_LENGTH = 8192
PLANE = 4
LINE = 4
SPANS = PLANE * LINE
MESH = pl.DeviceIdType.MESH
VMEM_LIMIT = 63 * 1024 * 1024
ANY = pl.BlockSpec(memory_space=pl.ANY)
VM = pl.BlockSpec(memory_space=pltpu.VMEM)
BF16 = jnp.bfloat16
F32 = jnp.float32


class Place:
    def __init__(self):
        s = lax.axis_index("seq")
        self.f = lax.axis_index("ffn")
        lo = s % SPANS
        self.base = s - lo
        self.z = lo // PLANE
        self.p = lo % PLANE

    def plane(self, m):
        return self.at(self.z, self.xor(m), self.f)

    def xor(self, m):
        p = self.p
        low, high = p % 2, p // 2
        if m & 1:
            low = 1 - low
        if m & 2:
            high = 1 - high
        return high * 2 + low

    def at(self, z, p, f):
        return (self.base + z * PLANE + p, f)

    def partner(self):
        return self.at(self.z, self.p, 1 - self.f)

    def up(self):
        return self.at(self.z + 1, self.p, self.f)

    def down(self):
        return self.at(self.z - 1, self.p, self.f)


def greet(peers):
    bar = pltpu.get_barrier_semaphore()
    count = 0
    for device, cond in peers:
        if cond is None:
            pl.semaphore_signal(bar, inc=1, device_id=device, device_id_type=MESH)
            count = count + 1
        else:

            @pl.when(cond)
            def _():
                pl.semaphore_signal(bar, inc=1, device_id=device, device_id_type=MESH)

            count = count + cond.astype(jnp.int32)
    pl.semaphore_wait(bar, count)


def remote(src, dst, send, recv, device):
    return pltpu.make_async_remote_copy(
        src_ref=src, dst_ref=dst, send_sem=send, recv_sem=recv, device_id=device, device_id_type=MESH
    )


def comm_call(kernel, outs, ins, scratch, cid, in_specs=None, out_specs=None):
    return pl.pallas_call(
        kernel,
        out_shape=outs,
        in_specs=in_specs if in_specs is not None else [ANY] * len(ins),
        out_specs=out_specs if out_specs is not None else [ANY] * len(outs),
        scratch_shapes=scratch,
        compiler_params=pltpu.CompilerParams(
            collective_id=cid, has_side_effects=True, vmem_limit_bytes=VMEM_LIMIT
        ),
    )(*ins)


DMA = pltpu.SemaphoreType.DMA


def nn(a, b):
    return jnp.dot(a, b, preferred_element_type=F32)


def nt(a, b):
    return lax.dot_general(a, b, (((1,), (1,)), ((), ())), preferred_element_type=F32)


def tn(a, b):
    return lax.dot_general(a, b, (((0,), (0,)), ((), ())), preferred_element_type=F32)


def rows_at(r, size):
    return pl.ds(pl.multiple_of(r, size), size)


def add_into(dst, cols, other, other_cols):
    @pl.loop(0, dst.shape[0], step=64)
    def _(r):
        at = rows_at(r, 64)
        dst[at, cols] = (dst[at, cols].astype(F32) + other[at, other_cols].astype(F32)).astype(BF16)


def start(copy):
    copy.start()
    return copy


def ffn_kernel(
    gated_ref, wo_ref, tok_ref, gain_ref, bias_ref, wu_ref, wd_ref, cot_ref,
    block_out, resid_out, gains, da, fu, fd,
    tok, resid_grad, share, wu, wd, rx0, rx1a, rx1b, rx2a, rx2b, resid, xn, act, dact, du, cot, dab, stage, tmp,
    lsem, gload, csend, crecv, xsend, xrecv, psend, precv, gsend, grecv, ksend, krecv, ssem,
):
    me = Place()
    p, f = me.p, me.f
    greet([(me.plane(1), None), (me.plane(2), None), (me.partner(), None)])
    rows, width = tok_ref.shape
    hidden = wu.shape[1]
    q = [me.xor(m) for m in range(4)]
    wide = width // 2
    hr = rows // 2
    span = 2 * rows
    ca, cb = pl.ds(0, wide), pl.ds(wide, wide)
    everything, whole = pl.ds(0, width), pl.ds(0, wide)
    own_half = [pl.ds(h * hr, hr) for h in range(2)]
    mine = [rows_at(h * rows + f * hr, hr) for h in range(2)]
    theirs = [rows_at(h * rows + (1 - f) * hr, hr) for h in range(2)]
    both = [pl.ds(h * rows, rows) for h in range(2)]

    order = (3, 1, 2, 0)
    part_width = gated_ref.shape[1]
    load_o = start(pltpu.make_async_copy(wo_ref, act, lsem.at[0]))
    load_t = pltpu.make_async_copy(tok_ref, tok, lsem.at[7])
    load_g = {
        m: start(
            pltpu.make_async_copy(
                gated_ref.at[rows_at(q[m] * span, span), :],
                xn.at[:, m * part_width : (m + 1) * part_width],
                gload.at[m],
            )
        )
        for m in order
    }
    load_t.start()
    load_d = start(pltpu.make_async_copy(wd_ref, wd, lsem.at[1]))
    load_c = [
        start(
            pltpu.make_async_copy(
                cot_ref.at[pl.ds(c * rows + h * hr, hr), :], cot.at[pl.ds(h * rows + c * hr, hr), :], lsem.at[3 + 2 * h + c]
            )
        )
        for h in range(2)
        for c in range(2)
    ]
    load_u = start(pltpu.make_async_copy(wu_ref, wu, lsem.at[2]))
    load_o.wait()
    first, sends = {}, {}

    def to_partner(m, h):
        first[m, h] = start(
            remote(
                share.at[m, rows_at((1 - f) * rows + h * hr, hr)], rx0.at[m, own_half[h]],
                csend.at[m, h], crecv.at[m, h], me.partner(),
            )
        )

    for m in order:
        load_g[m].wait()

        @pl.loop(0, width, step=512)
        def _(c):
            at = rows_at(c, 512)
            share[m, :, at] = nn(xn[:, m * part_width : (m + 1) * part_width], act[:, at]).astype(BF16)

        to_partner(m, 0)
    for m in order:
        to_partner(m, 1)

    def pass_on(m, h):
        first[m, h].wait_recv()
        at = own_half[h]
        add_into(rx0.at[m, at], everything, share.at[m, rows_at(f * rows + h * hr, hr)], everything)
        k = 0 if m == 3 else 1
        if m & 1:
            sends["a", k, h] = start(
                remote(rx0.at[m, at, ca], rx1a.at[k, at], xsend.at[k, h], xrecv.at[k, h], me.plane(1))
            )
        if m & 2:
            sends["b", k, h] = start(
                remote(rx0.at[m, at, cb], rx1b.at[k, at], xsend.at[2 + k, h], xrecv.at[2 + k, h], me.plane(2))
            )

    def second(h):
        at = own_half[h]
        sends["a", 0, h].wait_recv()
        add_into(rx1a.at[0, at], whole, rx0.at[2, at], ca)
        sends["a", 2, h] = start(
            remote(rx1a.at[0, at], rx2a.at[at], xsend.at[4, h], xrecv.at[4, h], me.plane(2))
        )
        sends["b", 0, h].wait_recv()
        add_into(rx1b.at[0, at], whole, rx0.at[1, at], cb)
        sends["b", 2, h] = start(
            remote(rx1b.at[0, at], rx2b.at[at], xsend.at[5, h], xrecv.at[5, h], me.plane(1))
        )

    for m in order:
        pass_on(m, 0)

    load_d.wait()
    for c in load_c:
        c.wait()

    @pl.loop(0, hidden, step=256)
    def _(c):
        at = rows_at(c, 256)
        dact[:, at] = nt(cot[...], wd[at, :])

    second(0)
    for m in order:
        pass_on(m, 1)
    load_u.wait()
    step = 32

    def norm(h):
        for key in (("a", 1, h), ("b", 1, h), ("a", 2, h), ("b", 2, h)):
            sends[key].wait_recv()

        @pl.loop(0, hr, step=step)
        def _(r):
            at = pl.ds(pl.multiple_of(h * hr + r, step), step)
            left = rx0[0, at, ca].astype(F32) + rx1a[1, at, :].astype(F32) + rx2a[at, :].astype(F32)
            right = rx0[0, at, cb].astype(F32) + rx1b[1, at, :].astype(F32) + rx2b[at, :].astype(F32)
            v = tok[at, :].astype(F32) + jnp.concatenate([left, right], axis=1)
            resid[at, :] = v
            centered = v - jnp.mean(v, axis=1, keepdims=True)
            scale = lax.rsqrt(jnp.mean(centered * centered, axis=1, keepdims=True) + 1e-05)
            xn[pl.ds(pl.multiple_of(h * rows + f * hr + r, step), step), :] = (
                centered * scale * gain_ref[...] + bias_ref[...]
            ).astype(BF16)

        return start(remote(xn.at[mine[h]], xn.at[mine[h]], psend.at[0, h], precv.at[0, h], me.partner()))

    def hidden_part(h):
        @pl.loop(0, hidden, step=512)
        def _(c):
            at = rows_at(c, 512)
            u = nn(xn[both[h], :], wu[:, at])
            e = 0.5 * (1.0 + lax.erf(u * 0.7071067811865476))
            act[both[h], at] = (u * e).astype(BF16)
            slope = e + u * jnp.exp(-0.5 * u * u) * 0.3989422804014327
            du[both[h], at] = (dact[both[h], at] * slope).astype(BF16)

    def back_part(h):
        @pl.loop(0, width, step=512)
        def _(c):
            at = rows_at(c, 512)
            tmp[...] = nt(du[both[h], :], wu[at, :])
            resid_grad[own_half[h], at] = tmp[rows_at(f * hr, hr), :]
            share[0, own_half[h], at] = tmp[rows_at((1 - f) * hr, hr), :].astype(BF16)

        return start(
            remote(share.at[0, own_half[h]], share.at[1, own_half[h]], psend.at[1, h], precv.at[1, h], me.partner())
        )

    def norm_back(h):
        @pl.loop(0, hr, step=step)
        def _(r):
            at = pl.ds(pl.multiple_of(h * hr + r, step), step)
            dx = resid_grad[at, :] + share[1, at, :].astype(F32)
            v = resid[at, :]
            centered = v - jnp.mean(v, axis=1, keepdims=True)
            scale = lax.rsqrt(jnp.mean(centered * centered, axis=1, keepdims=True) + 1e-05)
            hat = centered * scale
            gains[0:1, :] += jnp.sum(dx * hat, axis=0, keepdims=True)
            gains[1:2, :] += jnp.sum(dx, axis=0, keepdims=True)
            g = dx * gain_ref[...]
            back = scale * (
                g - jnp.mean(g, axis=1, keepdims=True) - hat * jnp.mean(g * hat, axis=1, keepdims=True)
            )
            back = back + cot[pl.ds(pl.multiple_of(h * rows + f * hr + r, step), step), :].astype(F32)
            resid_grad[at, :] = back
            dab[at, :] = back.astype(BF16)

    def out_part(h):
        @pl.loop(0, width, step=512)
        def _(c):
            at = rows_at(c, 512)
            tmp[...] = nn(act[both[h], :], wd[:, at])
            dact[pl.ds(h * rows, hr), at] = tmp[rows_at(f * hr, hr), :]
            share[2, own_half[h], at] = tmp[rows_at((1 - f) * hr, hr), :].astype(BF16)

        return start(
            remote(share.at[2, own_half[h]], share.at[3, own_half[h]], psend.at[2, h], precv.at[2, h], me.partner())
        )

    quarter = hr // 2

    def seat(m, h, k=None):
        base = (q[m] * 2 + f) * rows + h * hr
        if k is None:
            return da.at[pl.ds(pl.multiple_of(base, hr), hr), :]
        return da.at[pl.ds(pl.multiple_of(base + k * quarter, quarter), quarter), :]

    spread = {}

    def spread_begin(h):
        spread["own", h] = start(pltpu.make_async_copy(dab.at[own_half[h]], seat(0, h), gload.at[h]))
        for i in range(2):
            for to, k in ((1, i), (2, 1 - i)):
                sem = (to - 1) * 2 + i
                spread[to, i, h] = start(
                    remote(
                        dab.at[pl.ds(h * hr + k * quarter, quarter)], seat(0, h, k),
                        gsend.at[sem, h], grecv.at[sem, h], me.plane(to),
                    )
                )
        spread["core", 0, h] = start(
            remote(dab.at[own_half[h]], seat(0, h), ksend.at[0, h], krecv.at[0, h], me.partner())
        )

    def spread_on(h):
        spread[1, 0, h].wait_recv()
        spread["g1", h] = start(
            remote(seat(1, h, 0), seat(1, h, 0), gsend.at[4, h], grecv.at[4, h], me.plane(2))
        )
        spread[2, 0, h].wait_recv()
        spread["g2", h] = start(
            remote(seat(2, h, 1), seat(2, h, 1), gsend.at[5, h], grecv.at[5, h], me.plane(1))
        )

    def spread_end(h):
        for m in (1, 2):
            spread[m, 1, h].wait_recv()
            spread["core", m, h] = start(
                remote(seat(m, h), seat(m, h), ksend.at[m, h], krecv.at[m, h], me.partner())
            )
        spread["g1", h].wait_recv()
        spread["g2", h].wait_recv()
        spread["core", 3, h] = start(
            remote(seat(3, h), seat(3, h), ksend.at[3, h], krecv.at[3, h], me.partner())
        )

    gains[...] = jnp.zeros_like(gains)
    for c in first.values():
        c.wait_send()
    load_t.wait()
    swaps = [norm(0)]
    swaps[0].wait_recv()
    hidden_part(0)
    second(1)
    swaps.append(back_part(0))
    out_swaps = [out_part(0)]
    swaps[1].wait_recv()
    norm_back(0)
    spread_begin(0)
    swaps.append(norm(1))
    swaps[2].wait_recv()
    hidden_part(1)
    spread_on(0)
    swaps.append(back_part(1))
    out_swaps.append(out_part(1))
    swaps[3].wait_recv()
    norm_back(1)
    spread_begin(1)
    resid_copy = start(pltpu.make_async_copy(resid_grad, resid_out, lsem.at[0]))

    def weights_part(left, right, out):
        def spill(slot, i):
            return pltpu.make_async_copy(stage.at[slot], out.at[rows_at(i * 256, 256), :], ssem.at[slot])

        @pl.loop(0, width // 256)
        def _(i):
            slot = i % 3

            @pl.when(i >= 3)
            def _():
                spill(slot, i - 3).wait()

            stage[slot] = tn(left[:, rows_at(i * 256, 256)], right[...]).astype(BF16)
            spill(slot, i).start()

        for k in (3, 2, 1):
            i = width // 256 - k
            spill(i % 3, i).wait()

    weights_part(cot, act, fd)
    spread_on(1)
    spread_end(0)
    for h in range(2):
        out_swaps[h].wait_recv()

        @pl.loop(0, hr, step=step)
        def _(r):
            at = pl.ds(pl.multiple_of(h * hr + r, step), step)
            own = dact[pl.ds(pl.multiple_of(h * rows + r, step), step), :]
            tok[at, :] = (resid[at, :] + own + share[3, at, :].astype(F32)).astype(BF16)

    out_copy = start(pltpu.make_async_copy(tok, block_out, lsem.at[1]))
    weights_part(xn, du, fu)
    spread_end(1)
    resid_copy.wait()
    out_copy.wait()
    for h in range(2):
        spread["own", h].wait()
        for m in range(4):
            spread["core", m, h].wait()
        for key in ((1, 0, h), (1, 1, h), (2, 0, h), (2, 1, h), ("g1", h), ("g2", h)):
            spread[key].wait_send()
    for c in swaps + out_swaps + list(sends.values()):
        c.wait_send()


def ffn_part(gated, w_out, tokens, gain, bias, w_up, w_down, cotangent, cid):
    rows, width = tokens.shape
    assert PLANE * gated.shape[1] == width and w_out.shape == (2 * rows, w_up.shape[1])
    span, hidden = 2 * rows, w_up.shape[1]
    sd = jax.ShapeDtypeStruct
    return comm_call(
        ffn_kernel,
        [
            sd((rows, width), BF16),
            sd((rows, width), F32),
            sd((8, width), F32),
            sd((2 * PLANE * rows, width), BF16),
            sd((width, hidden), BF16),
            sd((width, hidden), BF16),
        ],
        [gated, w_out, tokens, gain[None], bias[None], w_up, w_down, cotangent],
        [
            pltpu.VMEM((rows, width), BF16),
            pltpu.VMEM((rows, width), F32),
            pltpu.VMEM((PLANE, span, width), BF16),
            pltpu.VMEM(w_up.shape, BF16),
            pltpu.VMEM(w_down.shape, BF16),
            pltpu.VMEM((PLANE, rows, width), BF16),
            pltpu.VMEM((2, rows, width // 2), BF16),
            pltpu.VMEM((2, rows, width // 2), BF16),
            pltpu.VMEM((rows, width // 2), BF16),
            pltpu.VMEM((rows, width // 2), BF16),
            pltpu.VMEM((rows, width), F32),
            pltpu.VMEM((span, width), BF16),
            pltpu.VMEM((span, hidden), BF16),
            pltpu.VMEM((span, hidden), F32),
            pltpu.VMEM((span, hidden), BF16),
            pltpu.VMEM((span, width), BF16),
            pltpu.VMEM((rows, width), BF16),
            pltpu.VMEM((3, 256, hidden), BF16),
            pltpu.VMEM((rows, 512), F32),
            DMA((8,)),
            DMA((PLANE,)),
            DMA((PLANE, 2)),
            DMA((PLANE, 2)),
            DMA((6, 2)),
            DMA((6, 2)),
            DMA((3, 2)),
            DMA((3, 2)),
            DMA((6, 2)),
            DMA((6, 2)),
            DMA((4, 2)),
            DMA((4, 2)),
            DMA((3,)),
        ],
        cid,
        in_specs=[ANY, ANY, ANY, VM, VM, ANY, ANY, ANY],
        out_specs=[ANY, ANY, VM, ANY, ANY, ANY],
    )


def attention_kernel(
    widths, by_rows,
    tok_ref, gain_ref, bias_ref, dec_ref, cbase, sbase, coff, soff, *refs,
):
    count = len(widths)
    shards_in, refs = refs[:count], refs[count:]
    (xg, q_out, k_out, v_out, gate_out, ret_out, gated_out, states_out, cos_out, sin_out, ccol_out, crow_out, scal_out), refs = (
        refs[:13], refs[13:],
    )
    full, refs = refs[:count], refs[count:]
    hold, refs = refs[:count], refs[count:]
    wl, refs = refs[: count - 1], refs[count - 1 :]
    (tok, ccol, crow, scal, xn, xv, q, k, v, gate, ret, gated, cos, sin, kv, st, sloc, sgot, decg,
     lsem, psend, precv, usend, dsend, zrecv, xsend, xrecv, csend, crecv, tsend, trecv, ssend, srecv, osem, wsem) = refs
    me = Place()
    z, p, f = me.z, me.p, me.f
    spot = z * PLANE + p
    chunk = hold[0].shape[0]
    deep = chunk * PLANE
    tokens, width = xv.shape
    rows = tok_ref.shape[0]
    keys, values = q.shape[1], v.shape[1]
    half = keys // 2
    blocks = tokens // STRETCH
    greet(
        [(me.plane(m), None) for m in (1, 2, 3)]
        + [(me.partner(), None), (me.up(), z < LINE - 1), (me.down(), z > 0)]
    )

    def part(i, at):
        w = widths[i]
        if by_rows[i]:
            return shards_in[i].at[pl.ds(pl.multiple_of(at * w, w), w), :]
        return shards_in[i].at[:, pl.ds(pl.multiple_of(at * w, w), w)]

    def slot(i, ss):
        at = pl.ds(pl.multiple_of(ss * chunk, chunk), chunk)
        return full[i].at[:, at] if by_rows[i] else full[i].at[at, :]

    def block(i, zz):
        at = pl.ds(pl.multiple_of(zz * deep, deep), deep)
        return full[i].at[:, at] if by_rows[i] else full[i].at[at, :]

    def up_copy(i, zz):
        return remote(block(i, zz), block(i, zz), usend.at[i, zz], zrecv.at[i, zz], me.up())

    def down_copy(i, zz):
        return remote(block(i, zz), block(i, zz), dsend.at[i, zz], zrecv.at[i, zz], me.down())

    def part_copies(i, src, at):
        return (
            remote(src, slot(i, at), usend.at[i, z], zrecv.at[i, z], me.up()),
            remote(src, slot(i, at), dsend.at[i, z], zrecv.at[i, z], me.down()),
        )

    def to_line(copies):
        @pl.when(z < LINE - 1)
        def _():
            copies[0].start()

        @pl.when(z > 0)
        def _():
            copies[1].start()

    ahead = 2
    load_t = start(pltpu.make_async_copy(tok_ref, tok, lsem.at[count + 1]))
    local, plane, held = [], [], []
    for i in range(count):
        held.append(start(pltpu.make_async_copy(part(i, p), hold[i], lsem.at[i])))
        local.append(pltpu.make_async_copy(hold[i], slot(i, spot), lsem.at[i]))
        plane.append(
            [
                start(remote(part(i, me.xor(m)), slot(i, spot), psend.at[i, m], precv.at[i, m], me.plane(m)))
                for m in (1, 2, 3)
            ]
        )
    for i in range(ahead):
        to_line(part_copies(i, part(i, p), spot))
    tiny = [start(remote(dec_ref, decg.at[p], tsend.at[m], trecv.at[m], me.plane(m))) for m in (1, 2, 3)]
    tiny_own = start(pltpu.make_async_copy(dec_ref, decg.at[p], tsend.at[0]))
    step = 32
    load_t.wait()

    @pl.loop(0, rows, step=step)
    def _(r):
        at = rows_at(r, step)
        t = tok[at, :].astype(F32)
        centered = t - jnp.mean(t, axis=1, keepdims=True)
        scale = lax.rsqrt(jnp.mean(centered * centered, axis=1, keepdims=True) + 1e-05)
        xn[at, :] = (centered * scale * gain_ref[...] + bias_ref[...]).astype(BF16)

    def seat(m, h=None):
        base = (me.xor(m) * 2 + f) * rows
        if h is None:
            return xv.at[rows_at(base, rows)]
        return xv.at[pl.ds(pl.multiple_of(base + h * (rows // 2), rows // 2), rows // 2)]

    x_own = start(pltpu.make_async_copy(xn, seat(0), lsem.at[count]))
    x1 = start(remote(xn, seat(0), xsend.at[0], xrecv.at[0], me.plane(1)))
    x2 = start(remote(xn, seat(0), xsend.at[1], xrecv.at[1], me.plane(2)))
    xc = start(remote(xn, seat(0), csend.at[0], crecv.at[0], me.partner()))
    for i in range(count):
        held[i].wait()
        local[i].start()

    def own(i):
        local[i].wait()
        for c in plane[i]:
            c.wait_recv()
        if i < ahead:
            for m in (1, 2, 3):
                at = z * PLANE + me.xor(m)
                to_line(part_copies(i, slot(i, at), at))
        else:
            to_line((up_copy(i, z), down_copy(i, z)))

    def forward(i, t):
        @pl.when(z - t >= 0)
        def _():
            up_copy(i, z - t).wait_recv()

            @pl.when(z < LINE - 1)
            def _():
                up_copy(i, z - t).start()

        @pl.when(z + t < LINE)
        def _():
            down_copy(i, z + t).wait_recv()

            @pl.when(z > 0)
            def _():
                down_copy(i, z + t).start()

    def fetch(i):
        forward(i, LINE - 1)
        return start(pltpu.make_async_copy(full[i], wl[i], wsem.at[i]))

    K, V, Q, G, O = range(count)
    own(K)
    own(V)
    forward(K, 1)
    forward(K, 2)
    own(Q)

    for c in tiny:
        c.wait()
    tiny_own.wait()
    heads = lax.broadcasted_iota(jnp.int32, decg.shape[1:], 0)
    lines = [jnp.sum(jnp.where(heads == p, decg[j], 0.0), axis=0, keepdims=True) for j in range(blocks)]
    lines = jnp.concatenate(lines + [jnp.zeros_like(lines[0])] * (8 - blocks), axis=0)
    i0 = lax.broadcasted_iota(jnp.int32, (STRETCH, STRETCH), 0)
    i1 = lax.broadcasted_iota(jnp.int32, (STRETCH, STRETCH), 1)
    row_sums = jnp.dot(
        lines, jnp.where(i0 <= i1, 1.0, 0.0), preferred_element_type=F32, precision=lax.Precision.HIGHEST
    )
    col_sums = lax.dot_general(
        jnp.where(i1 <= i0, 1.0, 0.0), lines, (((1,), (1,)), ((), ())),
        preferred_element_type=F32, precision=lax.Precision.HIGHEST,
    )
    total = jnp.zeros((1, 1), F32)
    for c in range(blocks):
        end = row_sums[c : c + 1, STRETCH - 1 : STRETCH]
        crow[c] = jnp.broadcast_to(row_sums[c : c + 1, :], (8, STRETCH))
        ccol[c * STRETCH : (c + 1) * STRETCH, :] = col_sums[:, c : c + 1]
        scal[c] = jnp.broadcast_to(jnp.exp(end), (8, 128))
        scal[blocks + c] = jnp.broadcast_to(jnp.exp(total), (8, 128))
        total = total + end
    scal[2 * blocks] = jnp.broadcast_to(total, (8, 128))

    fine = coff.shape[0]

    @pl.loop(0, tokens // fine)
    def _(a):
        at = rows_at(a * fine, fine)
        place = pl.ds(z * (tokens // fine) + a, 1)
        ca, sa = cbase[place, :], sbase[place, :]
        cos[at, :] = ca * coff[...] - sa * soff[...]
        sin[at, :] = sa * coff[...] + ca * soff[...]

    forward(V, 1)
    x1.wait_recv()
    g1 = start(remote(seat(1, 0), seat(1, 0), xsend.at[2], xrecv.at[2], me.plane(2)))
    c1 = start(remote(seat(1), seat(1), csend.at[1], crecv.at[1], me.partner()))
    x2.wait_recv()
    g2 = start(remote(seat(2, 1), seat(2, 1), xsend.at[3], xrecv.at[3], me.plane(1)))
    c2 = start(remote(seat(2), seat(2), csend.at[2], crecv.at[2], me.partner()))
    forward(V, 2)
    forward(Q, 1)
    own(G)
    forward(Q, 2)
    own(O)
    load_k = fetch(K)
    g1.wait_recv()
    g2.wait_recv()
    c3 = start(remote(seat(3), seat(3), csend.at[3], crecv.at[3], me.partner()))
    x_own.wait()
    for c in (xc, c1, c2, c3):
        c.wait_recv()
    outs = []

    def put(src, dst):
        outs.append(start(pltpu.make_async_copy(src, dst, osem.at[len(outs)])))

    put(xv, xg)
    put(ccol, ccol_out)
    put(crow, crow_out)
    put(scal, scal_out)
    put(cos, cos_out)
    put(sin, sin_out)
    load_k.wait()

    def turned(at, w, dst):
        y = nn(xv[at, :], w[...])
        a, b = y[:, :half], y[:, half:]
        dst[at, :half] = (a * cos[at, :] - b * sin[at, :]).astype(BF16)
        dst[at, half:] = (b * cos[at, :] + a * sin[at, :]).astype(BF16)

    @pl.loop(0, blocks)
    def _(c):
        turned(rows_at(c * STRETCH, STRETCH), wl[K], k)

    fetch(V).wait()

    @pl.loop(0, blocks)
    def _(c):
        at = rows_at(c * STRETCH, STRETCH)
        val = nn(xv[at, :], wl[V][...]).astype(BF16)
        v[at, :] = val
        end = crow[c, 0:1, STRETCH - 1 : STRETCH]
        kv[c] = tn(k[at, :], (val.astype(F32) * jnp.exp(end - ccol[at, :])).astype(BF16))

    put(k, k_out)
    put(v, v_out)
    sloc[...] = kv[0]
    kv[0] = jnp.zeros_like(sloc)
    for c in range(1, blocks):
        nxt = sloc[...] * scal[c, 0:1, 0:1] + kv[c]
        kv[c] = sloc[...]
        sloc[...] = nxt

    def state_copy(zz):
        return remote(st.at[0], sgot, ssend.at[zz], srecv.at[zz], me.up())

    def send_state():
        st[0] = sloc[...].astype(BF16)
        state_copy(0).start()

    @pl.when(z == 0)
    def _():
        send_state()

    def pass_state(zz):
        @pl.when(z == zz)
        def _():
            state_copy(0).wait_recv()
            if zz < LINE - 1:
                sloc[...] = sloc[...] + sgot[...].astype(F32) * jnp.exp(scal[2 * blocks, 0:1, 0:1])
                send_state()

    pass_state(1)
    forward(G, 1)
    forward(O, 1)
    fetch(Q).wait()
    t_size = 256

    @pl.loop(0, blocks)
    def _(c):
        blk = rows_at(c * STRETCH, STRETCH)
        turned(blk, wl[Q], q)
        row = crow[c, 0:1, :]
        for r in range(0, STRETCH, t_size):
            at = rows_at(c * STRETCH + r, t_size)
            col = ccol[at, :]
            t_index = lax.broadcasted_iota(jnp.int32, (t_size, STRETCH), 0) + r
            s_index = lax.broadcasted_iota(jnp.int32, (t_size, STRETCH), 1)
            mask = jnp.where(t_index >= s_index, jnp.exp(jnp.minimum(col - row, 0.0)), 0.0)
            scores = (nt(q[at, :], k[blk, :]) * mask).astype(BF16)
            ret[at, :] = nn(scores, v[blk, :])

    put(q, q_out)
    pass_state(2)
    forward(G, 2)
    forward(O, 2)
    pass_state(3)

    @pl.when((z > 0) & (z < LINE - 1))
    def _():
        state_copy(0).wait_send()

    @pl.when(z == 0)
    def _():
        state_copy(0).wait_send()
        sgot[...] = jnp.zeros_like(sgot)

    for c in range(blocks):
        st[c] = (kv[c] + sgot[...].astype(F32) * scal[blocks + c, 0:1, 0:1]).astype(BF16)

    @pl.loop(0, blocks)
    def _(c):
        at = rows_at(c * STRETCH, STRETCH)
        decayed = (q[at, :].astype(F32) * jnp.exp(ccol[at, :])).astype(BF16)
        ret[at, :] += nn(decayed, st[c])

    put(ret, ret_out)
    put(st, states_out)
    fetch(G).wait()

    @pl.loop(0, tokens, step=256)
    def _(r):
        at = rows_at(r, 256)
        g = nn(xv[at, :], wl[G][...])
        gate[at, :] = g
        t = ret[at, :]
        centered = t - jnp.mean(t, axis=1, keepdims=True)
        scale = lax.rsqrt(jnp.mean(centered * centered, axis=1, keepdims=True) + 1e-05)
        gated[at, :] = (g / (1.0 + jnp.exp(-g)) * centered * scale).astype(BF16)

    put(gate, gate_out)
    put(gated, gated_out)
    forward(O, LINE - 1)
    for c in (xc, c1, c2, c3, x1, x2, g1, g2):
        c.wait_send()
    for i in range(count):
        for c in plane[i]:
            c.wait_send()
        for zz in range(LINE):

            @pl.when((z < LINE - 1) & (zz <= z))
            def _():
                up_copy(i, zz).wait_send()

            @pl.when((z > 0) & (zz >= z))
            def _():
                down_copy(i, zz).wait_send()

    for c in outs:
        c.wait()


def attention(tokens, gain, bias, decays, tables, shards_in, by_rows, cid):
    rows, width = tokens.shape
    count = len(shards_in)
    chunk = shards_in[0].shape[0]
    group = 2 * PLANE * rows
    blocks = group // STRETCH
    parts = [
        (w.shape[0] // PLANE, chunk) if r else (chunk, w.shape[1] // PLANE) for w, r in zip(shards_in, by_rows)
    ]
    widths = [s[0] if r else s[1] for s, r in zip(parts, by_rows)]
    wholes = [(s[0], width) if r else (width, s[1]) for s, r in zip(parts, by_rows)]
    values, keys = widths[1], widths[0]
    half = keys // 2
    sd = jax.ShapeDtypeStruct
    outs = [
        sd((group, width), BF16),
        sd((group, keys), BF16),
        sd((group, keys), BF16),
        sd((group, values), BF16),
        sd((group, values), F32),
        sd((group, values), F32),
        sd((group, values), BF16),
        sd((blocks, keys, values), BF16),
        sd((group, half), F32),
        sd((group, half), F32),
        sd((group, 1), F32),
        sd((blocks, 8, STRETCH), F32),
        sd((2 * blocks + 1, 8, 128), F32),
    ] + [sd(s, BF16) for s in wholes]
    scratch = (
        [pltpu.VMEM(s, BF16) for s in parts]
        + [pltpu.VMEM(s, BF16) for s in wholes[:-1]]
        + [
            pltpu.VMEM((rows, width), BF16),
            pltpu.VMEM((group, 1), F32),
            pltpu.VMEM((blocks, 8, STRETCH), F32),
            pltpu.VMEM((2 * blocks + 1, 8, 128), F32),
            pltpu.VMEM((rows, width), BF16),
            pltpu.VMEM((group, width), BF16),
            pltpu.VMEM((group, keys), BF16),
            pltpu.VMEM((group, keys), BF16),
            pltpu.VMEM((group, values), BF16),
            pltpu.VMEM((group, values), F32),
            pltpu.VMEM((group, values), F32),
            pltpu.VMEM((group, values), BF16),
            pltpu.VMEM((group, half), F32),
            pltpu.VMEM((group, half), F32),
            pltpu.VMEM((blocks, keys, values), F32),
            pltpu.VMEM((blocks, keys, values), BF16),
            pltpu.VMEM((keys, values), F32),
            pltpu.VMEM((keys, values), BF16),
            pltpu.VMEM((PLANE,) + decays.shape, F32),
            DMA((count + 2,)),
            DMA((count, PLANE)),
            DMA((count, PLANE)),
            DMA((count, LINE)),
            DMA((count, LINE)),
            DMA((count, LINE)),
            DMA((4,)),
            DMA((4,)),
            DMA((4,)),
            DMA((4,)),
            DMA((PLANE,)),
            DMA((PLANE,)),
            DMA((1,)),
            DMA((1,)),
            DMA((16,)),
            DMA((count,)),
        ]
    )
    return comm_call(
        functools.partial(attention_kernel, widths, by_rows),
        outs,
        [tokens, gain[None], bias[None], decays] + list(tables) + list(shards_in),
        scratch,
        cid,
        in_specs=[ANY] + [VM] * 7 + [ANY] * count,
        out_specs=[ANY] * (13 + count),
    )


class LineSum:
    def __init__(self, me, own, rx, usend, urecv, dsend, drecv, add):
        self.me, self.own, self.rx, self.add = me, own, rx, add
        self.sems = usend, urecv, dsend, drecv

    def up(self, src, zz):
        return remote(src, self.rx.at[zz], self.sems[0].at[zz], self.sems[1].at[zz], self.me.up())

    def down(self, src, zz):
        slot = jnp.where(zz == self.me.z - 1, LINE, zz)
        return remote(src, self.rx.at[slot], self.sems[2].at[zz], self.sems[3].at[zz], self.me.down())

    def begin(self, order=(3, 2, 1), src=None):
        src = src or self.own
        for zz in order:

            @pl.when(self.me.z == 0)
            def _():
                self.up(src(zz), zz).start()

            @pl.when(self.me.z == LINE - 1)
            def _():
                self.down(src(LINE - 1 - zz), LINE - 1 - zz).start()

    def pass_up(self, zz):
        self.up(self.own(zz), zz).wait_recv()
        self.add(self.rx.at[zz], self.own(zz))
        self.up(self.rx.at[zz], zz).start()

    def pass_down(self, zz):
        self.down(self.own(zz), zz).wait_recv()
        self.add(self.rx.at[zz], self.own(zz))
        self.down(self.rx.at[zz], zz).start()

    def near(self, k):
        @pl.when(self.me.z == 1)
        def _():
            self.pass_up(LINE - 1 - k)

        @pl.when(self.me.z == 2)
        def _():
            self.pass_down(k)

    def far(self):
        @pl.when(self.me.z == 1)
        def _():
            self.pass_down(0)

        @pl.when(self.me.z == 2)
        def _():
            self.pass_up(LINE - 1)

    def arrive(self):
        z = self.me.z

        @pl.when(z > 0)
        def _():
            self.up(self.own(z), z).wait_recv()

        @pl.when(z < LINE - 1)
        def _():
            self.down(self.own(z), z).wait_recv()

    def finish(self):
        z = self.me.z
        for zz in range(LINE):

            @pl.when((z < LINE - 1) & (zz > z))
            def _():
                self.up(self.own(zz), zz).wait_send()

            @pl.when((z > 0) & (zz < z))
            def _():
                self.down(self.own(zz), zz).wait_send()


def add_rows(dst, src):
    rows = dst.shape[0]
    step = 32 if dst.shape[1] > 512 else 128

    @pl.loop(0, rows, step=step)
    def _(r):
        at = rows_at(r, step)
        dst[at, :] = (dst[at, :].astype(F32) + src[at, :].astype(F32)).astype(BF16)


def total_rows(z, dst, own, rx):
    rows = dst.shape[0]
    step = 32 if dst.shape[1] > 512 else 128

    @pl.loop(0, rows, step=step)
    def _(r):
        at = rows_at(r, step)
        v = own[at, :].astype(F32)
        v = v + jnp.where(z > 0, rx[z, at, :].astype(F32), 0.0)
        v = v + jnp.where(z < LINE - 1, rx[LINE, at, :].astype(F32), 0.0)
        dst[at, :] = v.astype(dst.dtype)


def line_sems():
    return [DMA((LINE,)) for _ in range(4)]


def retention_back_kernel(
    da_ref, wo_ref, gated_ref, gate_ref, ret_ref, q_ref, k_ref, v_ref, s_ref, cos_ref, sin_ref,
    ccol_in, crow_in, scal_in, xg_ref, fu_ref, fd_ref,
    dh_out, sums, gate_fin, f1, av_out, aq_out,
    ccol_ref, crow_ref, scal_ref, dh, da, wo, gated, gr, q, k, v, st, cos, sin, dr, xt, ao, ag, rxo, rxg, fin, qo, gb, lg, got, rxf, fo, pbuf, gbuf,
    lsem, gsem, xsem, fsend, frecv, osem, fosem, ssend, srecv, psend, precv, *line,
):
    me = Place()
    z, p = me.z, me.p
    greet(
        [(me.plane(m), None) for m in (1, 2, 3)]
        + [(me.up(), z < LINE - 1), (me.down(), z > 0)]
    )
    width = da.shape[1]
    tokens = da.shape[0]
    keys, values = q.shape[1], v.shape[1]
    blocks = tokens // STRETCH
    half = keys // 2
    pq = [me.xor(m) for m in range(4)]
    chunk = fu_ref.shape[0] // SPANS

    def f_block(h, zp, place):
        return (fu_ref, fd_ref)[h].at[pl.ds(pl.multiple_of((zp * PLANE + place) * chunk, chunk), chunk), :]

    early = (3, 0, 2)
    units = 2 * len(early)
    away = ((1, 3), (2, 3))
    kept = ((0, 2), (0, 1))
    nbr = (1, 2)

    def f_copy(h, zp, j):
        return remote(
            f_block(h, zp, pq[away[h][j]]), rxf.at[h, early.index(zp), j], fsend.at[h, zp, j], frecv.at[h, zp, j], me.plane(nbr[h])
        )

    deep = width // LINE
    ends_first = [jnp.where(z < LINE // 2, LINE - 1 - i, i) for i in range(LINE)]

    def slab(i):
        at = rows_at(ends_first[i] * deep, deep)
        return pltpu.make_async_copy(da_ref.at[:, at], da.at[:, at], lsem.at[12 + i])

    slab(0).start()
    loads = [
        start(pltpu.make_async_copy(a, b, lsem.at[i]))
        for i, (a, b) in enumerate(
            [(gated_ref, gated), (wo_ref, wo), (q_ref, q), (k_ref, k), (v_ref, v), (s_ref, st),
             (cos_ref, cos), (sin_ref, sin), (ccol_in, ccol_ref), (crow_in, crow_ref), (scal_in, scal_ref)]
        )
    ]
    for i in range(1, LINE):
        slab(i).start()
    for zp in early:
        for h in range(2):
            for j in range(2):
                f_copy(h, zp, j).start()

    def f_own(u):
        h, zp = u % 2, early[u // 2]
        return [
            pltpu.make_async_copy(f_block(h, zp, pq[kept[h][j]]), fo.at[u % 2, j], fosem.at[u % 2, j])
            for j in range(2)
        ]

    def f_out(u):
        h, zp = u % 2, early[u // 2]
        return pltpu.make_async_copy(rxf.at[h, u // 2], f1.at[h, zp], osem.at[u])

    for u in range(2):
        for c in f_own(u):
            c.start()

    def f_unit(u):
        h, zp = u % 2, early[u // 2]
        for j, c in enumerate(f_own(u)):
            c.wait()
            f_copy(h, zp, j).wait_recv()
            add_rows(rxf.at[h, u // 2, j], fo.at[u % 2, j])
        f_out(u).start()
        if u + 2 < units:
            for c in f_own(u + 2):
                c.start()

    def tile_rows(i):
        return rows_at(i * 256, 256)

    def gate_loads(i):
        at = tile_rows(i)
        slot = i % 3
        return (
            pltpu.make_async_copy(gate_ref.at[at, :], gr.at[slot, 0], gsem.at[slot, 0]),
            pltpu.make_async_copy(ret_ref.at[at, :], gr.at[slot, 1], gsem.at[slot, 1]),
        )

    for c in gate_loads(0) + gate_loads(1):
        c.start()

    out_sum = LineSum(me, lambda zz: ao.at[rows_at(zz * (width // LINE), width // LINE), :], rxo, *line[:4], add_rows)
    gate_sum = LineSum(me, lambda zz: ag.at[rows_at(zz * (width // LINE), width // LINE), :], rxg, *line[4:], add_rows)

    loads[0].wait()
    for turn in range(LINE):
        slab(turn).wait()

        @pl.loop(0, deep, step=256)
        def _(i):
            at = rows_at(ends_first[turn] * deep + i, 256)
            ao[at, :] = tn(da[:, at], gated[...]).astype(BF16)

        if turn < 2:
            out_sum.begin((LINE - 1 - turn,))
    for c in loads[1:]:
        c.wait()

    tiles = tokens // 256

    @pl.loop(0, tiles)
    def _(i):
        @pl.when(i + 2 < tiles)
        def _():
            for c in gate_loads(i + 2):
                c.start()

        for c in gate_loads(i):
            c.wait()
        at = tile_rows(i)
        slot = i % 3
        dgated = nt(da[at, :], wo[...])
        gate = gr[slot, 0]
        ret = gr[slot, 1]
        centered = ret - jnp.mean(ret, axis=1, keepdims=True)
        scale = lax.rsqrt(jnp.mean(centered * centered, axis=1, keepdims=True) + 1e-05)
        grouped = centered * scale
        sig = 1.0 / (1.0 + jnp.exp(-gate))
        silu = gate * sig
        dh[at, 2 * keys + values :] = (dgated * grouped * (sig * (1.0 + gate * (1.0 - sig)))).astype(BF16)
        dg = dgated * silu
        dr[at, :] = (
            scale * (dg - jnp.mean(dg, axis=1, keepdims=True) - grouped * jnp.mean(dg * grouped, axis=1, keepdims=True))
        ).astype(BF16)

    lg[...] = jnp.zeros_like(lg)

    @pl.loop(0, blocks)
    def _(c):
        at = rows_at(c * STRETCH, STRETCH)
        decayed = (q[at, :].astype(F32) * jnp.exp(ccol_ref[at, :])).astype(BF16)
        got_q = tn(decayed, dr[at, :])
        qo[c] = got_q
        lg[...] += scal_ref[blocks + c, 0:1, 0:1] * got_q

    state_copy = remote(gb.at[0], got, ssend.at[0], srecv.at[0], me.down())

    def pass_state(zz):
        @pl.when(z == zz)
        def _():
            if zz < LINE - 1:
                state_copy.wait_recv()
            if zz > 0:
                add = lg[...]
                if zz < LINE - 1:
                    add = add + got[...].astype(F32) * jnp.exp(scal_ref[2 * blocks, 0:1, 0:1])
                gb[0] = add.astype(BF16)
                state_copy.start()

    pass_state(LINE - 1)
    out_sum.begin((1,))
    out_sum.near(0)
    def x_tile(i):
        return pltpu.make_async_copy(xg_ref.at[:, rows_at(i * 256, 256)], xt.at[i % 3], xsem.at[i % 3])

    x_tile(0).start()
    x_tile(1).start()

    @pl.loop(0, width // 256)
    def _(i):
        @pl.when(i + 2 < width // 256)
        def _():
            x_tile(i + 2).start()

        x_tile(i).wait()
        ag[rows_at(i * 256, 256), :] = tn(xt[i % 3], dh[:, 2 * keys + values :]).astype(BF16)

    gate_sum.begin()
    out_sum.near(1)
    pass_state(2)
    f_unit(0)
    f_unit(1)
    out_sum.far()

    pass_state(1)
    pass_state(0)

    @pl.when(z > 0)
    def _():
        state_copy.wait_send()

    @pl.when(z < LINE - 1)
    def _():
        lg[...] = got[...].astype(F32)

    @pl.when(z == LINE - 1)
    def _():
        lg[...] = jnp.zeros_like(lg)

    for c in reversed(range(blocks)):
        gb[c] = lg[...].astype(BF16)
        if c:
            lg[...] = lg[...] * scal_ref[c, 0:1, 0:1] + qo[c]

    t_size = 256

    @pl.loop(0, blocks)
    def _(c):
        blk = rows_at(c * STRETCH, STRETCH)
        row = crow_ref[c, 0:1, :]
        end = crow_ref[c, 0:1, STRETCH - 1 : STRETCH]
        for r in range(0, STRETCH, t_size):
            at = rows_at(c * STRETCH + r, t_size)
            col = ccol_ref[at, :]
            t_index = lax.broadcasted_iota(jnp.int32, (t_size, STRETCH), 0) + r
            s_index = lax.broadcasted_iota(jnp.int32, (t_size, STRETCH), 1)
            mask = jnp.where(t_index >= s_index, jnp.exp(jnp.minimum(col - row, 0.0)), 0.0)
            pbuf[r : r + t_size, :] = (nt(q[at, :], k[blk, :]) * mask).astype(BF16)
            g = (nt(dr[at, :], v[blk, :]) * mask).astype(BF16)
            gbuf[r : r + t_size, :] = g
            dq = nt(dr[at, :], st[c]) * jnp.exp(col) + nn(g, k[blk, :])
            a, b = dq[:, :half], dq[:, half:]
            dh[at, :half] = (a * cos[at, :] + b * sin[at, :]).astype(BF16)
            dh[at, half:keys] = (b * cos[at, :] - a * sin[at, :]).astype(BF16)
        for r in range(0, STRETCH, t_size):
            at = rows_at(c * STRETCH + r, t_size)
            tail = jnp.exp(end - ccol_ref[at, :])
            w = (v[at, :].astype(F32) * tail).astype(BF16)
            dk = nt(w, gb[c]) + tn(gbuf[:, r : r + t_size], q[blk, :])
            a, b = dk[:, :half], dk[:, half:]
            dh[at, keys : keys + half] = (a * cos[at, :] + b * sin[at, :]).astype(BF16)
            dh[at, keys + half : 2 * keys] = (b * cos[at, :] - a * sin[at, :]).astype(BF16)
            dv = nn(k[at, :], gb[c]) * tail + tn(pbuf[:, r : r + t_size], dr[blk, :])
            dh[at, 2 * keys : 2 * keys + values] = dv.astype(BF16)

    dh_copy = start(pltpu.make_async_copy(dh, dh_out, lsem.at[2]))
    plane = []

    def deal(i, chain, a):
        chain.arrive()
        total_rows(z, fin.at[i], a.at[rows_at(z * (width // LINE), width // LINE), :], chain.rx)
        cols = pl.ds(i * values, values)
        for m in (1, 2, 3):
            plane.append(
                start(
                    remote(
                        fin.at[i, rows_at(pq[m] * chunk, chunk), :], sums.at[p, :, cols],
                        psend.at[i, m], precv.at[i, m], me.plane(m),
                    )
                )
            )
        plane.append(
            start(
                pltpu.make_async_copy(
                    fin.at[i, rows_at(p * chunk, chunk), :], sums.at[p, :, cols], psend.at[i, 0]
                )
            )
        )

    gate_sum.near(0)
    for u in range(2, 4):
        f_unit(u)
    deal(0, out_sum, ao)
    x_tile(0).start()
    x_tile(1).start()
    wide = 2 * keys + values

    @pl.loop(0, width // 256)
    def _(i):
        @pl.when(i + 2 < width // 256)
        def _():
            x_tile(i + 2).start()

        x_tile(i).wait()
        da[rows_at(i * 256, 256), :wide] = tn(xt[i % 3], dh[:, :wide]).astype(BF16)

    to_last = [
        start(pltpu.make_async_copy(da.at[:, : 2 * keys], aq_out, lsem.at[0])),
        start(pltpu.make_async_copy(da.at[:, 2 * keys : wide], av_out, lsem.at[1])),
    ]
    gate_sum.near(1)
    gate_sum.far()
    for u in range(4, 6):
        f_unit(u)
    gate_sum.arrive()
    total_rows(z, fin.at[1], ag.at[rows_at(z * deep, deep), :], rxg)
    to_last.append(start(pltpu.make_async_copy(fin.at[1], gate_fin, lsem.at[3])))
    for c in plane + to_last + [dh_copy]:
        c.wait()
    out_sum.finish()
    gate_sum.finish()
    for u in range(units):
        f_out(u).wait()
    for zp in early:
        for h in range(2):
            for j in range(2):
                f_copy(h, zp, j).wait_send()


def retention_back(da, wo, gated, gate, ret, q, k, v, states, cos, sin, ccol, crow, scal, xg, fu, fd, cid):
    tokens, width = da.shape
    keys, values = q.shape[1], v.shape[1]
    chunk = width // SPANS
    blocks = tokens // STRETCH
    hidden = fu.shape[1]
    deep = width // LINE
    return comm_call(
        retention_back_kernel,
        [
            jax.ShapeDtypeStruct((tokens, 2 * keys + 2 * values), BF16),
            jax.ShapeDtypeStruct((PLANE, chunk, values), BF16),
            jax.ShapeDtypeStruct((deep, values), BF16),
            jax.ShapeDtypeStruct((2, LINE, 2, chunk, hidden), BF16),
            jax.ShapeDtypeStruct((width, values), BF16),
            jax.ShapeDtypeStruct((width, 2 * keys), BF16),
        ],
        [da, wo, gated, gate, ret, q, k, v, states, cos, sin, ccol, crow, scal, xg, fu, fd],
        [
            pltpu.VMEM(ccol.shape, F32),
            pltpu.VMEM(crow.shape, F32),
            pltpu.VMEM(scal.shape, F32),
            pltpu.VMEM((tokens, 2 * keys + 2 * values), BF16),
            pltpu.VMEM((tokens, width), BF16),
            pltpu.VMEM(wo.shape, BF16),
            pltpu.VMEM(gated.shape, BF16),
            pltpu.VMEM((3, 2, 256, values), F32),
            pltpu.VMEM(q.shape, BF16),
            pltpu.VMEM(k.shape, BF16),
            pltpu.VMEM(v.shape, BF16),
            pltpu.VMEM(states.shape, BF16),
            pltpu.VMEM(cos.shape, F32),
            pltpu.VMEM(sin.shape, F32),
            pltpu.VMEM((tokens, values), BF16),
            pltpu.VMEM((3, tokens, 256), BF16),
            pltpu.VMEM((width, values), BF16),
            pltpu.VMEM((width, values), BF16),
            pltpu.VMEM((LINE + 1, deep, values), BF16),
            pltpu.VMEM((LINE + 1, deep, values), BF16),
            pltpu.VMEM((2, deep, values), BF16),
            pltpu.VMEM((blocks, keys, values), F32),
            pltpu.VMEM((blocks, keys, values), BF16),
            pltpu.VMEM((keys, values), F32),
            pltpu.VMEM((keys, values), BF16),
            pltpu.VMEM((2, LINE - 1, 2, chunk, hidden), BF16),
            pltpu.VMEM((2, 2, chunk, hidden), BF16),
            pltpu.VMEM((STRETCH, STRETCH), BF16),
            pltpu.VMEM((STRETCH, STRETCH), BF16),
            DMA((12 + LINE,)),
            DMA((3, 2)),
            DMA((3,)),
            DMA((2, LINE, 2)),
            DMA((2, LINE, 2)),
            DMA((2 * LINE,)),
            DMA((2, 2)),
            DMA((1,)),
            DMA((1,)),
            DMA((2, PLANE)),
            DMA((2, PLANE)),
        ]
        + line_sems()
        + line_sems(),
        cid,
        in_specs=[ANY] * 17,
        out_specs=[ANY] * 6,
    )


def last_kernel(
    dh_ref, av_ref, aq_ref, wq_ref, wk_ref, wv_ref, wg_ref, f1_ref, fu_ref, fd_ref, gate_ref, tok_ref, gain_ref, resid_ref, second_ref,
    grad_out, gains, fout, sums,
    tok, resid, rxl, flow, dh, wh, share, rx0, rx1a, rx1b, rx2a, rx2b, av, aq, rxv, rxq, fin, rf2, kf, rxfa, rxfb, grx,
    lsem, ksem, lsend, lrecv, fsend, frecv, csend, crecv, xsend, xrecv, gsend, grecv, psend, precv, *line,
):
    me = Place()
    z, p, f = me.z, me.p, me.f
    rounds = [
        [me.partner()],
        [me.plane(m) for m in (1, 2, 3)],
        [me.at((z + t) % LINE, p, f) for t in range(1, LINE)],
    ]
    greet([(d, None) for r in rounds for d in r])
    width, keys2, values = av.shape[0], aq.shape[1], av.shape[1]
    rows = tok_ref.shape[0]
    pq = [me.xor(m) for m in range(4)]
    chunk = width // SPANS
    deep = width // LINE

    late = 1

    def f_copy(h, zp):
        src = flow.at[h] if zp == late else f1_ref.at[h, zp, 1]
        return remote(src, rf2.at[h, zp], fsend.at[h, zp], frecv.at[h, zp], me.plane(2 - h))

    def f_block(h, place):
        return (fu_ref, fd_ref)[h].at[rows_at((late * PLANE + place) * chunk, chunk), :]

    def late_copy(h, j):
        place = pq[((1, 3), (2, 3))[h][j]]
        return remote(f_block(h, place), rxl.at[h, j], lsend.at[h, j], lrecv.at[h, j], me.plane(1 + h))

    def block_of(a, size):
        return lambda zz: a.at[rows_at(zz * size, size), :]

    v_sum = LineSum(me, block_of(av, deep), rxv, *line[:4], add_rows)
    q_sum = LineSum(me, block_of(aq, deep), rxq, *line[4:8], add_rows)
    fa_sum = LineSum(me, lambda zz: kf.at[0, zz], rxfa, *line[8:12], add_rows)
    fb_sum = LineSum(me, lambda zz: kf.at[1, zz], rxfb, *line[12:16], add_rows)
    v_sum.begin(src=block_of(av_ref, deep))
    q_sum.begin(src=block_of(aq_ref, deep))
    for j in (1, 0):
        for h in range(2):
            late_copy(h, j).start()
    for zp in (3, 0, 2):
        for h in range(2):
            f_copy(h, zp).start()
    load = start(pltpu.make_async_copy(dh_ref, dh, lsem.at[0]))
    owns = [
        start(pltpu.make_async_copy(av_ref, av, lsem.at[7])),
        start(pltpu.make_async_copy(aq_ref, aq, lsem.at[8])),
    ]
    loads, at = [], 0
    for i, w in enumerate((wq_ref, wk_ref, wv_ref, wg_ref)):
        size = w.shape[1]
        loads.append(start(pltpu.make_async_copy(w, wh.at[:, at : at + size], lsem.at[1 + i])))
        at += size
    keeps = []
    for h in range(2):
        for i, zp in enumerate((3, 0, 2)):
            keeps.append(start(pltpu.make_async_copy(f1_ref.at[h, zp, 0], kf.at[h, zp], ksem.at[h, i])))
        for j, dst in ((0, kf.at[h, late]), (1, flow.at[h])):
            place = pq[((0, 2), (0, 1))[h][j]]
            keeps.append(start(pltpu.make_async_copy(f_block(h, place), dst, ksem.at[h, 3 + j])))
    rest = [
        start(pltpu.make_async_copy(tok_ref, tok, lsem.at[5])),
        start(pltpu.make_async_copy(resid_ref, resid, lsem.at[6])),
    ]

    load.wait()
    plane = []

    def deal(i, chain, a):
        chain.arrive()
        total_rows(z, fin.at[i], a.at[rows_at(z * deep, deep), :], chain.rx)
        spread(i, fin.at[i])

    def spread(i, src):
        cols = pl.ds(i * values, values)
        for m in (1, 2, 3):
            plane.append(
                start(
                    remote(
                        src.at[rows_at(pq[m] * chunk, chunk), :], sums.at[p, :, cols],
                        psend.at[i, m], precv.at[i, m], me.plane(m),
                    )
                )
            )
        plane.append(
            start(
                pltpu.make_async_copy(
                    src.at[rows_at(p * chunk, chunk), :], sums.at[p, :, cols], psend.at[i, 0]
                )
            )
        )

    gate_load = start(pltpu.make_async_copy(gate_ref, fin.at[2], lsem.at[9]))
    for c in loads + owns + [gate_load]:
        c.wait()
    spread(2, fin.at[2])

    own_rows, their_rows = rows_at(f * rows, rows), rows_at((1 - f) * rows, rows)
    wide = width // 2
    ca, cb = pl.ds(0, wide), pl.ds(wide, wide)
    everything, whole = pl.ds(0, width), pl.ds(0, wide)
    first, sends = {}, {}

    def share_part(m):
        at_rows = rows_at(pq[m] * 2 * rows, 2 * rows)

        @pl.loop(0, width, step=256)
        def _(c):
            at = rows_at(c, 256)
            share[m, :, at] = nt(dh[at_rows, :], wh[at, :]).astype(BF16)

        first[m] = start(
            remote(share.at[m, their_rows], rx0.at[m], csend.at[m], crecv.at[m], me.partner())
        )

    def pass_on(m):
        first[m].wait_recv()
        add_into(rx0.at[m], everything, share.at[m, own_rows], everything)
        k = 0 if m == 3 else 1
        if m & 1:
            sends["a", k] = start(
                remote(rx0.at[m, :, ca], rx1a.at[k], xsend.at[k], xrecv.at[k], me.plane(1))
            )
        if m & 2:
            sends["b", k] = start(
                remote(rx0.at[m, :, cb], rx1b.at[k], xsend.at[2 + k], xrecv.at[2 + k], me.plane(2))
            )

    share_part(3)
    share_part(1)
    v_sum.near(0)
    share_part(2)
    for c in keeps:
        c.wait()
    for h in range(2):
        late_copy(h, 1).wait_recv()
        add_rows(flow.at[h], rxl.at[h, 1])
        f_copy(h, late).start()
    pass_on(3)
    pass_on(1)
    share_part(0)
    v_sum.near(1)
    pass_on(2)
    pass_on(0)
    for h in range(2):
        late_copy(h, 0).wait_recv()
        add_rows(kf.at[h, late], rxl.at[h, 0])
    v_sum.far()
    q_sum.near(0)
    for ends, turns in (((3, 0), (3,)), ((2, 1), (2, 1))):
        for zp in ends:
            for h in range(2):
                f_copy(h, zp).wait_recv()
                add_rows(kf.at[h, zp], rf2.at[h, zp])
        for zz in turns:
            fa_sum.begin((zz,))
            fb_sum.begin((zz,))
    q_sum.near(1)
    q_sum.far()
    deal(0, v_sum, av)
    sends["a", 0].wait_recv()
    add_into(rx1a.at[0], whole, rx0.at[2], ca)
    s2a = start(remote(rx1a.at[0], rx2a, xsend.at[4], xrecv.at[4], me.plane(2)))
    sends["b", 0].wait_recv()
    add_into(rx1b.at[0], whole, rx0.at[1], cb)
    s2b = start(remote(rx1b.at[0], rx2b, xsend.at[5], xrecv.at[5], me.plane(1)))
    fa_sum.near(0)
    sends["a", 1].wait_recv()
    sends["b", 1].wait_recv()
    deal(1, q_sum, aq)
    fb_sum.near(0)
    s2a.wait_recv()
    s2b.wait_recv()
    for c in rest:
        c.wait()
    gains[...] = jnp.zeros_like(gains)
    gains[2:4, :] = second_ref[0:2, :]
    step = 32

    @pl.loop(0, rows, step=step)
    def _(r):
        at = rows_at(r, step)
        left = rx0[0, at, ca].astype(F32) + rx1a[1, at, :].astype(F32) + rx2a[at, :].astype(F32)
        right = rx0[0, at, cb].astype(F32) + rx1b[1, at, :].astype(F32) + rx2b[at, :].astype(F32)
        dx = jnp.concatenate([left, right], axis=1)
        v = tok[at, :].astype(F32)
        centered = v - jnp.mean(v, axis=1, keepdims=True)
        scale = lax.rsqrt(jnp.mean(centered * centered, axis=1, keepdims=True) + 1e-05)
        hat = centered * scale
        gains[0:1, :] += jnp.sum(dx * hat, axis=0, keepdims=True)
        gains[1:2, :] += jnp.sum(dx, axis=0, keepdims=True)
        g = dx * gain_ref[...]
        back = scale * (
            g - jnp.mean(g, axis=1, keepdims=True) - hat * jnp.mean(g * hat, axis=1, keepdims=True)
        )
        tok[at, :] = (back + resid[at, :]).astype(BF16)

    out_copy = start(pltpu.make_async_copy(tok, grad_out, lsem.at[0]))

    def gain_copies(r):
        base = (0, 1, 4)[r]
        return [
            remote(gains, grx.at[base + i], gsend.at[base + i], grecv.at[base + i], d)
            for i, d in enumerate(rounds[r])
        ]

    def gain_begin(r):
        for c in gain_copies(r):
            c.start()

    def gain_end(r):
        for c in gain_copies(r):
            c.wait()
        for i in range(len(rounds[r])):
            gains[...] += grx[(0, 1, 4)[r] + i]

    gain_begin(0)
    fa_sum.near(1)
    fa_sum.far()
    gain_end(0)
    gain_begin(1)
    fb_sum.near(1)
    gain_end(1)
    gain_begin(2)
    fb_sum.far()
    fa_sum.arrive()
    total_rows(z, fout.at[0], kf.at[0, z], rxfa)
    fb_sum.arrive()
    total_rows(z, fout.at[1], kf.at[1, z], rxfb)
    gain_end(2)
    for c in plane + [out_copy]:
        c.wait()
    for h in range(2):
        for j in range(2):
            late_copy(h, j).wait_send()
    for chain in (v_sum, q_sum, fa_sum, fb_sum):
        chain.finish()
    for c in list(first.values()) + list(sends.values()) + [s2a, s2b]:
        c.wait_send()
    for zp in range(LINE):
        for h in range(2):
            f_copy(h, zp).wait_send()


def last_sums(dh, av, aq, wq, wk, wv, wg, f1, fu, fd, gate_fin, tokens, gain, resid, second, cid):
    width = av.shape[0]
    rows = tokens.shape[0]
    keys, values = wq.shape[1], wv.shape[1]
    assert 2 * keys == values
    chunk, deep = width // SPANS, width // LINE
    hidden = f1.shape[-1]
    return comm_call(
        last_kernel,
        [
            jax.ShapeDtypeStruct((rows, width), BF16),
            jax.ShapeDtypeStruct((8, width), F32),
            jax.ShapeDtypeStruct((2, chunk, hidden), BF16),
            jax.ShapeDtypeStruct((PLANE, chunk, 3 * values), BF16),
        ],
        [dh, av, aq, wq, wk, wv, wg, f1, fu, fd, gate_fin, tokens, gain[None], resid, second],
        [
            pltpu.VMEM((rows, width), BF16),
            pltpu.VMEM((rows, width), F32),
            pltpu.VMEM((2, 2, chunk, hidden), BF16),
            pltpu.VMEM((2, chunk, hidden), BF16),
            pltpu.VMEM(dh.shape, BF16),
            pltpu.VMEM((width, dh.shape[1]), BF16),
            pltpu.VMEM((PLANE, 2 * rows, width), BF16),
            pltpu.VMEM((PLANE, rows, width), BF16),
            pltpu.VMEM((2, rows, width // 2), BF16),
            pltpu.VMEM((2, rows, width // 2), BF16),
            pltpu.VMEM((rows, width // 2), BF16),
            pltpu.VMEM((rows, width // 2), BF16),
            pltpu.VMEM((width, values), BF16),
            pltpu.VMEM((width, 2 * keys), BF16),
            pltpu.VMEM((LINE + 1, deep, values), BF16),
            pltpu.VMEM((LINE + 1, deep, 2 * keys), BF16),
            pltpu.VMEM((3, deep, values), BF16),
            pltpu.VMEM((2, LINE, chunk, hidden), BF16),
            pltpu.VMEM((2, LINE, chunk, hidden), BF16),
            pltpu.VMEM((LINE + 1, chunk, hidden), BF16),
            pltpu.VMEM((LINE + 1, chunk, hidden), BF16),
            pltpu.VMEM((7, 8, width), F32),
            DMA((10,)),
            DMA((2, 5)),
            DMA((2, 2)),
            DMA((2, 2)),
            DMA((2, LINE)),
            DMA((2, LINE)),
            DMA((4,)),
            DMA((4,)),
            DMA((6,)),
            DMA((6,)),
            DMA((7,)),
            DMA((7,)),
            DMA((3, PLANE)),
            DMA((3, PLANE)),
        ]
        + line_sems()
        + line_sems()
        + line_sems()
        + line_sems(),
        cid,
        in_specs=[ANY] * 12 + [VM, ANY, VM],
        out_specs=[ANY, VM, VM, ANY],
    )


def outputs_kernel(
    last, first, ffn, low_out, low_grad, gains, q, k, v, gate, out, up, down, block_out, grad_tokens, *vectors
):
    values = v.shape[1]
    keys = q.shape[1]
    v[...] = last[0, :, :values].astype(F32)
    q[...] = last[0, :, values : values + keys].astype(F32)
    k[...] = last[0, :, values + keys : 2 * values].astype(F32)
    gate[...] = last[0, :, 2 * values :].astype(F32)
    out[...] = first[0].astype(F32).T
    up[...] = ffn[0].astype(F32)
    down[...] = ffn[1].astype(F32).T
    block_out[...] = low_out[...]
    grad_tokens[...] = low_grad[...]
    for i, g in enumerate(vectors):
        g[...] = gains[i, :]


def outputs(last, first, ffn, low_out, low_grad, gains, keys):
    heads, chunk, values = first.shape
    hidden = ffn.shape[-1]
    rows, width = low_out.shape
    piece, slab = hidden // heads, rows // heads
    sd = jax.ShapeDtypeStruct
    by_column = [pl.BlockSpec((chunk, size), lambda i: (0, i)) for size in (keys, keys, values, values)]
    by_row = pl.BlockSpec((values, chunk), lambda i: (i, 0))
    low = pl.BlockSpec((slab, width), lambda i: (i, 0))
    sums = [pl.BlockSpec((1, chunk, a.shape[-1]), lambda i: (i, 0, 0)) for a in (last, first)]
    return pl.pallas_call(
        outputs_kernel,
        grid=(heads,),
        in_specs=[
            *sums,
            pl.BlockSpec((2, chunk, piece), lambda i: (0, 0, i)),
            low,
            low,
            pl.BlockSpec(gains.shape, lambda i: (0, 0)),
        ],
        out_specs=by_column
        + [
            by_row,
            pl.BlockSpec((chunk, piece), lambda i: (0, i)),
            pl.BlockSpec((piece, chunk), lambda i: (i, 0)),
            low,
            low,
        ]
        + [pl.BlockSpec((width,), lambda i: (0,))] * 4,
        out_shape=[
            sd((chunk, heads * keys), F32),
            sd((chunk, heads * keys), F32),
            sd((chunk, heads * values), F32),
            sd((chunk, heads * values), F32),
            sd((heads * values, chunk), F32),
            sd((chunk, hidden), F32),
            sd((hidden, chunk), F32),
            sd((rows, width), BF16),
            sd((rows, width), BF16),
        ]
        + [sd((width,), F32)] * 4,
    )(last, first, ffn, low_out, low_grad, gains)


def angle_tables(fine, half_width):
    frequency = 10000.0 ** (-np.linspace(0.0, 1.0, half_width))
    coarse = fine * np.arange(SEQUENCE_LENGTH // fine)[:, None] * frequency[None, :]
    near = np.arange(fine)[:, None] * frequency[None, :]
    return [np.asarray(f(a), np.float32) for a in (coarse, near) for f in (np.cos, np.sin)]


def shards(
    tokens,
    ln1_gain,
    ln1_bias,
    w_query,
    w_key,
    w_value,
    w_gate,
    w_out,
    decay_log,
    ln2_gain,
    ln2_bias,
    w_up,
    w_down,
    cotangent,
):
    row_count, width = tokens.shape
    span_rows = cotangent.shape[0]
    heads = decay_log.shape[1]
    repeats = lax.axis_size("seq") // SPANS
    peers = [[lo + SPANS * k for k in range(repeats)] for lo in range(SPANS)]
    narrow = width // (SPANS * repeats)

    def wide_in(w, axis):
        if repeats == 1:
            return w
        return lax.all_gather(w, "seq", axis_index_groups=peers, axis=axis, tiled=True)

    def narrow_out(g, axis):
        if repeats == 1:
            return g
        return lax.psum_scatter(
            g, "seq", scatter_dimension=axis, axis_index_groups=peers, tiled=True
        )

    def features_in(a):
        if repeats == 1:
            return a
        return a.reshape(a.shape[:-1] + (repeats, SPANS, narrow)).swapaxes(-3, -2).reshape(a.shape)

    def features_out(a):
        if repeats == 1:
            return a
        return a.reshape(a.shape[:-1] + (SPANS, repeats, narrow)).swapaxes(-3, -2).reshape(a.shape)

    spot = lax.axis_index("seq") % SPANS
    z, p = spot // PLANE, spot % PLANE
    group_rows = span_rows * PLANE
    blocks = group_rows // STRETCH

    tokens, cotangent, w_down = features_in(tokens), features_in(cotangent), features_in(w_down)
    w_up = features_in(w_up.T).T if repeats > 1 else w_up
    ln1_gain, ln1_bias = features_in(ln1_gain), features_in(ln1_bias)
    ln2_gain, ln2_bias = features_in(ln2_gain), features_in(ln2_bias)
    decays = decay_log.T
    (
        normed, q_rot, k_rot, value, gate_proj, retained, gated_low, prev_states,
        cosine, sine_part, ccol, crow, scalars, key_w, value_w, query_w, gate_w, out_w,
    ) = attention(
        tokens,
        ln1_gain,
        ln1_bias,
        decays,
        angle_tables(64, w_key.shape[1] // heads // 2),
        [
            wide_in(w_key, 0),
            wide_in(w_value, 0),
            wide_in(w_query, 0),
            wide_in(w_gate, 0),
            wide_in(w_out, 1),
        ],
        (False, False, False, False, True),
        0,
    )
    block_out, grad_resid, gains_second, grad_attn, grad_up, grad_down = ffn_part(
        gated_low,
        out_w,
        tokens,
        ln2_gain,
        ln2_bias,
        w_up,
        w_down,
        cotangent,
        2,
    )
    grad_heads, sums_first, gate_sum, ffn_first, grad_value_w, grad_qk_w = retention_back(
        grad_attn,
        out_w,
        gated_low,
        gate_proj,
        retained,
        q_rot,
        k_rot,
        value,
        prev_states,
        cosine,
        sine_part,
        ccol,
        crow,
        scalars,
        normed,
        grad_up,
        grad_down,
        7,
    )
    grad_tokens, gains, ffn_sum, sums_last = last_sums(
        grad_heads,
        grad_value_w,
        grad_qk_w,
        query_w,
        key_w,
        value_w,
        gate_w,
        ffn_first,
        grad_up,
        grad_down,
        gate_sum,
        tokens,
        ln1_gain,
        grad_resid,
        gains_second,
        8,
    )
    if repeats > 1:
        gains = lax.psum(gains, "seq", axis_index_groups=peers)

    *sums, block_out, grad_tokens, gain_one, bias_one, gain_two, bias_two = outputs(
        sums_last, sums_first, ffn_sum, block_out, grad_tokens, gains, key_w.shape[1]
    )
    gain_one, bias_one, gain_two, bias_two = map(features_out, (gain_one, bias_one, gain_two, bias_two))
    sum_query, sum_key, sum_value, sum_gate, sum_out, sum_up, sum_down = (
        narrow_out(g, axis) for g, axis in zip(sums, (0, 0, 0, 0, 1, 0, 1))
    )
    return (
        features_out(block_out),
        features_out(grad_tokens),
        gain_one,
        bias_one,
        sum_query,
        sum_key,
        sum_value,
        sum_gate,
        sum_out,
        gain_two,
        bias_two,
        sum_up,
        sum_down,
    )


def solution(mesh):
    return jax.shard_map(
        shards,
        mesh=mesh,
        in_specs=(
            P(("seq", "ffn"), None),
            P(),
            P(),
            P("seq", "ffn"),
            P("seq", "ffn"),
            P("seq", "ffn"),
            P("seq", "ffn"),
            P("ffn", "seq"),
            P("seq", "ffn"),
            P(),
            P(),
            P(None, "ffn"),
            P("ffn", None),
            P("seq", None),
        ),
        out_specs=(
            P(("seq", "ffn"), None),
            P(("seq", "ffn"), None),
            P(),
            P(),
            P("seq", "ffn"),
            P("seq", "ffn"),
            P("seq", "ffn"),
            P("seq", "ffn"),
            P("ffn", "seq"),
            P(),
            P(),
            P("seq", "ffn"),
            P("ffn", "seq"),
        ),
        check_vma=False,
    )
```

```python
import functools

import jax
import jax.numpy as jnp
import numpy as np
from jax import lax
from jax.experimental import pallas as pl
from jax.experimental.pallas import tpu as pltpu
from jax.sharding import PartitionSpec as P

STRETCH = 512
SEQUENCE_LENGTH = 8192
PLANE = 4
LINE = 4
SPANS = PLANE * LINE
MESH = pl.DeviceIdType.MESH
VMEM_LIMIT = 63 * 1024 * 1024
ANY = pl.BlockSpec(memory_space=pl.ANY)
VM = pl.BlockSpec(memory_space=pltpu.VMEM)
BF16 = jnp.bfloat16
F32 = jnp.float32


class Place:
    def __init__(self):
        s = lax.axis_index("seq")
        self.f = lax.axis_index("ffn")
        lo = s % SPANS
        self.base = s - lo
        self.z = lo // PLANE
        self.p = lo % PLANE

    def plane(self, m):
        return self.at(self.z, self.xor(m), self.f)

    def xor(self, m):
        p = self.p
        low, high = p % 2, p // 2
        if m & 1:
            low = 1 - low
        if m & 2:
            high = 1 - high
        return high * 2 + low

    def at(self, z, p, f):
        return (self.base + z * PLANE + p, f)

    def partner(self):
        return self.at(self.z, self.p, 1 - self.f)

    def up(self):
        return self.at(self.z + 1, self.p, self.f)

    def down(self):
        return self.at(self.z - 1, self.p, self.f)


def greet(peers):
    meet(call(peers))


def meet(count):
    pl.semaphore_wait(pltpu.get_barrier_semaphore(), count)


def call(peers):
    bar = pltpu.get_barrier_semaphore()
    count = 0
    for device, cond in peers:
        if cond is None:
            pl.semaphore_signal(bar, inc=1, device_id=device, device_id_type=MESH)
            count = count + 1
        else:

            @pl.when(cond)
            def _():
                pl.semaphore_signal(bar, inc=1, device_id=device, device_id_type=MESH)

            count = count + cond.astype(jnp.int32)
    return count


def remote(src, dst, send, recv, device):
    return pltpu.make_async_remote_copy(
        src_ref=src, dst_ref=dst, send_sem=send, recv_sem=recv, device_id=device, device_id_type=MESH
    )


def comm_call(kernel, outs, ins, scratch, cid, in_specs=None, out_specs=None):
    return pl.pallas_call(
        kernel,
        out_shape=outs,
        in_specs=in_specs if in_specs is not None else [ANY] * len(ins),
        out_specs=out_specs if out_specs is not None else [ANY] * len(outs),
        scratch_shapes=scratch,
        compiler_params=pltpu.CompilerParams(
            collective_id=cid, has_side_effects=True, vmem_limit_bytes=VMEM_LIMIT
        ),
    )(*ins)


DMA = pltpu.SemaphoreType.DMA


def nn(a, b):
    return jnp.dot(a, b, preferred_element_type=F32)


def nt(a, b):
    return lax.dot_general(a, b, (((1,), (1,)), ((), ())), preferred_element_type=F32)


def tn(a, b):
    return lax.dot_general(a, b, (((0,), (0,)), ((), ())), preferred_element_type=F32)


def rows_at(r, size):
    return pl.ds(pl.multiple_of(r, size), size)


def add_into(dst, cols, other, other_cols):
    @pl.loop(0, dst.shape[0], step=64)
    def _(r):
        at = rows_at(r, 64)
        dst[at, cols] = (dst[at, cols].astype(F32) + other[at, other_cols].astype(F32)).astype(BF16)


def start(copy):
    copy.start()
    return copy


def ffn_kernel(
    gated_ref, wo_ref, tok_ref, gain_ref, bias_ref, wu_ref, wd_ref, cot_ref,
    block_out, resid_out, gains, da, fu, fd,
    tok, resid_grad, share, wu, wd, rx0, rx1a, rx1b, rx2a, rx2b, resid, xn, act, dact, du, cot, dab, stage, tmp,
    lsem, gload, csend, crecv, xsend, xrecv, psend, precv, gsend, grecv, ksend, krecv, ssem, osem,
):
    me = Place()
    p, f = me.p, me.f
    greeted = call([(me.plane(1), None), (me.plane(2), None), (me.partner(), None)])
    rows, width = tok_ref.shape
    hidden = wu.shape[1]
    q = [me.xor(m) for m in range(4)]
    wide = width // 2
    hr = rows // 2
    span = 2 * rows
    ca, cb = pl.ds(0, wide), pl.ds(wide, wide)
    everything, whole = pl.ds(0, width), pl.ds(0, wide)
    own_half = [pl.ds(h * hr, hr) for h in range(2)]
    mine = [rows_at(h * rows + f * hr, hr) for h in range(2)]
    theirs = [rows_at(h * rows + (1 - f) * hr, hr) for h in range(2)]
    both = [pl.ds(h * rows, rows) for h in range(2)]

    order = (3, 1, 2, 0)
    part_width = gated_ref.shape[1]
    def out_slab(i):
        at = rows_at(i * 512, 512)
        return pltpu.make_async_copy(wo_ref.at[:, at], act.at[:, at], osem.at[i])

    slabs = width // 512
    out_slab(0).start()
    load_t = pltpu.make_async_copy(tok_ref, tok, lsem.at[7])
    load_g = {
        m: start(
            pltpu.make_async_copy(
                gated_ref.at[rows_at(q[m] * span, span), :],
                xn.at[:, m * part_width : (m + 1) * part_width],
                gload.at[m],
            )
        )
        for m in order
    }
    for i in range(1, slabs):
        out_slab(i).start()
    load_t.start()
    load_d = start(pltpu.make_async_copy(wd_ref, wd, lsem.at[1]))
    load_c = [
        start(
            pltpu.make_async_copy(
                cot_ref.at[pl.ds(c * rows + h * hr, hr), :], cot.at[pl.ds(h * rows + c * hr, hr), :], lsem.at[3 + 2 * h + c]
            )
        )
        for h in range(2)
        for c in range(2)
    ]
    load_u = start(pltpu.make_async_copy(wu_ref, wu, lsem.at[2]))
    first, sends = {}, {}

    def to_partner(m, h):
        first[m, h] = start(
            remote(
                share.at[m, rows_at((1 - f) * rows + h * hr, hr)], rx0.at[m, own_half[h]],
                csend.at[m, h], crecv.at[m, h], me.partner(),
            )
        )

    for m in order:
        load_g[m].wait()

        @pl.loop(0, slabs)
        def _(i):
            if m == order[0]:
                out_slab(i).wait()
            at = rows_at(i * 512, 512)
            share[m, :, at] = nn(xn[:, m * part_width : (m + 1) * part_width], act[:, at]).astype(BF16)

        if m == order[0]:
            meet(greeted)
        to_partner(m, 0)
    for m in order:
        to_partner(m, 1)

    def pass_on(m, h):
        first[m, h].wait_recv()
        at = own_half[h]
        add_into(rx0.at[m, at], everything, share.at[m, rows_at(f * rows + h * hr, hr)], everything)
        k = 0 if m == 3 else 1
        if m & 1:
            sends["a", k, h] = start(
                remote(rx0.at[m, at, ca], rx1a.at[k, at], xsend.at[k, h], xrecv.at[k, h], me.plane(1))
            )
        if m & 2:
            sends["b", k, h] = start(
                remote(rx0.at[m, at, cb], rx1b.at[k, at], xsend.at[2 + k, h], xrecv.at[2 + k, h], me.plane(2))
            )

    def second(h):
        at = own_half[h]
        sends["a", 0, h].wait_recv()
        add_into(rx1a.at[0, at], whole, rx0.at[2, at], ca)
        sends["a", 2, h] = start(
            remote(rx1a.at[0, at], rx2a.at[at], xsend.at[4, h], xrecv.at[4, h], me.plane(2))
        )
        sends["b", 0, h].wait_recv()
        add_into(rx1b.at[0, at], whole, rx0.at[1, at], cb)
        sends["b", 2, h] = start(
            remote(rx1b.at[0, at], rx2b.at[at], xsend.at[5, h], xrecv.at[5, h], me.plane(1))
        )

    for m in order:
        pass_on(m, 0)

    load_d.wait()
    for c in load_c:
        c.wait()

    @pl.loop(0, hidden, step=256)
    def _(c):
        at = rows_at(c, 256)
        dact[:, at] = nt(cot[...], wd[at, :])

    second(0)
    for m in order:
        pass_on(m, 1)
    load_u.wait()
    step = 32

    def norm(h):
        for key in (("a", 1, h), ("b", 1, h), ("a", 2, h), ("b", 2, h)):
            sends[key].wait_recv()

        @pl.loop(0, hr, step=step)
        def _(r):
            at = pl.ds(pl.multiple_of(h * hr + r, step), step)
            left = rx0[0, at, ca].astype(F32) + rx1a[1, at, :].astype(F32) + rx2a[at, :].astype(F32)
            right = rx0[0, at, cb].astype(F32) + rx1b[1, at, :].astype(F32) + rx2b[at, :].astype(F32)
            v = tok[at, :].astype(F32) + jnp.concatenate([left, right], axis=1)
            resid[at, :] = v
            centered = v - jnp.mean(v, axis=1, keepdims=True)
            scale = lax.rsqrt(jnp.mean(centered * centered, axis=1, keepdims=True) + 1e-05)
            xn[pl.ds(pl.multiple_of(h * rows + f * hr + r, step), step), :] = (
                centered * scale * gain_ref[...] + bias_ref[...]
            ).astype(BF16)

        return start(remote(xn.at[mine[h]], xn.at[mine[h]], psend.at[0, h], precv.at[0, h], me.partner()))

    def hidden_part(h):
        @pl.loop(0, hidden, step=512)
        def _(c):
            at = rows_at(c, 512)
            u = nn(xn[both[h], :], wu[:, at])
            e = 0.5 * (1.0 + lax.erf(u * 0.7071067811865476))
            act[both[h], at] = (u * e).astype(BF16)
            slope = e + u * jnp.exp(-0.5 * u * u) * 0.3989422804014327
            du[both[h], at] = (dact[both[h], at] * slope).astype(BF16)

    def back_part(h):
        @pl.loop(0, width, step=512)
        def _(c):
            at = rows_at(c, 512)
            tmp[...] = nt(du[both[h], :], wu[at, :])
            resid_grad[own_half[h], at] = tmp[rows_at(f * hr, hr), :]
            share[0, own_half[h], at] = tmp[rows_at((1 - f) * hr, hr), :].astype(BF16)

        return start(
            remote(share.at[0, own_half[h]], share.at[1, own_half[h]], psend.at[1, h], precv.at[1, h], me.partner())
        )

    def norm_back(h):
        @pl.loop(0, hr, step=step)
        def _(r):
            at = pl.ds(pl.multiple_of(h * hr + r, step), step)
            dx = resid_grad[at, :] + share[1, at, :].astype(F32)
            v = resid[at, :]
            centered = v - jnp.mean(v, axis=1, keepdims=True)
            scale = lax.rsqrt(jnp.mean(centered * centered, axis=1, keepdims=True) + 1e-05)
            hat = centered * scale
            gains[0:1, :] += jnp.sum(dx * hat, axis=0, keepdims=True)
            gains[1:2, :] += jnp.sum(dx, axis=0, keepdims=True)
            g = dx * gain_ref[...]
            back = scale * (
                g - jnp.mean(g, axis=1, keepdims=True) - hat * jnp.mean(g * hat, axis=1, keepdims=True)
            )
            back = back + cot[pl.ds(pl.multiple_of(h * rows + f * hr + r, step), step), :].astype(F32)
            resid_grad[at, :] = back
            dab[at, :] = back.astype(BF16)

    def out_part(h):
        @pl.loop(0, width, step=512)
        def _(c):
            at = rows_at(c, 512)
            tmp[...] = nn(act[both[h], :], wd[:, at])
            dact[pl.ds(h * rows, hr), at] = tmp[rows_at(f * hr, hr), :]
            share[2, own_half[h], at] = tmp[rows_at((1 - f) * hr, hr), :].astype(BF16)

        return start(
            remote(share.at[2, own_half[h]], share.at[3, own_half[h]], psend.at[2, h], precv.at[2, h], me.partner())
        )

    quarter = hr // 2

    def seat(m, h, k=None):
        base = (q[m] * 2 + f) * rows + h * hr
        if k is None:
            return da.at[pl.ds(pl.multiple_of(base, hr), hr), :]
        return da.at[pl.ds(pl.multiple_of(base + k * quarter, quarter), quarter), :]

    spread = {}

    def spread_begin(h):
        spread["own", h] = start(pltpu.make_async_copy(dab.at[own_half[h]], seat(0, h), gload.at[h]))
        for i in range(2):
            for to, k in ((1, i), (2, 1 - i)):
                sem = (to - 1) * 2 + i
                spread[to, i, h] = start(
                    remote(
                        dab.at[pl.ds(h * hr + k * quarter, quarter)], seat(0, h, k),
                        gsend.at[sem, h], grecv.at[sem, h], me.plane(to),
                    )
                )
        spread["core", 0, h] = start(
            remote(dab.at[own_half[h]], seat(0, h), ksend.at[0, h], krecv.at[0, h], me.partner())
        )

    def spread_on(h):
        spread[1, 0, h].wait_recv()
        spread["g1", h] = start(
            remote(seat(1, h, 0), seat(1, h, 0), gsend.at[4, h], grecv.at[4, h], me.plane(2))
        )
        spread[2, 0, h].wait_recv()
        spread["g2", h] = start(
            remote(seat(2, h, 1), seat(2, h, 1), gsend.at[5, h], grecv.at[5, h], me.plane(1))
        )

    def spread_end(h):
        for m in (1, 2):
            spread[m, 1, h].wait_recv()
            spread["core", m, h] = start(
                remote(seat(m, h), seat(m, h), ksend.at[m, h], krecv.at[m, h], me.partner())
            )
        spread["g1", h].wait_recv()
        spread["g2", h].wait_recv()
        spread["core", 3, h] = start(
            remote(seat(3, h), seat(3, h), ksend.at[3, h], krecv.at[3, h], me.partner())
        )

    gains[...] = jnp.zeros_like(gains)
    for c in first.values():
        c.wait_send()
    load_t.wait()
    swaps = [norm(0)]
    swaps[0].wait_recv()
    hidden_part(0)
    second(1)
    swaps.append(back_part(0))
    out_swaps = [out_part(0)]
    swaps[1].wait_recv()
    norm_back(0)
    spread_begin(0)
    swaps.append(norm(1))
    swaps[2].wait_recv()
    hidden_part(1)
    spread_on(0)
    swaps.append(back_part(1))
    out_swaps.append(out_part(1))
    swaps[3].wait_recv()
    norm_back(1)
    spread_begin(1)
    resid_copy = start(pltpu.make_async_copy(resid_grad, resid_out, lsem.at[0]))

    def weights_part(left, right, out):
        def spill(slot, i):
            return pltpu.make_async_copy(stage.at[slot], out.at[rows_at(i * 256, 256), :], ssem.at[slot])

        @pl.loop(0, width // 256)
        def _(i):
            slot = i % 3

            @pl.when(i >= 3)
            def _():
                spill(slot, i - 3).wait()

            stage[slot] = tn(left[:, rows_at(i * 256, 256)], right[...]).astype(BF16)
            spill(slot, i).start()

        for k in (3, 2, 1):
            i = width // 256 - k
            spill(i % 3, i).wait()

    weights_part(cot, act, fd)
    spread_on(1)
    spread_end(0)
    for h in range(2):
        out_swaps[h].wait_recv()

        @pl.loop(0, hr, step=step)
        def _(r):
            at = pl.ds(pl.multiple_of(h * hr + r, step), step)
            own = dact[pl.ds(pl.multiple_of(h * rows + r, step), step), :]
            tok[at, :] = (resid[at, :] + own + share[3, at, :].astype(F32)).astype(BF16)

    out_copy = start(pltpu.make_async_copy(tok, block_out, lsem.at[1]))
    weights_part(xn, du, fu)
    spread_end(1)
    resid_copy.wait()
    out_copy.wait()
    for h in range(2):
        spread["own", h].wait()
        for m in range(4):
            spread["core", m, h].wait()
        for key in ((1, 0, h), (1, 1, h), (2, 0, h), (2, 1, h), ("g1", h), ("g2", h)):
            spread[key].wait_send()
    for c in swaps + out_swaps + list(sends.values()):
        c.wait_send()


def ffn_part(gated, w_out, tokens, gain, bias, w_up, w_down, cotangent, cid):
    rows, width = tokens.shape
    assert PLANE * gated.shape[1] == width and w_out.shape == (2 * rows, w_up.shape[1])
    span, hidden = 2 * rows, w_up.shape[1]
    sd = jax.ShapeDtypeStruct
    return comm_call(
        ffn_kernel,
        [
            sd((rows, width), BF16),
            sd((rows, width), F32),
            sd((8, width), F32),
            sd((2 * PLANE * rows, width), BF16),
            sd((width, hidden), BF16),
            sd((width, hidden), BF16),
        ],
        [gated, w_out, tokens, gain[None], bias[None], w_up, w_down, cotangent],
        [
            pltpu.VMEM((rows, width), BF16),
            pltpu.VMEM((rows, width), F32),
            pltpu.VMEM((PLANE, span, width), BF16),
            pltpu.VMEM(w_up.shape, BF16),
            pltpu.VMEM(w_down.shape, BF16),
            pltpu.VMEM((PLANE, rows, width), BF16),
            pltpu.VMEM((2, rows, width // 2), BF16),
            pltpu.VMEM((2, rows, width // 2), BF16),
            pltpu.VMEM((rows, width // 2), BF16),
            pltpu.VMEM((rows, width // 2), BF16),
            pltpu.VMEM((rows, width), F32),
            pltpu.VMEM((span, width), BF16),
            pltpu.VMEM((span, hidden), BF16),
            pltpu.VMEM((span, hidden), F32),
            pltpu.VMEM((span, hidden), BF16),
            pltpu.VMEM((span, width), BF16),
            pltpu.VMEM((rows, width), BF16),
            pltpu.VMEM((3, 256, hidden), BF16),
            pltpu.VMEM((rows, 512), F32),
            DMA((8,)),
            DMA((PLANE,)),
            DMA((PLANE, 2)),
            DMA((PLANE, 2)),
            DMA((6, 2)),
            DMA((6, 2)),
            DMA((3, 2)),
            DMA((3, 2)),
            DMA((6, 2)),
            DMA((6, 2)),
            DMA((4, 2)),
            DMA((4, 2)),
            DMA((3,)),
            DMA((width // 512,)),
        ],
        cid,
        in_specs=[ANY, ANY, ANY, VM, VM, ANY, ANY, ANY],
        out_specs=[ANY, ANY, VM, ANY, ANY, ANY],
    )


def attention_kernel(
    widths, by_rows,
    tok_ref, gain_ref, bias_ref, dec_ref, cbase, sbase, coff, soff, *refs,
):
    count = len(widths)
    shards_in, refs = refs[:count], refs[count:]
    (xg, q_out, k_out, v_out, gate_out, ret_out, gated_out, states_out, cos_out, sin_out, ccol_out, crow_out, scal_out), refs = (
        refs[:13], refs[13:],
    )
    full, refs = refs[:count], refs[count:]
    hold, refs = refs[:count], refs[count:]
    wl, refs = refs[: count - 1], refs[count - 1 :]
    (tok, ccol, crow, scal, xn, xv, q, k, v, gate, ret, gated, cos, sin, kv, st, sloc, sgot, decg,
     lsem, psend, precv, usend, dsend, zrecv, xsend, xrecv, csend, crecv, tsend, trecv, ssend, srecv, osem, wsem) = refs
    me = Place()
    z, p, f = me.z, me.p, me.f
    spot = z * PLANE + p
    chunk = hold[0].shape[0]
    deep = chunk * PLANE
    tokens, width = xv.shape
    rows = tok_ref.shape[0]
    keys, values = q.shape[1], v.shape[1]
    half = keys // 2
    blocks = tokens // STRETCH
    greet(
        [(me.plane(m), None) for m in (1, 2, 3)]
        + [(me.partner(), None), (me.up(), z < LINE - 1), (me.down(), z > 0)]
    )

    def part(i, at):
        w = widths[i]
        if by_rows[i]:
            return shards_in[i].at[pl.ds(pl.multiple_of(at * w, w), w), :]
        return shards_in[i].at[:, pl.ds(pl.multiple_of(at * w, w), w)]

    def slot(i, ss):
        at = pl.ds(pl.multiple_of(ss * chunk, chunk), chunk)
        return full[i].at[:, at] if by_rows[i] else full[i].at[at, :]

    def block(i, zz):
        at = pl.ds(pl.multiple_of(zz * deep, deep), deep)
        return full[i].at[:, at] if by_rows[i] else full[i].at[at, :]

    def up_copy(i, zz):
        return remote(block(i, zz), block(i, zz), usend.at[i, zz], zrecv.at[i, zz], me.up())

    def down_copy(i, zz):
        return remote(block(i, zz), block(i, zz), dsend.at[i, zz], zrecv.at[i, zz], me.down())

    def part_copies(i, src, at):
        return (
            remote(src, slot(i, at), usend.at[i, z], zrecv.at[i, z], me.up()),
            remote(src, slot(i, at), dsend.at[i, z], zrecv.at[i, z], me.down()),
        )

    def to_line(copies):
        @pl.when(z < LINE - 1)
        def _():
            copies[0].start()

        @pl.when(z > 0)
        def _():
            copies[1].start()

    ahead = 2
    load_t = start(pltpu.make_async_copy(tok_ref, tok, lsem.at[count + 1]))
    local, plane, held = [], [], []
    for i in range(count):
        held.append(start(pltpu.make_async_copy(part(i, p), hold[i], lsem.at[i])))
        local.append(pltpu.make_async_copy(hold[i], slot(i, spot), lsem.at[i]))
        plane.append(
            [
                start(remote(part(i, me.xor(m)), slot(i, spot), psend.at[i, m], precv.at[i, m], me.plane(m)))
                for m in (1, 2, 3)
            ]
        )
    for i in range(ahead):
        to_line(part_copies(i, part(i, p), spot))
    tiny = [start(remote(dec_ref, decg.at[p], tsend.at[m], trecv.at[m], me.plane(m))) for m in (1, 2, 3)]
    tiny_own = start(pltpu.make_async_copy(dec_ref, decg.at[p], tsend.at[0]))
    step = 32
    load_t.wait()

    @pl.loop(0, rows, step=step)
    def _(r):
        at = rows_at(r, step)
        t = tok[at, :].astype(F32)
        centered = t - jnp.mean(t, axis=1, keepdims=True)
        scale = lax.rsqrt(jnp.mean(centered * centered, axis=1, keepdims=True) + 1e-05)
        xn[at, :] = (centered * scale * gain_ref[...] + bias_ref[...]).astype(BF16)

    def seat(m, h=None):
        base = (me.xor(m) * 2 + f) * rows
        if h is None:
            return xv.at[rows_at(base, rows)]
        return xv.at[pl.ds(pl.multiple_of(base + h * (rows // 2), rows // 2), rows // 2)]

    x_own = start(pltpu.make_async_copy(xn, seat(0), lsem.at[count]))
    x1 = start(remote(xn, seat(0), xsend.at[0], xrecv.at[0], me.plane(1)))
    x2 = start(remote(xn, seat(0), xsend.at[1], xrecv.at[1], me.plane(2)))
    xc = start(remote(xn, seat(0), csend.at[0], crecv.at[0], me.partner()))
    for i in range(count):
        held[i].wait()
        local[i].start()

    def own(i):
        local[i].wait()
        for c in plane[i]:
            c.wait_recv()
        if i < ahead:
            for m in (1, 2, 3):
                at = z * PLANE + me.xor(m)
                to_line(part_copies(i, slot(i, at), at))
        else:
            to_line((up_copy(i, z), down_copy(i, z)))

    def forward(i, t):
        @pl.when(z - t >= 0)
        def _():
            up_copy(i, z - t).wait_recv()

            @pl.when(z < LINE - 1)
            def _():
                up_copy(i, z - t).start()

        @pl.when(z + t < LINE)
        def _():
            down_copy(i, z + t).wait_recv()

            @pl.when(z > 0)
            def _():
                down_copy(i, z + t).start()

    def fetch(i):
        forward(i, LINE - 1)
        return start(pltpu.make_async_copy(full[i], wl[i], wsem.at[i]))

    K, V, Q, G, O = range(count)
    own(K)
    own(V)
    forward(K, 1)
    forward(K, 2)
    own(Q)

    for c in tiny:
        c.wait()
    tiny_own.wait()
    heads = lax.broadcasted_iota(jnp.int32, decg.shape[1:], 0)
    lines = [jnp.sum(jnp.where(heads == p, decg[j], 0.0), axis=0, keepdims=True) for j in range(blocks)]
    lines = jnp.concatenate(lines + [jnp.zeros_like(lines[0])] * (8 - blocks), axis=0)
    i0 = lax.broadcasted_iota(jnp.int32, (STRETCH, STRETCH), 0)
    i1 = lax.broadcasted_iota(jnp.int32, (STRETCH, STRETCH), 1)
    row_sums = jnp.dot(
        lines, jnp.where(i0 <= i1, 1.0, 0.0), preferred_element_type=F32, precision=lax.Precision.HIGHEST
    )
    col_sums = lax.dot_general(
        jnp.where(i1 <= i0, 1.0, 0.0), lines, (((1,), (1,)), ((), ())),
        preferred_element_type=F32, precision=lax.Precision.HIGHEST,
    )
    total = jnp.zeros((1, 1), F32)
    for c in range(blocks):
        end = row_sums[c : c + 1, STRETCH - 1 : STRETCH]
        crow[c] = jnp.broadcast_to(row_sums[c : c + 1, :], (8, STRETCH))
        ccol[c * STRETCH : (c + 1) * STRETCH, :] = col_sums[:, c : c + 1]
        scal[c] = jnp.broadcast_to(jnp.exp(end), (8, 128))
        scal[blocks + c] = jnp.broadcast_to(jnp.exp(total), (8, 128))
        total = total + end
    scal[2 * blocks] = jnp.broadcast_to(total, (8, 128))

    fine = coff.shape[0]

    @pl.loop(0, tokens // fine)
    def _(a):
        at = rows_at(a * fine, fine)
        place = pl.ds(z * (tokens // fine) + a, 1)
        ca, sa = cbase[place, :], sbase[place, :]
        cos[at, :] = ca * coff[...] - sa * soff[...]
        sin[at, :] = sa * coff[...] + ca * soff[...]

    forward(V, 1)
    x1.wait_recv()
    g1 = start(remote(seat(1, 0), seat(1, 0), xsend.at[2], xrecv.at[2], me.plane(2)))
    c1 = start(remote(seat(1), seat(1), csend.at[1], crecv.at[1], me.partner()))
    x2.wait_recv()
    g2 = start(remote(seat(2, 1), seat(2, 1), xsend.at[3], xrecv.at[3], me.plane(1)))
    c2 = start(remote(seat(2), seat(2), csend.at[2], crecv.at[2], me.partner()))
    forward(V, 2)
    forward(Q, 1)
    own(G)
    forward(Q, 2)
    own(O)
    load_k = fetch(K)
    g1.wait_recv()
    g2.wait_recv()
    c3 = start(remote(seat(3), seat(3), csend.at[3], crecv.at[3], me.partner()))
    x_own.wait()
    for c in (xc, c1, c2, c3):
        c.wait_recv()
    outs = []

    def put(src, dst):
        outs.append(start(pltpu.make_async_copy(src, dst, osem.at[len(outs)])))

    put(xv, xg)
    put(ccol, ccol_out)
    put(crow, crow_out)
    put(scal, scal_out)
    put(cos, cos_out)
    put(sin, sin_out)
    load_k.wait()

    def turned(at, w, dst):
        y = nn(xv[at, :], w[...])
        a, b = y[:, :half], y[:, half:]
        dst[at, :half] = (a * cos[at, :] - b * sin[at, :]).astype(BF16)
        dst[at, half:] = (b * cos[at, :] + a * sin[at, :]).astype(BF16)

    @pl.loop(0, blocks)
    def _(c):
        turned(rows_at(c * STRETCH, STRETCH), wl[K], k)

    fetch(V).wait()

    @pl.loop(0, blocks)
    def _(c):
        at = rows_at(c * STRETCH, STRETCH)
        val = nn(xv[at, :], wl[V][...]).astype(BF16)
        v[at, :] = val
        end = crow[c, 0:1, STRETCH - 1 : STRETCH]
        kv[c] = tn(k[at, :], (val.astype(F32) * jnp.exp(end - ccol[at, :])).astype(BF16))

    put(k, k_out)
    put(v, v_out)
    sloc[...] = kv[0]
    kv[0] = jnp.zeros_like(sloc)
    for c in range(1, blocks):
        nxt = sloc[...] * scal[c, 0:1, 0:1] + kv[c]
        kv[c] = sloc[...]
        sloc[...] = nxt

    def state_copy(zz):
        return remote(st.at[0], sgot, ssend.at[zz], srecv.at[zz], me.up())

    def send_state():
        st[0] = sloc[...].astype(BF16)
        state_copy(0).start()

    @pl.when(z == 0)
    def _():
        send_state()

    def pass_state(zz):
        @pl.when(z == zz)
        def _():
            state_copy(0).wait_recv()
            if zz < LINE - 1:
                sloc[...] = sloc[...] + sgot[...].astype(F32) * jnp.exp(scal[2 * blocks, 0:1, 0:1])
                send_state()

    pass_state(1)
    forward(G, 1)
    forward(O, 1)
    fetch(Q).wait()
    t_size = 256

    @pl.loop(0, blocks)
    def _(c):
        blk = rows_at(c * STRETCH, STRETCH)
        turned(blk, wl[Q], q)
        row = crow[c, 0:1, :]
        for r in range(0, STRETCH, t_size):
            at = rows_at(c * STRETCH + r, t_size)
            col = ccol[at, :]
            t_index = lax.broadcasted_iota(jnp.int32, (t_size, STRETCH), 0) + r
            s_index = lax.broadcasted_iota(jnp.int32, (t_size, STRETCH), 1)
            mask = jnp.where(t_index >= s_index, jnp.exp(jnp.minimum(col - row, 0.0)), 0.0)
            scores = (nt(q[at, :], k[blk, :]) * mask).astype(BF16)
            ret[at, :] = nn(scores, v[blk, :])

    put(q, q_out)
    pass_state(2)
    forward(G, 2)
    forward(O, 2)
    pass_state(3)

    @pl.when((z > 0) & (z < LINE - 1))
    def _():
        state_copy(0).wait_send()

    @pl.when(z == 0)
    def _():
        state_copy(0).wait_send()
        sgot[...] = jnp.zeros_like(sgot)

    for c in range(blocks):
        st[c] = (kv[c] + sgot[...].astype(F32) * scal[blocks + c, 0:1, 0:1]).astype(BF16)

    @pl.loop(0, blocks)
    def _(c):
        at = rows_at(c * STRETCH, STRETCH)
        decayed = (q[at, :].astype(F32) * jnp.exp(ccol[at, :])).astype(BF16)
        ret[at, :] += nn(decayed, st[c])

    put(ret, ret_out)
    put(st, states_out)
    fetch(G).wait()

    @pl.loop(0, tokens, step=256)
    def _(r):
        at = rows_at(r, 256)
        g = nn(xv[at, :], wl[G][...])
        gate[at, :] = g
        t = ret[at, :]
        centered = t - jnp.mean(t, axis=1, keepdims=True)
        scale = lax.rsqrt(jnp.mean(centered * centered, axis=1, keepdims=True) + 1e-05)
        gated[at, :] = (g / (1.0 + jnp.exp(-g)) * centered * scale).astype(BF16)

    put(gate, gate_out)
    put(gated, gated_out)
    forward(O, LINE - 1)
    for c in (xc, c1, c2, c3, x1, x2, g1, g2):
        c.wait_send()
    for i in range(count):
        for c in plane[i]:
            c.wait_send()
        for zz in range(LINE):

            @pl.when((z < LINE - 1) & (zz <= z))
            def _():
                up_copy(i, zz).wait_send()

            @pl.when((z > 0) & (zz >= z))
            def _():
                down_copy(i, zz).wait_send()

    for c in outs:
        c.wait()


def attention(tokens, gain, bias, decays, tables, shards_in, by_rows, cid):
    rows, width = tokens.shape
    count = len(shards_in)
    chunk = shards_in[0].shape[0]
    group = 2 * PLANE * rows
    blocks = group // STRETCH
    parts = [
        (w.shape[0] // PLANE, chunk) if r else (chunk, w.shape[1] // PLANE) for w, r in zip(shards_in, by_rows)
    ]
    widths = [s[0] if r else s[1] for s, r in zip(parts, by_rows)]
    wholes = [(s[0], width) if r else (width, s[1]) for s, r in zip(parts, by_rows)]
    values, keys = widths[1], widths[0]
    half = keys // 2
    sd = jax.ShapeDtypeStruct
    outs = [
        sd((group, width), BF16),
        sd((group, keys), BF16),
        sd((group, keys), BF16),
        sd((group, values), BF16),
        sd((group, values), F32),
        sd((group, values), F32),
        sd((group, values), BF16),
        sd((blocks, keys, values), BF16),
        sd((group, half), F32),
        sd((group, half), F32),
        sd((group, 1), F32),
        sd((blocks, 8, STRETCH), F32),
        sd((2 * blocks + 1, 8, 128), F32),
    ] + [sd(s, BF16) for s in wholes]
    scratch = (
        [pltpu.VMEM(s, BF16) for s in parts]
        + [pltpu.VMEM(s, BF16) for s in wholes[:-1]]
        + [
            pltpu.VMEM((rows, width), BF16),
            pltpu.VMEM((group, 1), F32),
            pltpu.VMEM((blocks, 8, STRETCH), F32),
            pltpu.VMEM((2 * blocks + 1, 8, 128), F32),
            pltpu.VMEM((rows, width), BF16),
            pltpu.VMEM((group, width), BF16),
            pltpu.VMEM((group, keys), BF16),
            pltpu.VMEM((group, keys), BF16),
            pltpu.VMEM((group, values), BF16),
            pltpu.VMEM((group, values), F32),
            pltpu.VMEM((group, values), F32),
            pltpu.VMEM((group, values), BF16),
            pltpu.VMEM((group, half), F32),
            pltpu.VMEM((group, half), F32),
            pltpu.VMEM((blocks, keys, values), F32),
            pltpu.VMEM((blocks, keys, values), BF16),
            pltpu.VMEM((keys, values), F32),
            pltpu.VMEM((keys, values), BF16),
            pltpu.VMEM((PLANE,) + decays.shape, F32),
            DMA((count + 2,)),
            DMA((count, PLANE)),
            DMA((count, PLANE)),
            DMA((count, LINE)),
            DMA((count, LINE)),
            DMA((count, LINE)),
            DMA((4,)),
            DMA((4,)),
            DMA((4,)),
            DMA((4,)),
            DMA((PLANE,)),
            DMA((PLANE,)),
            DMA((1,)),
            DMA((1,)),
            DMA((16,)),
            DMA((count,)),
        ]
    )
    return comm_call(
        functools.partial(attention_kernel, widths, by_rows),
        outs,
        [tokens, gain[None], bias[None], decays] + list(tables) + list(shards_in),
        scratch,
        cid,
        in_specs=[ANY] + [VM] * 7 + [ANY] * count,
        out_specs=[ANY] * (13 + count),
    )


class LineSum:
    def __init__(self, me, own, rx, usend, urecv, dsend, drecv, add):
        self.me, self.own, self.rx, self.add = me, own, rx, add
        self.sems = usend, urecv, dsend, drecv

    def up(self, src, zz):
        return remote(src, self.rx.at[zz], self.sems[0].at[zz], self.sems[1].at[zz], self.me.up())

    def down(self, src, zz):
        slot = jnp.where(zz == self.me.z - 1, LINE, zz)
        return remote(src, self.rx.at[slot], self.sems[2].at[zz], self.sems[3].at[zz], self.me.down())

    def begin(self, order=(3, 2, 1), src=None):
        src = src or self.own
        for zz in order:

            @pl.when(self.me.z == 0)
            def _():
                self.up(src(zz), zz).start()

            @pl.when(self.me.z == LINE - 1)
            def _():
                self.down(src(LINE - 1 - zz), LINE - 1 - zz).start()

    def pass_up(self, zz):
        self.up(self.own(zz), zz).wait_recv()
        self.add(self.rx.at[zz], self.own(zz))
        self.up(self.rx.at[zz], zz).start()

    def pass_down(self, zz):
        self.down(self.own(zz), zz).wait_recv()
        self.add(self.rx.at[zz], self.own(zz))
        self.down(self.rx.at[zz], zz).start()

    def near(self, k):
        @pl.when(self.me.z == 1)
        def _():
            self.pass_up(LINE - 1 - k)

        @pl.when(self.me.z == 2)
        def _():
            self.pass_down(k)

    def far(self):
        @pl.when(self.me.z == 1)
        def _():
            self.pass_down(0)

        @pl.when(self.me.z == 2)
        def _():
            self.pass_up(LINE - 1)

    def arrive(self):
        z = self.me.z

        @pl.when(z > 0)
        def _():
            self.up(self.own(z), z).wait_recv()

        @pl.when(z < LINE - 1)
        def _():
            self.down(self.own(z), z).wait_recv()

    def finish(self):
        z = self.me.z
        for zz in range(LINE):

            @pl.when((z < LINE - 1) & (zz > z))
            def _():
                self.up(self.own(zz), zz).wait_send()

            @pl.when((z > 0) & (zz < z))
            def _():
                self.down(self.own(zz), zz).wait_send()


def add_rows(dst, src):
    rows = dst.shape[0]
    step = 32 if dst.shape[1] > 512 else 128

    @pl.loop(0, rows, step=step)
    def _(r):
        at = rows_at(r, step)
        dst[at, :] = (dst[at, :].astype(F32) + src[at, :].astype(F32)).astype(BF16)


def total_rows(z, dst, own, rx):
    rows = dst.shape[0]
    step = 32 if dst.shape[1] > 512 else 128

    @pl.loop(0, rows, step=step)
    def _(r):
        at = rows_at(r, step)
        v = own[at, :].astype(F32)
        v = v + jnp.where(z > 0, rx[z, at, :].astype(F32), 0.0)
        v = v + jnp.where(z < LINE - 1, rx[LINE, at, :].astype(F32), 0.0)
        dst[at, :] = v.astype(dst.dtype)


def line_sems():
    return [DMA((LINE,)) for _ in range(4)]


def retention_back_kernel(
    da_ref, wo_ref, gated_ref, gate_ref, ret_ref, q_ref, k_ref, v_ref, s_ref, cos_ref, sin_ref,
    ccol_in, crow_in, scal_in, xg_ref, fu_ref, fd_ref,
    dh_out, sums, gate_fin, f1, av_out, aq_out,
    ccol_ref, crow_ref, scal_ref, dh, da, wo, gated, gr, q, k, v, st, cos, sin, dr, xt, ao, ag, rxo, rxg, fin, qo, gb, lg, got, rxf, fo, pbuf, gbuf,
    lsem, gsem, xsem, fsend, frecv, osem, fosem, ssend, srecv, psend, precv, *line,
):
    me = Place()
    z, p = me.z, me.p
    greeted = call(
        [(me.plane(m), None) for m in (1, 2, 3)]
        + [(me.up(), z < LINE - 1), (me.down(), z > 0)]
    )
    width = da.shape[1]
    tokens = da.shape[0]
    keys, values = q.shape[1], v.shape[1]
    blocks = tokens // STRETCH
    half = keys // 2
    pq = [me.xor(m) for m in range(4)]
    chunk = fu_ref.shape[0] // SPANS

    def f_block(h, zp, place):
        return (fu_ref, fd_ref)[h].at[pl.ds(pl.multiple_of((zp * PLANE + place) * chunk, chunk), chunk), :]

    units = [(h, zp, (0, 1)) for zp in (3, 0, 2) for h in range(2)] + [(h, 1, (1,)) for h in range(2)]

    def f_slot(h, zp, j):
        return rxf.at[h, 2 * (3, 0, 2, 1).index(zp) + (j if zp != 1 else 0)]
    away = ((1, 3), (2, 3))
    kept = ((0, 2), (0, 1))
    nbr = (1, 2)

    def f_copy(h, zp, j):
        return remote(
            f_block(h, zp, pq[away[h][j]]), f_slot(h, zp, j), fsend.at[h, zp, j], frecv.at[h, zp, j], me.plane(nbr[h])
        )

    deep = width // LINE
    ends_first = [jnp.where(z < LINE // 2, LINE - 1 - i, i) for i in range(LINE)]

    def slab(i):
        at = rows_at(ends_first[i] * deep, deep)
        return pltpu.make_async_copy(da_ref.at[:, at], da.at[:, at], lsem.at[12 + i])

    slab(0).start()
    loads = [
        start(pltpu.make_async_copy(a, b, lsem.at[i]))
        for i, (a, b) in enumerate(
            [(gated_ref, gated), (wo_ref, wo), (q_ref, q), (k_ref, k), (v_ref, v), (s_ref, st),
             (cos_ref, cos), (sin_ref, sin), (ccol_in, ccol_ref), (crow_in, crow_ref), (scal_in, scal_ref)]
        )
    ]
    for i in range(1, LINE):
        slab(i).start()

    def f_own(u):
        h, zp, js = units[u]
        return [
            pltpu.make_async_copy(f_block(h, zp, pq[kept[h][j]]), fo.at[u % 2, j], fosem.at[u % 2, j])
            for j in js
        ]

    def f_out(u):
        h, zp, js = units[u]
        return [pltpu.make_async_copy(f_slot(h, zp, j), f1.at[h, zp, j], osem.at[u, j]) for j in js]

    for u in range(2):
        for c in f_own(u):
            c.start()

    def f_unit(u):
        h, zp, js = units[u]
        for j, c in zip(js, f_own(u)):
            c.wait()
            f_copy(h, zp, j).wait_recv()
            add_rows(f_slot(h, zp, j), fo.at[u % 2, j])
        for c in f_out(u):
            c.start()
        if u + 2 < len(units):
            for c in f_own(u + 2):
                c.start()

    def tile_rows(i):
        return rows_at(i * 256, 256)

    def gate_loads(i):
        at = tile_rows(i)
        slot = i % 3
        return (
            pltpu.make_async_copy(gate_ref.at[at, :], gr.at[slot, 0], gsem.at[slot, 0]),
            pltpu.make_async_copy(ret_ref.at[at, :], gr.at[slot, 1], gsem.at[slot, 1]),
        )

    for c in gate_loads(0) + gate_loads(1):
        c.start()

    out_sum = LineSum(me, lambda zz: ao.at[rows_at(zz * (width // LINE), width // LINE), :], rxo, *line[:4], add_rows)
    gate_sum = LineSum(me, lambda zz: ag.at[rows_at(zz * (width // LINE), width // LINE), :], rxg, *line[4:], add_rows)

    loads[0].wait()
    for turn in range(LINE):
        slab(turn).wait()

        @pl.loop(0, deep, step=256)
        def _(i):
            at = rows_at(ends_first[turn] * deep + i, 256)
            ao[at, :] = tn(da[:, at], gated[...]).astype(BF16)

        if turn == 0:
            meet(greeted)
        if turn < 2:
            out_sum.begin((LINE - 1 - turn,))
        if turn == 0:
            for h, zp, js in units:
                for j in js:
                    f_copy(h, zp, j).start()
    for c in loads[1:]:
        c.wait()

    tiles = tokens // 256

    @pl.loop(0, tiles)
    def _(i):
        @pl.when(i + 2 < tiles)
        def _():
            for c in gate_loads(i + 2):
                c.start()

        for c in gate_loads(i):
            c.wait()
        at = tile_rows(i)
        slot = i % 3
        dgated = nt(da[at, :], wo[...])
        gate = gr[slot, 0]
        ret = gr[slot, 1]
        centered = ret - jnp.mean(ret, axis=1, keepdims=True)
        scale = lax.rsqrt(jnp.mean(centered * centered, axis=1, keepdims=True) + 1e-05)
        grouped = centered * scale
        sig = 1.0 / (1.0 + jnp.exp(-gate))
        silu = gate * sig
        dh[at, 2 * keys + values :] = (dgated * grouped * (sig * (1.0 + gate * (1.0 - sig)))).astype(BF16)
        dg = dgated * silu
        dr[at, :] = (
            scale * (dg - jnp.mean(dg, axis=1, keepdims=True) - grouped * jnp.mean(dg * grouped, axis=1, keepdims=True))
        ).astype(BF16)

    lg[...] = jnp.zeros_like(lg)

    @pl.loop(0, blocks)
    def _(c):
        at = rows_at(c * STRETCH, STRETCH)
        decayed = (q[at, :].astype(F32) * jnp.exp(ccol_ref[at, :])).astype(BF16)
        got_q = tn(decayed, dr[at, :])
        qo[c] = got_q
        lg[...] += scal_ref[blocks + c, 0:1, 0:1] * got_q

    state_copy = remote(gb.at[0], got, ssend.at[0], srecv.at[0], me.down())

    def pass_state(zz):
        @pl.when(z == zz)
        def _():
            if zz < LINE - 1:
                state_copy.wait_recv()
            if zz > 0:
                add = lg[...]
                if zz < LINE - 1:
                    add = add + got[...].astype(F32) * jnp.exp(scal_ref[2 * blocks, 0:1, 0:1])
                gb[0] = add.astype(BF16)
                state_copy.start()

    pass_state(LINE - 1)
    out_sum.begin((1,))
    out_sum.near(0)
    def x_tile(i):
        return pltpu.make_async_copy(xg_ref.at[:, rows_at(i * 256, 256)], xt.at[i % 3], xsem.at[i % 3])

    x_tile(0).start()
    x_tile(1).start()

    @pl.loop(0, width // 256)
    def _(i):
        @pl.when(i + 2 < width // 256)
        def _():
            x_tile(i + 2).start()

        x_tile(i).wait()
        ag[rows_at(i * 256, 256), :] = tn(xt[i % 3], dh[:, 2 * keys + values :]).astype(BF16)

    gate_sum.begin()
    out_sum.near(1)
    pass_state(2)
    f_unit(0)
    f_unit(1)
    out_sum.far()

    pass_state(1)
    pass_state(0)

    @pl.when(z > 0)
    def _():
        state_copy.wait_send()

    @pl.when(z < LINE - 1)
    def _():
        lg[...] = got[...].astype(F32)

    @pl.when(z == LINE - 1)
    def _():
        lg[...] = jnp.zeros_like(lg)

    for c in reversed(range(blocks)):
        gb[c] = lg[...].astype(BF16)
        if c:
            lg[...] = lg[...] * scal_ref[c, 0:1, 0:1] + qo[c]

    t_size = 256

    @pl.loop(0, blocks)
    def _(c):
        blk = rows_at(c * STRETCH, STRETCH)
        row = crow_ref[c, 0:1, :]
        end = crow_ref[c, 0:1, STRETCH - 1 : STRETCH]
        for r in range(0, STRETCH, t_size):
            at = rows_at(c * STRETCH + r, t_size)
            col = ccol_ref[at, :]
            t_index = lax.broadcasted_iota(jnp.int32, (t_size, STRETCH), 0) + r
            s_index = lax.broadcasted_iota(jnp.int32, (t_size, STRETCH), 1)
            mask = jnp.where(t_index >= s_index, jnp.exp(jnp.minimum(col - row, 0.0)), 0.0)
            pbuf[r : r + t_size, :] = (nt(q[at, :], k[blk, :]) * mask).astype(BF16)
            g = (nt(dr[at, :], v[blk, :]) * mask).astype(BF16)
            gbuf[r : r + t_size, :] = g
            dq = nt(dr[at, :], st[c]) * jnp.exp(col) + nn(g, k[blk, :])
            a, b = dq[:, :half], dq[:, half:]
            dh[at, :half] = (a * cos[at, :] + b * sin[at, :]).astype(BF16)
            dh[at, half:keys] = (b * cos[at, :] - a * sin[at, :]).astype(BF16)
        for r in range(0, STRETCH, t_size):
            at = rows_at(c * STRETCH + r, t_size)
            tail = jnp.exp(end - ccol_ref[at, :])
            w = (v[at, :].astype(F32) * tail).astype(BF16)
            dk = nt(w, gb[c]) + tn(gbuf[:, r : r + t_size], q[blk, :])
            a, b = dk[:, :half], dk[:, half:]
            dh[at, keys : keys + half] = (a * cos[at, :] + b * sin[at, :]).astype(BF16)
            dh[at, keys + half : 2 * keys] = (b * cos[at, :] - a * sin[at, :]).astype(BF16)
            dv = nn(k[at, :], gb[c]) * tail + tn(pbuf[:, r : r + t_size], dr[blk, :])
            dh[at, 2 * keys : 2 * keys + values] = dv.astype(BF16)

    dh_copy = start(pltpu.make_async_copy(dh, dh_out, lsem.at[2]))
    plane = []

    def deal(i, chain, a):
        chain.arrive()
        total_rows(z, fin.at[i], a.at[rows_at(z * (width // LINE), width // LINE), :], chain.rx)
        cols = pl.ds(i * values, values)
        for m in (1, 2, 3):
            plane.append(
                start(
                    remote(
                        fin.at[i, rows_at(pq[m] * chunk, chunk), :], sums.at[p, :, cols],
                        psend.at[i, m], precv.at[i, m], me.plane(m),
                    )
                )
            )
        plane.append(
            start(
                pltpu.make_async_copy(
                    fin.at[i, rows_at(p * chunk, chunk), :], sums.at[p, :, cols], psend.at[i, 0]
                )
            )
        )

    gate_sum.near(0)
    for u in range(2, 4):
        f_unit(u)
    deal(0, out_sum, ao)
    gate_sum.near(1)
    gate_sum.far()
    x_tile(0).start()
    x_tile(1).start()
    wide = 2 * keys + values

    @pl.loop(0, width // 256)
    def _(i):
        @pl.when(i + 2 < width // 256)
        def _():
            x_tile(i + 2).start()

        x_tile(i).wait()
        da[rows_at(i * 256, 256), :wide] = tn(xt[i % 3], dh[:, :wide]).astype(BF16)

    to_last = [
        start(pltpu.make_async_copy(da.at[:, : 2 * keys], aq_out, lsem.at[0])),
        start(pltpu.make_async_copy(da.at[:, 2 * keys : wide], av_out, lsem.at[1])),
    ]
    for u in range(4, len(units)):
        f_unit(u)
    gate_sum.arrive()
    total_rows(z, fin.at[1], ag.at[rows_at(z * deep, deep), :], rxg)
    to_last.append(start(pltpu.make_async_copy(fin.at[1], gate_fin, lsem.at[3])))
    for c in plane + to_last + [dh_copy]:
        c.wait()
    out_sum.finish()
    gate_sum.finish()
    for u, (h, zp, js) in enumerate(units):
        for c in f_out(u):
            c.wait()
        for j in js:
            f_copy(h, zp, j).wait_send()


def retention_back(da, wo, gated, gate, ret, q, k, v, states, cos, sin, ccol, crow, scal, xg, fu, fd, cid):
    tokens, width = da.shape
    keys, values = q.shape[1], v.shape[1]
    chunk = width // SPANS
    blocks = tokens // STRETCH
    hidden = fu.shape[1]
    deep = width // LINE
    return comm_call(
        retention_back_kernel,
        [
            jax.ShapeDtypeStruct((tokens, 2 * keys + 2 * values), BF16),
            jax.ShapeDtypeStruct((PLANE, chunk, values), BF16),
            jax.ShapeDtypeStruct((deep, values), BF16),
            jax.ShapeDtypeStruct((2, LINE, 2, chunk, hidden), BF16),
            jax.ShapeDtypeStruct((width, values), BF16),
            jax.ShapeDtypeStruct((width, 2 * keys), BF16),
        ],
        [da, wo, gated, gate, ret, q, k, v, states, cos, sin, ccol, crow, scal, xg, fu, fd],
        [
            pltpu.VMEM(ccol.shape, F32),
            pltpu.VMEM(crow.shape, F32),
            pltpu.VMEM(scal.shape, F32),
            pltpu.VMEM((tokens, 2 * keys + 2 * values), BF16),
            pltpu.VMEM((tokens, width), BF16),
            pltpu.VMEM(wo.shape, BF16),
            pltpu.VMEM(gated.shape, BF16),
            pltpu.VMEM((3, 2, 256, values), F32),
            pltpu.VMEM(q.shape, BF16),
            pltpu.VMEM(k.shape, BF16),
            pltpu.VMEM(v.shape, BF16),
            pltpu.VMEM(states.shape, BF16),
            pltpu.VMEM(cos.shape, F32),
            pltpu.VMEM(sin.shape, F32),
            pltpu.VMEM((tokens, values), BF16),
            pltpu.VMEM((3, tokens, 256), BF16),
            pltpu.VMEM((width, values), BF16),
            pltpu.VMEM((width, values), BF16),
            pltpu.VMEM((LINE + 1, deep, values), BF16),
            pltpu.VMEM((LINE + 1, deep, values), BF16),
            pltpu.VMEM((2, deep, values), BF16),
            pltpu.VMEM((blocks, keys, values), F32),
            pltpu.VMEM((blocks, keys, values), BF16),
            pltpu.VMEM((keys, values), F32),
            pltpu.VMEM((keys, values), BF16),
            pltpu.VMEM((2, 2 * LINE - 1, chunk, hidden), BF16),
            pltpu.VMEM((2, 2, chunk, hidden), BF16),
            pltpu.VMEM((STRETCH, STRETCH), BF16),
            pltpu.VMEM((STRETCH, STRETCH), BF16),
            DMA((12 + LINE,)),
            DMA((3, 2)),
            DMA((3,)),
            DMA((2, LINE, 2)),
            DMA((2, LINE, 2)),
            DMA((2 * LINE, 2)),
            DMA((2, 2)),
            DMA((1,)),
            DMA((1,)),
            DMA((2, PLANE)),
            DMA((2, PLANE)),
        ]
        + line_sems()
        + line_sems(),
        cid,
        in_specs=[ANY] * 17,
        out_specs=[ANY] * 6,
    )


def last_kernel(
    dh_ref, av_ref, aq_ref, wq_ref, wk_ref, wv_ref, wg_ref, f1_ref, fu_ref, fd_ref, gate_ref, tok_ref, gain_ref, resid_ref, second_ref,
    grad_out, gains, fout, sums,
    tok, resid, rxl, dh, wh, share, rx0, rx1a, rx1b, rx2a, rx2b, av, aq, rxv, rxq, fin, rf2, kf, rxfa, rxfb, grx,
    lsem, ksem, lsend, lrecv, fsend, frecv, csend, crecv, xsend, xrecv, gsend, grecv, psend, precv, *line,
):
    me = Place()
    z, p, f = me.z, me.p, me.f
    rounds = [
        [me.at((z + t) % LINE, p, f) for t in range(1, LINE)],
        [me.partner()],
        [me.plane(m) for m in (1, 2, 3)],
    ]
    greet([(d, None) for r in rounds for d in r])
    width, keys2, values = av.shape[0], aq.shape[1], av.shape[1]
    rows = tok_ref.shape[0]
    pq = [me.xor(m) for m in range(4)]
    chunk = width // SPANS
    deep = width // LINE

    late = 1

    def f_copy(h, zp):
        return remote(f1_ref.at[h, zp, 1], rf2.at[h, zp], fsend.at[h, zp], frecv.at[h, zp], me.plane(2 - h))

    def f_block(h, place):
        return (fu_ref, fd_ref)[h].at[rows_at((late * PLANE + place) * chunk, chunk), :]

    def late_copy(h):
        return remote(f_block(h, pq[1 + h]), rxl.at[h], lsend.at[h], lrecv.at[h], me.plane(1 + h))

    def block_of(a, size):
        return lambda zz: a.at[rows_at(zz * size, size), :]

    v_sum = LineSum(me, block_of(av, deep), rxv, *line[:4], add_rows)
    q_sum = LineSum(me, block_of(aq, deep), rxq, *line[4:8], add_rows)
    fa_sum = LineSum(me, lambda zz: kf.at[0, zz], rxfa, *line[8:12], add_rows)
    fb_sum = LineSum(me, lambda zz: kf.at[1, zz], rxfb, *line[12:16], add_rows)
    v_sum.begin(src=block_of(av_ref, deep))
    q_sum.begin(src=block_of(aq_ref, deep))
    for zp in (3, 0, 2, 1):
        for h in range(2):
            f_copy(h, zp).start()
    for h in range(2):
        late_copy(h).start()
    load = start(pltpu.make_async_copy(dh_ref, dh, lsem.at[0]))
    owns = [
        start(pltpu.make_async_copy(av_ref, av, lsem.at[7])),
        start(pltpu.make_async_copy(aq_ref, aq, lsem.at[8])),
    ]
    loads, at = [], 0
    for i, w in enumerate((wq_ref, wk_ref, wv_ref, wg_ref)):
        size = w.shape[1]
        loads.append(start(pltpu.make_async_copy(w, wh.at[:, at : at + size], lsem.at[1 + i])))
        at += size
    keeps = []
    for h in range(2):
        for i, zp in enumerate((3, 0, 2)):
            keeps.append(start(pltpu.make_async_copy(f1_ref.at[h, zp, 0], kf.at[h, zp], ksem.at[h, i])))
        keeps.append(start(pltpu.make_async_copy(f_block(h, p), kf.at[h, late], ksem.at[h, 3])))
    rest = [
        start(pltpu.make_async_copy(tok_ref, tok, lsem.at[5])),
        start(pltpu.make_async_copy(resid_ref, resid, lsem.at[6])),
    ]

    load.wait()
    plane = []

    def deal(i, chain, a):
        chain.arrive()
        total_rows(z, fin.at[i], a.at[rows_at(z * deep, deep), :], chain.rx)
        spread(i, fin.at[i])

    def spread(i, src):
        cols = pl.ds(i * values, values)
        for m in (1, 2, 3):
            plane.append(
                start(
                    remote(
                        src.at[rows_at(pq[m] * chunk, chunk), :], sums.at[p, :, cols],
                        psend.at[i, m], precv.at[i, m], me.plane(m),
                    )
                )
            )
        plane.append(
            start(
                pltpu.make_async_copy(
                    src.at[rows_at(p * chunk, chunk), :], sums.at[p, :, cols], psend.at[i, 0]
                )
            )
        )

    gate_load = start(pltpu.make_async_copy(gate_ref, fin.at[2], lsem.at[9]))
    for c in loads + owns + [gate_load]:
        c.wait()

    own_rows, their_rows = rows_at(f * rows, rows), rows_at((1 - f) * rows, rows)
    wide = width // 2
    ca, cb = pl.ds(0, wide), pl.ds(wide, wide)
    everything, whole = pl.ds(0, width), pl.ds(0, wide)
    first, sends = {}, {}

    def share_part(m):
        at_rows = rows_at(pq[m] * 2 * rows, 2 * rows)

        @pl.loop(0, width, step=256)
        def _(c):
            at = rows_at(c, 256)
            share[m, :, at] = nt(dh[at_rows, :], wh[at, :]).astype(BF16)

        first[m] = start(
            remote(share.at[m, their_rows], rx0.at[m], csend.at[m], crecv.at[m], me.partner())
        )

    def pass_on(m):
        first[m].wait_recv()
        add_into(rx0.at[m], everything, share.at[m, own_rows], everything)
        k = 0 if m == 3 else 1
        if m & 1:
            sends["a", k] = start(
                remote(rx0.at[m, :, ca], rx1a.at[k], xsend.at[k], xrecv.at[k], me.plane(1))
            )
        if m & 2:
            sends["b", k] = start(
                remote(rx0.at[m, :, cb], rx1b.at[k], xsend.at[2 + k], xrecv.at[2 + k], me.plane(2))
            )

    share_part(3)
    share_part(1)
    pass_on(3)
    v_sum.near(0)
    share_part(2)
    pass_on(1)
    share_part(0)
    pass_on(2)
    v_sum.near(1)
    pass_on(0)
    for c in keeps:
        c.wait()
    v_sum.far()
    q_sum.near(0)
    for ends, turns in (((3, 0), (3,)), ((2, 1), (2,))):
        for zp in ends:
            for h in range(2):
                f_copy(h, zp).wait_recv()
                add_rows(kf.at[h, zp], rf2.at[h, zp])
                if zp == late:
                    late_copy(h).wait_recv()
                    add_rows(kf.at[h, zp], rxl.at[h])
        for zz in turns:
            fa_sum.begin((zz,))
            fb_sum.begin((zz,))
    q_sum.near(1)
    q_sum.far()
    sends["a", 0].wait_recv()
    add_into(rx1a.at[0], whole, rx0.at[2], ca)
    s2a = start(remote(rx1a.at[0], rx2a, xsend.at[4], xrecv.at[4], me.plane(2)))
    sends["b", 0].wait_recv()
    add_into(rx1b.at[0], whole, rx0.at[1], cb)
    s2b = start(remote(rx1b.at[0], rx2b, xsend.at[5], xrecv.at[5], me.plane(1)))
    spread(2, fin.at[2])
    deal(0, v_sum, av)
    fa_sum.near(0)
    sends["a", 1].wait_recv()
    sends["b", 1].wait_recv()
    deal(1, q_sum, aq)
    fb_sum.near(0)
    s2a.wait_recv()
    s2b.wait_recv()
    for c in rest:
        c.wait()
    gains[...] = jnp.zeros_like(gains)
    gains[2:4, :] = second_ref[0:2, :]
    step = 32

    @pl.loop(0, rows, step=step)
    def _(r):
        at = rows_at(r, step)
        left = rx0[0, at, ca].astype(F32) + rx1a[1, at, :].astype(F32) + rx2a[at, :].astype(F32)
        right = rx0[0, at, cb].astype(F32) + rx1b[1, at, :].astype(F32) + rx2b[at, :].astype(F32)
        dx = jnp.concatenate([left, right], axis=1)
        v = tok[at, :].astype(F32)
        centered = v - jnp.mean(v, axis=1, keepdims=True)
        scale = lax.rsqrt(jnp.mean(centered * centered, axis=1, keepdims=True) + 1e-05)
        hat = centered * scale
        gains[0:1, :] += jnp.sum(dx * hat, axis=0, keepdims=True)
        gains[1:2, :] += jnp.sum(dx, axis=0, keepdims=True)
        g = dx * gain_ref[...]
        back = scale * (
            g - jnp.mean(g, axis=1, keepdims=True) - hat * jnp.mean(g * hat, axis=1, keepdims=True)
        )
        tok[at, :] = (back + resid[at, :]).astype(BF16)

    out_copy = start(pltpu.make_async_copy(tok, grad_out, lsem.at[0]))

    def gain_copies(r):
        base = (0, 3, 4)[r]
        return [
            remote(gains, grx.at[base + i], gsend.at[base + i], grecv.at[base + i], d)
            for i, d in enumerate(rounds[r])
        ]

    def gain_begin(r):
        for c in gain_copies(r):
            c.start()

    def gain_end(r):
        for c in gain_copies(r):
            c.wait()
        for i in range(len(rounds[r])):
            gains[...] += grx[(0, 3, 4)[r] + i]

    gain_begin(0)
    fa_sum.begin((1,))
    fb_sum.begin((1,))
    fa_sum.near(1)
    fa_sum.far()
    gain_end(0)
    gain_begin(1)
    fb_sum.near(1)
    gain_end(1)
    gain_begin(2)
    fb_sum.far()
    gain_end(2)
    fa_sum.arrive()
    total_rows(z, fout.at[0], kf.at[0, z], rxfa)
    fb_sum.arrive()
    total_rows(z, fout.at[1], kf.at[1, z], rxfb)
    for c in plane + [out_copy]:
        c.wait()
    for h in range(2):
        late_copy(h).wait_send()
    for chain in (v_sum, q_sum, fa_sum, fb_sum):
        chain.finish()
    for c in list(first.values()) + list(sends.values()) + [s2a, s2b]:
        c.wait_send()
    for zp in range(LINE):
        for h in range(2):
            f_copy(h, zp).wait_send()


def last_sums(dh, av, aq, wq, wk, wv, wg, f1, fu, fd, gate_fin, tokens, gain, resid, second, cid):
    width = av.shape[0]
    rows = tokens.shape[0]
    keys, values = wq.shape[1], wv.shape[1]
    assert 2 * keys == values
    chunk, deep = width // SPANS, width // LINE
    hidden = f1.shape[-1]
    return comm_call(
        last_kernel,
        [
            jax.ShapeDtypeStruct((rows, width), BF16),
            jax.ShapeDtypeStruct((8, width), F32),
            jax.ShapeDtypeStruct((2, chunk, hidden), BF16),
            jax.ShapeDtypeStruct((PLANE, chunk, 3 * values), BF16),
        ],
        [dh, av, aq, wq, wk, wv, wg, f1, fu, fd, gate_fin, tokens, gain[None], resid, second],
        [
            pltpu.VMEM((rows, width), BF16),
            pltpu.VMEM((rows, width), F32),
            pltpu.VMEM((2, chunk, hidden), BF16),
            pltpu.VMEM(dh.shape, BF16),
            pltpu.VMEM((width, dh.shape[1]), BF16),
            pltpu.VMEM((PLANE, 2 * rows, width), BF16),
            pltpu.VMEM((PLANE, rows, width), BF16),
            pltpu.VMEM((2, rows, width // 2), BF16),
            pltpu.VMEM((2, rows, width // 2), BF16),
            pltpu.VMEM((rows, width // 2), BF16),
            pltpu.VMEM((rows, width // 2), BF16),
            pltpu.VMEM((width, values), BF16),
            pltpu.VMEM((width, 2 * keys), BF16),
            pltpu.VMEM((LINE + 1, deep, values), BF16),
            pltpu.VMEM((LINE + 1, deep, 2 * keys), BF16),
            pltpu.VMEM((3, deep, values), BF16),
            pltpu.VMEM((2, LINE, chunk, hidden), BF16),
            pltpu.VMEM((2, LINE, chunk, hidden), BF16),
            pltpu.VMEM((LINE + 1, chunk, hidden), BF16),
            pltpu.VMEM((LINE + 1, chunk, hidden), BF16),
            pltpu.VMEM((7, 8, width), F32),
            DMA((10,)),
            DMA((2, 4)),
            DMA((2,)),
            DMA((2,)),
            DMA((2, LINE)),
            DMA((2, LINE)),
            DMA((4,)),
            DMA((4,)),
            DMA((6,)),
            DMA((6,)),
            DMA((7,)),
            DMA((7,)),
            DMA((3, PLANE)),
            DMA((3, PLANE)),
        ]
        + line_sems()
        + line_sems()
        + line_sems()
        + line_sems(),
        cid,
        in_specs=[ANY] * 12 + [VM, ANY, VM],
        out_specs=[ANY, VM, VM, ANY],
    )


def outputs_kernel(
    last, first, ffn, low_out, low_grad, gains, q, k, v, gate, out, up, down, block_out, grad_tokens, *vectors
):
    values = v.shape[1]
    keys = q.shape[1]
    v[...] = last[0, :, :values].astype(F32)
    q[...] = last[0, :, values : values + keys].astype(F32)
    k[...] = last[0, :, values + keys : 2 * values].astype(F32)
    gate[...] = last[0, :, 2 * values :].astype(F32)
    out[...] = first[0].astype(F32).T
    up[...] = ffn[0].astype(F32)
    down[...] = ffn[1].astype(F32).T
    block_out[...] = low_out[...]
    grad_tokens[...] = low_grad[...]
    for i, g in enumerate(vectors):
        g[...] = gains[i, :]


def outputs(last, first, ffn, low_out, low_grad, gains, keys):
    heads, chunk, values = first.shape
    hidden = ffn.shape[-1]
    rows, width = low_out.shape
    piece, slab = hidden // heads, rows // heads
    sd = jax.ShapeDtypeStruct
    by_column = [pl.BlockSpec((chunk, size), lambda i: (0, i)) for size in (keys, keys, values, values)]
    by_row = pl.BlockSpec((values, chunk), lambda i: (i, 0))
    low = pl.BlockSpec((slab, width), lambda i: (i, 0))
    sums = [pl.BlockSpec((1, chunk, a.shape[-1]), lambda i: (i, 0, 0)) for a in (last, first)]
    return pl.pallas_call(
        outputs_kernel,
        grid=(heads,),
        in_specs=[
            *sums,
            pl.BlockSpec((2, chunk, piece), lambda i: (0, 0, i)),
            low,
            low,
            pl.BlockSpec(gains.shape, lambda i: (0, 0)),
        ],
        out_specs=by_column
        + [
            by_row,
            pl.BlockSpec((chunk, piece), lambda i: (0, i)),
            pl.BlockSpec((piece, chunk), lambda i: (i, 0)),
            low,
            low,
        ]
        + [pl.BlockSpec((width,), lambda i: (0,))] * 4,
        out_shape=[
            sd((chunk, heads * keys), F32),
            sd((chunk, heads * keys), F32),
            sd((chunk, heads * values), F32),
            sd((chunk, heads * values), F32),
            sd((heads * values, chunk), F32),
            sd((chunk, hidden), F32),
            sd((hidden, chunk), F32),
            sd((rows, width), BF16),
            sd((rows, width), BF16),
        ]
        + [sd((width,), F32)] * 4,
    )(last, first, ffn, low_out, low_grad, gains)


def angle_tables(fine, half_width):
    frequency = 10000.0 ** (-np.linspace(0.0, 1.0, half_width))
    coarse = fine * np.arange(SEQUENCE_LENGTH // fine)[:, None] * frequency[None, :]
    near = np.arange(fine)[:, None] * frequency[None, :]
    return [np.asarray(f(a), np.float32) for a in (coarse, near) for f in (np.cos, np.sin)]


def shards(
    tokens,
    ln1_gain,
    ln1_bias,
    w_query,
    w_key,
    w_value,
    w_gate,
    w_out,
    decay_log,
    ln2_gain,
    ln2_bias,
    w_up,
    w_down,
    cotangent,
):
    row_count, width = tokens.shape
    span_rows = cotangent.shape[0]
    heads = decay_log.shape[1]
    repeats = lax.axis_size("seq") // SPANS
    peers = [[lo + SPANS * k for k in range(repeats)] for lo in range(SPANS)]
    narrow = width // (SPANS * repeats)

    def wide_in(w, axis):
        if repeats == 1:
            return w
        return lax.all_gather(w, "seq", axis_index_groups=peers, axis=axis, tiled=True)

    def narrow_out(g, axis):
        if repeats == 1:
            return g
        return lax.psum_scatter(
            g, "seq", scatter_dimension=axis, axis_index_groups=peers, tiled=True
        )

    def features_in(a):
        if repeats == 1:
            return a
        return a.reshape(a.shape[:-1] + (repeats, SPANS, narrow)).swapaxes(-3, -2).reshape(a.shape)

    def features_out(a):
        if repeats == 1:
            return a
        return a.reshape(a.shape[:-1] + (SPANS, repeats, narrow)).swapaxes(-3, -2).reshape(a.shape)

    spot = lax.axis_index("seq") % SPANS
    z, p = spot // PLANE, spot % PLANE
    group_rows = span_rows * PLANE
    blocks = group_rows // STRETCH

    tokens, cotangent, w_down = features_in(tokens), features_in(cotangent), features_in(w_down)
    w_up = features_in(w_up.T).T if repeats > 1 else w_up
    ln1_gain, ln1_bias = features_in(ln1_gain), features_in(ln1_bias)
    ln2_gain, ln2_bias = features_in(ln2_gain), features_in(ln2_bias)
    decays = decay_log.T
    (
        normed, q_rot, k_rot, value, gate_proj, retained, gated_low, prev_states,
        cosine, sine_part, ccol, crow, scalars, key_w, value_w, query_w, gate_w, out_w,
    ) = attention(
        tokens,
        ln1_gain,
        ln1_bias,
        decays,
        angle_tables(64, w_key.shape[1] // heads // 2),
        [
            wide_in(w_key, 0),
            wide_in(w_value, 0),
            wide_in(w_query, 0),
            wide_in(w_gate, 0),
            wide_in(w_out, 1),
        ],
        (False, False, False, False, True),
        0,
    )
    block_out, grad_resid, gains_second, grad_attn, grad_up, grad_down = ffn_part(
        gated_low,
        out_w,
        tokens,
        ln2_gain,
        ln2_bias,
        w_up,
        w_down,
        cotangent,
        2,
    )
    grad_heads, sums_first, gate_sum, ffn_first, grad_value_w, grad_qk_w = retention_back(
        grad_attn,
        out_w,
        gated_low,
        gate_proj,
        retained,
        q_rot,
        k_rot,
        value,
        prev_states,
        cosine,
        sine_part,
        ccol,
        crow,
        scalars,
        normed,
        grad_up,
        grad_down,
        7,
    )
    grad_tokens, gains, ffn_sum, sums_last = last_sums(
        grad_heads,
        grad_value_w,
        grad_qk_w,
        query_w,
        key_w,
        value_w,
        gate_w,
        ffn_first,
        grad_up,
        grad_down,
        gate_sum,
        tokens,
        ln1_gain,
        grad_resid,
        gains_second,
        8,
    )
    if repeats > 1:
        gains = lax.psum(gains, "seq", axis_index_groups=peers)

    *sums, block_out, grad_tokens, gain_one, bias_one, gain_two, bias_two = outputs(
        sums_last, sums_first, ffn_sum, block_out, grad_tokens, gains, key_w.shape[1]
    )
    gain_one, bias_one, gain_two, bias_two = map(features_out, (gain_one, bias_one, gain_two, bias_two))
    sum_query, sum_key, sum_value, sum_gate, sum_out, sum_up, sum_down = (
        narrow_out(g, axis) for g, axis in zip(sums, (0, 0, 0, 0, 1, 0, 1))
    )
    return (
        features_out(block_out),
        features_out(grad_tokens),
        gain_one,
        bias_one,
        sum_query,
        sum_key,
        sum_value,
        sum_gate,
        sum_out,
        gain_two,
        bias_two,
        sum_up,
        sum_down,
    )


def solution(mesh):
    return jax.shard_map(
        shards,
        mesh=mesh,
        in_specs=(
            P(("seq", "ffn"), None),
            P(),
            P(),
            P("seq", "ffn"),
            P("seq", "ffn"),
            P("seq", "ffn"),
            P("seq", "ffn"),
            P("ffn", "seq"),
            P("seq", "ffn"),
            P(),
            P(),
            P(None, "ffn"),
            P("ffn", None),
            P("seq", None),
        ),
        out_specs=(
            P(("seq", "ffn"), None),
            P(("seq", "ffn"), None),
            P(),
            P(),
            P("seq", "ffn"),
            P("seq", "ffn"),
            P("seq", "ffn"),
            P("seq", "ffn"),
            P("ffn", "seq"),
            P(),
            P(),
            P("seq", "ffn"),
            P("ffn", "seq"),
        ),
        check_vma=False,
    )
```

```python
import functools

import jax
import jax.numpy as jnp
import numpy as np
from jax import lax
from jax.experimental import pallas as pl
from jax.experimental.pallas import tpu as pltpu
from jax.sharding import PartitionSpec as P

STRETCH = 512
SEQUENCE_LENGTH = 8192
PLANE = 4
LINE = 4
SPANS = PLANE * LINE
MESH = pl.DeviceIdType.MESH
VMEM_LIMIT = 63 * 1024 * 1024
ANY = pl.BlockSpec(memory_space=pl.ANY)
VM = pl.BlockSpec(memory_space=pltpu.VMEM)
BF16 = jnp.bfloat16
F32 = jnp.float32


class Place:
    def __init__(self):
        s = lax.axis_index("seq")
        self.f = lax.axis_index("ffn")
        lo = s % SPANS
        self.base = s - lo
        self.z = lo // PLANE
        self.p = lo % PLANE

    def plane(self, m):
        return self.at(self.z, self.xor(m), self.f)

    def xor(self, m):
        p = self.p
        low, high = p % 2, p // 2
        if m & 1:
            low = 1 - low
        if m & 2:
            high = 1 - high
        return high * 2 + low

    def at(self, z, p, f):
        return (self.base + z * PLANE + p, f)

    def partner(self):
        return self.at(self.z, self.p, 1 - self.f)

    def up(self):
        return self.at(self.z + 1, self.p, self.f)

    def down(self):
        return self.at(self.z - 1, self.p, self.f)


def greet(peers):
    meet(call(peers))


def meet(count):
    pl.semaphore_wait(pltpu.get_barrier_semaphore(), count)


def call(peers):
    bar = pltpu.get_barrier_semaphore()
    count = 0
    for device, cond in peers:
        if cond is None:
            pl.semaphore_signal(bar, inc=1, device_id=device, device_id_type=MESH)
            count = count + 1
        else:

            @pl.when(cond)
            def _():
                pl.semaphore_signal(bar, inc=1, device_id=device, device_id_type=MESH)

            count = count + cond.astype(jnp.int32)
    return count


def remote(src, dst, send, recv, device):
    return pltpu.make_async_remote_copy(
        src_ref=src, dst_ref=dst, send_sem=send, recv_sem=recv, device_id=device, device_id_type=MESH
    )


def comm_call(kernel, outs, ins, scratch, cid, in_specs=None, out_specs=None):
    return pl.pallas_call(
        kernel,
        out_shape=outs,
        in_specs=in_specs if in_specs is not None else [ANY] * len(ins),
        out_specs=out_specs if out_specs is not None else [ANY] * len(outs),
        scratch_shapes=scratch,
        compiler_params=pltpu.CompilerParams(
            collective_id=cid, has_side_effects=True, vmem_limit_bytes=VMEM_LIMIT
        ),
    )(*ins)


DMA = pltpu.SemaphoreType.DMA


def nn(a, b):
    return jnp.dot(a, b, preferred_element_type=F32)


def nt(a, b):
    return lax.dot_general(a, b, (((1,), (1,)), ((), ())), preferred_element_type=F32)


def tn(a, b):
    return lax.dot_general(a, b, (((0,), (0,)), ((), ())), preferred_element_type=F32)


def rows_at(r, size):
    return pl.ds(pl.multiple_of(r, size), size)


def add_into(dst, cols, other, other_cols):
    @pl.loop(0, dst.shape[0], step=64)
    def _(r):
        at = rows_at(r, 64)
        dst[at, cols] = (dst[at, cols].astype(F32) + other[at, other_cols].astype(F32)).astype(BF16)


def start(copy):
    copy.start()
    return copy


def ffn_kernel(
    gated_ref, wo_ref, tok_ref, gain_ref, bias_ref, wu_ref, wd_ref, cot_ref,
    block_out, resid_out, gains, da, fu, fd,
    tok, resid_grad, share, wu, wd, rx0, rx1a, rx1b, rx2a, rx2b, resid, xn, act, dact, du, cot, dab, stage, tmp,
    lsem, gload, csend, crecv, xsend, xrecv, psend, precv, gsend, grecv, ksend, krecv, ssem, osem,
):
    me = Place()
    p, f = me.p, me.f
    greeted = call([(me.plane(1), None), (me.plane(2), None), (me.partner(), None)])
    rows, width = tok_ref.shape
    hidden = wu.shape[1]
    q = [me.xor(m) for m in range(4)]
    wide = width // 2
    hr = rows // 2
    span = 2 * rows
    ca, cb = pl.ds(0, wide), pl.ds(wide, wide)
    everything, whole = pl.ds(0, width), pl.ds(0, wide)
    own_half = [pl.ds(h * hr, hr) for h in range(2)]
    mine = [rows_at(h * rows + f * hr, hr) for h in range(2)]
    theirs = [rows_at(h * rows + (1 - f) * hr, hr) for h in range(2)]
    both = [pl.ds(h * rows, rows) for h in range(2)]

    order = (3, 1, 2, 0)
    part_width = gated_ref.shape[1]
    def out_slab(i):
        at = rows_at(i * 512, 512)
        return pltpu.make_async_copy(wo_ref.at[:, at], act.at[:, at], osem.at[i])

    slabs = width // 512
    out_slab(0).start()
    load_t = pltpu.make_async_copy(tok_ref, tok, lsem.at[7])
    load_g = {
        m: start(
            pltpu.make_async_copy(
                gated_ref.at[rows_at(q[m] * span, span), :],
                xn.at[:, m * part_width : (m + 1) * part_width],
                gload.at[m],
            )
        )
        for m in order
    }
    for i in range(1, slabs):
        out_slab(i).start()
    load_t.start()
    load_d = start(pltpu.make_async_copy(wd_ref, wd, lsem.at[1]))
    load_c = [
        start(
            pltpu.make_async_copy(
                cot_ref.at[pl.ds(c * rows + h * hr, hr), :], cot.at[pl.ds(h * rows + c * hr, hr), :], lsem.at[3 + 2 * h + c]
            )
        )
        for h in range(2)
        for c in range(2)
    ]
    load_u = start(pltpu.make_async_copy(wu_ref, wu, lsem.at[2]))
    first, sends = {}, {}

    def to_partner(m, h):
        first[m, h] = start(
            remote(
                share.at[m, rows_at((1 - f) * rows + h * hr, hr)], rx0.at[m, own_half[h]],
                csend.at[m, h], crecv.at[m, h], me.partner(),
            )
        )

    for m in order:
        load_g[m].wait()

        @pl.loop(0, slabs)
        def _(i):
            if m == order[0]:
                out_slab(i).wait()
            at = rows_at(i * 512, 512)
            share[m, :, at] = nn(xn[:, m * part_width : (m + 1) * part_width], act[:, at]).astype(BF16)

        if m == order[0]:
            meet(greeted)
        to_partner(m, 0)
    for m in order:
        to_partner(m, 1)

    def pass_on(m, h):
        first[m, h].wait_recv()
        at = own_half[h]
        add_into(rx0.at[m, at], everything, share.at[m, rows_at(f * rows + h * hr, hr)], everything)
        k = 0 if m == 3 else 1
        if m & 1:
            sends["a", k, h] = start(
                remote(rx0.at[m, at, ca], rx1a.at[k, at], xsend.at[k, h], xrecv.at[k, h], me.plane(1))
            )
        if m & 2:
            sends["b", k, h] = start(
                remote(rx0.at[m, at, cb], rx1b.at[k, at], xsend.at[2 + k, h], xrecv.at[2 + k, h], me.plane(2))
            )

    def second(h):
        at = own_half[h]
        sends["a", 0, h].wait_recv()
        add_into(rx1a.at[0, at], whole, rx0.at[2, at], ca)
        sends["a", 2, h] = start(
            remote(rx1a.at[0, at], rx2a.at[at], xsend.at[4, h], xrecv.at[4, h], me.plane(2))
        )
        sends["b", 0, h].wait_recv()
        add_into(rx1b.at[0, at], whole, rx0.at[1, at], cb)
        sends["b", 2, h] = start(
            remote(rx1b.at[0, at], rx2b.at[at], xsend.at[5, h], xrecv.at[5, h], me.plane(1))
        )

    for m in order:
        pass_on(m, 0)

    load_d.wait()
    for c in load_c:
        c.wait()

    @pl.loop(0, hidden, step=256)
    def _(c):
        at = rows_at(c, 256)
        dact[:, at] = nt(cot[...], wd[at, :])

    second(0)
    for m in order:
        pass_on(m, 1)
    load_u.wait()
    step = 32

    def norm(h):
        for key in (("a", 1, h), ("b", 1, h), ("a", 2, h), ("b", 2, h)):
            sends[key].wait_recv()

        @pl.loop(0, hr, step=step)
        def _(r):
            at = pl.ds(pl.multiple_of(h * hr + r, step), step)
            left = rx0[0, at, ca].astype(F32) + rx1a[1, at, :].astype(F32) + rx2a[at, :].astype(F32)
            right = rx0[0, at, cb].astype(F32) + rx1b[1, at, :].astype(F32) + rx2b[at, :].astype(F32)
            v = tok[at, :].astype(F32) + jnp.concatenate([left, right], axis=1)
            resid[at, :] = v
            centered = v - jnp.mean(v, axis=1, keepdims=True)
            scale = lax.rsqrt(jnp.mean(centered * centered, axis=1, keepdims=True) + 1e-05)
            xn[pl.ds(pl.multiple_of(h * rows + f * hr + r, step), step), :] = (
                centered * scale * gain_ref[...] + bias_ref[...]
            ).astype(BF16)

        return start(remote(xn.at[mine[h]], xn.at[mine[h]], psend.at[0, h], precv.at[0, h], me.partner()))

    def hidden_part(h):
        @pl.loop(0, hidden, step=512)
        def _(c):
            at = rows_at(c, 512)
            u = nn(xn[both[h], :], wu[:, at])
            e = 0.5 * (1.0 + lax.erf(u * 0.7071067811865476))
            act[both[h], at] = (u * e).astype(BF16)
            slope = e + u * jnp.exp(-0.5 * u * u) * 0.3989422804014327
            du[both[h], at] = (dact[both[h], at] * slope).astype(BF16)

    def back_part(h):
        @pl.loop(0, width, step=512)
        def _(c):
            at = rows_at(c, 512)
            tmp[...] = nt(du[both[h], :], wu[at, :])
            resid_grad[own_half[h], at] = tmp[rows_at(f * hr, hr), :]
            share[0, own_half[h], at] = tmp[rows_at((1 - f) * hr, hr), :].astype(BF16)

        return start(
            remote(share.at[0, own_half[h]], share.at[1, own_half[h]], psend.at[1, h], precv.at[1, h], me.partner())
        )

    def norm_back(h):
        @pl.loop(0, hr, step=step)
        def _(r):
            at = pl.ds(pl.multiple_of(h * hr + r, step), step)
            dx = resid_grad[at, :] + share[1, at, :].astype(F32)
            v = resid[at, :]
            centered = v - jnp.mean(v, axis=1, keepdims=True)
            scale = lax.rsqrt(jnp.mean(centered * centered, axis=1, keepdims=True) + 1e-05)
            hat = centered * scale
            gains[0:1, :] += jnp.sum(dx * hat, axis=0, keepdims=True)
            gains[1:2, :] += jnp.sum(dx, axis=0, keepdims=True)
            g = dx * gain_ref[...]
            back = scale * (
                g - jnp.mean(g, axis=1, keepdims=True) - hat * jnp.mean(g * hat, axis=1, keepdims=True)
            )
            back = back + cot[pl.ds(pl.multiple_of(h * rows + f * hr + r, step), step), :].astype(F32)
            resid_grad[at, :] = back
            dab[at, :] = back.astype(BF16)

    def out_part(h):
        @pl.loop(0, width, step=512)
        def _(c):
            at = rows_at(c, 512)
            tmp[...] = nn(act[both[h], :], wd[:, at])
            dact[pl.ds(h * rows, hr), at] = tmp[rows_at(f * hr, hr), :]
            share[2, own_half[h], at] = tmp[rows_at((1 - f) * hr, hr), :].astype(BF16)

        return start(
            remote(share.at[2, own_half[h]], share.at[3, own_half[h]], psend.at[2, h], precv.at[2, h], me.partner())
        )

    quarter = hr // 2

    def seat(m, h, k=None):
        base = (q[m] * 2 + f) * rows + h * hr
        if k is None:
            return da.at[pl.ds(pl.multiple_of(base, hr), hr), :]
        return da.at[pl.ds(pl.multiple_of(base + k * quarter, quarter), quarter), :]

    spread = {}

    def spread_begin(h):
        spread["own", h] = start(pltpu.make_async_copy(dab.at[own_half[h]], seat(0, h), gload.at[h]))
        for i in range(2):
            for to, k in ((1, i), (2, 1 - i)):
                sem = (to - 1) * 2 + i
                spread[to, i, h] = start(
                    remote(
                        dab.at[pl.ds(h * hr + k * quarter, quarter)], seat(0, h, k),
                        gsend.at[sem, h], grecv.at[sem, h], me.plane(to),
                    )
                )
        spread["core", 0, h] = start(
            remote(dab.at[own_half[h]], seat(0, h), ksend.at[0, h], krecv.at[0, h], me.partner())
        )

    def spread_on(h):
        spread[1, 0, h].wait_recv()
        spread["g1", h] = start(
            remote(seat(1, h, 0), seat(1, h, 0), gsend.at[4, h], grecv.at[4, h], me.plane(2))
        )
        spread[2, 0, h].wait_recv()
        spread["g2", h] = start(
            remote(seat(2, h, 1), seat(2, h, 1), gsend.at[5, h], grecv.at[5, h], me.plane(1))
        )

    def spread_end(h):
        for m in (1, 2):
            spread[m, 1, h].wait_recv()
            spread["core", m, h] = start(
                remote(seat(m, h), seat(m, h), ksend.at[m, h], krecv.at[m, h], me.partner())
            )
        spread["g1", h].wait_recv()
        spread["g2", h].wait_recv()
        spread["core", 3, h] = start(
            remote(seat(3, h), seat(3, h), ksend.at[3, h], krecv.at[3, h], me.partner())
        )

    gains[...] = jnp.zeros_like(gains)
    for c in first.values():
        c.wait_send()
    load_t.wait()
    swaps = [norm(0)]
    swaps[0].wait_recv()
    hidden_part(0)
    second(1)
    swaps.append(back_part(0))
    out_swaps = [out_part(0)]
    swaps[1].wait_recv()
    norm_back(0)
    spread_begin(0)
    swaps.append(norm(1))
    swaps[2].wait_recv()
    hidden_part(1)
    spread_on(0)
    swaps.append(back_part(1))
    out_swaps.append(out_part(1))
    swaps[3].wait_recv()
    norm_back(1)
    spread_begin(1)
    resid_copy = start(pltpu.make_async_copy(resid_grad, resid_out, lsem.at[0]))

    def weights_part(left, right, out):
        def spill(slot, i):
            return pltpu.make_async_copy(stage.at[slot], out.at[rows_at(i * 256, 256), :], ssem.at[slot])

        @pl.loop(0, width // 256)
        def _(i):
            slot = i % 3

            @pl.when(i >= 3)
            def _():
                spill(slot, i - 3).wait()

            stage[slot] = tn(left[:, rows_at(i * 256, 256)], right[...]).astype(BF16)
            spill(slot, i).start()

        for k in (3, 2, 1):
            i = width // 256 - k
            spill(i % 3, i).wait()

    weights_part(cot, act, fd)
    spread_on(1)
    spread_end(0)
    for h in range(2):
        out_swaps[h].wait_recv()

        @pl.loop(0, hr, step=step)
        def _(r):
            at = pl.ds(pl.multiple_of(h * hr + r, step), step)
            own = dact[pl.ds(pl.multiple_of(h * rows + r, step), step), :]
            tok[at, :] = (resid[at, :] + own + share[3, at, :].astype(F32)).astype(BF16)

    out_copy = start(pltpu.make_async_copy(tok, block_out, lsem.at[1]))
    weights_part(xn, du, fu)
    spread_end(1)
    resid_copy.wait()
    out_copy.wait()
    for h in range(2):
        spread["own", h].wait()
        for m in range(4):
            spread["core", m, h].wait()
        for key in ((1, 0, h), (1, 1, h), (2, 0, h), (2, 1, h), ("g1", h), ("g2", h)):
            spread[key].wait_send()
    for c in swaps + out_swaps + list(sends.values()):
        c.wait_send()


def ffn_part(gated, w_out, tokens, gain, bias, w_up, w_down, cotangent, cid):
    rows, width = tokens.shape
    assert PLANE * gated.shape[1] == width and w_out.shape == (2 * rows, w_up.shape[1])
    span, hidden = 2 * rows, w_up.shape[1]
    sd = jax.ShapeDtypeStruct
    return comm_call(
        ffn_kernel,
        [
            sd((rows, width), BF16),
            sd((rows, width), F32),
            sd((8, width), F32),
            sd((2 * PLANE * rows, width), BF16),
            sd((width, hidden), BF16),
            sd((width, hidden), BF16),
        ],
        [gated, w_out, tokens, gain[None], bias[None], w_up, w_down, cotangent],
        [
            pltpu.VMEM((rows, width), BF16),
            pltpu.VMEM((rows, width), F32),
            pltpu.VMEM((PLANE, span, width), BF16),
            pltpu.VMEM(w_up.shape, BF16),
            pltpu.VMEM(w_down.shape, BF16),
            pltpu.VMEM((PLANE, rows, width), BF16),
            pltpu.VMEM((2, rows, width // 2), BF16),
            pltpu.VMEM((2, rows, width // 2), BF16),
            pltpu.VMEM((rows, width // 2), BF16),
            pltpu.VMEM((rows, width // 2), BF16),
            pltpu.VMEM((rows, width), F32),
            pltpu.VMEM((span, width), BF16),
            pltpu.VMEM((span, hidden), BF16),
            pltpu.VMEM((span, hidden), F32),
            pltpu.VMEM((span, hidden), BF16),
            pltpu.VMEM((span, width), BF16),
            pltpu.VMEM((rows, width), BF16),
            pltpu.VMEM((3, 256, hidden), BF16),
            pltpu.VMEM((rows, 512), F32),
            DMA((8,)),
            DMA((PLANE,)),
            DMA((PLANE, 2)),
            DMA((PLANE, 2)),
            DMA((6, 2)),
            DMA((6, 2)),
            DMA((3, 2)),
            DMA((3, 2)),
            DMA((6, 2)),
            DMA((6, 2)),
            DMA((4, 2)),
            DMA((4, 2)),
            DMA((3,)),
            DMA((width // 512,)),
        ],
        cid,
        in_specs=[ANY, ANY, ANY, VM, VM, ANY, ANY, ANY],
        out_specs=[ANY, ANY, VM, ANY, ANY, ANY],
    )


def attention_kernel(
    widths, by_rows,
    tok_ref, gain_ref, bias_ref, dec_ref, cbase, sbase, coff, soff, *refs,
):
    count = len(widths)
    shards_in, refs = refs[:count], refs[count:]
    (xg, q_out, k_out, v_out, gate_out, ret_out, gated_out, states_out, cos_out, sin_out, ccol_out, crow_out, scal_out), refs = (
        refs[:13], refs[13:],
    )
    full, refs = refs[:count], refs[count:]
    hold, refs = refs[:count], refs[count:]
    wl, refs = refs[: count - 1], refs[count - 1 :]
    (tok, ccol, crow, scal, xn, xv, q, k, v, gate, ret, gated, cos, sin, kv, st, sloc, sgot, decg,
     lsem, psend, precv, usend, dsend, zrecv, xsend, xrecv, csend, crecv, tsend, trecv, ssend, srecv, osem, wsem) = refs
    me = Place()
    z, p, f = me.z, me.p, me.f
    spot = z * PLANE + p
    chunk = hold[0].shape[0]
    deep = chunk * PLANE
    tokens, width = xv.shape
    rows = tok_ref.shape[0]
    keys, values = q.shape[1], v.shape[1]
    half = keys // 2
    blocks = tokens // STRETCH
    greet(
        [(me.plane(m), None) for m in (1, 2, 3)]
        + [(me.partner(), None), (me.up(), z < LINE - 1), (me.down(), z > 0)]
    )

    def part(i, at):
        w = widths[i]
        if by_rows[i]:
            return shards_in[i].at[pl.ds(pl.multiple_of(at * w, w), w), :]
        return shards_in[i].at[:, pl.ds(pl.multiple_of(at * w, w), w)]

    def slot(i, ss):
        at = pl.ds(pl.multiple_of(ss * chunk, chunk), chunk)
        return full[i].at[:, at] if by_rows[i] else full[i].at[at, :]

    def block(i, zz):
        at = pl.ds(pl.multiple_of(zz * deep, deep), deep)
        return full[i].at[:, at] if by_rows[i] else full[i].at[at, :]

    def up_copy(i, zz):
        return remote(block(i, zz), block(i, zz), usend.at[i, zz], zrecv.at[i, zz], me.up())

    def down_copy(i, zz):
        return remote(block(i, zz), block(i, zz), dsend.at[i, zz], zrecv.at[i, zz], me.down())

    def part_copies(i, src, at):
        return (
            remote(src, slot(i, at), usend.at[i, z], zrecv.at[i, z], me.up()),
            remote(src, slot(i, at), dsend.at[i, z], zrecv.at[i, z], me.down()),
        )

    def to_line(copies):
        @pl.when(z < LINE - 1)
        def _():
            copies[0].start()

        @pl.when(z > 0)
        def _():
            copies[1].start()

    ahead = 2
    for i in range(ahead):
        to_line(part_copies(i, part(i, p), spot))
    load_t = start(pltpu.make_async_copy(tok_ref, tok, lsem.at[count + 1]))
    local, plane, held = [], [], []
    for i in range(count):
        held.append(start(pltpu.make_async_copy(part(i, p), hold[i], lsem.at[i])))
        local.append(pltpu.make_async_copy(hold[i], slot(i, spot), lsem.at[i]))
        plane.append(
            [
                start(remote(part(i, me.xor(m)), slot(i, spot), psend.at[i, m], precv.at[i, m], me.plane(m)))
                for m in (1, 2, 3)
            ]
        )
    tiny = [start(remote(dec_ref, decg.at[p], tsend.at[m], trecv.at[m], me.plane(m))) for m in (1, 2, 3)]
    tiny_own = start(pltpu.make_async_copy(dec_ref, decg.at[p], tsend.at[0]))
    step = 32
    load_t.wait()

    @pl.loop(0, rows, step=step)
    def _(r):
        at = rows_at(r, step)
        t = tok[at, :].astype(F32)
        centered = t - jnp.mean(t, axis=1, keepdims=True)
        scale = lax.rsqrt(jnp.mean(centered * centered, axis=1, keepdims=True) + 1e-05)
        xn[at, :] = (centered * scale * gain_ref[...] + bias_ref[...]).astype(BF16)

    def seat(m, h=None):
        base = (me.xor(m) * 2 + f) * rows
        if h is None:
            return xv.at[rows_at(base, rows)]
        return xv.at[pl.ds(pl.multiple_of(base + h * (rows // 2), rows // 2), rows // 2)]

    x_own = start(pltpu.make_async_copy(xn, seat(0), lsem.at[count]))
    x1 = start(remote(xn, seat(0), xsend.at[0], xrecv.at[0], me.plane(1)))
    x2 = start(remote(xn, seat(0), xsend.at[1], xrecv.at[1], me.plane(2)))
    xc = start(remote(xn, seat(0), csend.at[0], crecv.at[0], me.partner()))
    for i in range(count):
        held[i].wait()
        local[i].start()

    def own(i):
        local[i].wait()
        for c in plane[i]:
            c.wait_recv()
        if i < ahead:
            for m in (1, 2, 3):
                at = z * PLANE + me.xor(m)
                to_line(part_copies(i, slot(i, at), at))
        else:
            to_line((up_copy(i, z), down_copy(i, z)))

    def forward(i, t):
        @pl.when(z - t >= 0)
        def _():
            up_copy(i, z - t).wait_recv()

            @pl.when(z < LINE - 1)
            def _():
                up_copy(i, z - t).start()

        @pl.when(z + t < LINE)
        def _():
            down_copy(i, z + t).wait_recv()

            @pl.when(z > 0)
            def _():
                down_copy(i, z + t).start()

    def fetch(i):
        forward(i, LINE - 1)
        return start(pltpu.make_async_copy(full[i], wl[i], wsem.at[i]))

    K, V, Q, G, O = range(count)
    own(K)
    own(V)
    forward(K, 1)
    forward(K, 2)
    own(Q)

    for c in tiny:
        c.wait()
    tiny_own.wait()
    heads = lax.broadcasted_iota(jnp.int32, decg.shape[1:], 0)
    lines = [jnp.sum(jnp.where(heads == p, decg[j], 0.0), axis=0, keepdims=True) for j in range(blocks)]
    lines = jnp.concatenate(lines + [jnp.zeros_like(lines[0])] * (8 - blocks), axis=0)
    i0 = lax.broadcasted_iota(jnp.int32, (STRETCH, STRETCH), 0)
    i1 = lax.broadcasted_iota(jnp.int32, (STRETCH, STRETCH), 1)
    row_sums = jnp.dot(
        lines, jnp.where(i0 <= i1, 1.0, 0.0), preferred_element_type=F32, precision=lax.Precision.HIGHEST
    )
    col_sums = lax.dot_general(
        jnp.where(i1 <= i0, 1.0, 0.0), lines, (((1,), (1,)), ((), ())),
        preferred_element_type=F32, precision=lax.Precision.HIGHEST,
    )
    total = jnp.zeros((1, 1), F32)
    for c in range(blocks):
        end = row_sums[c : c + 1, STRETCH - 1 : STRETCH]
        crow[c] = jnp.broadcast_to(row_sums[c : c + 1, :], (8, STRETCH))
        ccol[c * STRETCH : (c + 1) * STRETCH, :] = col_sums[:, c : c + 1]
        scal[c] = jnp.broadcast_to(jnp.exp(end), (8, 128))
        scal[blocks + c] = jnp.broadcast_to(jnp.exp(total), (8, 128))
        total = total + end
    scal[2 * blocks] = jnp.broadcast_to(total, (8, 128))

    fine = coff.shape[0]

    @pl.loop(0, tokens // fine)
    def _(a):
        at = rows_at(a * fine, fine)
        place = pl.ds(z * (tokens // fine) + a, 1)
        ca, sa = cbase[place, :], sbase[place, :]
        cos[at, :] = ca * coff[...] - sa * soff[...]
        sin[at, :] = sa * coff[...] + ca * soff[...]

    forward(V, 1)
    x1.wait_recv()
    g1 = start(remote(seat(1, 0), seat(1, 0), xsend.at[2], xrecv.at[2], me.plane(2)))
    c1 = start(remote(seat(1), seat(1), csend.at[1], crecv.at[1], me.partner()))
    x2.wait_recv()
    g2 = start(remote(seat(2, 1), seat(2, 1), xsend.at[3], xrecv.at[3], me.plane(1)))
    c2 = start(remote(seat(2), seat(2), csend.at[2], crecv.at[2], me.partner()))
    forward(V, 2)
    forward(Q, 1)
    own(G)
    forward(Q, 2)
    own(O)
    load_k = fetch(K)
    g1.wait_recv()
    g2.wait_recv()
    c3 = start(remote(seat(3), seat(3), csend.at[3], crecv.at[3], me.partner()))
    x_own.wait()
    for c in (xc, c1, c2, c3):
        c.wait_recv()
    outs = []

    def put(src, dst):
        outs.append(start(pltpu.make_async_copy(src, dst, osem.at[len(outs)])))

    put(xv, xg)
    put(ccol, ccol_out)
    put(crow, crow_out)
    put(scal, scal_out)
    put(cos, cos_out)
    put(sin, sin_out)
    load_k.wait()

    def turned(at, w, dst):
        y = nn(xv[at, :], w[...])
        a, b = y[:, :half], y[:, half:]
        dst[at, :half] = (a * cos[at, :] - b * sin[at, :]).astype(BF16)
        dst[at, half:] = (b * cos[at, :] + a * sin[at, :]).astype(BF16)

    @pl.loop(0, blocks)
    def _(c):
        turned(rows_at(c * STRETCH, STRETCH), wl[K], k)

    fetch(V).wait()

    @pl.loop(0, blocks)
    def _(c):
        at = rows_at(c * STRETCH, STRETCH)
        val = nn(xv[at, :], wl[V][...]).astype(BF16)
        v[at, :] = val
        end = crow[c, 0:1, STRETCH - 1 : STRETCH]
        kv[c] = tn(k[at, :], (val.astype(F32) * jnp.exp(end - ccol[at, :])).astype(BF16))

    put(k, k_out)
    put(v, v_out)
    sloc[...] = kv[0]
    kv[0] = jnp.zeros_like(sloc)
    for c in range(1, blocks):
        nxt = sloc[...] * scal[c, 0:1, 0:1] + kv[c]
        kv[c] = sloc[...]
        sloc[...] = nxt

    def state_copy(zz):
        return remote(st.at[0], sgot, ssend.at[zz], srecv.at[zz], me.up())

    def send_state():
        st[0] = sloc[...].astype(BF16)
        state_copy(0).start()

    @pl.when(z == 0)
    def _():
        send_state()

    def pass_state(zz):
        @pl.when(z == zz)
        def _():
            state_copy(0).wait_recv()
            if zz < LINE - 1:
                sloc[...] = sloc[...] + sgot[...].astype(F32) * jnp.exp(scal[2 * blocks, 0:1, 0:1])
                send_state()

    pass_state(1)
    forward(G, 1)
    forward(O, 1)
    fetch(Q).wait()
    t_size = 256

    @pl.loop(0, blocks)
    def _(c):
        blk = rows_at(c * STRETCH, STRETCH)
        turned(blk, wl[Q], q)
        row = crow[c, 0:1, :]
        for r in range(0, STRETCH, t_size):
            at = rows_at(c * STRETCH + r, t_size)
            col = ccol[at, :]
            t_index = lax.broadcasted_iota(jnp.int32, (t_size, STRETCH), 0) + r
            s_index = lax.broadcasted_iota(jnp.int32, (t_size, STRETCH), 1)
            mask = jnp.where(t_index >= s_index, jnp.exp(jnp.minimum(col - row, 0.0)), 0.0)
            scores = (nt(q[at, :], k[blk, :]) * mask).astype(BF16)
            ret[at, :] = nn(scores, v[blk, :])

    put(q, q_out)
    pass_state(2)
    forward(G, 2)
    forward(O, 2)
    pass_state(3)

    @pl.when((z > 0) & (z < LINE - 1))
    def _():
        state_copy(0).wait_send()

    @pl.when(z == 0)
    def _():
        state_copy(0).wait_send()
        sgot[...] = jnp.zeros_like(sgot)

    for c in range(blocks):
        st[c] = (kv[c] + sgot[...].astype(F32) * scal[blocks + c, 0:1, 0:1]).astype(BF16)

    @pl.loop(0, blocks)
    def _(c):
        at = rows_at(c * STRETCH, STRETCH)
        decayed = (q[at, :].astype(F32) * jnp.exp(ccol[at, :])).astype(BF16)
        ret[at, :] += nn(decayed, st[c])

    put(ret, ret_out)
    put(st, states_out)
    fetch(G).wait()

    @pl.loop(0, tokens, step=256)
    def _(r):
        at = rows_at(r, 256)
        g = nn(xv[at, :], wl[G][...])
        gate[at, :] = g
        t = ret[at, :]
        centered = t - jnp.mean(t, axis=1, keepdims=True)
        scale = lax.rsqrt(jnp.mean(centered * centered, axis=1, keepdims=True) + 1e-05)
        gated[at, :] = (g / (1.0 + jnp.exp(-g)) * centered * scale).astype(BF16)

    put(gate, gate_out)
    put(gated, gated_out)
    forward(O, LINE - 1)
    for c in (xc, c1, c2, c3, x1, x2, g1, g2):
        c.wait_send()
    for i in range(count):
        for c in plane[i]:
            c.wait_send()
        for zz in range(LINE):

            @pl.when((z < LINE - 1) & (zz <= z))
            def _():
                up_copy(i, zz).wait_send()

            @pl.when((z > 0) & (zz >= z))
            def _():
                down_copy(i, zz).wait_send()

    for c in outs:
        c.wait()


def attention(tokens, gain, bias, decays, tables, shards_in, by_rows, cid):
    rows, width = tokens.shape
    count = len(shards_in)
    chunk = shards_in[0].shape[0]
    group = 2 * PLANE * rows
    blocks = group // STRETCH
    parts = [
        (w.shape[0] // PLANE, chunk) if r else (chunk, w.shape[1] // PLANE) for w, r in zip(shards_in, by_rows)
    ]
    widths = [s[0] if r else s[1] for s, r in zip(parts, by_rows)]
    wholes = [(s[0], width) if r else (width, s[1]) for s, r in zip(parts, by_rows)]
    values, keys = widths[1], widths[0]
    half = keys // 2
    sd = jax.ShapeDtypeStruct
    outs = [
        sd((group, width), BF16),
        sd((group, keys), BF16),
        sd((group, keys), BF16),
        sd((group, values), BF16),
        sd((group, values), F32),
        sd((group, values), F32),
        sd((group, values), BF16),
        sd((blocks, keys, values), BF16),
        sd((group, half), F32),
        sd((group, half), F32),
        sd((group, 1), F32),
        sd((blocks, 8, STRETCH), F32),
        sd((2 * blocks + 1, 8, 128), F32),
    ] + [sd(s, BF16) for s in wholes]
    scratch = (
        [pltpu.VMEM(s, BF16) for s in parts]
        + [pltpu.VMEM(s, BF16) for s in wholes[:-1]]
        + [
            pltpu.VMEM((rows, width), BF16),
            pltpu.VMEM((group, 1), F32),
            pltpu.VMEM((blocks, 8, STRETCH), F32),
            pltpu.VMEM((2 * blocks + 1, 8, 128), F32),
            pltpu.VMEM((rows, width), BF16),
            pltpu.VMEM((group, width), BF16),
            pltpu.VMEM((group, keys), BF16),
            pltpu.VMEM((group, keys), BF16),
            pltpu.VMEM((group, values), BF16),
            pltpu.VMEM((group, values), F32),
            pltpu.VMEM((group, values), F32),
            pltpu.VMEM((group, values), BF16),
            pltpu.VMEM((group, half), F32),
            pltpu.VMEM((group, half), F32),
            pltpu.VMEM((blocks, keys, values), F32),
            pltpu.VMEM((blocks, keys, values), BF16),
            pltpu.VMEM((keys, values), F32),
            pltpu.VMEM((keys, values), BF16),
            pltpu.VMEM((PLANE,) + decays.shape, F32),
            DMA((count + 2,)),
            DMA((count, PLANE)),
            DMA((count, PLANE)),
            DMA((count, LINE)),
            DMA((count, LINE)),
            DMA((count, LINE)),
            DMA((4,)),
            DMA((4,)),
            DMA((4,)),
            DMA((4,)),
            DMA((PLANE,)),
            DMA((PLANE,)),
            DMA((1,)),
            DMA((1,)),
            DMA((16,)),
            DMA((count,)),
        ]
    )
    return comm_call(
        functools.partial(attention_kernel, widths, by_rows),
        outs,
        [tokens, gain[None], bias[None], decays] + list(tables) + list(shards_in),
        scratch,
        cid,
        in_specs=[ANY] + [VM] * 7 + [ANY] * count,
        out_specs=[ANY] * (13 + count),
    )


class LineSum:
    def __init__(self, me, own, rx, usend, urecv, dsend, drecv, add):
        self.me, self.own, self.rx, self.add = me, own, rx, add
        self.sems = usend, urecv, dsend, drecv

    def up(self, src, zz):
        return remote(src, self.rx.at[zz], self.sems[0].at[zz], self.sems[1].at[zz], self.me.up())

    def down(self, src, zz):
        slot = jnp.where(zz == self.me.z - 1, LINE, zz)
        return remote(src, self.rx.at[slot], self.sems[2].at[zz], self.sems[3].at[zz], self.me.down())

    def begin(self, order=(3, 2, 1), src=None):
        src = src or self.own
        for zz in order:

            @pl.when(self.me.z == 0)
            def _():
                self.up(src(zz), zz).start()

            @pl.when(self.me.z == LINE - 1)
            def _():
                self.down(src(LINE - 1 - zz), LINE - 1 - zz).start()

    def pass_up(self, zz):
        self.up(self.own(zz), zz).wait_recv()
        self.add(self.rx.at[zz], self.own(zz))
        self.up(self.rx.at[zz], zz).start()

    def pass_down(self, zz):
        self.down(self.own(zz), zz).wait_recv()
        self.add(self.rx.at[zz], self.own(zz))
        self.down(self.rx.at[zz], zz).start()

    def near(self, k):
        @pl.when(self.me.z == 1)
        def _():
            self.pass_up(LINE - 1 - k)

        @pl.when(self.me.z == 2)
        def _():
            self.pass_down(k)

    def far(self):
        @pl.when(self.me.z == 1)
        def _():
            self.pass_down(0)

        @pl.when(self.me.z == 2)
        def _():
            self.pass_up(LINE - 1)

    def arrive(self):
        z = self.me.z

        @pl.when(z > 0)
        def _():
            self.up(self.own(z), z).wait_recv()

        @pl.when(z < LINE - 1)
        def _():
            self.down(self.own(z), z).wait_recv()

    def finish(self):
        z = self.me.z
        for zz in range(LINE):

            @pl.when((z < LINE - 1) & (zz > z))
            def _():
                self.up(self.own(zz), zz).wait_send()

            @pl.when((z > 0) & (zz < z))
            def _():
                self.down(self.own(zz), zz).wait_send()


def add_rows(dst, src):
    rows = dst.shape[0]
    step = 32 if dst.shape[1] > 512 else 128

    @pl.loop(0, rows, step=step)
    def _(r):
        at = rows_at(r, step)
        dst[at, :] = (dst[at, :].astype(F32) + src[at, :].astype(F32)).astype(BF16)


def total_rows(z, dst, own, rx):
    rows = dst.shape[0]
    step = 32 if dst.shape[1] > 512 else 128

    @pl.loop(0, rows, step=step)
    def _(r):
        at = rows_at(r, step)
        v = own[at, :].astype(F32)
        v = v + jnp.where(z > 0, rx[z, at, :].astype(F32), 0.0)
        v = v + jnp.where(z < LINE - 1, rx[LINE, at, :].astype(F32), 0.0)
        dst[at, :] = v.astype(dst.dtype)


def line_sems():
    return [DMA((LINE,)) for _ in range(4)]


def retention_back_kernel(
    da_ref, wo_ref, gated_ref, gate_ref, ret_ref, q_ref, k_ref, v_ref, s_ref, cos_ref, sin_ref,
    ccol_in, crow_in, scal_in, xg_ref, fu_ref, fd_ref,
    dh_out, sums, gate_fin, f1, av_out, aq_out,
    ccol_ref, crow_ref, scal_ref, dh, da, wo, gated, gr, q, k, v, st, cos, sin, dr, xt, ao, ag, rxo, rxg, fin, qo, gb, lg, got, rxf, fo, pbuf, gbuf,
    lsem, gsem, xsem, fsend, frecv, osem, fosem, ssend, srecv, psend, precv, *line,
):
    me = Place()
    z, p = me.z, me.p
    greeted = call(
        [(me.plane(m), None) for m in (1, 2, 3)]
        + [(me.up(), z < LINE - 1), (me.down(), z > 0)]
    )
    width = da.shape[1]
    tokens = da.shape[0]
    keys, values = q.shape[1], v.shape[1]
    blocks = tokens // STRETCH
    half = keys // 2
    pq = [me.xor(m) for m in range(4)]
    chunk = fu_ref.shape[0] // SPANS

    def f_block(h, zp, place):
        return (fu_ref, fd_ref)[h].at[pl.ds(pl.multiple_of((zp * PLANE + place) * chunk, chunk), chunk), :]

    units = [(h, zp, (0, 1)) for zp in (3, 0, 2) for h in range(2)] + [(h, 1, (1,)) for h in range(2)]

    def f_slot(h, zp, j):
        return rxf.at[h, 2 * (3, 0, 2, 1).index(zp) + (j if zp != 1 else 0)]
    away = ((1, 3), (2, 3))
    kept = ((0, 2), (0, 1))
    nbr = (1, 2)

    def f_copy(h, zp, j):
        return remote(
            f_block(h, zp, pq[away[h][j]]), f_slot(h, zp, j), fsend.at[h, zp, j], frecv.at[h, zp, j], me.plane(nbr[h])
        )

    deep = width // LINE
    ends_first = [jnp.where(z < LINE // 2, LINE - 1 - i, i) for i in range(LINE)]

    def slab(i):
        at = rows_at(ends_first[i] * deep, deep)
        return pltpu.make_async_copy(da_ref.at[:, at], da.at[:, at], lsem.at[12 + i])

    slab(0).start()
    loads = [
        start(pltpu.make_async_copy(a, b, lsem.at[i]))
        for i, (a, b) in enumerate(
            [(gated_ref, gated), (wo_ref, wo), (q_ref, q), (k_ref, k), (v_ref, v), (s_ref, st),
             (cos_ref, cos), (sin_ref, sin), (ccol_in, ccol_ref), (crow_in, crow_ref), (scal_in, scal_ref)]
        )
    ]
    for i in range(1, LINE):
        slab(i).start()

    def f_own(u):
        h, zp, js = units[u]
        return [
            pltpu.make_async_copy(f_block(h, zp, pq[kept[h][j]]), fo.at[u % 2, j], fosem.at[u % 2, j])
            for j in js
        ]

    def f_out(u):
        h, zp, js = units[u]
        return [pltpu.make_async_copy(f_slot(h, zp, j), f1.at[h, zp, j], osem.at[u, j]) for j in js]

    for u in range(2):
        for c in f_own(u):
            c.start()

    def f_unit(u):
        h, zp, js = units[u]
        for j, c in zip(js, f_own(u)):
            c.wait()
            f_copy(h, zp, j).wait_recv()
            add_rows(f_slot(h, zp, j), fo.at[u % 2, j])
        for c in f_out(u):
            c.start()
        if u + 2 < len(units):
            for c in f_own(u + 2):
                c.start()

    def tile_rows(i):
        return rows_at(i * 256, 256)

    def gate_loads(i):
        at = tile_rows(i)
        slot = i % 3
        return (
            pltpu.make_async_copy(gate_ref.at[at, :], gr.at[slot, 0], gsem.at[slot, 0]),
            pltpu.make_async_copy(ret_ref.at[at, :], gr.at[slot, 1], gsem.at[slot, 1]),
        )

    for c in gate_loads(0) + gate_loads(1):
        c.start()

    out_sum = LineSum(me, lambda zz: ao.at[rows_at(zz * (width // LINE), width // LINE), :], rxo, *line[:4], add_rows)
    gate_sum = LineSum(me, lambda zz: ag.at[rows_at(zz * (width // LINE), width // LINE), :], rxg, *line[4:], add_rows)

    loads[0].wait()
    for turn in range(LINE):
        slab(turn).wait()

        @pl.loop(0, deep, step=256)
        def _(i):
            at = rows_at(ends_first[turn] * deep + i, 256)
            ao[at, :] = tn(da[:, at], gated[...]).astype(BF16)

        if turn == 0:
            meet(greeted)
        if turn < 2:
            out_sum.begin((LINE - 1 - turn,))
        if turn == 0:
            for h, zp, js in units:
                for j in js:
                    f_copy(h, zp, j).start()
    for c in loads[1:]:
        c.wait()

    tiles = tokens // 256

    @pl.loop(0, tiles)
    def _(i):
        @pl.when(i + 2 < tiles)
        def _():
            for c in gate_loads(i + 2):
                c.start()

        for c in gate_loads(i):
            c.wait()
        at = tile_rows(i)
        slot = i % 3
        dgated = nt(da[at, :], wo[...])
        gate = gr[slot, 0]
        ret = gr[slot, 1]
        centered = ret - jnp.mean(ret, axis=1, keepdims=True)
        scale = lax.rsqrt(jnp.mean(centered * centered, axis=1, keepdims=True) + 1e-05)
        grouped = centered * scale
        sig = 1.0 / (1.0 + jnp.exp(-gate))
        silu = gate * sig
        dh[at, 2 * keys + values :] = (dgated * grouped * (sig * (1.0 + gate * (1.0 - sig)))).astype(BF16)
        dg = dgated * silu
        dr[at, :] = (
            scale * (dg - jnp.mean(dg, axis=1, keepdims=True) - grouped * jnp.mean(dg * grouped, axis=1, keepdims=True))
        ).astype(BF16)

    lg[...] = jnp.zeros_like(lg)

    @pl.loop(0, blocks)
    def _(c):
        at = rows_at(c * STRETCH, STRETCH)
        decayed = (q[at, :].astype(F32) * jnp.exp(ccol_ref[at, :])).astype(BF16)
        got_q = tn(decayed, dr[at, :])
        qo[c] = got_q
        lg[...] += scal_ref[blocks + c, 0:1, 0:1] * got_q

    state_copy = remote(gb.at[0], got, ssend.at[0], srecv.at[0], me.down())

    def pass_state(zz):
        @pl.when(z == zz)
        def _():
            if zz < LINE - 1:
                state_copy.wait_recv()
            if zz > 0:
                add = lg[...]
                if zz < LINE - 1:
                    add = add + got[...].astype(F32) * jnp.exp(scal_ref[2 * blocks, 0:1, 0:1])
                gb[0] = add.astype(BF16)
                state_copy.start()

    pass_state(LINE - 1)
    out_sum.begin((1,))
    out_sum.near(0)
    def x_tile(i):
        return pltpu.make_async_copy(xg_ref.at[:, rows_at(i * 256, 256)], xt.at[i % 3], xsem.at[i % 3])

    x_tile(0).start()
    x_tile(1).start()

    @pl.loop(0, width // 256)
    def _(i):
        @pl.when(i + 2 < width // 256)
        def _():
            x_tile(i + 2).start()

        x_tile(i).wait()
        ag[rows_at(i * 256, 256), :] = tn(xt[i % 3], dh[:, 2 * keys + values :]).astype(BF16)

    gate_sum.begin()
    out_sum.near(1)
    pass_state(2)
    f_unit(0)
    f_unit(1)
    out_sum.far()

    pass_state(1)
    pass_state(0)

    @pl.when(z > 0)
    def _():
        state_copy.wait_send()

    @pl.when(z < LINE - 1)
    def _():
        lg[...] = got[...].astype(F32)

    @pl.when(z == LINE - 1)
    def _():
        lg[...] = jnp.zeros_like(lg)

    for c in reversed(range(blocks)):
        gb[c] = lg[...].astype(BF16)
        if c:
            lg[...] = lg[...] * scal_ref[c, 0:1, 0:1] + qo[c]

    t_size = 256

    @pl.loop(0, blocks)
    def _(c):
        blk = rows_at(c * STRETCH, STRETCH)
        row = crow_ref[c, 0:1, :]
        end = crow_ref[c, 0:1, STRETCH - 1 : STRETCH]
        for r in range(0, STRETCH, t_size):
            at = rows_at(c * STRETCH + r, t_size)
            col = ccol_ref[at, :]
            t_index = lax.broadcasted_iota(jnp.int32, (t_size, STRETCH), 0) + r
            s_index = lax.broadcasted_iota(jnp.int32, (t_size, STRETCH), 1)
            mask = jnp.where(t_index >= s_index, jnp.exp(jnp.minimum(col - row, 0.0)), 0.0)
            pbuf[r : r + t_size, :] = (nt(q[at, :], k[blk, :]) * mask).astype(BF16)
            g = (nt(dr[at, :], v[blk, :]) * mask).astype(BF16)
            gbuf[r : r + t_size, :] = g
            dq = nt(dr[at, :], st[c]) * jnp.exp(col) + nn(g, k[blk, :])
            a, b = dq[:, :half], dq[:, half:]
            dh[at, :half] = (a * cos[at, :] + b * sin[at, :]).astype(BF16)
            dh[at, half:keys] = (b * cos[at, :] - a * sin[at, :]).astype(BF16)
        for r in range(0, STRETCH, t_size):
            at = rows_at(c * STRETCH + r, t_size)
            tail = jnp.exp(end - ccol_ref[at, :])
            w = (v[at, :].astype(F32) * tail).astype(BF16)
            dk = nt(w, gb[c]) + tn(gbuf[:, r : r + t_size], q[blk, :])
            a, b = dk[:, :half], dk[:, half:]
            dh[at, keys : keys + half] = (a * cos[at, :] + b * sin[at, :]).astype(BF16)
            dh[at, keys + half : 2 * keys] = (b * cos[at, :] - a * sin[at, :]).astype(BF16)
            dv = nn(k[at, :], gb[c]) * tail + tn(pbuf[:, r : r + t_size], dr[blk, :])
            dh[at, 2 * keys : 2 * keys + values] = dv.astype(BF16)

    dh_copy = start(pltpu.make_async_copy(dh, dh_out, lsem.at[2]))
    plane = []

    def deal(i, chain, a):
        chain.arrive()
        total_rows(z, fin.at[i], a.at[rows_at(z * (width // LINE), width // LINE), :], chain.rx)
        cols = pl.ds(i * values, values)
        for m in (1, 2, 3):
            plane.append(
                start(
                    remote(
                        fin.at[i, rows_at(pq[m] * chunk, chunk), :], sums.at[p, :, cols],
                        psend.at[i, m], precv.at[i, m], me.plane(m),
                    )
                )
            )
        plane.append(
            start(
                pltpu.make_async_copy(
                    fin.at[i, rows_at(p * chunk, chunk), :], sums.at[p, :, cols], psend.at[i, 0]
                )
            )
        )

    gate_sum.near(0)
    for u in range(2, 4):
        f_unit(u)
    deal(0, out_sum, ao)
    gate_sum.near(1)
    gate_sum.far()
    x_tile(0).start()
    x_tile(1).start()
    wide = 2 * keys + values

    @pl.loop(0, width // 256)
    def _(i):
        @pl.when(i + 2 < width // 256)
        def _():
            x_tile(i + 2).start()

        x_tile(i).wait()
        da[rows_at(i * 256, 256), :wide] = tn(xt[i % 3], dh[:, :wide]).astype(BF16)

    to_last = [
        start(pltpu.make_async_copy(da.at[:, : 2 * keys], aq_out, lsem.at[0])),
        start(pltpu.make_async_copy(da.at[:, 2 * keys : wide], av_out, lsem.at[1])),
    ]
    for u in range(4, len(units)):
        f_unit(u)
    gate_sum.arrive()
    total_rows(z, fin.at[1], ag.at[rows_at(z * deep, deep), :], rxg)
    to_last.append(start(pltpu.make_async_copy(fin.at[1], gate_fin, lsem.at[3])))
    for c in plane + to_last + [dh_copy]:
        c.wait()
    out_sum.finish()
    gate_sum.finish()
    for u, (h, zp, js) in enumerate(units):
        for c in f_out(u):
            c.wait()
        for j in js:
            f_copy(h, zp, j).wait_send()


def retention_back(da, wo, gated, gate, ret, q, k, v, states, cos, sin, ccol, crow, scal, xg, fu, fd, cid):
    tokens, width = da.shape
    keys, values = q.shape[1], v.shape[1]
    chunk = width // SPANS
    blocks = tokens // STRETCH
    hidden = fu.shape[1]
    deep = width // LINE
    return comm_call(
        retention_back_kernel,
        [
            jax.ShapeDtypeStruct((tokens, 2 * keys + 2 * values), BF16),
            jax.ShapeDtypeStruct((PLANE, chunk, values), BF16),
            jax.ShapeDtypeStruct((deep, values), BF16),
            jax.ShapeDtypeStruct((2, LINE, 2, chunk, hidden), BF16),
            jax.ShapeDtypeStruct((width, values), BF16),
            jax.ShapeDtypeStruct((width, 2 * keys), BF16),
        ],
        [da, wo, gated, gate, ret, q, k, v, states, cos, sin, ccol, crow, scal, xg, fu, fd],
        [
            pltpu.VMEM(ccol.shape, F32),
            pltpu.VMEM(crow.shape, F32),
            pltpu.VMEM(scal.shape, F32),
            pltpu.VMEM((tokens, 2 * keys + 2 * values), BF16),
            pltpu.VMEM((tokens, width), BF16),
            pltpu.VMEM(wo.shape, BF16),
            pltpu.VMEM(gated.shape, BF16),
            pltpu.VMEM((3, 2, 256, values), F32),
            pltpu.VMEM(q.shape, BF16),
            pltpu.VMEM(k.shape, BF16),
            pltpu.VMEM(v.shape, BF16),
            pltpu.VMEM(states.shape, BF16),
            pltpu.VMEM(cos.shape, F32),
            pltpu.VMEM(sin.shape, F32),
            pltpu.VMEM((tokens, values), BF16),
            pltpu.VMEM((3, tokens, 256), BF16),
            pltpu.VMEM((width, values), BF16),
            pltpu.VMEM((width, values), BF16),
            pltpu.VMEM((LINE + 1, deep, values), BF16),
            pltpu.VMEM((LINE + 1, deep, values), BF16),
            pltpu.VMEM((2, deep, values), BF16),
            pltpu.VMEM((blocks, keys, values), F32),
            pltpu.VMEM((blocks, keys, values), BF16),
            pltpu.VMEM((keys, values), F32),
            pltpu.VMEM((keys, values), BF16),
            pltpu.VMEM((2, 2 * LINE - 1, chunk, hidden), BF16),
            pltpu.VMEM((2, 2, chunk, hidden), BF16),
            pltpu.VMEM((STRETCH, STRETCH), BF16),
            pltpu.VMEM((STRETCH, STRETCH), BF16),
            DMA((12 + LINE,)),
            DMA((3, 2)),
            DMA((3,)),
            DMA((2, LINE, 2)),
            DMA((2, LINE, 2)),
            DMA((2 * LINE, 2)),
            DMA((2, 2)),
            DMA((1,)),
            DMA((1,)),
            DMA((2, PLANE)),
            DMA((2, PLANE)),
        ]
        + line_sems()
        + line_sems(),
        cid,
        in_specs=[ANY] * 17,
        out_specs=[ANY] * 6,
    )


def last_kernel(
    dh_ref, av_ref, aq_ref, wq_ref, wk_ref, wv_ref, wg_ref, f1_ref, fu_ref, fd_ref, gate_ref, tok_ref, gain_ref, resid_ref, second_ref,
    grad_out, gains, fout, sums,
    tok, resid, rxl, dh, wh, share, rx0, rx1a, rx1b, rx2a, rx2b, av, aq, rxv, rxq, fin, rf2, kf, rxfa, rxfb, grx,
    lsem, ksem, lsend, lrecv, fsend, frecv, csend, crecv, xsend, xrecv, gsend, grecv, psend, precv, *line,
):
    me = Place()
    z, p, f = me.z, me.p, me.f
    rounds = [
        [me.at((z + t) % LINE, p, f) for t in range(1, LINE)],
        [me.partner()],
        [me.plane(m) for m in (1, 2, 3)],
    ]
    greet([(d, None) for r in rounds for d in r])
    width, keys2, values = av.shape[0], aq.shape[1], av.shape[1]
    rows = tok_ref.shape[0]
    pq = [me.xor(m) for m in range(4)]
    chunk = width // SPANS
    deep = width // LINE

    late = 1

    def f_copy(h, zp):
        return remote(f1_ref.at[h, zp, 1], rf2.at[h, zp], fsend.at[h, zp], frecv.at[h, zp], me.plane(2 - h))

    def f_block(h, place):
        return (fu_ref, fd_ref)[h].at[rows_at((late * PLANE + place) * chunk, chunk), :]

    def late_copy(h):
        return remote(f_block(h, pq[1 + h]), rxl.at[h], lsend.at[h], lrecv.at[h], me.plane(1 + h))

    def block_of(a, size):
        return lambda zz: a.at[rows_at(zz * size, size), :]

    v_sum = LineSum(me, block_of(av, deep), rxv, *line[:4], add_rows)
    q_sum = LineSum(me, block_of(aq, deep), rxq, *line[4:8], add_rows)
    fa_sum = LineSum(me, lambda zz: kf.at[0, zz], rxfa, *line[8:12], add_rows)
    fb_sum = LineSum(me, lambda zz: kf.at[1, zz], rxfb, *line[12:16], add_rows)
    v_sum.begin(src=block_of(av_ref, deep))
    q_sum.begin(src=block_of(aq_ref, deep))
    for zp in (3, 0, 2, 1):
        for h in range(2):
            f_copy(h, zp).start()
    for h in range(2):
        late_copy(h).start()
    load = start(pltpu.make_async_copy(dh_ref, dh, lsem.at[0]))
    owns = [
        start(pltpu.make_async_copy(av_ref, av, lsem.at[7])),
        start(pltpu.make_async_copy(aq_ref, aq, lsem.at[8])),
    ]
    loads, at = [], 0
    for i, w in enumerate((wq_ref, wk_ref, wv_ref, wg_ref)):
        size = w.shape[1]
        loads.append(start(pltpu.make_async_copy(w, wh.at[:, at : at + size], lsem.at[1 + i])))
        at += size
    keeps = []
    for h in range(2):
        for i, zp in enumerate((3, 0, 2)):
            keeps.append(start(pltpu.make_async_copy(f1_ref.at[h, zp, 0], kf.at[h, zp], ksem.at[h, i])))
        keeps.append(start(pltpu.make_async_copy(f_block(h, p), kf.at[h, late], ksem.at[h, 3])))
    rest = [
        start(pltpu.make_async_copy(tok_ref, tok, lsem.at[5])),
        start(pltpu.make_async_copy(resid_ref, resid, lsem.at[6])),
    ]

    load.wait()
    plane = []

    def deal(i, chain, a):
        chain.arrive()
        total_rows(z, fin.at[i], a.at[rows_at(z * deep, deep), :], chain.rx)
        spread(i, fin.at[i])

    def spread(i, src):
        cols = pl.ds(i * values, values)
        for m in (1, 2, 3):
            plane.append(
                start(
                    remote(
                        src.at[rows_at(pq[m] * chunk, chunk), :], sums.at[p, :, cols],
                        psend.at[i, m], precv.at[i, m], me.plane(m),
                    )
                )
            )
        plane.append(
            start(
                pltpu.make_async_copy(
                    src.at[rows_at(p * chunk, chunk), :], sums.at[p, :, cols], psend.at[i, 0]
                )
            )
        )

    gate_load = start(pltpu.make_async_copy(gate_ref, fin.at[2], lsem.at[9]))
    for c in loads + owns + [gate_load]:
        c.wait()

    own_rows, their_rows = rows_at(f * rows, rows), rows_at((1 - f) * rows, rows)
    wide = width // 2
    ca, cb = pl.ds(0, wide), pl.ds(wide, wide)
    everything, whole = pl.ds(0, width), pl.ds(0, wide)
    first, sends = {}, {}

    def share_part(m):
        at_rows = rows_at(pq[m] * 2 * rows, 2 * rows)

        @pl.loop(0, width, step=256)
        def _(c):
            at = rows_at(c, 256)
            share[m, :, at] = nt(dh[at_rows, :], wh[at, :]).astype(BF16)

        first[m] = start(
            remote(share.at[m, their_rows], rx0.at[m], csend.at[m], crecv.at[m], me.partner())
        )

    def pass_on(m):
        first[m].wait_recv()
        add_into(rx0.at[m], everything, share.at[m, own_rows], everything)
        k = 0 if m == 3 else 1
        if m & 1:
            sends["a", k] = start(
                remote(rx0.at[m, :, ca], rx1a.at[k], xsend.at[k], xrecv.at[k], me.plane(1))
            )
        if m & 2:
            sends["b", k] = start(
                remote(rx0.at[m, :, cb], rx1b.at[k], xsend.at[2 + k], xrecv.at[2 + k], me.plane(2))
            )

    share_part(3)
    share_part(1)
    pass_on(3)
    v_sum.near(0)
    share_part(2)
    pass_on(1)
    share_part(0)
    pass_on(2)
    v_sum.near(1)
    pass_on(0)
    for c in keeps:
        c.wait()
    v_sum.far()
    q_sum.near(0)
    for ends, turns in (((3, 0), (3,)), ((2, 1), (2,))):
        for zp in ends:
            for h in range(2):
                f_copy(h, zp).wait_recv()
                add_rows(kf.at[h, zp], rf2.at[h, zp])
                if zp == late:
                    late_copy(h).wait_recv()
                    add_rows(kf.at[h, zp], rxl.at[h])
        for zz in turns:
            fa_sum.begin((zz,))
            fb_sum.begin((zz,))
    q_sum.near(1)
    q_sum.far()
    sends["a", 0].wait_recv()
    add_into(rx1a.at[0], whole, rx0.at[2], ca)
    s2a = start(remote(rx1a.at[0], rx2a, xsend.at[4], xrecv.at[4], me.plane(2)))
    sends["b", 0].wait_recv()
    add_into(rx1b.at[0], whole, rx0.at[1], cb)
    s2b = start(remote(rx1b.at[0], rx2b, xsend.at[5], xrecv.at[5], me.plane(1)))
    spread(2, fin.at[2])
    deal(0, v_sum, av)
    fa_sum.near(0)
    sends["a", 1].wait_recv()
    sends["b", 1].wait_recv()
    deal(1, q_sum, aq)
    fb_sum.near(0)
    s2a.wait_recv()
    s2b.wait_recv()
    for c in rest:
        c.wait()
    gains[...] = jnp.zeros_like(gains)
    gains[2:4, :] = second_ref[0:2, :]
    step = 32

    @pl.loop(0, rows, step=step)
    def _(r):
        at = rows_at(r, step)
        left = rx0[0, at, ca].astype(F32) + rx1a[1, at, :].astype(F32) + rx2a[at, :].astype(F32)
        right = rx0[0, at, cb].astype(F32) + rx1b[1, at, :].astype(F32) + rx2b[at, :].astype(F32)
        dx = jnp.concatenate([left, right], axis=1)
        v = tok[at, :].astype(F32)
        centered = v - jnp.mean(v, axis=1, keepdims=True)
        scale = lax.rsqrt(jnp.mean(centered * centered, axis=1, keepdims=True) + 1e-05)
        hat = centered * scale
        gains[0:1, :] += jnp.sum(dx * hat, axis=0, keepdims=True)
        gains[1:2, :] += jnp.sum(dx, axis=0, keepdims=True)
        g = dx * gain_ref[...]
        back = scale * (
            g - jnp.mean(g, axis=1, keepdims=True) - hat * jnp.mean(g * hat, axis=1, keepdims=True)
        )
        tok[at, :] = (back + resid[at, :]).astype(BF16)

    out_copy = start(pltpu.make_async_copy(tok, grad_out, lsem.at[0]))

    def gain_copies(r):
        base = (0, 3, 4)[r]
        return [
            remote(gains, grx.at[base + i], gsend.at[base + i], grecv.at[base + i], d)
            for i, d in enumerate(rounds[r])
        ]

    def gain_begin(r):
        for c in gain_copies(r):
            c.start()

    def gain_end(r):
        for c in gain_copies(r):
            c.wait()
        for i in range(len(rounds[r])):
            gains[...] += grx[(0, 3, 4)[r] + i]

    gain_begin(0)
    fa_sum.begin((1,))
    fb_sum.begin((1,))
    fa_sum.near(1)
    fa_sum.far()
    gain_end(0)
    gain_begin(1)
    fb_sum.near(1)
    gain_end(1)
    gain_begin(2)
    fb_sum.far()
    gain_end(2)
    fa_sum.arrive()
    total_rows(z, fout.at[0], kf.at[0, z], rxfa)
    fb_sum.arrive()
    total_rows(z, fout.at[1], kf.at[1, z], rxfb)
    for c in plane + [out_copy]:
        c.wait()
    for h in range(2):
        late_copy(h).wait_send()
    for chain in (v_sum, q_sum, fa_sum, fb_sum):
        chain.finish()
    for c in list(first.values()) + list(sends.values()) + [s2a, s2b]:
        c.wait_send()
    for zp in range(LINE):
        for h in range(2):
            f_copy(h, zp).wait_send()


def last_sums(dh, av, aq, wq, wk, wv, wg, f1, fu, fd, gate_fin, tokens, gain, resid, second, cid):
    width = av.shape[0]
    rows = tokens.shape[0]
    keys, values = wq.shape[1], wv.shape[1]
    assert 2 * keys == values
    chunk, deep = width // SPANS, width // LINE
    hidden = f1.shape[-1]
    return comm_call(
        last_kernel,
        [
            jax.ShapeDtypeStruct((rows, width), BF16),
            jax.ShapeDtypeStruct((8, width), F32),
            jax.ShapeDtypeStruct((2, chunk, hidden), BF16),
            jax.ShapeDtypeStruct((PLANE, chunk, 3 * values), BF16),
        ],
        [dh, av, aq, wq, wk, wv, wg, f1, fu, fd, gate_fin, tokens, gain[None], resid, second],
        [
            pltpu.VMEM((rows, width), BF16),
            pltpu.VMEM((rows, width), F32),
            pltpu.VMEM((2, chunk, hidden), BF16),
            pltpu.VMEM(dh.shape, BF16),
            pltpu.VMEM((width, dh.shape[1]), BF16),
            pltpu.VMEM((PLANE, 2 * rows, width), BF16),
            pltpu.VMEM((PLANE, rows, width), BF16),
            pltpu.VMEM((2, rows, width // 2), BF16),
            pltpu.VMEM((2, rows, width // 2), BF16),
            pltpu.VMEM((rows, width // 2), BF16),
            pltpu.VMEM((rows, width // 2), BF16),
            pltpu.VMEM((width, values), BF16),
            pltpu.VMEM((width, 2 * keys), BF16),
            pltpu.VMEM((LINE + 1, deep, values), BF16),
            pltpu.VMEM((LINE + 1, deep, 2 * keys), BF16),
            pltpu.VMEM((3, deep, values), BF16),
            pltpu.VMEM((2, LINE, chunk, hidden), BF16),
            pltpu.VMEM((2, LINE, chunk, hidden), BF16),
            pltpu.VMEM((LINE + 1, chunk, hidden), BF16),
            pltpu.VMEM((LINE + 1, chunk, hidden), BF16),
            pltpu.VMEM((7, 8, width), F32),
            DMA((10,)),
            DMA((2, 4)),
            DMA((2,)),
            DMA((2,)),
            DMA((2, LINE)),
            DMA((2, LINE)),
            DMA((4,)),
            DMA((4,)),
            DMA((6,)),
            DMA((6,)),
            DMA((7,)),
            DMA((7,)),
            DMA((3, PLANE)),
            DMA((3, PLANE)),
        ]
        + line_sems()
        + line_sems()
        + line_sems()
        + line_sems(),
        cid,
        in_specs=[ANY] * 12 + [VM, ANY, VM],
        out_specs=[ANY, VM, VM, ANY],
    )


def outputs_kernel(
    last, first, ffn, low_out, low_grad, gains, q, k, v, gate, out, up, down, block_out, grad_tokens, *vectors
):
    values = v.shape[1]
    keys = q.shape[1]
    v[...] = last[0, :, :values].astype(F32)
    q[...] = last[0, :, values : values + keys].astype(F32)
    k[...] = last[0, :, values + keys : 2 * values].astype(F32)
    gate[...] = last[0, :, 2 * values :].astype(F32)
    out[...] = first[0].astype(F32).T
    up[...] = ffn[0].astype(F32)
    down[...] = ffn[1].astype(F32).T
    block_out[...] = low_out[...]
    grad_tokens[...] = low_grad[...]
    for i, g in enumerate(vectors):
        g[...] = gains[i, :]


def outputs(last, first, ffn, low_out, low_grad, gains, keys):
    heads, chunk, values = first.shape
    hidden = ffn.shape[-1]
    rows, width = low_out.shape
    piece, slab = hidden // heads, rows // heads
    sd = jax.ShapeDtypeStruct
    by_column = [pl.BlockSpec((chunk, size), lambda i: (0, i)) for size in (keys, keys, values, values)]
    by_row = pl.BlockSpec((values, chunk), lambda i: (i, 0))
    low = pl.BlockSpec((slab, width), lambda i: (i, 0))
    sums = [pl.BlockSpec((1, chunk, a.shape[-1]), lambda i: (i, 0, 0)) for a in (last, first)]
    return pl.pallas_call(
        outputs_kernel,
        grid=(heads,),
        in_specs=[
            *sums,
            pl.BlockSpec((2, chunk, piece), lambda i: (0, 0, i)),
            low,
            low,
            pl.BlockSpec(gains.shape, lambda i: (0, 0)),
        ],
        out_specs=by_column
        + [
            by_row,
            pl.BlockSpec((chunk, piece), lambda i: (0, i)),
            pl.BlockSpec((piece, chunk), lambda i: (i, 0)),
            low,
            low,
        ]
        + [pl.BlockSpec((width,), lambda i: (0,))] * 4,
        out_shape=[
            sd((chunk, heads * keys), F32),
            sd((chunk, heads * keys), F32),
            sd((chunk, heads * values), F32),
            sd((chunk, heads * values), F32),
            sd((heads * values, chunk), F32),
            sd((chunk, hidden), F32),
            sd((hidden, chunk), F32),
            sd((rows, width), BF16),
            sd((rows, width), BF16),
        ]
        + [sd((width,), F32)] * 4,
    )(last, first, ffn, low_out, low_grad, gains)


def angle_tables(fine, half_width):
    frequency = 10000.0 ** (-np.linspace(0.0, 1.0, half_width))
    coarse = fine * np.arange(SEQUENCE_LENGTH // fine)[:, None] * frequency[None, :]
    near = np.arange(fine)[:, None] * frequency[None, :]
    return [np.asarray(f(a), np.float32) for a in (coarse, near) for f in (np.cos, np.sin)]


def shards(
    tokens,
    ln1_gain,
    ln1_bias,
    w_query,
    w_key,
    w_value,
    w_gate,
    w_out,
    decay_log,
    ln2_gain,
    ln2_bias,
    w_up,
    w_down,
    cotangent,
):
    row_count, width = tokens.shape
    span_rows = cotangent.shape[0]
    heads = decay_log.shape[1]
    repeats = lax.axis_size("seq") // SPANS
    peers = [[lo + SPANS * k for k in range(repeats)] for lo in range(SPANS)]
    narrow = width // (SPANS * repeats)

    def wide_in(w, axis):
        if repeats == 1:
            return w
        return lax.all_gather(w, "seq", axis_index_groups=peers, axis=axis, tiled=True)

    def narrow_out(g, axis):
        if repeats == 1:
            return g
        return lax.psum_scatter(
            g, "seq", scatter_dimension=axis, axis_index_groups=peers, tiled=True
        )

    def features_in(a):
        if repeats == 1:
            return a
        return a.reshape(a.shape[:-1] + (repeats, SPANS, narrow)).swapaxes(-3, -2).reshape(a.shape)

    def features_out(a):
        if repeats == 1:
            return a
        return a.reshape(a.shape[:-1] + (SPANS, repeats, narrow)).swapaxes(-3, -2).reshape(a.shape)

    spot = lax.axis_index("seq") % SPANS
    z, p = spot // PLANE, spot % PLANE
    group_rows = span_rows * PLANE
    blocks = group_rows // STRETCH

    tokens, cotangent, w_down = features_in(tokens), features_in(cotangent), features_in(w_down)
    w_up = features_in(w_up.T).T if repeats > 1 else w_up
    ln1_gain, ln1_bias = features_in(ln1_gain), features_in(ln1_bias)
    ln2_gain, ln2_bias = features_in(ln2_gain), features_in(ln2_bias)
    decays = jnp.pad(decay_log.T, ((0, 8 - heads), (0, 0)))
    (
        normed, q_rot, k_rot, value, gate_proj, retained, gated_low, prev_states,
        cosine, sine_part, ccol, crow, scalars, key_w, value_w, query_w, gate_w, out_w,
    ) = attention(
        tokens,
        ln1_gain,
        ln1_bias,
        decays,
        angle_tables(64, w_key.shape[1] // heads // 2),
        [
            wide_in(w_key, 0),
            wide_in(w_value, 0),
            wide_in(w_query, 0),
            wide_in(w_gate, 0),
            wide_in(w_out, 1),
        ],
        (False, False, False, False, True),
        0,
    )
    block_out, grad_resid, gains_second, grad_attn, grad_up, grad_down = ffn_part(
        gated_low,
        out_w,
        tokens,
        ln2_gain,
        ln2_bias,
        w_up,
        w_down,
        cotangent,
        2,
    )
    grad_heads, sums_first, gate_sum, ffn_first, grad_value_w, grad_qk_w = retention_back(
        grad_attn,
        out_w,
        gated_low,
        gate_proj,
        retained,
        q_rot,
        k_rot,
        value,
        prev_states,
        cosine,
        sine_part,
        ccol,
        crow,
        scalars,
        normed,
        grad_up,
        grad_down,
        7,
    )
    grad_tokens, gains, ffn_sum, sums_last = last_sums(
        grad_heads,
        grad_value_w,
        grad_qk_w,
        query_w,
        key_w,
        value_w,
        gate_w,
        ffn_first,
        grad_up,
        grad_down,
        gate_sum,
        tokens,
        ln1_gain,
        grad_resid,
        gains_second,
        8,
    )
    if repeats > 1:
        gains = lax.psum(gains, "seq", axis_index_groups=peers)

    *sums, block_out, grad_tokens, gain_one, bias_one, gain_two, bias_two = outputs(
        sums_last, sums_first, ffn_sum, block_out, grad_tokens, gains, key_w.shape[1]
    )
    gain_one, bias_one, gain_two, bias_two = map(features_out, (gain_one, bias_one, gain_two, bias_two))
    sum_query, sum_key, sum_value, sum_gate, sum_out, sum_up, sum_down = (
        narrow_out(g, axis) for g, axis in zip(sums, (0, 0, 0, 0, 1, 0, 1))
    )
    return (
        features_out(block_out),
        features_out(grad_tokens),
        gain_one,
        bias_one,
        sum_query,
        sum_key,
        sum_value,
        sum_gate,
        sum_out,
        gain_two,
        bias_two,
        sum_up,
        sum_down,
    )


def solution(mesh):
    return jax.shard_map(
        shards,
        mesh=mesh,
        in_specs=(
            P(("seq", "ffn"), None),
            P(),
            P(),
            P("seq", "ffn"),
            P("seq", "ffn"),
            P("seq", "ffn"),
            P("seq", "ffn"),
            P("ffn", "seq"),
            P("seq", "ffn"),
            P(),
            P(),
            P(None, "ffn"),
            P("ffn", None),
            P("seq", None),
        ),
        out_specs=(
            P(("seq", "ffn"), None),
            P(("seq", "ffn"), None),
            P(),
            P(),
            P("seq", "ffn"),
            P("seq", "ffn"),
            P("seq", "ffn"),
            P("seq", "ffn"),
            P("ffn", "seq"),
            P(),
            P(),
            P("seq", "ffn"),
            P("ffn", "seq"),
        ),
        check_vma=False,
    )
```

```python
import functools

import jax
import jax.numpy as jnp
import numpy as np
from jax import lax
from jax.experimental import pallas as pl
from jax.experimental.pallas import tpu as pltpu
from jax.sharding import PartitionSpec as P

STRETCH = 512
SEQUENCE_LENGTH = 8192
PLANE = 4
LINE = 4
SPANS = PLANE * LINE
MESH = pl.DeviceIdType.MESH
VMEM_LIMIT = 63 * 1024 * 1024
ANY = pl.BlockSpec(memory_space=pl.ANY)
VM = pl.BlockSpec(memory_space=pltpu.VMEM)
BF16 = jnp.bfloat16
F32 = jnp.float32


class Place:
    def __init__(self):
        s = lax.axis_index("seq")
        self.f = lax.axis_index("ffn")
        lo = s % SPANS
        self.base = s - lo
        self.z = lo // PLANE
        self.p = lo % PLANE

    def plane(self, m):
        return self.at(self.z, self.xor(m), self.f)

    def xor(self, m):
        p = self.p
        low, high = p % 2, p // 2
        if m & 1:
            low = 1 - low
        if m & 2:
            high = 1 - high
        return high * 2 + low

    def at(self, z, p, f):
        return (self.base + z * PLANE + p, f)

    def partner(self):
        return self.at(self.z, self.p, 1 - self.f)

    def up(self):
        return self.at(self.z + 1, self.p, self.f)

    def down(self):
        return self.at(self.z - 1, self.p, self.f)


def greet(peers):
    meet(call(peers))


def meet(count):
    pl.semaphore_wait(pltpu.get_barrier_semaphore(), count)


def call(peers):
    bar = pltpu.get_barrier_semaphore()
    count = 0
    for device, cond in peers:
        if cond is None:
            pl.semaphore_signal(bar, inc=1, device_id=device, device_id_type=MESH)
            count = count + 1
        else:

            @pl.when(cond)
            def _():
                pl.semaphore_signal(bar, inc=1, device_id=device, device_id_type=MESH)

            count = count + cond.astype(jnp.int32)
    return count


def remote(src, dst, send, recv, device):
    return pltpu.make_async_remote_copy(
        src_ref=src, dst_ref=dst, send_sem=send, recv_sem=recv, device_id=device, device_id_type=MESH
    )


def comm_call(kernel, outs, ins, scratch, cid, in_specs=None, out_specs=None):
    return pl.pallas_call(
        kernel,
        out_shape=outs,
        in_specs=in_specs if in_specs is not None else [ANY] * len(ins),
        out_specs=out_specs if out_specs is not None else [ANY] * len(outs),
        scratch_shapes=scratch,
        compiler_params=pltpu.CompilerParams(
            collective_id=cid, has_side_effects=True, vmem_limit_bytes=VMEM_LIMIT
        ),
    )(*ins)


DMA = pltpu.SemaphoreType.DMA


def nn(a, b):
    return jnp.dot(a, b, preferred_element_type=F32)


def nt(a, b):
    return lax.dot_general(a, b, (((1,), (1,)), ((), ())), preferred_element_type=F32)


def tn(a, b):
    return lax.dot_general(a, b, (((0,), (0,)), ((), ())), preferred_element_type=F32)


def rows_at(r, size):
    return pl.ds(pl.multiple_of(r, size), size)


def add_into(dst, cols, other, other_cols):
    @pl.loop(0, dst.shape[0], step=64)
    def _(r):
        at = rows_at(r, 64)
        dst[at, cols] = (dst[at, cols].astype(F32) + other[at, other_cols].astype(F32)).astype(BF16)


def start(copy):
    copy.start()
    return copy


def ffn_kernel(
    gated_ref, wo_ref, tok_ref, gain_ref, bias_ref, wu_ref, wd_ref, cot_ref,
    block_out, resid_out, gains, da, fu, fd,
    tok, resid_grad, share, wu, wd, rx0, rx1a, rx1b, rx2a, rx2b, resid, xn, act, dact, du, cot, dab, stage, tmp,
    lsem, gload, csend, crecv, xsend, xrecv, psend, precv, gsend, grecv, ksend, krecv, ssem, osem,
):
    me = Place()
    p, f = me.p, me.f
    greeted = call([(me.plane(1), None), (me.plane(2), None), (me.partner(), None)])
    rows, width = tok_ref.shape
    hidden = wu.shape[1]
    q = [me.xor(m) for m in range(4)]
    wide = width // 2
    hr = rows // 2
    span = 2 * rows
    ca, cb = pl.ds(0, wide), pl.ds(wide, wide)
    everything, whole = pl.ds(0, width), pl.ds(0, wide)
    own_half = [pl.ds(h * hr, hr) for h in range(2)]
    mine = [rows_at(h * rows + f * hr, hr) for h in range(2)]
    theirs = [rows_at(h * rows + (1 - f) * hr, hr) for h in range(2)]
    both = [pl.ds(h * rows, rows) for h in range(2)]

    order = (3, 1, 2, 0)
    part_width = gated_ref.shape[1]
    def out_slab(i):
        at = rows_at(i * 512, 512)
        return pltpu.make_async_copy(wo_ref.at[:, at], act.at[:, at], osem.at[i])

    slabs = width // 512
    out_slab(0).start()
    load_t = pltpu.make_async_copy(tok_ref, tok, lsem.at[7])
    load_g = {
        m: start(
            pltpu.make_async_copy(
                gated_ref.at[rows_at(q[m] * span, span), :],
                xn.at[:, m * part_width : (m + 1) * part_width],
                gload.at[m],
            )
        )
        for m in order
    }
    for i in range(1, slabs):
        out_slab(i).start()
    load_t.start()
    load_d = start(pltpu.make_async_copy(wd_ref, wd, lsem.at[1]))
    load_c = [
        start(
            pltpu.make_async_copy(
                cot_ref.at[pl.ds(c * rows + h * hr, hr), :], cot.at[pl.ds(h * rows + c * hr, hr), :], lsem.at[3 + 2 * h + c]
            )
        )
        for h in range(2)
        for c in range(2)
    ]
    load_u = start(pltpu.make_async_copy(wu_ref, wu, lsem.at[2]))
    first, sends = {}, {}

    def to_partner(m, h):
        first[m, h] = start(
            remote(
                share.at[m, rows_at((1 - f) * rows + h * hr, hr)], rx0.at[m, own_half[h]],
                csend.at[m, h], crecv.at[m, h], me.partner(),
            )
        )

    def make(m):
        load_g[m].wait()

        @pl.loop(0, slabs)
        def _(i):
            if m == order[0]:
                out_slab(i).wait()
            at = rows_at(i * 512, 512)
            share[m, :, at] = nn(xn[:, m * part_width : (m + 1) * part_width], act[:, at]).astype(BF16)

        if m == order[0]:
            meet(greeted)
        to_partner(m, 0)

    def pass_on(m, h):
        first[m, h].wait_recv()
        at = own_half[h]
        add_into(rx0.at[m, at], everything, share.at[m, rows_at(f * rows + h * hr, hr)], everything)
        k = 0 if m == 3 else 1
        if m & 1:
            sends["a", k, h] = start(
                remote(rx0.at[m, at, ca], rx1a.at[k, at], xsend.at[k, h], xrecv.at[k, h], me.plane(1))
            )
        if m & 2:
            sends["b", k, h] = start(
                remote(rx0.at[m, at, cb], rx1b.at[k, at], xsend.at[2 + k, h], xrecv.at[2 + k, h], me.plane(2))
            )

    def second(h):
        at = own_half[h]
        sends["a", 0, h].wait_recv()
        add_into(rx1a.at[0, at], whole, rx0.at[2, at], ca)
        sends["a", 2, h] = start(
            remote(rx1a.at[0, at], rx2a.at[at], xsend.at[4, h], xrecv.at[4, h], me.plane(2))
        )
        sends["b", 0, h].wait_recv()
        add_into(rx1b.at[0, at], whole, rx0.at[1, at], cb)
        sends["b", 2, h] = start(
            remote(rx1b.at[0, at], rx2b.at[at], xsend.at[5, h], xrecv.at[5, h], me.plane(1))
        )

    make(3)
    make(1)
    pass_on(3, 0)
    make(2)
    pass_on(1, 0)
    make(0)
    pass_on(2, 0)
    pass_on(0, 0)
    for m in order:
        to_partner(m, 1)

    load_d.wait()
    for c in load_c:
        c.wait()

    @pl.loop(0, hidden, step=512)
    def _(c):
        at = rows_at(c, 512)
        dact[:, at] = nt(cot[...], wd[at, :])

    second(0)
    for m in order:
        pass_on(m, 1)
    load_u.wait()
    step = 32

    def norm(h):
        for key in (("a", 1, h), ("b", 1, h), ("a", 2, h), ("b", 2, h)):
            sends[key].wait_recv()

        @pl.loop(0, hr, step=step)
        def _(r):
            at = pl.ds(pl.multiple_of(h * hr + r, step), step)
            left = rx0[0, at, ca].astype(F32) + rx1a[1, at, :].astype(F32) + rx2a[at, :].astype(F32)
            right = rx0[0, at, cb].astype(F32) + rx1b[1, at, :].astype(F32) + rx2b[at, :].astype(F32)
            v = tok[at, :].astype(F32) + jnp.concatenate([left, right], axis=1)
            resid[at, :] = v
            centered = v - jnp.mean(v, axis=1, keepdims=True)
            scale = lax.rsqrt(jnp.mean(centered * centered, axis=1, keepdims=True) + 1e-05)
            xn[pl.ds(pl.multiple_of(h * rows + f * hr + r, step), step), :] = (
                centered * scale * gain_ref[...] + bias_ref[...]
            ).astype(BF16)

        return start(remote(xn.at[mine[h]], xn.at[mine[h]], psend.at[0, h], precv.at[0, h], me.partner()))

    def hidden_part(h):
        @pl.loop(0, hidden, step=512)
        def _(c):
            at = rows_at(c, 512)
            u = nn(xn[both[h], :], wu[:, at])
            e = 0.5 * (1.0 + lax.erf(u * 0.7071067811865476))
            act[both[h], at] = (u * e).astype(BF16)
            slope = e + u * jnp.exp(-0.5 * u * u) * 0.3989422804014327
            du[both[h], at] = (dact[both[h], at] * slope).astype(BF16)

    def back_part(h):
        @pl.loop(0, width, step=512)
        def _(c):
            at = rows_at(c, 512)
            tmp[...] = nt(du[both[h], :], wu[at, :])
            resid_grad[own_half[h], at] = tmp[rows_at(f * hr, hr), :]
            share[0, own_half[h], at] = tmp[rows_at((1 - f) * hr, hr), :].astype(BF16)

        return start(
            remote(share.at[0, own_half[h]], share.at[1, own_half[h]], psend.at[1, h], precv.at[1, h], me.partner())
        )

    def norm_back(h):
        @pl.loop(0, hr, step=step)
        def _(r):
            at = pl.ds(pl.multiple_of(h * hr + r, step), step)
            dx = resid_grad[at, :] + share[1, at, :].astype(F32)
            v = resid[at, :]
            centered = v - jnp.mean(v, axis=1, keepdims=True)
            scale = lax.rsqrt(jnp.mean(centered * centered, axis=1, keepdims=True) + 1e-05)
            hat = centered * scale
            gains[0:1, :] += jnp.sum(dx * hat, axis=0, keepdims=True)
            gains[1:2, :] += jnp.sum(dx, axis=0, keepdims=True)
            g = dx * gain_ref[...]
            back = scale * (
                g - jnp.mean(g, axis=1, keepdims=True) - hat * jnp.mean(g * hat, axis=1, keepdims=True)
            )
            back = back + cot[pl.ds(pl.multiple_of(h * rows + f * hr + r, step), step), :].astype(F32)
            resid_grad[at, :] = back
            dab[at, :] = back.astype(BF16)

    def out_part(h):
        @pl.loop(0, width, step=512)
        def _(c):
            at = rows_at(c, 512)
            tmp[...] = nn(act[both[h], :], wd[:, at])
            dact[pl.ds(h * rows, hr), at] = tmp[rows_at(f * hr, hr), :]
            share[2, own_half[h], at] = tmp[rows_at((1 - f) * hr, hr), :].astype(BF16)

        return start(
            remote(share.at[2, own_half[h]], share.at[3, own_half[h]], psend.at[2, h], precv.at[2, h], me.partner())
        )

    quarter = hr // 2

    def seat(m, h, k=None):
        base = (q[m] * 2 + f) * rows + h * hr
        if k is None:
            return da.at[pl.ds(pl.multiple_of(base, hr), hr), :]
        return da.at[pl.ds(pl.multiple_of(base + k * quarter, quarter), quarter), :]

    spread = {}

    def spread_begin(h):
        spread["own", h] = start(pltpu.make_async_copy(dab.at[own_half[h]], seat(0, h), gload.at[h]))
        for i in range(2):
            for to, k in ((1, i), (2, 1 - i)):
                sem = (to - 1) * 2 + i
                spread[to, i, h] = start(
                    remote(
                        dab.at[pl.ds(h * hr + k * quarter, quarter)], seat(0, h, k),
                        gsend.at[sem, h], grecv.at[sem, h], me.plane(to),
                    )
                )
        spread["core", 0, h] = start(
            remote(dab.at[own_half[h]], seat(0, h), ksend.at[0, h], krecv.at[0, h], me.partner())
        )

    def spread_on(h):
        spread[1, 0, h].wait_recv()
        spread["g1", h] = start(
            remote(seat(1, h, 0), seat(1, h, 0), gsend.at[4, h], grecv.at[4, h], me.plane(2))
        )
        spread[2, 0, h].wait_recv()
        spread["g2", h] = start(
            remote(seat(2, h, 1), seat(2, h, 1), gsend.at[5, h], grecv.at[5, h], me.plane(1))
        )

    def spread_end(h):
        for m in (1, 2):
            spread[m, 1, h].wait_recv()
            spread["core", m, h] = start(
                remote(seat(m, h), seat(m, h), ksend.at[m, h], krecv.at[m, h], me.partner())
            )
        spread["g1", h].wait_recv()
        spread["g2", h].wait_recv()
        spread["core", 3, h] = start(
            remote(seat(3, h), seat(3, h), ksend.at[3, h], krecv.at[3, h], me.partner())
        )

    gains[...] = jnp.zeros_like(gains)
    for c in first.values():
        c.wait_send()
    load_t.wait()
    swaps = [norm(0)]
    swaps[0].wait_recv()
    hidden_part(0)
    second(1)
    swaps.append(back_part(0))
    out_swaps = [out_part(0)]
    swaps[1].wait_recv()
    norm_back(0)
    spread_begin(0)
    swaps.append(norm(1))
    swaps[2].wait_recv()
    hidden_part(1)
    spread_on(0)
    swaps.append(back_part(1))
    out_swaps.append(out_part(1))
    swaps[3].wait_recv()
    norm_back(1)
    spread_begin(1)
    resid_copy = start(pltpu.make_async_copy(resid_grad, resid_out, lsem.at[0]))

    def weights_part(left, right, out):
        def spill(slot, i):
            return pltpu.make_async_copy(stage.at[slot], out.at[rows_at(i * 256, 256), :], ssem.at[slot])

        @pl.loop(0, width // 256)
        def _(i):
            slot = i % 3

            @pl.when(i >= 3)
            def _():
                spill(slot, i - 3).wait()

            stage[slot] = tn(left[:, rows_at(i * 256, 256)], right[...]).astype(BF16)
            spill(slot, i).start()

        for k in (3, 2, 1):
            i = width // 256 - k
            spill(i % 3, i).wait()

    weights_part(cot, act, fd)
    spread_on(1)
    spread_end(0)
    for h in range(2):
        out_swaps[h].wait_recv()

        @pl.loop(0, hr, step=step)
        def _(r):
            at = pl.ds(pl.multiple_of(h * hr + r, step), step)
            own = dact[pl.ds(pl.multiple_of(h * rows + r, step), step), :]
            tok[at, :] = (resid[at, :] + own + share[3, at, :].astype(F32)).astype(BF16)

    out_copy = start(pltpu.make_async_copy(tok, block_out, lsem.at[1]))
    weights_part(xn, du, fu)
    spread_end(1)
    resid_copy.wait()
    out_copy.wait()
    for h in range(2):
        spread["own", h].wait()
        for m in range(4):
            spread["core", m, h].wait()
        for key in ((1, 0, h), (1, 1, h), (2, 0, h), (2, 1, h), ("g1", h), ("g2", h)):
            spread[key].wait_send()
    for c in swaps + out_swaps + list(sends.values()):
        c.wait_send()


def ffn_part(gated, w_out, tokens, gain, bias, w_up, w_down, cotangent, cid):
    rows, width = tokens.shape
    assert PLANE * gated.shape[1] == width and w_out.shape == (2 * rows, w_up.shape[1])
    span, hidden = 2 * rows, w_up.shape[1]
    sd = jax.ShapeDtypeStruct
    return comm_call(
        ffn_kernel,
        [
            sd((rows, width), BF16),
            sd((rows, width), F32),
            sd((8, width), F32),
            sd((2 * PLANE * rows, width), BF16),
            sd((width, hidden), BF16),
            sd((width, hidden), BF16),
        ],
        [gated, w_out, tokens, gain[None], bias[None], w_up, w_down, cotangent],
        [
            pltpu.VMEM((rows, width), BF16),
            pltpu.VMEM((rows, width), F32),
            pltpu.VMEM((PLANE, span, width), BF16),
            pltpu.VMEM(w_up.shape, BF16),
            pltpu.VMEM(w_down.shape, BF16),
            pltpu.VMEM((PLANE, rows, width), BF16),
            pltpu.VMEM((2, rows, width // 2), BF16),
            pltpu.VMEM((2, rows, width // 2), BF16),
            pltpu.VMEM((rows, width // 2), BF16),
            pltpu.VMEM((rows, width // 2), BF16),
            pltpu.VMEM((rows, width), F32),
            pltpu.VMEM((span, width), BF16),
            pltpu.VMEM((span, hidden), BF16),
            pltpu.VMEM((span, hidden), F32),
            pltpu.VMEM((span, hidden), BF16),
            pltpu.VMEM((span, width), BF16),
            pltpu.VMEM((rows, width), BF16),
            pltpu.VMEM((3, 256, hidden), BF16),
            pltpu.VMEM((rows, 512), F32),
            DMA((8,)),
            DMA((PLANE,)),
            DMA((PLANE, 2)),
            DMA((PLANE, 2)),
            DMA((6, 2)),
            DMA((6, 2)),
            DMA((3, 2)),
            DMA((3, 2)),
            DMA((6, 2)),
            DMA((6, 2)),
            DMA((4, 2)),
            DMA((4, 2)),
            DMA((3,)),
            DMA((width // 512,)),
        ],
        cid,
        in_specs=[ANY, ANY, ANY, VM, VM, ANY, ANY, ANY],
        out_specs=[ANY, ANY, VM, ANY, ANY, ANY],
    )


def attention_kernel(
    widths, by_rows,
    tok_ref, gain_ref, bias_ref, dec_ref, cbase, sbase, coff, soff, *refs,
):
    count = len(widths)
    shards_in, refs = refs[:count], refs[count:]
    (xg, q_out, k_out, v_out, gate_out, ret_out, gated_out, states_out, cos_out, sin_out, ccol_out, crow_out, scal_out), refs = (
        refs[:13], refs[13:],
    )
    full, refs = refs[:count], refs[count:]
    hold, refs = refs[:count], refs[count:]
    wl, refs = refs[: count - 1], refs[count - 1 :]
    (tok, ccol, crow, scal, xn, xv, q, k, v, gate, ret, gated, cos, sin, kv, st, sloc, sgot, decg,
     lsem, psend, precv, usend, dsend, zrecv, xsend, xrecv, csend, crecv, tsend, trecv, ssend, srecv, osem, wsem) = refs
    me = Place()
    z, p, f = me.z, me.p, me.f
    spot = z * PLANE + p
    chunk = hold[0].shape[0]
    deep = chunk * PLANE
    tokens, width = xv.shape
    rows = tok_ref.shape[0]
    keys, values = q.shape[1], v.shape[1]
    half = keys // 2
    blocks = tokens // STRETCH
    greet(
        [(me.plane(m), None) for m in (1, 2, 3)]
        + [(me.partner(), None), (me.up(), z < LINE - 1), (me.down(), z > 0)]
    )

    def part(i, at):
        w = widths[i]
        if by_rows[i]:
            return shards_in[i].at[pl.ds(pl.multiple_of(at * w, w), w), :]
        return shards_in[i].at[:, pl.ds(pl.multiple_of(at * w, w), w)]

    def slot(i, ss):
        at = pl.ds(pl.multiple_of(ss * chunk, chunk), chunk)
        return full[i].at[:, at] if by_rows[i] else full[i].at[at, :]

    def block(i, zz):
        at = pl.ds(pl.multiple_of(zz * deep, deep), deep)
        return full[i].at[:, at] if by_rows[i] else full[i].at[at, :]

    def up_copy(i, zz):
        return remote(block(i, zz), block(i, zz), usend.at[i, zz], zrecv.at[i, zz], me.up())

    def down_copy(i, zz):
        return remote(block(i, zz), block(i, zz), dsend.at[i, zz], zrecv.at[i, zz], me.down())

    def part_copies(i, src, at):
        return (
            remote(src, slot(i, at), usend.at[i, z], zrecv.at[i, z], me.up()),
            remote(src, slot(i, at), dsend.at[i, z], zrecv.at[i, z], me.down()),
        )

    def to_line(copies):
        @pl.when(z < LINE - 1)
        def _():
            copies[0].start()

        @pl.when(z > 0)
        def _():
            copies[1].start()

    ahead = 2
    for i in range(ahead):
        to_line(part_copies(i, part(i, p), spot))
    load_t = start(pltpu.make_async_copy(tok_ref, tok, lsem.at[count + 1]))
    local, plane, held = [], [], []
    for i in range(count):
        held.append(start(pltpu.make_async_copy(part(i, p), hold[i], lsem.at[i])))
        local.append(pltpu.make_async_copy(hold[i], slot(i, spot), lsem.at[i]))
        plane.append(
            [
                start(remote(part(i, me.xor(m)), slot(i, spot), psend.at[i, m], precv.at[i, m], me.plane(m)))
                for m in (1, 2, 3)
            ]
        )
    tiny = [start(remote(dec_ref, decg.at[p], tsend.at[m], trecv.at[m], me.plane(m))) for m in (1, 2, 3)]
    tiny_own = start(pltpu.make_async_copy(dec_ref, decg.at[p], tsend.at[0]))
    step = 32
    load_t.wait()

    @pl.loop(0, rows, step=step)
    def _(r):
        at = rows_at(r, step)
        t = tok[at, :].astype(F32)
        centered = t - jnp.mean(t, axis=1, keepdims=True)
        scale = lax.rsqrt(jnp.mean(centered * centered, axis=1, keepdims=True) + 1e-05)
        xn[at, :] = (centered * scale * gain_ref[...] + bias_ref[...]).astype(BF16)

    def seat(m, h=None):
        base = (me.xor(m) * 2 + f) * rows
        if h is None:
            return xv.at[rows_at(base, rows)]
        return xv.at[pl.ds(pl.multiple_of(base + h * (rows // 2), rows // 2), rows // 2)]

    x_own = start(pltpu.make_async_copy(xn, seat(0), lsem.at[count]))
    x1 = start(remote(xn, seat(0), xsend.at[0], xrecv.at[0], me.plane(1)))
    x2 = start(remote(xn, seat(0), xsend.at[1], xrecv.at[1], me.plane(2)))
    xc = start(remote(xn, seat(0), csend.at[0], crecv.at[0], me.partner()))
    for i in range(count):
        held[i].wait()
        local[i].start()

    def own(i):
        local[i].wait()
        for c in plane[i]:
            c.wait_recv()
        if i < ahead:
            for m in (1, 2, 3):
                at = z * PLANE + me.xor(m)
                to_line(part_copies(i, slot(i, at), at))
        else:
            to_line((up_copy(i, z), down_copy(i, z)))

    def forward(i, t):
        @pl.when(z - t >= 0)
        def _():
            up_copy(i, z - t).wait_recv()

            @pl.when(z < LINE - 1)
            def _():
                up_copy(i, z - t).start()

        @pl.when(z + t < LINE)
        def _():
            down_copy(i, z + t).wait_recv()

            @pl.when(z > 0)
            def _():
                down_copy(i, z + t).start()

    def fetch(i):
        forward(i, LINE - 1)
        return start(pltpu.make_async_copy(full[i], wl[i], wsem.at[i]))

    K, V, Q, G, O = range(count)
    own(K)
    own(V)
    forward(K, 1)
    forward(K, 2)
    own(Q)

    for c in tiny:
        c.wait()
    tiny_own.wait()
    heads = lax.broadcasted_iota(jnp.int32, decg.shape[1:], 0)
    lines = [jnp.sum(jnp.where(heads == p, decg[j], 0.0), axis=0, keepdims=True) for j in range(blocks)]
    lines = jnp.concatenate(lines + [jnp.zeros_like(lines[0])] * (8 - blocks), axis=0)
    i0 = lax.broadcasted_iota(jnp.int32, (STRETCH, STRETCH), 0)
    i1 = lax.broadcasted_iota(jnp.int32, (STRETCH, STRETCH), 1)
    row_sums = jnp.dot(
        lines, jnp.where(i0 <= i1, 1.0, 0.0), preferred_element_type=F32, precision=lax.Precision.HIGHEST
    )
    col_sums = lax.dot_general(
        jnp.where(i1 <= i0, 1.0, 0.0), lines, (((1,), (1,)), ((), ())),
        preferred_element_type=F32, precision=lax.Precision.HIGHEST,
    )
    total = jnp.zeros((1, 1), F32)
    for c in range(blocks):
        end = row_sums[c : c + 1, STRETCH - 1 : STRETCH]
        crow[c] = jnp.broadcast_to(row_sums[c : c + 1, :], (8, STRETCH))
        ccol[c * STRETCH : (c + 1) * STRETCH, :] = col_sums[:, c : c + 1]
        scal[c] = jnp.broadcast_to(jnp.exp(end), (8, 128))
        scal[blocks + c] = jnp.broadcast_to(jnp.exp(total), (8, 128))
        total = total + end
    scal[2 * blocks] = jnp.broadcast_to(total, (8, 128))

    fine = coff.shape[0]

    @pl.loop(0, tokens // fine)
    def _(a):
        at = rows_at(a * fine, fine)
        place = pl.ds(z * (tokens // fine) + a, 1)
        ca, sa = cbase[place, :], sbase[place, :]
        cos[at, :] = ca * coff[...] - sa * soff[...]
        sin[at, :] = sa * coff[...] + ca * soff[...]

    forward(V, 1)
    x1.wait_recv()
    g1 = start(remote(seat(1, 0), seat(1, 0), xsend.at[2], xrecv.at[2], me.plane(2)))
    c1 = start(remote(seat(1), seat(1), csend.at[1], crecv.at[1], me.partner()))
    x2.wait_recv()
    g2 = start(remote(seat(2, 1), seat(2, 1), xsend.at[3], xrecv.at[3], me.plane(1)))
    c2 = start(remote(seat(2), seat(2), csend.at[2], crecv.at[2], me.partner()))
    forward(V, 2)
    forward(Q, 1)
    own(G)
    forward(Q, 2)
    own(O)
    load_k = fetch(K)
    g1.wait_recv()
    g2.wait_recv()
    c3 = start(remote(seat(3), seat(3), csend.at[3], crecv.at[3], me.partner()))
    x_own.wait()
    for c in (xc, c1, c2, c3):
        c.wait_recv()
    outs = []

    def put(src, dst):
        outs.append(start(pltpu.make_async_copy(src, dst, osem.at[len(outs)])))

    put(xv, xg)
    put(ccol, ccol_out)
    put(crow, crow_out)
    put(scal, scal_out)
    put(cos, cos_out)
    put(sin, sin_out)
    load_k.wait()

    def turned(at, w, dst):
        y = nn(xv[at, :], w[...])
        a, b = y[:, :half], y[:, half:]
        dst[at, :half] = (a * cos[at, :] - b * sin[at, :]).astype(BF16)
        dst[at, half:] = (b * cos[at, :] + a * sin[at, :]).astype(BF16)

    @pl.loop(0, blocks)
    def _(c):
        turned(rows_at(c * STRETCH, STRETCH), wl[K], k)

    fetch(V).wait()

    @pl.loop(0, blocks)
    def _(c):
        at = rows_at(c * STRETCH, STRETCH)
        val = nn(xv[at, :], wl[V][...]).astype(BF16)
        v[at, :] = val
        end = crow[c, 0:1, STRETCH - 1 : STRETCH]
        kv[c] = tn(k[at, :], (val.astype(F32) * jnp.exp(end - ccol[at, :])).astype(BF16))

    put(k, k_out)
    put(v, v_out)
    sloc[...] = kv[0]
    kv[0] = jnp.zeros_like(sloc)
    for c in range(1, blocks):
        nxt = sloc[...] * scal[c, 0:1, 0:1] + kv[c]
        kv[c] = sloc[...]
        sloc[...] = nxt

    def state_copy(zz):
        return remote(st.at[0], sgot, ssend.at[zz], srecv.at[zz], me.up())

    def send_state():
        st[0] = sloc[...].astype(BF16)
        state_copy(0).start()

    @pl.when(z == 0)
    def _():
        send_state()

    def pass_state(zz):
        @pl.when(z == zz)
        def _():
            state_copy(0).wait_recv()
            if zz < LINE - 1:
                sloc[...] = sloc[...] + sgot[...].astype(F32) * jnp.exp(scal[2 * blocks, 0:1, 0:1])
                send_state()

    pass_state(1)
    forward(G, 1)
    forward(O, 1)
    fetch(Q).wait()
    t_size = 256

    @pl.loop(0, blocks)
    def _(c):
        blk = rows_at(c * STRETCH, STRETCH)
        turned(blk, wl[Q], q)
        row = crow[c, 0:1, :]
        for r in range(0, STRETCH, t_size):
            at = rows_at(c * STRETCH + r, t_size)
            col = ccol[at, :]
            t_index = lax.broadcasted_iota(jnp.int32, (t_size, STRETCH), 0) + r
            s_index = lax.broadcasted_iota(jnp.int32, (t_size, STRETCH), 1)
            mask = jnp.where(t_index >= s_index, jnp.exp(jnp.minimum(col - row, 0.0)), 0.0)
            scores = (nt(q[at, :], k[blk, :]) * mask).astype(BF16)
            ret[at, :] = nn(scores, v[blk, :])

    put(q, q_out)
    pass_state(2)
    forward(G, 2)
    forward(O, 2)
    pass_state(3)

    @pl.when((z > 0) & (z < LINE - 1))
    def _():
        state_copy(0).wait_send()

    @pl.when(z == 0)
    def _():
        state_copy(0).wait_send()
        sgot[...] = jnp.zeros_like(sgot)

    for c in range(blocks):
        st[c] = (kv[c] + sgot[...].astype(F32) * scal[blocks + c, 0:1, 0:1]).astype(BF16)

    @pl.loop(0, blocks)
    def _(c):
        at = rows_at(c * STRETCH, STRETCH)
        decayed = (q[at, :].astype(F32) * jnp.exp(ccol[at, :])).astype(BF16)
        ret[at, :] += nn(decayed, st[c])

    put(ret, ret_out)
    put(st, states_out)
    fetch(G).wait()

    @pl.loop(0, tokens, step=256)
    def _(r):
        at = rows_at(r, 256)
        g = nn(xv[at, :], wl[G][...])
        gate[at, :] = g
        t = ret[at, :]
        centered = t - jnp.mean(t, axis=1, keepdims=True)
        scale = lax.rsqrt(jnp.mean(centered * centered, axis=1, keepdims=True) + 1e-05)
        gated[at, :] = (g / (1.0 + jnp.exp(-g)) * centered * scale).astype(BF16)

    put(gate, gate_out)
    put(gated, gated_out)
    forward(O, LINE - 1)
    for c in (xc, c1, c2, c3, x1, x2, g1, g2):
        c.wait_send()
    for i in range(count):
        for c in plane[i]:
            c.wait_send()
        for zz in range(LINE):

            @pl.when((z < LINE - 1) & (zz <= z))
            def _():
                up_copy(i, zz).wait_send()

            @pl.when((z > 0) & (zz >= z))
            def _():
                down_copy(i, zz).wait_send()

    for c in outs:
        c.wait()


def attention(tokens, gain, bias, decays, tables, shards_in, by_rows, cid):
    rows, width = tokens.shape
    count = len(shards_in)
    chunk = shards_in[0].shape[0]
    group = 2 * PLANE * rows
    blocks = group // STRETCH
    parts = [
        (w.shape[0] // PLANE, chunk) if r else (chunk, w.shape[1] // PLANE) for w, r in zip(shards_in, by_rows)
    ]
    widths = [s[0] if r else s[1] for s, r in zip(parts, by_rows)]
    wholes = [(s[0], width) if r else (width, s[1]) for s, r in zip(parts, by_rows)]
    values, keys = widths[1], widths[0]
    half = keys // 2
    sd = jax.ShapeDtypeStruct
    outs = [
        sd((group, width), BF16),
        sd((group, keys), BF16),
        sd((group, keys), BF16),
        sd((group, values), BF16),
        sd((group, values), F32),
        sd((group, values), F32),
        sd((group, values), BF16),
        sd((blocks, keys, values), BF16),
        sd((group, half), F32),
        sd((group, half), F32),
        sd((group, 1), F32),
        sd((blocks, 8, STRETCH), F32),
        sd((2 * blocks + 1, 8, 128), F32),
    ] + [sd(s, BF16) for s in wholes]
    scratch = (
        [pltpu.VMEM(s, BF16) for s in parts]
        + [pltpu.VMEM(s, BF16) for s in wholes[:-1]]
        + [
            pltpu.VMEM((rows, width), BF16),
            pltpu.VMEM((group, 1), F32),
            pltpu.VMEM((blocks, 8, STRETCH), F32),
            pltpu.VMEM((2 * blocks + 1, 8, 128), F32),
            pltpu.VMEM((rows, width), BF16),
            pltpu.VMEM((group, width), BF16),
            pltpu.VMEM((group, keys), BF16),
            pltpu.VMEM((group, keys), BF16),
            pltpu.VMEM((group, values), BF16),
            pltpu.VMEM((group, values), F32),
            pltpu.VMEM((group, values), F32),
            pltpu.VMEM((group, values), BF16),
            pltpu.VMEM((group, half), F32),
            pltpu.VMEM((group, half), F32),
            pltpu.VMEM((blocks, keys, values), F32),
            pltpu.VMEM((blocks, keys, values), BF16),
            pltpu.VMEM((keys, values), F32),
            pltpu.VMEM((keys, values), BF16),
            pltpu.VMEM((PLANE,) + decays.shape, F32),
            DMA((count + 2,)),
            DMA((count, PLANE)),
            DMA((count, PLANE)),
            DMA((count, LINE)),
            DMA((count, LINE)),
            DMA((count, LINE)),
            DMA((4,)),
            DMA((4,)),
            DMA((4,)),
            DMA((4,)),
            DMA((PLANE,)),
            DMA((PLANE,)),
            DMA((1,)),
            DMA((1,)),
            DMA((16,)),
            DMA((count,)),
        ]
    )
    return comm_call(
        functools.partial(attention_kernel, widths, by_rows),
        outs,
        [tokens, gain[None], bias[None], decays] + list(tables) + list(shards_in),
        scratch,
        cid,
        in_specs=[ANY] + [VM] * 7 + [ANY] * count,
        out_specs=[ANY] * (13 + count),
    )


class LineSum:
    def __init__(self, me, own, rx, usend, urecv, dsend, drecv, add):
        self.me, self.own, self.rx, self.add = me, own, rx, add
        self.sems = usend, urecv, dsend, drecv

    def up(self, src, zz):
        return remote(src, self.rx.at[zz], self.sems[0].at[zz], self.sems[1].at[zz], self.me.up())

    def down(self, src, zz):
        slot = jnp.where(zz == self.me.z - 1, LINE, zz)
        return remote(src, self.rx.at[slot], self.sems[2].at[zz], self.sems[3].at[zz], self.me.down())

    def begin(self, order=(3, 2, 1), src=None):
        src = src or self.own
        for zz in order:

            @pl.when(self.me.z == 0)
            def _():
                self.up(src(zz), zz).start()

            @pl.when(self.me.z == LINE - 1)
            def _():
                self.down(src(LINE - 1 - zz), LINE - 1 - zz).start()

    def pass_up(self, zz):
        self.up(self.own(zz), zz).wait_recv()
        self.add(self.rx.at[zz], self.own(zz))
        self.up(self.rx.at[zz], zz).start()

    def pass_down(self, zz):
        self.down(self.own(zz), zz).wait_recv()
        self.add(self.rx.at[zz], self.own(zz))
        self.down(self.rx.at[zz], zz).start()

    def near(self, k):
        @pl.when(self.me.z == 1)
        def _():
            self.pass_up(LINE - 1 - k)

        @pl.when(self.me.z == 2)
        def _():
            self.pass_down(k)

    def far(self):
        @pl.when(self.me.z == 1)
        def _():
            self.pass_down(0)

        @pl.when(self.me.z == 2)
        def _():
            self.pass_up(LINE - 1)

    def arrive(self):
        z = self.me.z

        @pl.when(z > 0)
        def _():
            self.up(self.own(z), z).wait_recv()

        @pl.when(z < LINE - 1)
        def _():
            self.down(self.own(z), z).wait_recv()

    def finish(self):
        z = self.me.z
        for zz in range(LINE):

            @pl.when((z < LINE - 1) & (zz > z))
            def _():
                self.up(self.own(zz), zz).wait_send()

            @pl.when((z > 0) & (zz < z))
            def _():
                self.down(self.own(zz), zz).wait_send()


def add_rows(dst, src):
    rows = dst.shape[0]
    step = 32 if dst.shape[1] > 512 else 128

    @pl.loop(0, rows, step=step)
    def _(r):
        at = rows_at(r, step)
        dst[at, :] = (dst[at, :].astype(F32) + src[at, :].astype(F32)).astype(BF16)


def total_rows(z, dst, own, rx):
    rows = dst.shape[0]
    step = 32 if dst.shape[1] > 512 else 128

    @pl.loop(0, rows, step=step)
    def _(r):
        at = rows_at(r, step)
        v = own[at, :].astype(F32)
        v = v + jnp.where(z > 0, rx[z, at, :].astype(F32), 0.0)
        v = v + jnp.where(z < LINE - 1, rx[LINE, at, :].astype(F32), 0.0)
        dst[at, :] = v.astype(dst.dtype)


def line_sems():
    return [DMA((LINE,)) for _ in range(4)]


def retention_back_kernel(
    da_ref, wo_ref, gated_ref, gate_ref, ret_ref, q_ref, k_ref, v_ref, s_ref, cos_ref, sin_ref,
    ccol_in, crow_in, scal_in, xg_ref, fu_ref, fd_ref,
    dh_out, sums, gate_fin, f1, av_out, aq_out,
    ccol_ref, crow_ref, scal_ref, dh, da, wo, gated, gr, q, k, v, st, cos, sin, dr, xt, ao, ag, rxo, rxg, fin, qo, gb, lg, got, rxf, fo, pbuf, gbuf,
    lsem, gsem, xsem, fsend, frecv, osem, fosem, ssend, srecv, psend, precv, *line,
):
    me = Place()
    z, p = me.z, me.p
    greeted = call(
        [(me.plane(m), None) for m in (1, 2, 3)]
        + [(me.up(), z < LINE - 1), (me.down(), z > 0)]
    )
    width = da.shape[1]
    tokens = da.shape[0]
    keys, values = q.shape[1], v.shape[1]
    blocks = tokens // STRETCH
    half = keys // 2
    pq = [me.xor(m) for m in range(4)]
    chunk = fu_ref.shape[0] // SPANS

    def f_block(h, zp, place):
        return (fu_ref, fd_ref)[h].at[pl.ds(pl.multiple_of((zp * PLANE + place) * chunk, chunk), chunk), :]

    units = [(h, zp, (0, 1)) for zp in (3, 0, 2) for h in range(2)] + [(h, 1, (1,)) for h in range(2)]

    def f_slot(h, zp, j):
        return rxf.at[h, 2 * (3, 0, 2, 1).index(zp) + (j if zp != 1 else 0)]
    away = ((1, 3), (2, 3))
    kept = ((0, 2), (0, 1))
    nbr = (1, 2)

    def f_copy(h, zp, j):
        return remote(
            f_block(h, zp, pq[away[h][j]]), f_slot(h, zp, j), fsend.at[h, zp, j], frecv.at[h, zp, j], me.plane(nbr[h])
        )

    deep = width // LINE
    ends_first = [jnp.where(z < LINE // 2, LINE - 1 - i, i) for i in range(LINE)]

    def slab(i):
        at = rows_at(ends_first[i] * deep, deep)
        return pltpu.make_async_copy(da_ref.at[:, at], da.at[:, at], lsem.at[12 + i])

    slab(0).start()
    loads = [
        start(pltpu.make_async_copy(a, b, lsem.at[i]))
        for i, (a, b) in enumerate(
            [(gated_ref, gated), (wo_ref, wo), (q_ref, q), (k_ref, k), (v_ref, v), (s_ref, st),
             (cos_ref, cos), (sin_ref, sin), (ccol_in, ccol_ref), (crow_in, crow_ref), (scal_in, scal_ref)]
        )
    ]
    for i in range(1, LINE):
        slab(i).start()

    def f_own(u):
        h, zp, js = units[u]
        return [
            pltpu.make_async_copy(f_block(h, zp, pq[kept[h][j]]), fo.at[u % 2, j], fosem.at[u % 2, j])
            for j in js
        ]

    def f_out(u):
        h, zp, js = units[u]
        return [pltpu.make_async_copy(f_slot(h, zp, j), f1.at[h, zp, j], osem.at[u, j]) for j in js]

    for u in range(2):
        for c in f_own(u):
            c.start()

    def f_unit(u):
        h, zp, js = units[u]
        for j, c in zip(js, f_own(u)):
            c.wait()
            f_copy(h, zp, j).wait_recv()
            add_rows(f_slot(h, zp, j), fo.at[u % 2, j])
        for c in f_out(u):
            c.start()
        if u + 2 < len(units):
            for c in f_own(u + 2):
                c.start()

    def tile_rows(i):
        return rows_at(i * 256, 256)

    def gate_loads(i):
        at = tile_rows(i)
        slot = i % 3
        return (
            pltpu.make_async_copy(gate_ref.at[at, :], gr.at[slot, 0], gsem.at[slot, 0]),
            pltpu.make_async_copy(ret_ref.at[at, :], gr.at[slot, 1], gsem.at[slot, 1]),
        )

    for c in gate_loads(0) + gate_loads(1):
        c.start()

    out_sum = LineSum(me, lambda zz: ao.at[rows_at(zz * (width // LINE), width // LINE), :], rxo, *line[:4], add_rows)
    gate_sum = LineSum(me, lambda zz: ag.at[rows_at(zz * (width // LINE), width // LINE), :], rxg, *line[4:], add_rows)

    loads[0].wait()
    for turn in range(LINE):
        slab(turn).wait()

        @pl.loop(0, deep, step=256)
        def _(i):
            at = rows_at(ends_first[turn] * deep + i, 256)
            ao[at, :] = tn(da[:, at], gated[...]).astype(BF16)

        if turn == 0:
            meet(greeted)
        if turn < 2:
            out_sum.begin((LINE - 1 - turn,))
        if turn == 0:
            for h, zp, js in units:
                for j in js:
                    f_copy(h, zp, j).start()
    for c in loads[1:]:
        c.wait()

    tiles = tokens // 256

    @pl.loop(0, tiles)
    def _(i):
        @pl.when(i + 2 < tiles)
        def _():
            for c in gate_loads(i + 2):
                c.start()

        for c in gate_loads(i):
            c.wait()
        at = tile_rows(i)
        slot = i % 3
        dgated = nt(da[at, :], wo[...])
        gate = gr[slot, 0]
        ret = gr[slot, 1]
        centered = ret - jnp.mean(ret, axis=1, keepdims=True)
        scale = lax.rsqrt(jnp.mean(centered * centered, axis=1, keepdims=True) + 1e-05)
        grouped = centered * scale
        sig = 1.0 / (1.0 + jnp.exp(-gate))
        silu = gate * sig
        dh[at, 2 * keys + values :] = (dgated * grouped * (sig * (1.0 + gate * (1.0 - sig)))).astype(BF16)
        dg = dgated * silu
        dr[at, :] = (
            scale * (dg - jnp.mean(dg, axis=1, keepdims=True) - grouped * jnp.mean(dg * grouped, axis=1, keepdims=True))
        ).astype(BF16)

    lg[...] = jnp.zeros_like(lg)

    @pl.loop(0, blocks)
    def _(c):
        at = rows_at(c * STRETCH, STRETCH)
        decayed = (q[at, :].astype(F32) * jnp.exp(ccol_ref[at, :])).astype(BF16)
        got_q = tn(decayed, dr[at, :])
        qo[c] = got_q
        lg[...] += scal_ref[blocks + c, 0:1, 0:1] * got_q

    state_copy = remote(gb.at[0], got, ssend.at[0], srecv.at[0], me.down())

    def pass_state(zz):
        @pl.when(z == zz)
        def _():
            if zz < LINE - 1:
                state_copy.wait_recv()
            if zz > 0:
                add = lg[...]
                if zz < LINE - 1:
                    add = add + got[...].astype(F32) * jnp.exp(scal_ref[2 * blocks, 0:1, 0:1])
                gb[0] = add.astype(BF16)
                state_copy.start()

    pass_state(LINE - 1)
    out_sum.begin((1,))
    out_sum.near(0)
    def x_tile(i):
        return pltpu.make_async_copy(xg_ref.at[:, rows_at(i * 256, 256)], xt.at[i % 3], xsem.at[i % 3])

    x_tile(0).start()
    x_tile(1).start()

    @pl.loop(0, width // 256)
    def _(i):
        @pl.when(i + 2 < width // 256)
        def _():
            x_tile(i + 2).start()

        x_tile(i).wait()
        ag[rows_at(i * 256, 256), :] = tn(xt[i % 3], dh[:, 2 * keys + values :]).astype(BF16)

    gate_sum.begin()
    out_sum.near(1)
    pass_state(2)
    f_unit(0)
    f_unit(1)
    out_sum.far()

    pass_state(1)
    pass_state(0)

    @pl.when(z > 0)
    def _():
        state_copy.wait_send()

    @pl.when(z < LINE - 1)
    def _():
        lg[...] = got[...].astype(F32)

    @pl.when(z == LINE - 1)
    def _():
        lg[...] = jnp.zeros_like(lg)

    for c in reversed(range(blocks)):
        gb[c] = lg[...].astype(BF16)
        if c:
            lg[...] = lg[...] * scal_ref[c, 0:1, 0:1] + qo[c]

    t_size = 256

    @pl.loop(0, blocks)
    def _(c):
        blk = rows_at(c * STRETCH, STRETCH)
        row = crow_ref[c, 0:1, :]
        end = crow_ref[c, 0:1, STRETCH - 1 : STRETCH]
        for r in range(0, STRETCH, t_size):
            at = rows_at(c * STRETCH + r, t_size)
            col = ccol_ref[at, :]
            t_index = lax.broadcasted_iota(jnp.int32, (t_size, STRETCH), 0) + r
            s_index = lax.broadcasted_iota(jnp.int32, (t_size, STRETCH), 1)
            mask = jnp.where(t_index >= s_index, jnp.exp(jnp.minimum(col - row, 0.0)), 0.0)
            pbuf[r : r + t_size, :] = (nt(q[at, :], k[blk, :]) * mask).astype(BF16)
            g = (nt(dr[at, :], v[blk, :]) * mask).astype(BF16)
            gbuf[r : r + t_size, :] = g
            dq = nt(dr[at, :], st[c]) * jnp.exp(col) + nn(g, k[blk, :])
            a, b = dq[:, :half], dq[:, half:]
            dh[at, :half] = (a * cos[at, :] + b * sin[at, :]).astype(BF16)
            dh[at, half:keys] = (b * cos[at, :] - a * sin[at, :]).astype(BF16)
        for r in range(0, STRETCH, t_size):
            at = rows_at(c * STRETCH + r, t_size)
            tail = jnp.exp(end - ccol_ref[at, :])
            w = (v[at, :].astype(F32) * tail).astype(BF16)
            dk = nt(w, gb[c]) + tn(gbuf[:, r : r + t_size], q[blk, :])
            a, b = dk[:, :half], dk[:, half:]
            dh[at, keys : keys + half] = (a * cos[at, :] + b * sin[at, :]).astype(BF16)
            dh[at, keys + half : 2 * keys] = (b * cos[at, :] - a * sin[at, :]).astype(BF16)
            dv = nn(k[at, :], gb[c]) * tail + tn(pbuf[:, r : r + t_size], dr[blk, :])
            dh[at, 2 * keys : 2 * keys + values] = dv.astype(BF16)

    dh_copy = start(pltpu.make_async_copy(dh, dh_out, lsem.at[2]))
    plane = []

    def deal(i, chain, a):
        chain.arrive()
        total_rows(z, fin.at[i], a.at[rows_at(z * (width // LINE), width // LINE), :], chain.rx)
        cols = pl.ds(i * values, values)
        for m in (1, 2, 3):
            plane.append(
                start(
                    remote(
                        fin.at[i, rows_at(pq[m] * chunk, chunk), :], sums.at[p, :, cols],
                        psend.at[i, m], precv.at[i, m], me.plane(m),
                    )
                )
            )
        plane.append(
            start(
                pltpu.make_async_copy(
                    fin.at[i, rows_at(p * chunk, chunk), :], sums.at[p, :, cols], psend.at[i, 0]
                )
            )
        )

    gate_sum.near(0)
    for u in range(2, 4):
        f_unit(u)
    deal(0, out_sum, ao)
    gate_sum.near(1)
    gate_sum.far()
    x_tile(0).start()
    x_tile(1).start()
    wide = 2 * keys + values

    @pl.loop(0, width // 256)
    def _(i):
        @pl.when(i + 2 < width // 256)
        def _():
            x_tile(i + 2).start()

        x_tile(i).wait()
        da[rows_at(i * 256, 256), :wide] = tn(xt[i % 3], dh[:, :wide]).astype(BF16)

    to_last = [
        start(pltpu.make_async_copy(da.at[:, : 2 * keys], aq_out, lsem.at[0])),
        start(pltpu.make_async_copy(da.at[:, 2 * keys : wide], av_out, lsem.at[1])),
    ]
    for u in range(4, len(units)):
        f_unit(u)
    gate_sum.arrive()
    total_rows(z, fin.at[1], ag.at[rows_at(z * deep, deep), :], rxg)
    to_last.append(start(pltpu.make_async_copy(fin.at[1], gate_fin, lsem.at[3])))
    for c in plane + to_last + [dh_copy]:
        c.wait()
    out_sum.finish()
    gate_sum.finish()
    for u, (h, zp, js) in enumerate(units):
        for c in f_out(u):
            c.wait()
        for j in js:
            f_copy(h, zp, j).wait_send()


def retention_back(da, wo, gated, gate, ret, q, k, v, states, cos, sin, ccol, crow, scal, xg, fu, fd, cid):
    tokens, width = da.shape
    keys, values = q.shape[1], v.shape[1]
    chunk = width // SPANS
    blocks = tokens // STRETCH
    hidden = fu.shape[1]
    deep = width // LINE
    return comm_call(
        retention_back_kernel,
        [
            jax.ShapeDtypeStruct((tokens, 2 * keys + 2 * values), BF16),
            jax.ShapeDtypeStruct((PLANE, chunk, values), BF16),
            jax.ShapeDtypeStruct((deep, values), BF16),
            jax.ShapeDtypeStruct((2, LINE, 2, chunk, hidden), BF16),
            jax.ShapeDtypeStruct((width, values), BF16),
            jax.ShapeDtypeStruct((width, 2 * keys), BF16),
        ],
        [da, wo, gated, gate, ret, q, k, v, states, cos, sin, ccol, crow, scal, xg, fu, fd],
        [
            pltpu.VMEM(ccol.shape, F32),
            pltpu.VMEM(crow.shape, F32),
            pltpu.VMEM(scal.shape, F32),
            pltpu.VMEM((tokens, 2 * keys + 2 * values), BF16),
            pltpu.VMEM((tokens, width), BF16),
            pltpu.VMEM(wo.shape, BF16),
            pltpu.VMEM(gated.shape, BF16),
            pltpu.VMEM((3, 2, 256, values), F32),
            pltpu.VMEM(q.shape, BF16),
            pltpu.VMEM(k.shape, BF16),
            pltpu.VMEM(v.shape, BF16),
            pltpu.VMEM(states.shape, BF16),
            pltpu.VMEM(cos.shape, F32),
            pltpu.VMEM(sin.shape, F32),
            pltpu.VMEM((tokens, values), BF16),
            pltpu.VMEM((3, tokens, 256), BF16),
            pltpu.VMEM((width, values), BF16),
            pltpu.VMEM((width, values), BF16),
            pltpu.VMEM((LINE + 1, deep, values), BF16),
            pltpu.VMEM((LINE + 1, deep, values), BF16),
            pltpu.VMEM((2, deep, values), BF16),
            pltpu.VMEM((blocks, keys, values), F32),
            pltpu.VMEM((blocks, keys, values), BF16),
            pltpu.VMEM((keys, values), F32),
            pltpu.VMEM((keys, values), BF16),
            pltpu.VMEM((2, 2 * LINE - 1, chunk, hidden), BF16),
            pltpu.VMEM((2, 2, chunk, hidden), BF16),
            pltpu.VMEM((STRETCH, STRETCH), BF16),
            pltpu.VMEM((STRETCH, STRETCH), BF16),
            DMA((12 + LINE,)),
            DMA((3, 2)),
            DMA((3,)),
            DMA((2, LINE, 2)),
            DMA((2, LINE, 2)),
            DMA((2 * LINE, 2)),
            DMA((2, 2)),
            DMA((1,)),
            DMA((1,)),
            DMA((2, PLANE)),
            DMA((2, PLANE)),
        ]
        + line_sems()
        + line_sems(),
        cid,
        in_specs=[ANY] * 17,
        out_specs=[ANY] * 6,
    )


def last_kernel(
    dh_ref, av_ref, aq_ref, wq_ref, wk_ref, wv_ref, wg_ref, f1_ref, fu_ref, fd_ref, gate_ref, tok_ref, gain_ref, resid_ref, second_ref,
    grad_out, gains, fout, sums,
    tok, resid, rxl, dh, wh, share, rx0, rx1a, rx1b, rx2a, rx2b, av, aq, rxv, rxq, fin, rf2, kf, rxfa, rxfb, grx,
    lsem, ksem, lsend, lrecv, fsend, frecv, csend, crecv, xsend, xrecv, gsend, grecv, psend, precv, *line,
):
    me = Place()
    z, p, f = me.z, me.p, me.f
    rounds = [
        [me.at((z + t) % LINE, p, f) for t in range(1, LINE)],
        [me.partner()],
        [me.plane(m) for m in (1, 2, 3)],
    ]
    greet([(d, None) for r in rounds for d in r])
    width, keys2, values = av.shape[0], aq.shape[1], av.shape[1]
    rows = tok_ref.shape[0]
    pq = [me.xor(m) for m in range(4)]
    chunk = width // SPANS
    deep = width // LINE

    late = 1

    def f_copy(h, zp):
        return remote(f1_ref.at[h, zp, 1], rf2.at[h, zp], fsend.at[h, zp], frecv.at[h, zp], me.plane(2 - h))

    def f_block(h, place):
        return (fu_ref, fd_ref)[h].at[rows_at((late * PLANE + place) * chunk, chunk), :]

    def late_copy(h):
        return remote(f_block(h, pq[1 + h]), rxl.at[h], lsend.at[h], lrecv.at[h], me.plane(1 + h))

    def block_of(a, size):
        return lambda zz: a.at[rows_at(zz * size, size), :]

    v_sum = LineSum(me, block_of(av, deep), rxv, *line[:4], add_rows)
    q_sum = LineSum(me, block_of(aq, deep), rxq, *line[4:8], add_rows)
    fa_sum = LineSum(me, lambda zz: kf.at[0, zz], rxfa, *line[8:12], add_rows)
    fb_sum = LineSum(me, lambda zz: kf.at[1, zz], rxfb, *line[12:16], add_rows)
    v_sum.begin(src=block_of(av_ref, deep))
    q_sum.begin(src=block_of(aq_ref, deep))
    for zp in (3, 0, 2, 1):
        for h in range(2):
            f_copy(h, zp).start()
    for h in range(2):
        late_copy(h).start()
    load = start(pltpu.make_async_copy(dh_ref, dh, lsem.at[0]))
    owns = [
        start(pltpu.make_async_copy(av_ref, av, lsem.at[7])),
        start(pltpu.make_async_copy(aq_ref, aq, lsem.at[8])),
    ]
    loads, at = [], 0
    for i, w in enumerate((wq_ref, wk_ref, wv_ref, wg_ref)):
        size = w.shape[1]
        loads.append(start(pltpu.make_async_copy(w, wh.at[:, at : at + size], lsem.at[1 + i])))
        at += size
    keeps = []
    for h in range(2):
        for i, zp in enumerate((3, 0, 2)):
            keeps.append(start(pltpu.make_async_copy(f1_ref.at[h, zp, 0], kf.at[h, zp], ksem.at[h, i])))
        keeps.append(start(pltpu.make_async_copy(f_block(h, p), kf.at[h, late], ksem.at[h, 3])))
    rest = [
        start(pltpu.make_async_copy(tok_ref, tok, lsem.at[5])),
        start(pltpu.make_async_copy(resid_ref, resid, lsem.at[6])),
    ]

    load.wait()
    plane = []

    def deal(i, chain, a):
        chain.arrive()
        total_rows(z, fin.at[i], a.at[rows_at(z * deep, deep), :], chain.rx)
        spread(i, fin.at[i])

    def spread(i, src):
        cols = pl.ds(i * values, values)
        for m in (1, 2, 3):
            plane.append(
                start(
                    remote(
                        src.at[rows_at(pq[m] * chunk, chunk), :], sums.at[p, :, cols],
                        psend.at[i, m], precv.at[i, m], me.plane(m),
                    )
                )
            )
        plane.append(
            start(
                pltpu.make_async_copy(
                    src.at[rows_at(p * chunk, chunk), :], sums.at[p, :, cols], psend.at[i, 0]
                )
            )
        )

    gate_load = start(pltpu.make_async_copy(gate_ref, fin.at[2], lsem.at[9]))
    for c in loads + owns + [gate_load]:
        c.wait()

    own_rows, their_rows = rows_at(f * rows, rows), rows_at((1 - f) * rows, rows)
    wide = width // 2
    ca, cb = pl.ds(0, wide), pl.ds(wide, wide)
    everything, whole = pl.ds(0, width), pl.ds(0, wide)
    first, sends = {}, {}

    def share_part(m):
        at_rows = rows_at(pq[m] * 2 * rows, 2 * rows)

        @pl.loop(0, width, step=256)
        def _(c):
            at = rows_at(c, 256)
            share[m, :, at] = nt(dh[at_rows, :], wh[at, :]).astype(BF16)

        first[m] = start(
            remote(share.at[m, their_rows], rx0.at[m], csend.at[m], crecv.at[m], me.partner())
        )

    def pass_on(m):
        first[m].wait_recv()
        add_into(rx0.at[m], everything, share.at[m, own_rows], everything)
        k = 0 if m == 3 else 1
        if m & 1:
            sends["a", k] = start(
                remote(rx0.at[m, :, ca], rx1a.at[k], xsend.at[k], xrecv.at[k], me.plane(1))
            )
        if m & 2:
            sends["b", k] = start(
                remote(rx0.at[m, :, cb], rx1b.at[k], xsend.at[2 + k], xrecv.at[2 + k], me.plane(2))
            )

    share_part(3)
    share_part(1)
    pass_on(3)
    v_sum.near(0)
    share_part(2)
    pass_on(1)
    share_part(0)
    pass_on(2)
    v_sum.near(1)
    pass_on(0)
    for c in keeps:
        c.wait()
    v_sum.far()
    q_sum.near(0)
    for ends, turns in (((3, 0), (3,)), ((2, 1), (2,))):
        for zp in ends:
            for h in range(2):
                f_copy(h, zp).wait_recv()
                add_rows(kf.at[h, zp], rf2.at[h, zp])
                if zp == late:
                    late_copy(h).wait_recv()
                    add_rows(kf.at[h, zp], rxl.at[h])
        for zz in turns:
            fa_sum.begin((zz,))
            fb_sum.begin((zz,))
    q_sum.near(1)
    q_sum.far()
    sends["a", 0].wait_recv()
    add_into(rx1a.at[0], whole, rx0.at[2], ca)
    s2a = start(remote(rx1a.at[0], rx2a, xsend.at[4], xrecv.at[4], me.plane(2)))
    sends["b", 0].wait_recv()
    add_into(rx1b.at[0], whole, rx0.at[1], cb)
    s2b = start(remote(rx1b.at[0], rx2b, xsend.at[5], xrecv.at[5], me.plane(1)))
    spread(2, fin.at[2])
    deal(0, v_sum, av)
    fa_sum.near(0)
    sends["a", 1].wait_recv()
    sends["b", 1].wait_recv()
    deal(1, q_sum, aq)
    fb_sum.near(0)
    s2a.wait_recv()
    s2b.wait_recv()
    for c in rest:
        c.wait()
    gains[...] = jnp.zeros_like(gains)
    gains[2:4, :] = second_ref[0:2, :]
    step = 32

    @pl.loop(0, rows, step=step)
    def _(r):
        at = rows_at(r, step)
        left = rx0[0, at, ca].astype(F32) + rx1a[1, at, :].astype(F32) + rx2a[at, :].astype(F32)
        right = rx0[0, at, cb].astype(F32) + rx1b[1, at, :].astype(F32) + rx2b[at, :].astype(F32)
        dx = jnp.concatenate([left, right], axis=1)
        v = tok[at, :].astype(F32)
        centered = v - jnp.mean(v, axis=1, keepdims=True)
        scale = lax.rsqrt(jnp.mean(centered * centered, axis=1, keepdims=True) + 1e-05)
        hat = centered * scale
        gains[0:1, :] += jnp.sum(dx * hat, axis=0, keepdims=True)
        gains[1:2, :] += jnp.sum(dx, axis=0, keepdims=True)
        g = dx * gain_ref[...]
        back = scale * (
            g - jnp.mean(g, axis=1, keepdims=True) - hat * jnp.mean(g * hat, axis=1, keepdims=True)
        )
        tok[at, :] = (back + resid[at, :]).astype(BF16)

    out_copy = start(pltpu.make_async_copy(tok, grad_out, lsem.at[0]))

    def gain_copies(r):
        base = (0, 3, 4)[r]
        return [
            remote(gains, grx.at[base + i], gsend.at[base + i], grecv.at[base + i], d)
            for i, d in enumerate(rounds[r])
        ]

    def gain_begin(r):
        for c in gain_copies(r):
            c.start()

    def gain_end(r):
        for c in gain_copies(r):
            c.wait()
        for i in range(len(rounds[r])):
            gains[...] += grx[(0, 3, 4)[r] + i]

    gain_begin(0)
    fa_sum.begin((1,))
    fb_sum.begin((1,))
    fa_sum.near(1)
    fa_sum.far()
    gain_end(0)
    gain_begin(1)
    fb_sum.near(1)
    gain_end(1)
    gain_begin(2)
    fb_sum.far()
    gain_end(2)
    fa_sum.arrive()
    total_rows(z, fout.at[0], kf.at[0, z], rxfa)
    fb_sum.arrive()
    total_rows(z, fout.at[1], kf.at[1, z], rxfb)
    for c in plane + [out_copy]:
        c.wait()
    for h in range(2):
        late_copy(h).wait_send()
    for chain in (v_sum, q_sum, fa_sum, fb_sum):
        chain.finish()
    for c in list(first.values()) + list(sends.values()) + [s2a, s2b]:
        c.wait_send()
    for zp in range(LINE):
        for h in range(2):
            f_copy(h, zp).wait_send()


def last_sums(dh, av, aq, wq, wk, wv, wg, f1, fu, fd, gate_fin, tokens, gain, resid, second, cid):
    width = av.shape[0]
    rows = tokens.shape[0]
    keys, values = wq.shape[1], wv.shape[1]
    assert 2 * keys == values
    chunk, deep = width // SPANS, width // LINE
    hidden = f1.shape[-1]
    return comm_call(
        last_kernel,
        [
            jax.ShapeDtypeStruct((rows, width), BF16),
            jax.ShapeDtypeStruct((8, width), F32),
            jax.ShapeDtypeStruct((2, chunk, hidden), BF16),
            jax.ShapeDtypeStruct((PLANE, chunk, 3 * values), BF16),
        ],
        [dh, av, aq, wq, wk, wv, wg, f1, fu, fd, gate_fin, tokens, gain[None], resid, second],
        [
            pltpu.VMEM((rows, width), BF16),
            pltpu.VMEM((rows, width), F32),
            pltpu.VMEM((2, chunk, hidden), BF16),
            pltpu.VMEM(dh.shape, BF16),
            pltpu.VMEM((width, dh.shape[1]), BF16),
            pltpu.VMEM((PLANE, 2 * rows, width), BF16),
            pltpu.VMEM((PLANE, rows, width), BF16),
            pltpu.VMEM((2, rows, width // 2), BF16),
            pltpu.VMEM((2, rows, width // 2), BF16),
            pltpu.VMEM((rows, width // 2), BF16),
            pltpu.VMEM((rows, width // 2), BF16),
            pltpu.VMEM((width, values), BF16),
            pltpu.VMEM((width, 2 * keys), BF16),
            pltpu.VMEM((LINE + 1, deep, values), BF16),
            pltpu.VMEM((LINE + 1, deep, 2 * keys), BF16),
            pltpu.VMEM((3, deep, values), BF16),
            pltpu.VMEM((2, LINE, chunk, hidden), BF16),
            pltpu.VMEM((2, LINE, chunk, hidden), BF16),
            pltpu.VMEM((LINE + 1, chunk, hidden), BF16),
            pltpu.VMEM((LINE + 1, chunk, hidden), BF16),
            pltpu.VMEM((7, 8, width), F32),
            DMA((10,)),
            DMA((2, 4)),
            DMA((2,)),
            DMA((2,)),
            DMA((2, LINE)),
            DMA((2, LINE)),
            DMA((4,)),
            DMA((4,)),
            DMA((6,)),
            DMA((6,)),
            DMA((7,)),
            DMA((7,)),
            DMA((3, PLANE)),
            DMA((3, PLANE)),
        ]
        + line_sems()
        + line_sems()
        + line_sems()
        + line_sems(),
        cid,
        in_specs=[ANY] * 12 + [VM, ANY, VM],
        out_specs=[ANY, VM, VM, ANY],
    )


def outputs_kernel(
    last, first, ffn, low_out, low_grad, gains, q, k, v, gate, out, up, down, block_out, grad_tokens, *vectors
):
    values = v.shape[1]
    keys = q.shape[1]
    v[...] = last[0, :, :values].astype(F32)
    q[...] = last[0, :, values : values + keys].astype(F32)
    k[...] = last[0, :, values + keys : 2 * values].astype(F32)
    gate[...] = last[0, :, 2 * values :].astype(F32)
    out[...] = first[0].astype(F32).T
    up[...] = ffn[0].astype(F32)
    down[...] = ffn[1].astype(F32).T
    block_out[...] = low_out[...]
    grad_tokens[...] = low_grad[...]
    for i, g in enumerate(vectors):
        g[...] = gains[i, :]


def outputs(last, first, ffn, low_out, low_grad, gains, keys):
    heads, chunk, values = first.shape
    hidden = ffn.shape[-1]
    rows, width = low_out.shape
    piece, slab = hidden // heads, rows // heads
    sd = jax.ShapeDtypeStruct
    by_column = [pl.BlockSpec((chunk, size), lambda i: (0, i)) for size in (keys, keys, values, values)]
    by_row = pl.BlockSpec((values, chunk), lambda i: (i, 0))
    low = pl.BlockSpec((slab, width), lambda i: (i, 0))
    sums = [pl.BlockSpec((1, chunk, a.shape[-1]), lambda i: (i, 0, 0)) for a in (last, first)]
    return pl.pallas_call(
        outputs_kernel,
        grid=(heads,),
        in_specs=[
            *sums,
            pl.BlockSpec((2, chunk, piece), lambda i: (0, 0, i)),
            low,
            low,
            pl.BlockSpec(gains.shape, lambda i: (0, 0)),
        ],
        out_specs=by_column
        + [
            by_row,
            pl.BlockSpec((chunk, piece), lambda i: (0, i)),
            pl.BlockSpec((piece, chunk), lambda i: (i, 0)),
            low,
            low,
        ]
        + [pl.BlockSpec((width,), lambda i: (0,))] * 4,
        out_shape=[
            sd((chunk, heads * keys), F32),
            sd((chunk, heads * keys), F32),
            sd((chunk, heads * values), F32),
            sd((chunk, heads * values), F32),
            sd((heads * values, chunk), F32),
            sd((chunk, hidden), F32),
            sd((hidden, chunk), F32),
            sd((rows, width), BF16),
            sd((rows, width), BF16),
        ]
        + [sd((width,), F32)] * 4,
    )(last, first, ffn, low_out, low_grad, gains)


def angle_tables(fine, half_width):
    frequency = 10000.0 ** (-np.linspace(0.0, 1.0, half_width))
    coarse = fine * np.arange(SEQUENCE_LENGTH // fine)[:, None] * frequency[None, :]
    near = np.arange(fine)[:, None] * frequency[None, :]
    return [np.asarray(f(a), np.float32) for a in (coarse, near) for f in (np.cos, np.sin)]


def shards(
    tokens,
    ln1_gain,
    ln1_bias,
    w_query,
    w_key,
    w_value,
    w_gate,
    w_out,
    decay_log,
    ln2_gain,
    ln2_bias,
    w_up,
    w_down,
    cotangent,
):
    row_count, width = tokens.shape
    span_rows = cotangent.shape[0]
    heads = decay_log.shape[1]
    repeats = lax.axis_size("seq") // SPANS
    peers = [[lo + SPANS * k for k in range(repeats)] for lo in range(SPANS)]
    narrow = width // (SPANS * repeats)

    def wide_in(w, axis):
        if repeats == 1:
            return w
        return lax.all_gather(w, "seq", axis_index_groups=peers, axis=axis, tiled=True)

    def narrow_out(g, axis):
        if repeats == 1:
            return g
        return lax.psum_scatter(
            g, "seq", scatter_dimension=axis, axis_index_groups=peers, tiled=True
        )

    def features_in(a):
        if repeats == 1:
            return a
        return a.reshape(a.shape[:-1] + (repeats, SPANS, narrow)).swapaxes(-3, -2).reshape(a.shape)

    def features_out(a):
        if repeats == 1:
            return a
        return a.reshape(a.shape[:-1] + (SPANS, repeats, narrow)).swapaxes(-3, -2).reshape(a.shape)

    spot = lax.axis_index("seq") % SPANS
    z, p = spot // PLANE, spot % PLANE
    group_rows = span_rows * PLANE
    blocks = group_rows // STRETCH

    tokens, cotangent, w_down = features_in(tokens), features_in(cotangent), features_in(w_down)
    w_up = features_in(w_up.T).T if repeats > 1 else w_up
    ln1_gain, ln1_bias = features_in(ln1_gain), features_in(ln1_bias)
    ln2_gain, ln2_bias = features_in(ln2_gain), features_in(ln2_bias)
    decays = jnp.pad(decay_log.T, ((0, 8 - heads), (0, 0)))
    (
        normed, q_rot, k_rot, value, gate_proj, retained, gated_low, prev_states,
        cosine, sine_part, ccol, crow, scalars, key_w, value_w, query_w, gate_w, out_w,
    ) = attention(
        tokens,
        ln1_gain,
        ln1_bias,
        decays,
        angle_tables(64, w_key.shape[1] // heads // 2),
        [
            wide_in(w_key, 0),
            wide_in(w_value, 0),
            wide_in(w_query, 0),
            wide_in(w_gate, 0),
            wide_in(w_out, 1),
        ],
        (False, False, False, False, True),
        0,
    )
    block_out, grad_resid, gains_second, grad_attn, grad_up, grad_down = ffn_part(
        gated_low,
        out_w,
        tokens,
        ln2_gain,
        ln2_bias,
        w_up,
        w_down,
        cotangent,
        2,
    )
    grad_heads, sums_first, gate_sum, ffn_first, grad_value_w, grad_qk_w = retention_back(
        grad_attn,
        out_w,
        gated_low,
        gate_proj,
        retained,
        q_rot,
        k_rot,
        value,
        prev_states,
        cosine,
        sine_part,
        ccol,
        crow,
        scalars,
        normed,
        grad_up,
        grad_down,
        7,
    )
    grad_tokens, gains, ffn_sum, sums_last = last_sums(
        grad_heads,
        grad_value_w,
        grad_qk_w,
        query_w,
        key_w,
        value_w,
        gate_w,
        ffn_first,
        grad_up,
        grad_down,
        gate_sum,
        tokens,
        ln1_gain,
        grad_resid,
        gains_second,
        8,
    )
    if repeats > 1:
        gains = lax.psum(gains, "seq", axis_index_groups=peers)

    *sums, block_out, grad_tokens, gain_one, bias_one, gain_two, bias_two = outputs(
        sums_last, sums_first, ffn_sum, block_out, grad_tokens, gains, key_w.shape[1]
    )
    gain_one, bias_one, gain_two, bias_two = map(features_out, (gain_one, bias_one, gain_two, bias_two))
    sum_query, sum_key, sum_value, sum_gate, sum_out, sum_up, sum_down = (
        narrow_out(g, axis) for g, axis in zip(sums, (0, 0, 0, 0, 1, 0, 1))
    )
    return (
        features_out(block_out),
        features_out(grad_tokens),
        gain_one,
        bias_one,
        sum_query,
        sum_key,
        sum_value,
        sum_gate,
        sum_out,
        gain_two,
        bias_two,
        sum_up,
        sum_down,
    )


def solution(mesh):
    return jax.shard_map(
        shards,
        mesh=mesh,
        in_specs=(
            P(("seq", "ffn"), None),
            P(),
            P(),
            P("seq", "ffn"),
            P("seq", "ffn"),
            P("seq", "ffn"),
            P("seq", "ffn"),
            P("ffn", "seq"),
            P("seq", "ffn"),
            P(),
            P(),
            P(None, "ffn"),
            P("ffn", None),
            P("seq", None),
        ),
        out_specs=(
            P(("seq", "ffn"), None),
            P(("seq", "ffn"), None),
            P(),
            P(),
            P("seq", "ffn"),
            P("seq", "ffn"),
            P("seq", "ffn"),
            P("seq", "ffn"),
            P("ffn", "seq"),
            P(),
            P(),
            P("seq", "ffn"),
            P("ffn", "seq"),
        ),
        check_vma=False,
    )
```

```python
import functools

import jax
import jax.numpy as jnp
import numpy as np
from jax import lax
from jax.experimental import pallas as pl
from jax.experimental.pallas import tpu as pltpu
from jax.sharding import PartitionSpec as P

STRETCH = 512
SEQUENCE_LENGTH = 8192
PLANE = 4
LINE = 4
SPANS = PLANE * LINE
MESH = pl.DeviceIdType.MESH
VMEM_LIMIT = 63 * 1024 * 1024
ANY = pl.BlockSpec(memory_space=pl.ANY)
VM = pl.BlockSpec(memory_space=pltpu.VMEM)
BF16 = jnp.bfloat16
F32 = jnp.float32


class Place:
    def __init__(self):
        s = lax.axis_index("seq")
        self.f = lax.axis_index("ffn")
        lo = s % SPANS
        self.base = s - lo
        self.z = lo // PLANE
        self.p = lo % PLANE

    def plane(self, m):
        return self.at(self.z, self.xor(m), self.f)

    def xor(self, m):
        p = self.p
        low, high = p % 2, p // 2
        if m & 1:
            low = 1 - low
        if m & 2:
            high = 1 - high
        return high * 2 + low

    def at(self, z, p, f):
        return (self.base + z * PLANE + p, f)

    def partner(self):
        return self.at(self.z, self.p, 1 - self.f)

    def up(self):
        return self.at(self.z + 1, self.p, self.f)

    def down(self):
        return self.at(self.z - 1, self.p, self.f)


def greet(peers):
    meet(call(peers))


def meet(count):
    pl.semaphore_wait(pltpu.get_barrier_semaphore(), count)


def call(peers):
    bar = pltpu.get_barrier_semaphore()
    count = 0
    for device, cond in peers:
        if cond is None:
            pl.semaphore_signal(bar, inc=1, device_id=device, device_id_type=MESH)
            count = count + 1
        else:

            @pl.when(cond)
            def _():
                pl.semaphore_signal(bar, inc=1, device_id=device, device_id_type=MESH)

            count = count + cond.astype(jnp.int32)
    return count


def remote(src, dst, send, recv, device):
    return pltpu.make_async_remote_copy(
        src_ref=src, dst_ref=dst, send_sem=send, recv_sem=recv, device_id=device, device_id_type=MESH
    )


def comm_call(kernel, outs, ins, scratch, cid, in_specs=None, out_specs=None):
    return pl.pallas_call(
        kernel,
        out_shape=outs,
        in_specs=in_specs if in_specs is not None else [ANY] * len(ins),
        out_specs=out_specs if out_specs is not None else [ANY] * len(outs),
        scratch_shapes=scratch,
        compiler_params=pltpu.CompilerParams(
            collective_id=cid, has_side_effects=True, vmem_limit_bytes=VMEM_LIMIT
        ),
    )(*ins)


DMA = pltpu.SemaphoreType.DMA


def nn(a, b):
    return jnp.dot(a, b, preferred_element_type=F32)


def nt(a, b):
    return lax.dot_general(a, b, (((1,), (1,)), ((), ())), preferred_element_type=F32)


def tn(a, b):
    return lax.dot_general(a, b, (((0,), (0,)), ((), ())), preferred_element_type=F32)


def rows_at(r, size):
    return pl.ds(pl.multiple_of(r, size), size)


def add_into(dst, cols, other, other_cols):
    @pl.loop(0, dst.shape[0], step=64)
    def _(r):
        at = rows_at(r, 64)
        dst[at, cols] = (dst[at, cols].astype(F32) + other[at, other_cols].astype(F32)).astype(BF16)


def start(copy):
    copy.start()
    return copy


def ffn_kernel(
    gated_ref, wo_ref, tok_ref, gain_ref, bias_ref, wu_ref, wd_ref, cot_ref,
    block_out, resid_out, gains, da, fu, fd,
    tok, resid_grad, share, wu, wd, rx0, rx1a, rx1b, rx2a, rx2b, resid, xn, act, dact, du, cot, dab, stage, tmp,
    lsem, gload, csend, crecv, xsend, xrecv, psend, precv, gsend, grecv, ksend, krecv, ssem, osem,
):
    me = Place()
    p, f = me.p, me.f
    greeted = call([(me.plane(1), None), (me.plane(2), None), (me.partner(), None)])
    rows, width = tok_ref.shape
    hidden = wu.shape[1]
    q = [me.xor(m) for m in range(4)]
    wide = width // 2
    hr = rows // 2
    span = 2 * rows
    ca, cb = pl.ds(0, wide), pl.ds(wide, wide)
    everything, whole = pl.ds(0, width), pl.ds(0, wide)
    own_half = [pl.ds(h * hr, hr) for h in range(2)]
    mine = [rows_at(h * rows + f * hr, hr) for h in range(2)]
    theirs = [rows_at(h * rows + (1 - f) * hr, hr) for h in range(2)]
    both = [pl.ds(h * rows, rows) for h in range(2)]

    order = (3, 1, 2, 0)
    part_width = gated_ref.shape[1]
    def out_slab(i):
        at = rows_at(i * 512, 512)
        return pltpu.make_async_copy(wo_ref.at[:, at], act.at[:, at], osem.at[i])

    slabs = width // 512
    out_slab(0).start()
    load_t = pltpu.make_async_copy(tok_ref, tok, lsem.at[7])
    load_g = {
        m: start(
            pltpu.make_async_copy(
                gated_ref.at[rows_at(q[m] * span, span), :],
                xn.at[:, m * part_width : (m + 1) * part_width],
                gload.at[m],
            )
        )
        for m in order
    }
    for i in range(1, slabs):
        out_slab(i).start()
    load_t.start()
    load_d = start(pltpu.make_async_copy(wd_ref, wd, lsem.at[1]))
    load_c = [
        start(
            pltpu.make_async_copy(
                cot_ref.at[pl.ds(c * rows + h * hr, hr), :], cot.at[pl.ds(h * rows + c * hr, hr), :], lsem.at[3 + 2 * h + c]
            )
        )
        for h in range(2)
        for c in range(2)
    ]
    load_u = start(pltpu.make_async_copy(wu_ref, wu, lsem.at[2]))
    first, sends = {}, {}

    def to_partner(m, h):
        first[m, h] = start(
            remote(
                share.at[m, rows_at((1 - f) * rows + h * hr, hr)], rx0.at[m, own_half[h]],
                csend.at[m, h], crecv.at[m, h], me.partner(),
            )
        )

    def make(m):
        load_g[m].wait()

        @pl.loop(0, slabs)
        def _(i):
            if m == order[0]:
                out_slab(i).wait()
            at = rows_at(i * 512, 512)
            share[m, :, at] = nn(xn[:, m * part_width : (m + 1) * part_width], act[:, at]).astype(BF16)

        if m == order[0]:
            meet(greeted)
        to_partner(m, 0)

    def pass_on(m, h):
        first[m, h].wait_recv()
        at = own_half[h]
        add_into(rx0.at[m, at], everything, share.at[m, rows_at(f * rows + h * hr, hr)], everything)
        k = 0 if m == 3 else 1
        if m & 1:
            sends["a", k, h] = start(
                remote(rx0.at[m, at, ca], rx1a.at[k, at], xsend.at[k, h], xrecv.at[k, h], me.plane(1))
            )
        if m & 2:
            sends["b", k, h] = start(
                remote(rx0.at[m, at, cb], rx1b.at[k, at], xsend.at[2 + k, h], xrecv.at[2 + k, h], me.plane(2))
            )

    def second(h):
        at = own_half[h]
        sends["a", 0, h].wait_recv()
        add_into(rx1a.at[0, at], whole, rx0.at[2, at], ca)
        sends["a", 2, h] = start(
            remote(rx1a.at[0, at], rx2a.at[at], xsend.at[4, h], xrecv.at[4, h], me.plane(2))
        )
        sends["b", 0, h].wait_recv()
        add_into(rx1b.at[0, at], whole, rx0.at[1, at], cb)
        sends["b", 2, h] = start(
            remote(rx1b.at[0, at], rx2b.at[at], xsend.at[5, h], xrecv.at[5, h], me.plane(1))
        )

    make(3)
    make(1)
    pass_on(3, 0)
    make(2)
    pass_on(1, 0)
    make(0)
    pass_on(2, 0)
    pass_on(0, 0)
    for m in order:
        to_partner(m, 1)

    load_d.wait()
    for c in load_c:
        c.wait()

    @pl.loop(0, hidden, step=512)
    def _(c):
        at = rows_at(c, 512)
        dact[:, at] = nt(cot[...], wd[at, :])

    second(0)
    for m in order:
        pass_on(m, 1)
    load_u.wait()
    step = 32

    def norm(h):
        for key in (("a", 1, h), ("b", 1, h), ("a", 2, h), ("b", 2, h)):
            sends[key].wait_recv()

        @pl.loop(0, hr, step=step)
        def _(r):
            at = pl.ds(pl.multiple_of(h * hr + r, step), step)
            left = rx0[0, at, ca].astype(F32) + rx1a[1, at, :].astype(F32) + rx2a[at, :].astype(F32)
            right = rx0[0, at, cb].astype(F32) + rx1b[1, at, :].astype(F32) + rx2b[at, :].astype(F32)
            v = tok[at, :].astype(F32) + jnp.concatenate([left, right], axis=1)
            resid[at, :] = v
            centered = v - jnp.mean(v, axis=1, keepdims=True)
            scale = lax.rsqrt(jnp.mean(centered * centered, axis=1, keepdims=True) + 1e-05)
            xn[pl.ds(pl.multiple_of(h * rows + f * hr + r, step), step), :] = (
                centered * scale * gain_ref[...] + bias_ref[...]
            ).astype(BF16)

        return start(remote(xn.at[mine[h]], xn.at[mine[h]], psend.at[0, h], precv.at[0, h], me.partner()))

    def hidden_part(h):
        @pl.loop(0, hidden, step=512)
        def _(c):
            at = rows_at(c, 512)
            u = nn(xn[both[h], :], wu[:, at])
            e = 0.5 * (1.0 + lax.erf(u * 0.7071067811865476))
            act[both[h], at] = (u * e).astype(BF16)
            slope = e + u * jnp.exp(-0.5 * u * u) * 0.3989422804014327
            du[both[h], at] = (dact[both[h], at] * slope).astype(BF16)

    def back_part(h):
        @pl.loop(0, width, step=512)
        def _(c):
            at = rows_at(c, 512)
            tmp[...] = nt(du[both[h], :], wu[at, :])
            resid_grad[own_half[h], at] = tmp[rows_at(f * hr, hr), :]
            share[0, own_half[h], at] = tmp[rows_at((1 - f) * hr, hr), :].astype(BF16)

        return start(
            remote(share.at[0, own_half[h]], share.at[1, own_half[h]], psend.at[1, h], precv.at[1, h], me.partner())
        )

    def norm_back(h):
        @pl.loop(0, hr, step=step)
        def _(r):
            at = pl.ds(pl.multiple_of(h * hr + r, step), step)
            dx = resid_grad[at, :] + share[1, at, :].astype(F32)
            v = resid[at, :]
            centered = v - jnp.mean(v, axis=1, keepdims=True)
            scale = lax.rsqrt(jnp.mean(centered * centered, axis=1, keepdims=True) + 1e-05)
            hat = centered * scale
            gains[0:1, :] += jnp.sum(dx * hat, axis=0, keepdims=True)
            gains[1:2, :] += jnp.sum(dx, axis=0, keepdims=True)
            g = dx * gain_ref[...]
            back = scale * (
                g - jnp.mean(g, axis=1, keepdims=True) - hat * jnp.mean(g * hat, axis=1, keepdims=True)
            )
            back = back + cot[pl.ds(pl.multiple_of(h * rows + f * hr + r, step), step), :].astype(F32)
            resid_grad[at, :] = back
            dab[at, :] = back.astype(BF16)

    def out_part(h):
        @pl.loop(0, width, step=512)
        def _(c):
            at = rows_at(c, 512)
            tmp[...] = nn(act[both[h], :], wd[:, at])
            dact[pl.ds(h * rows, hr), at] = tmp[rows_at(f * hr, hr), :]
            share[2, own_half[h], at] = tmp[rows_at((1 - f) * hr, hr), :].astype(BF16)

        return start(
            remote(share.at[2, own_half[h]], share.at[3, own_half[h]], psend.at[2, h], precv.at[2, h], me.partner())
        )

    quarter = hr // 2

    def seat(m, h, k=None):
        base = (q[m] * 2 + f) * rows + h * hr
        if k is None:
            return da.at[pl.ds(pl.multiple_of(base, hr), hr), :]
        return da.at[pl.ds(pl.multiple_of(base + k * quarter, quarter), quarter), :]

    spread = {}

    def spread_begin(h):
        spread["own", h] = start(pltpu.make_async_copy(dab.at[own_half[h]], seat(0, h), gload.at[h]))
        for i in range(2):
            for to, k in ((1, i), (2, 1 - i)):
                sem = (to - 1) * 2 + i
                spread[to, i, h] = start(
                    remote(
                        dab.at[pl.ds(h * hr + k * quarter, quarter)], seat(0, h, k),
                        gsend.at[sem, h], grecv.at[sem, h], me.plane(to),
                    )
                )
        spread["core", 0, h] = start(
            remote(dab.at[own_half[h]], seat(0, h), ksend.at[0, h], krecv.at[0, h], me.partner())
        )

    def spread_on(h):
        spread[1, 0, h].wait_recv()
        spread["g1", h] = start(
            remote(seat(1, h, 0), seat(1, h, 0), gsend.at[4, h], grecv.at[4, h], me.plane(2))
        )
        spread[2, 0, h].wait_recv()
        spread["g2", h] = start(
            remote(seat(2, h, 1), seat(2, h, 1), gsend.at[5, h], grecv.at[5, h], me.plane(1))
        )

    def spread_end(h):
        for m in (1, 2):
            spread[m, 1, h].wait_recv()
            spread["core", m, h] = start(
                remote(seat(m, h), seat(m, h), ksend.at[m, h], krecv.at[m, h], me.partner())
            )
        spread["g1", h].wait_recv()
        spread["g2", h].wait_recv()
        spread["core", 3, h] = start(
            remote(seat(3, h), seat(3, h), ksend.at[3, h], krecv.at[3, h], me.partner())
        )

    gains[...] = jnp.zeros_like(gains)
    for c in first.values():
        c.wait_send()
    load_t.wait()
    swaps = [norm(0)]
    swaps[0].wait_recv()
    hidden_part(0)
    second(1)
    swaps.append(back_part(0))
    out_swaps = [out_part(0)]
    swaps[1].wait_recv()
    norm_back(0)
    spread_begin(0)
    swaps.append(norm(1))
    swaps[2].wait_recv()
    hidden_part(1)
    spread_on(0)
    swaps.append(back_part(1))
    out_swaps.append(out_part(1))
    swaps[3].wait_recv()
    norm_back(1)
    spread_begin(1)
    resid_copy = start(pltpu.make_async_copy(resid_grad, resid_out, lsem.at[0]))

    def weights_part(left, right, out):
        def spill(slot, i):
            return pltpu.make_async_copy(stage.at[slot], out.at[rows_at(i * 256, 256), :], ssem.at[slot])

        @pl.loop(0, width // 256)
        def _(i):
            slot = i % 3

            @pl.when(i >= 3)
            def _():
                spill(slot, i - 3).wait()

            stage[slot] = tn(left[:, rows_at(i * 256, 256)], right[...]).astype(BF16)
            spill(slot, i).start()

        for k in (3, 2, 1):
            i = width // 256 - k
            spill(i % 3, i).wait()

    weights_part(cot, act, fd)
    spread_on(1)
    spread_end(0)
    for h in range(2):
        out_swaps[h].wait_recv()

        @pl.loop(0, hr, step=step)
        def _(r):
            at = pl.ds(pl.multiple_of(h * hr + r, step), step)
            own = dact[pl.ds(pl.multiple_of(h * rows + r, step), step), :]
            tok[at, :] = (resid[at, :] + own + share[3, at, :].astype(F32)).astype(BF16)

    out_copy = start(pltpu.make_async_copy(tok, block_out, lsem.at[1]))
    weights_part(xn, du, fu)
    spread_end(1)
    resid_copy.wait()
    out_copy.wait()
    for h in range(2):
        spread["own", h].wait()
        for m in range(4):
            spread["core", m, h].wait()
        for key in ((1, 0, h), (1, 1, h), (2, 0, h), (2, 1, h), ("g1", h), ("g2", h)):
            spread[key].wait_send()
    for c in swaps + out_swaps + list(sends.values()):
        c.wait_send()


def ffn_part(gated, w_out, tokens, gain, bias, w_up, w_down, cotangent, cid):
    rows, width = tokens.shape
    assert PLANE * gated.shape[1] == width and w_out.shape == (2 * rows, w_up.shape[1])
    span, hidden = 2 * rows, w_up.shape[1]
    sd = jax.ShapeDtypeStruct
    return comm_call(
        ffn_kernel,
        [
            sd((rows, width), BF16),
            sd((rows, width), F32),
            sd((8, width), F32),
            sd((2 * PLANE * rows, width), BF16),
            sd((width, hidden), BF16),
            sd((width, hidden), BF16),
        ],
        [gated, w_out, tokens, gain[None], bias[None], w_up, w_down, cotangent],
        [
            pltpu.VMEM((rows, width), BF16),
            pltpu.VMEM((rows, width), F32),
            pltpu.VMEM((PLANE, span, width), BF16),
            pltpu.VMEM(w_up.shape, BF16),
            pltpu.VMEM(w_down.shape, BF16),
            pltpu.VMEM((PLANE, rows, width), BF16),
            pltpu.VMEM((2, rows, width // 2), BF16),
            pltpu.VMEM((2, rows, width // 2), BF16),
            pltpu.VMEM((rows, width // 2), BF16),
            pltpu.VMEM((rows, width // 2), BF16),
            pltpu.VMEM((rows, width), F32),
            pltpu.VMEM((span, width), BF16),
            pltpu.VMEM((span, hidden), BF16),
            pltpu.VMEM((span, hidden), F32),
            pltpu.VMEM((span, hidden), BF16),
            pltpu.VMEM((span, width), BF16),
            pltpu.VMEM((rows, width), BF16),
            pltpu.VMEM((3, 256, hidden), BF16),
            pltpu.VMEM((rows, 512), F32),
            DMA((8,)),
            DMA((PLANE,)),
            DMA((PLANE, 2)),
            DMA((PLANE, 2)),
            DMA((6, 2)),
            DMA((6, 2)),
            DMA((3, 2)),
            DMA((3, 2)),
            DMA((6, 2)),
            DMA((6, 2)),
            DMA((4, 2)),
            DMA((4, 2)),
            DMA((3,)),
            DMA((width // 512,)),
        ],
        cid,
        in_specs=[ANY, ANY, ANY, VM, VM, ANY, ANY, ANY],
        out_specs=[ANY, ANY, VM, ANY, ANY, ANY],
    )


def attention_kernel(
    widths, by_rows,
    tok_ref, gain_ref, bias_ref, dec_ref, cbase, sbase, coff, soff, *refs,
):
    count = len(widths)
    shards_in, refs = refs[:count], refs[count:]
    (xg, q_out, k_out, v_out, gate_out, ret_out, gated_out, states_out, cos_out, sin_out, ccol_out, crow_out, scal_out), refs = (
        refs[:13], refs[13:],
    )
    full, refs = refs[:count], refs[count:]
    hold, refs = refs[:count], refs[count:]
    wl, refs = refs[: count - 1], refs[count - 1 :]
    (tok, ccol, crow, scal, xn, xv, q, k, v, gate, ret, gated, cos, sin, kv, st, sloc, sgot, decg,
     lsem, psend, precv, usend, dsend, zrecv, xsend, xrecv, csend, crecv, tsend, trecv, ssend, srecv, osem, wsem) = refs
    me = Place()
    z, p, f = me.z, me.p, me.f
    spot = z * PLANE + p
    chunk = hold[0].shape[0]
    deep = chunk * PLANE
    tokens, width = xv.shape
    rows = tok_ref.shape[0]
    keys, values = q.shape[1], v.shape[1]
    half = keys // 2
    blocks = tokens // STRETCH
    greet(
        [(me.plane(m), None) for m in (1, 2, 3)]
        + [(me.partner(), None), (me.up(), z < LINE - 1), (me.down(), z > 0)]
    )

    def part(i, at):
        w = widths[i]
        if by_rows[i]:
            return shards_in[i].at[pl.ds(pl.multiple_of(at * w, w), w), :]
        return shards_in[i].at[:, pl.ds(pl.multiple_of(at * w, w), w)]

    def slot(i, ss):
        at = pl.ds(pl.multiple_of(ss * chunk, chunk), chunk)
        return full[i].at[:, at] if by_rows[i] else full[i].at[at, :]

    def block(i, zz):
        at = pl.ds(pl.multiple_of(zz * deep, deep), deep)
        return full[i].at[:, at] if by_rows[i] else full[i].at[at, :]

    def up_copy(i, zz):
        return remote(block(i, zz), block(i, zz), usend.at[i, zz], zrecv.at[i, zz], me.up())

    def down_copy(i, zz):
        return remote(block(i, zz), block(i, zz), dsend.at[i, zz], zrecv.at[i, zz], me.down())

    def part_copies(i, src, at):
        return (
            remote(src, slot(i, at), usend.at[i, z], zrecv.at[i, z], me.up()),
            remote(src, slot(i, at), dsend.at[i, z], zrecv.at[i, z], me.down()),
        )

    def to_line(copies):
        @pl.when(z < LINE - 1)
        def _():
            copies[0].start()

        @pl.when(z > 0)
        def _():
            copies[1].start()

    ahead = count
    for i in range(ahead):
        to_line(part_copies(i, part(i, p), spot))
    load_t = start(pltpu.make_async_copy(tok_ref, tok, lsem.at[count + 1]))
    local, plane, held = [], [], []
    for i in range(count):
        held.append(start(pltpu.make_async_copy(part(i, p), hold[i], lsem.at[i])))
        local.append(pltpu.make_async_copy(hold[i], slot(i, spot), lsem.at[i]))
        plane.append(
            [
                start(remote(part(i, me.xor(m)), slot(i, spot), psend.at[i, m], precv.at[i, m], me.plane(m)))
                for m in (1, 2, 3)
            ]
        )
    tiny = [start(remote(dec_ref, decg.at[p], tsend.at[m], trecv.at[m], me.plane(m))) for m in (1, 2, 3)]
    tiny_own = start(pltpu.make_async_copy(dec_ref, decg.at[p], tsend.at[0]))
    step = 32
    load_t.wait()

    @pl.loop(0, rows, step=step)
    def _(r):
        at = rows_at(r, step)
        t = tok[at, :].astype(F32)
        centered = t - jnp.mean(t, axis=1, keepdims=True)
        scale = lax.rsqrt(jnp.mean(centered * centered, axis=1, keepdims=True) + 1e-05)
        xn[at, :] = (centered * scale * gain_ref[...] + bias_ref[...]).astype(BF16)

    def seat(m, h=None):
        base = (me.xor(m) * 2 + f) * rows
        if h is None:
            return xv.at[rows_at(base, rows)]
        return xv.at[pl.ds(pl.multiple_of(base + h * (rows // 2), rows // 2), rows // 2)]

    x_own = start(pltpu.make_async_copy(xn, seat(0), lsem.at[count]))
    x1 = start(remote(xn, seat(0), xsend.at[0], xrecv.at[0], me.plane(1)))
    x2 = start(remote(xn, seat(0), xsend.at[1], xrecv.at[1], me.plane(2)))
    xc = start(remote(xn, seat(0), csend.at[0], crecv.at[0], me.partner()))
    for i in range(count):
        held[i].wait()
        local[i].start()

    def own(i):
        local[i].wait()
        for c in plane[i]:
            c.wait_recv()
        if i < ahead:
            for m in (1, 2, 3):
                at = z * PLANE + me.xor(m)
                to_line(part_copies(i, slot(i, at), at))
        else:
            to_line((up_copy(i, z), down_copy(i, z)))

    def forward(i, t):
        @pl.when(z - t >= 0)
        def _():
            up_copy(i, z - t).wait_recv()

            @pl.when(z < LINE - 1)
            def _():
                up_copy(i, z - t).start()

        @pl.when(z + t < LINE)
        def _():
            down_copy(i, z + t).wait_recv()

            @pl.when(z > 0)
            def _():
                down_copy(i, z + t).start()

    def fetch(i):
        forward(i, LINE - 1)
        return start(pltpu.make_async_copy(full[i], wl[i], wsem.at[i]))

    K, V, Q, G, O = range(count)
    own(K)
    own(V)
    forward(K, 1)
    forward(K, 2)
    own(Q)

    for c in tiny:
        c.wait()
    tiny_own.wait()
    heads = lax.broadcasted_iota(jnp.int32, decg.shape[1:], 0)
    lines = [jnp.sum(jnp.where(heads == p, decg[j], 0.0), axis=0, keepdims=True) for j in range(blocks)]
    lines = jnp.concatenate(lines + [jnp.zeros_like(lines[0])] * (8 - blocks), axis=0)
    i0 = lax.broadcasted_iota(jnp.int32, (STRETCH, STRETCH), 0)
    i1 = lax.broadcasted_iota(jnp.int32, (STRETCH, STRETCH), 1)
    row_sums = jnp.dot(
        lines, jnp.where(i0 <= i1, 1.0, 0.0), preferred_element_type=F32, precision=lax.Precision.HIGHEST
    )
    col_sums = lax.dot_general(
        jnp.where(i1 <= i0, 1.0, 0.0), lines, (((1,), (1,)), ((), ())),
        preferred_element_type=F32, precision=lax.Precision.HIGHEST,
    )
    total = jnp.zeros((1, 1), F32)
    for c in range(blocks):
        end = row_sums[c : c + 1, STRETCH - 1 : STRETCH]
        crow[c] = jnp.broadcast_to(row_sums[c : c + 1, :], (8, STRETCH))
        ccol[c * STRETCH : (c + 1) * STRETCH, :] = col_sums[:, c : c + 1]
        scal[c] = jnp.broadcast_to(jnp.exp(end), (8, 128))
        scal[blocks + c] = jnp.broadcast_to(jnp.exp(total), (8, 128))
        total = total + end
    scal[2 * blocks] = jnp.broadcast_to(total, (8, 128))

    fine = coff.shape[0]

    @pl.loop(0, tokens // fine)
    def _(a):
        at = rows_at(a * fine, fine)
        place = pl.ds(z * (tokens // fine) + a, 1)
        ca, sa = cbase[place, :], sbase[place, :]
        cos[at, :] = ca * coff[...] - sa * soff[...]
        sin[at, :] = sa * coff[...] + ca * soff[...]

    forward(V, 1)
    x1.wait_recv()
    g1 = start(remote(seat(1, 0), seat(1, 0), xsend.at[2], xrecv.at[2], me.plane(2)))
    c1 = start(remote(seat(1), seat(1), csend.at[1], crecv.at[1], me.partner()))
    x2.wait_recv()
    g2 = start(remote(seat(2, 1), seat(2, 1), xsend.at[3], xrecv.at[3], me.plane(1)))
    c2 = start(remote(seat(2), seat(2), csend.at[2], crecv.at[2], me.partner()))
    forward(V, 2)
    forward(Q, 1)
    own(G)
    forward(Q, 2)
    own(O)
    load_k = fetch(K)
    g1.wait_recv()
    g2.wait_recv()
    c3 = start(remote(seat(3), seat(3), csend.at[3], crecv.at[3], me.partner()))
    x_own.wait()
    for c in (xc, c1, c2, c3):
        c.wait_recv()
    outs = []

    def put(src, dst):
        outs.append(start(pltpu.make_async_copy(src, dst, osem.at[len(outs)])))

    put(xv, xg)
    put(ccol, ccol_out)
    put(crow, crow_out)
    put(scal, scal_out)
    put(cos, cos_out)
    put(sin, sin_out)
    load_k.wait()

    def turned(at, w, dst):
        y = nn(xv[at, :], w[...])
        a, b = y[:, :half], y[:, half:]
        dst[at, :half] = (a * cos[at, :] - b * sin[at, :]).astype(BF16)
        dst[at, half:] = (b * cos[at, :] + a * sin[at, :]).astype(BF16)

    @pl.loop(0, blocks)
    def _(c):
        turned(rows_at(c * STRETCH, STRETCH), wl[K], k)

    fetch(V).wait()

    @pl.loop(0, blocks)
    def _(c):
        at = rows_at(c * STRETCH, STRETCH)
        val = nn(xv[at, :], wl[V][...]).astype(BF16)
        v[at, :] = val
        end = crow[c, 0:1, STRETCH - 1 : STRETCH]
        kv[c] = tn(k[at, :], (val.astype(F32) * jnp.exp(end - ccol[at, :])).astype(BF16))

    put(k, k_out)
    put(v, v_out)
    sloc[...] = kv[0]
    kv[0] = jnp.zeros_like(sloc)
    for c in range(1, blocks):
        nxt = sloc[...] * scal[c, 0:1, 0:1] + kv[c]
        kv[c] = sloc[...]
        sloc[...] = nxt

    def state_copy(zz):
        return remote(st.at[0], sgot, ssend.at[zz], srecv.at[zz], me.up())

    def send_state():
        st[0] = sloc[...].astype(BF16)
        state_copy(0).start()

    @pl.when(z == 0)
    def _():
        send_state()

    def pass_state(zz):
        @pl.when(z == zz)
        def _():
            state_copy(0).wait_recv()
            if zz < LINE - 1:
                sloc[...] = sloc[...] + sgot[...].astype(F32) * jnp.exp(scal[2 * blocks, 0:1, 0:1])
                send_state()

    pass_state(1)
    forward(G, 1)
    forward(O, 1)
    fetch(Q).wait()
    t_size = 256

    @pl.loop(0, blocks)
    def _(c):
        blk = rows_at(c * STRETCH, STRETCH)
        turned(blk, wl[Q], q)
        row = crow[c, 0:1, :]
        for r in range(0, STRETCH, t_size):
            at = rows_at(c * STRETCH + r, t_size)
            col = ccol[at, :]
            t_index = lax.broadcasted_iota(jnp.int32, (t_size, STRETCH), 0) + r
            s_index = lax.broadcasted_iota(jnp.int32, (t_size, STRETCH), 1)
            mask = jnp.where(t_index >= s_index, jnp.exp(jnp.minimum(col - row, 0.0)), 0.0)
            scores = (nt(q[at, :], k[blk, :]) * mask).astype(BF16)
            ret[at, :] = nn(scores, v[blk, :])

    put(q, q_out)
    pass_state(2)
    forward(G, 2)
    forward(O, 2)
    pass_state(3)

    @pl.when((z > 0) & (z < LINE - 1))
    def _():
        state_copy(0).wait_send()

    @pl.when(z == 0)
    def _():
        state_copy(0).wait_send()
        sgot[...] = jnp.zeros_like(sgot)

    for c in range(blocks):
        st[c] = (kv[c] + sgot[...].astype(F32) * scal[blocks + c, 0:1, 0:1]).astype(BF16)

    @pl.loop(0, blocks)
    def _(c):
        at = rows_at(c * STRETCH, STRETCH)
        decayed = (q[at, :].astype(F32) * jnp.exp(ccol[at, :])).astype(BF16)
        ret[at, :] += nn(decayed, st[c])

    put(ret, ret_out)
    put(st, states_out)
    fetch(G).wait()

    @pl.loop(0, tokens, step=256)
    def _(r):
        at = rows_at(r, 256)
        g = nn(xv[at, :], wl[G][...])
        gate[at, :] = g
        t = ret[at, :]
        centered = t - jnp.mean(t, axis=1, keepdims=True)
        scale = lax.rsqrt(jnp.mean(centered * centered, axis=1, keepdims=True) + 1e-05)
        gated[at, :] = (g / (1.0 + jnp.exp(-g)) * centered * scale).astype(BF16)

    put(gate, gate_out)
    put(gated, gated_out)
    forward(O, LINE - 1)
    for c in (xc, c1, c2, c3, x1, x2, g1, g2):
        c.wait_send()
    for i in range(count):
        for c in plane[i]:
            c.wait_send()
        for zz in range(LINE):

            @pl.when((z < LINE - 1) & (zz <= z))
            def _():
                up_copy(i, zz).wait_send()

            @pl.when((z > 0) & (zz >= z))
            def _():
                down_copy(i, zz).wait_send()

    for c in outs:
        c.wait()


def attention(tokens, gain, bias, decays, tables, shards_in, by_rows, cid):
    rows, width = tokens.shape
    count = len(shards_in)
    chunk = shards_in[0].shape[0]
    group = 2 * PLANE * rows
    blocks = group // STRETCH
    parts = [
        (w.shape[0] // PLANE, chunk) if r else (chunk, w.shape[1] // PLANE) for w, r in zip(shards_in, by_rows)
    ]
    widths = [s[0] if r else s[1] for s, r in zip(parts, by_rows)]
    wholes = [(s[0], width) if r else (width, s[1]) for s, r in zip(parts, by_rows)]
    values, keys = widths[1], widths[0]
    half = keys // 2
    sd = jax.ShapeDtypeStruct
    outs = [
        sd((group, width), BF16),
        sd((group, keys), BF16),
        sd((group, keys), BF16),
        sd((group, values), BF16),
        sd((group, values), F32),
        sd((group, values), F32),
        sd((group, values), BF16),
        sd((blocks, keys, values), BF16),
        sd((group, half), F32),
        sd((group, half), F32),
        sd((group, 1), F32),
        sd((blocks, 8, STRETCH), F32),
        sd((2 * blocks + 1, 8, 128), F32),
    ] + [sd(s, BF16) for s in wholes]
    scratch = (
        [pltpu.VMEM(s, BF16) for s in parts]
        + [pltpu.VMEM(s, BF16) for s in wholes[:-1]]
        + [
            pltpu.VMEM((rows, width), BF16),
            pltpu.VMEM((group, 1), F32),
            pltpu.VMEM((blocks, 8, STRETCH), F32),
            pltpu.VMEM((2 * blocks + 1, 8, 128), F32),
            pltpu.VMEM((rows, width), BF16),
            pltpu.VMEM((group, width), BF16),
            pltpu.VMEM((group, keys), BF16),
            pltpu.VMEM((group, keys), BF16),
            pltpu.VMEM((group, values), BF16),
            pltpu.VMEM((group, values), F32),
            pltpu.VMEM((group, values), F32),
            pltpu.VMEM((group, values), BF16),
            pltpu.VMEM((group, half), F32),
            pltpu.VMEM((group, half), F32),
            pltpu.VMEM((blocks, keys, values), F32),
            pltpu.VMEM((blocks, keys, values), BF16),
            pltpu.VMEM((keys, values), F32),
            pltpu.VMEM((keys, values), BF16),
            pltpu.VMEM((PLANE,) + decays.shape, F32),
            DMA((count + 2,)),
            DMA((count, PLANE)),
            DMA((count, PLANE)),
            DMA((count, LINE)),
            DMA((count, LINE)),
            DMA((count, LINE)),
            DMA((4,)),
            DMA((4,)),
            DMA((4,)),
            DMA((4,)),
            DMA((PLANE,)),
            DMA((PLANE,)),
            DMA((1,)),
            DMA((1,)),
            DMA((16,)),
            DMA((count,)),
        ]
    )
    return comm_call(
        functools.partial(attention_kernel, widths, by_rows),
        outs,
        [tokens, gain[None], bias[None], decays] + list(tables) + list(shards_in),
        scratch,
        cid,
        in_specs=[ANY] + [VM] * 7 + [ANY] * count,
        out_specs=[ANY] * (13 + count),
    )


class LineSum:
    def __init__(self, me, own, rx, usend, urecv, dsend, drecv, add):
        self.me, self.own, self.rx, self.add = me, own, rx, add
        self.sems = usend, urecv, dsend, drecv

    def up(self, src, zz):
        return remote(src, self.rx.at[zz], self.sems[0].at[zz], self.sems[1].at[zz], self.me.up())

    def down(self, src, zz):
        slot = jnp.where(zz == self.me.z - 1, LINE, zz)
        return remote(src, self.rx.at[slot], self.sems[2].at[zz], self.sems[3].at[zz], self.me.down())

    def begin(self, order=(3, 2, 1), src=None):
        src = src or self.own
        for zz in order:

            @pl.when(self.me.z == 0)
            def _():
                self.up(src(zz), zz).start()

            @pl.when(self.me.z == LINE - 1)
            def _():
                self.down(src(LINE - 1 - zz), LINE - 1 - zz).start()

    def pass_up(self, zz):
        self.up(self.own(zz), zz).wait_recv()
        self.add(self.rx.at[zz], self.own(zz))
        self.up(self.rx.at[zz], zz).start()

    def pass_down(self, zz):
        self.down(self.own(zz), zz).wait_recv()
        self.add(self.rx.at[zz], self.own(zz))
        self.down(self.rx.at[zz], zz).start()

    def near(self, k):
        @pl.when(self.me.z == 1)
        def _():
            self.pass_up(LINE - 1 - k)

        @pl.when(self.me.z == 2)
        def _():
            self.pass_down(k)

    def far(self):
        @pl.when(self.me.z == 1)
        def _():
            self.pass_down(0)

        @pl.when(self.me.z == 2)
        def _():
            self.pass_up(LINE - 1)

    def arrive(self):
        z = self.me.z

        @pl.when(z > 0)
        def _():
            self.up(self.own(z), z).wait_recv()

        @pl.when(z < LINE - 1)
        def _():
            self.down(self.own(z), z).wait_recv()

    def finish(self):
        z = self.me.z
        for zz in range(LINE):

            @pl.when((z < LINE - 1) & (zz > z))
            def _():
                self.up(self.own(zz), zz).wait_send()

            @pl.when((z > 0) & (zz < z))
            def _():
                self.down(self.own(zz), zz).wait_send()


def add_rows(dst, src):
    rows = dst.shape[0]
    step = 32 if dst.shape[1] > 512 else 128

    @pl.loop(0, rows, step=step)
    def _(r):
        at = rows_at(r, step)
        dst[at, :] = (dst[at, :].astype(F32) + src[at, :].astype(F32)).astype(BF16)


def total_rows(z, dst, own, rx):
    rows = dst.shape[0]
    step = 32 if dst.shape[1] > 512 else 128

    @pl.loop(0, rows, step=step)
    def _(r):
        at = rows_at(r, step)
        v = own[at, :].astype(F32)
        v = v + jnp.where(z > 0, rx[z, at, :].astype(F32), 0.0)
        v = v + jnp.where(z < LINE - 1, rx[LINE, at, :].astype(F32), 0.0)
        dst[at, :] = v.astype(dst.dtype)


def line_sems():
    return [DMA((LINE,)) for _ in range(4)]


def retention_back_kernel(
    da_ref, wo_ref, gated_ref, gate_ref, ret_ref, q_ref, k_ref, v_ref, s_ref, cos_ref, sin_ref,
    ccol_in, crow_in, scal_in, xg_ref, fu_ref, fd_ref,
    dh_out, sums, gate_fin, f1, av_out, aq_out,
    ccol_ref, crow_ref, scal_ref, dh, da, wo, gated, gr, q, k, v, st, cos, sin, dr, xt, ao, ag, rxo, rxg, fin, qo, gb, lg, got, rxf, fo, pbuf, gbuf,
    lsem, gsem, xsem, fsend, frecv, osem, fosem, ssend, srecv, psend, precv, *line,
):
    me = Place()
    z, p = me.z, me.p
    greeted = call(
        [(me.plane(m), None) for m in (1, 2, 3)]
        + [(me.up(), z < LINE - 1), (me.down(), z > 0)]
    )
    width = da.shape[1]
    tokens = da.shape[0]
    keys, values = q.shape[1], v.shape[1]
    blocks = tokens // STRETCH
    half = keys // 2
    pq = [me.xor(m) for m in range(4)]
    chunk = fu_ref.shape[0] // SPANS

    def f_block(h, zp, place):
        return (fu_ref, fd_ref)[h].at[pl.ds(pl.multiple_of((zp * PLANE + place) * chunk, chunk), chunk), :]

    units = [(h, zp, (0, 1)) for zp in (3, 0, 2) for h in range(2)] + [(h, 1, (1,)) for h in range(2)]

    def f_slot(h, zp, j):
        return rxf.at[h, 2 * (3, 0, 2, 1).index(zp) + (j if zp != 1 else 0)]
    away = ((1, 3), (2, 3))
    kept = ((0, 2), (0, 1))
    nbr = (1, 2)

    def f_copy(h, zp, j):
        return remote(
            f_block(h, zp, pq[away[h][j]]), f_slot(h, zp, j), fsend.at[h, zp, j], frecv.at[h, zp, j], me.plane(nbr[h])
        )

    deep = width // LINE
    ends_first = [jnp.where(z < LINE // 2, LINE - 1 - i, i) for i in range(LINE)]

    def slab(i):
        at = rows_at(ends_first[i] * deep, deep)
        return pltpu.make_async_copy(da_ref.at[:, at], da.at[:, at], lsem.at[12 + i])

    slab(0).start()
    loads = [
        start(pltpu.make_async_copy(a, b, lsem.at[i]))
        for i, (a, b) in enumerate(
            [(gated_ref, gated), (wo_ref, wo), (q_ref, q), (k_ref, k), (v_ref, v), (s_ref, st),
             (cos_ref, cos), (sin_ref, sin), (ccol_in, ccol_ref), (crow_in, crow_ref), (scal_in, scal_ref)]
        )
    ]
    for i in range(1, LINE):
        slab(i).start()

    def f_own(u):
        h, zp, js = units[u]
        return [
            pltpu.make_async_copy(f_block(h, zp, pq[kept[h][j]]), fo.at[u % 2, j], fosem.at[u % 2, j])
            for j in js
        ]

    def f_out(u):
        h, zp, js = units[u]
        return [pltpu.make_async_copy(f_slot(h, zp, j), f1.at[h, zp, j], osem.at[u, j]) for j in js]

    for u in range(2):
        for c in f_own(u):
            c.start()

    def f_unit(u):
        h, zp, js = units[u]
        for j, c in zip(js, f_own(u)):
            c.wait()
            f_copy(h, zp, j).wait_recv()
            add_rows(f_slot(h, zp, j), fo.at[u % 2, j])
        for c in f_out(u):
            c.start()
        if u + 2 < len(units):
            for c in f_own(u + 2):
                c.start()

    def tile_rows(i):
        return rows_at(i * 256, 256)

    def gate_loads(i):
        at = tile_rows(i)
        slot = i % 3
        return (
            pltpu.make_async_copy(gate_ref.at[at, :], gr.at[slot, 0], gsem.at[slot, 0]),
            pltpu.make_async_copy(ret_ref.at[at, :], gr.at[slot, 1], gsem.at[slot, 1]),
        )

    for c in gate_loads(0) + gate_loads(1):
        c.start()

    out_sum = LineSum(me, lambda zz: ao.at[rows_at(zz * (width // LINE), width // LINE), :], rxo, *line[:4], add_rows)
    gate_sum = LineSum(me, lambda zz: ag.at[rows_at(zz * (width // LINE), width // LINE), :], rxg, *line[4:], add_rows)

    loads[0].wait()
    for turn in range(LINE):
        slab(turn).wait()

        @pl.loop(0, deep, step=256)
        def _(i):
            at = rows_at(ends_first[turn] * deep + i, 256)
            ao[at, :] = tn(da[:, at], gated[...]).astype(BF16)

        if turn == 0:
            meet(greeted)
        if turn < 2:
            out_sum.begin((LINE - 1 - turn,))
        if turn == 0:
            for h, zp, js in units:
                for j in js:
                    f_copy(h, zp, j).start()
    for c in loads[1:]:
        c.wait()

    tiles = tokens // 256

    @pl.loop(0, tiles)
    def _(i):
        @pl.when(i + 2 < tiles)
        def _():
            for c in gate_loads(i + 2):
                c.start()

        for c in gate_loads(i):
            c.wait()
        at = tile_rows(i)
        slot = i % 3
        dgated = nt(da[at, :], wo[...])
        gate = gr[slot, 0]
        ret = gr[slot, 1]
        centered = ret - jnp.mean(ret, axis=1, keepdims=True)
        scale = lax.rsqrt(jnp.mean(centered * centered, axis=1, keepdims=True) + 1e-05)
        grouped = centered * scale
        sig = 1.0 / (1.0 + jnp.exp(-gate))
        silu = gate * sig
        dh[at, 2 * keys + values :] = (dgated * grouped * (sig * (1.0 + gate * (1.0 - sig)))).astype(BF16)
        dg = dgated * silu
        dr[at, :] = (
            scale * (dg - jnp.mean(dg, axis=1, keepdims=True) - grouped * jnp.mean(dg * grouped, axis=1, keepdims=True))
        ).astype(BF16)

    lg[...] = jnp.zeros_like(lg)

    @pl.loop(0, blocks)
    def _(c):
        at = rows_at(c * STRETCH, STRETCH)
        decayed = (q[at, :].astype(F32) * jnp.exp(ccol_ref[at, :])).astype(BF16)
        got_q = tn(decayed, dr[at, :])
        qo[c] = got_q
        lg[...] += scal_ref[blocks + c, 0:1, 0:1] * got_q

    state_copy = remote(gb.at[0], got, ssend.at[0], srecv.at[0], me.down())

    def pass_state(zz):
        @pl.when(z == zz)
        def _():
            if zz < LINE - 1:
                state_copy.wait_recv()
            if zz > 0:
                add = lg[...]
                if zz < LINE - 1:
                    add = add + got[...].astype(F32) * jnp.exp(scal_ref[2 * blocks, 0:1, 0:1])
                gb[0] = add.astype(BF16)
                state_copy.start()

    pass_state(LINE - 1)
    out_sum.begin((1,))
    out_sum.near(0)
    def x_tile(i):
        return pltpu.make_async_copy(xg_ref.at[:, rows_at(i * 256, 256)], xt.at[i % 3], xsem.at[i % 3])

    x_tile(0).start()
    x_tile(1).start()

    @pl.loop(0, width // 256)
    def _(i):
        @pl.when(i + 2 < width // 256)
        def _():
            x_tile(i + 2).start()

        x_tile(i).wait()
        ag[rows_at(i * 256, 256), :] = tn(xt[i % 3], dh[:, 2 * keys + values :]).astype(BF16)

    gate_sum.begin()
    out_sum.near(1)
    pass_state(2)
    f_unit(0)
    f_unit(1)
    out_sum.far()

    pass_state(1)
    pass_state(0)

    @pl.when(z > 0)
    def _():
        state_copy.wait_send()

    @pl.when(z < LINE - 1)
    def _():
        lg[...] = got[...].astype(F32)

    @pl.when(z == LINE - 1)
    def _():
        lg[...] = jnp.zeros_like(lg)

    for c in reversed(range(blocks)):
        gb[c] = lg[...].astype(BF16)
        if c:
            lg[...] = lg[...] * scal_ref[c, 0:1, 0:1] + qo[c]

    t_size = 256

    @pl.loop(0, blocks)
    def _(c):
        blk = rows_at(c * STRETCH, STRETCH)
        row = crow_ref[c, 0:1, :]
        end = crow_ref[c, 0:1, STRETCH - 1 : STRETCH]
        for r in range(0, STRETCH, t_size):
            at = rows_at(c * STRETCH + r, t_size)
            col = ccol_ref[at, :]
            t_index = lax.broadcasted_iota(jnp.int32, (t_size, STRETCH), 0) + r
            s_index = lax.broadcasted_iota(jnp.int32, (t_size, STRETCH), 1)
            mask = jnp.where(t_index >= s_index, jnp.exp(jnp.minimum(col - row, 0.0)), 0.0)
            pbuf[r : r + t_size, :] = (nt(q[at, :], k[blk, :]) * mask).astype(BF16)
            g = (nt(dr[at, :], v[blk, :]) * mask).astype(BF16)
            gbuf[r : r + t_size, :] = g
            dq = nt(dr[at, :], st[c]) * jnp.exp(col) + nn(g, k[blk, :])
            a, b = dq[:, :half], dq[:, half:]
            dh[at, :half] = (a * cos[at, :] + b * sin[at, :]).astype(BF16)
            dh[at, half:keys] = (b * cos[at, :] - a * sin[at, :]).astype(BF16)
        for r in range(0, STRETCH, t_size):
            at = rows_at(c * STRETCH + r, t_size)
            tail = jnp.exp(end - ccol_ref[at, :])
            w = (v[at, :].astype(F32) * tail).astype(BF16)
            dk = nt(w, gb[c]) + tn(gbuf[:, r : r + t_size], q[blk, :])
            a, b = dk[:, :half], dk[:, half:]
            dh[at, keys : keys + half] = (a * cos[at, :] + b * sin[at, :]).astype(BF16)
            dh[at, keys + half : 2 * keys] = (b * cos[at, :] - a * sin[at, :]).astype(BF16)
            dv = nn(k[at, :], gb[c]) * tail + tn(pbuf[:, r : r + t_size], dr[blk, :])
            dh[at, 2 * keys : 2 * keys + values] = dv.astype(BF16)

    dh_copy = start(pltpu.make_async_copy(dh, dh_out, lsem.at[2]))
    plane = []

    def deal(i, chain, a):
        chain.arrive()
        total_rows(z, fin.at[i], a.at[rows_at(z * (width // LINE), width // LINE), :], chain.rx)
        cols = pl.ds(i * values, values)
        for m in (1, 2, 3):
            plane.append(
                start(
                    remote(
                        fin.at[i, rows_at(pq[m] * chunk, chunk), :], sums.at[p, :, cols],
                        psend.at[i, m], precv.at[i, m], me.plane(m),
                    )
                )
            )
        plane.append(
            start(
                pltpu.make_async_copy(
                    fin.at[i, rows_at(p * chunk, chunk), :], sums.at[p, :, cols], psend.at[i, 0]
                )
            )
        )

    gate_sum.near(0)
    for u in range(2, 4):
        f_unit(u)
    deal(0, out_sum, ao)
    gate_sum.near(1)
    gate_sum.far()
    x_tile(0).start()
    x_tile(1).start()
    wide = 2 * keys + values

    @pl.loop(0, width // 256)
    def _(i):
        @pl.when(i + 2 < width // 256)
        def _():
            x_tile(i + 2).start()

        x_tile(i).wait()
        da[rows_at(i * 256, 256), :wide] = tn(xt[i % 3], dh[:, :wide]).astype(BF16)

    to_last = [
        start(pltpu.make_async_copy(da.at[:, : 2 * keys], aq_out, lsem.at[0])),
        start(pltpu.make_async_copy(da.at[:, 2 * keys : wide], av_out, lsem.at[1])),
    ]
    for u in range(4, len(units)):
        f_unit(u)
    gate_sum.arrive()
    total_rows(z, fin.at[1], ag.at[rows_at(z * deep, deep), :], rxg)
    to_last.append(start(pltpu.make_async_copy(fin.at[1], gate_fin, lsem.at[3])))
    for c in plane + to_last + [dh_copy]:
        c.wait()
    out_sum.finish()
    gate_sum.finish()
    for u, (h, zp, js) in enumerate(units):
        for c in f_out(u):
            c.wait()
        for j in js:
            f_copy(h, zp, j).wait_send()


def retention_back(da, wo, gated, gate, ret, q, k, v, states, cos, sin, ccol, crow, scal, xg, fu, fd, cid):
    tokens, width = da.shape
    keys, values = q.shape[1], v.shape[1]
    chunk = width // SPANS
    blocks = tokens // STRETCH
    hidden = fu.shape[1]
    deep = width // LINE
    return comm_call(
        retention_back_kernel,
        [
            jax.ShapeDtypeStruct((tokens, 2 * keys + 2 * values), BF16),
            jax.ShapeDtypeStruct((PLANE, chunk, values), BF16),
            jax.ShapeDtypeStruct((deep, values), BF16),
            jax.ShapeDtypeStruct((2, LINE, 2, chunk, hidden), BF16),
            jax.ShapeDtypeStruct((width, values), BF16),
            jax.ShapeDtypeStruct((width, 2 * keys), BF16),
        ],
        [da, wo, gated, gate, ret, q, k, v, states, cos, sin, ccol, crow, scal, xg, fu, fd],
        [
            pltpu.VMEM(ccol.shape, F32),
            pltpu.VMEM(crow.shape, F32),
            pltpu.VMEM(scal.shape, F32),
            pltpu.VMEM((tokens, 2 * keys + 2 * values), BF16),
            pltpu.VMEM((tokens, width), BF16),
            pltpu.VMEM(wo.shape, BF16),
            pltpu.VMEM(gated.shape, BF16),
            pltpu.VMEM((3, 2, 256, values), F32),
            pltpu.VMEM(q.shape, BF16),
            pltpu.VMEM(k.shape, BF16),
            pltpu.VMEM(v.shape, BF16),
            pltpu.VMEM(states.shape, BF16),
            pltpu.VMEM(cos.shape, F32),
            pltpu.VMEM(sin.shape, F32),
            pltpu.VMEM((tokens, values), BF16),
            pltpu.VMEM((3, tokens, 256), BF16),
            pltpu.VMEM((width, values), BF16),
            pltpu.VMEM((width, values), BF16),
            pltpu.VMEM((LINE + 1, deep, values), BF16),
            pltpu.VMEM((LINE + 1, deep, values), BF16),
            pltpu.VMEM((2, deep, values), BF16),
            pltpu.VMEM((blocks, keys, values), F32),
            pltpu.VMEM((blocks, keys, values), BF16),
            pltpu.VMEM((keys, values), F32),
            pltpu.VMEM((keys, values), BF16),
            pltpu.VMEM((2, 2 * LINE - 1, chunk, hidden), BF16),
            pltpu.VMEM((2, 2, chunk, hidden), BF16),
            pltpu.VMEM((STRETCH, STRETCH), BF16),
            pltpu.VMEM((STRETCH, STRETCH), BF16),
            DMA((12 + LINE,)),
            DMA((3, 2)),
            DMA((3,)),
            DMA((2, LINE, 2)),
            DMA((2, LINE, 2)),
            DMA((2 * LINE, 2)),
            DMA((2, 2)),
            DMA((1,)),
            DMA((1,)),
            DMA((2, PLANE)),
            DMA((2, PLANE)),
        ]
        + line_sems()
        + line_sems(),
        cid,
        in_specs=[ANY] * 17,
        out_specs=[ANY] * 6,
    )


def last_kernel(
    dh_ref, av_ref, aq_ref, wq_ref, wk_ref, wv_ref, wg_ref, f1_ref, fu_ref, fd_ref, gate_ref, tok_ref, gain_ref, resid_ref, second_ref,
    grad_out, gains, fout, sums,
    tok, resid, rxl, dh, wh, share, rx0, rx1a, rx1b, rx2a, rx2b, av, aq, rxv, rxq, fin, rf2, kf, rxfa, rxfb, grx,
    lsem, ksem, lsend, lrecv, fsend, frecv, csend, crecv, xsend, xrecv, gsend, grecv, psend, precv, *line,
):
    me = Place()
    z, p, f = me.z, me.p, me.f
    rounds = [
        [me.at((z + t) % LINE, p, f) for t in range(1, LINE)],
        [me.partner()],
        [me.plane(m) for m in (1, 2, 3)],
    ]
    greet([(d, None) for r in rounds for d in r])
    width, keys2, values = av.shape[0], aq.shape[1], av.shape[1]
    rows = tok_ref.shape[0]
    pq = [me.xor(m) for m in range(4)]
    chunk = width // SPANS
    deep = width // LINE

    late = 1

    def f_copy(h, zp):
        return remote(f1_ref.at[h, zp, 1], rf2.at[h, zp], fsend.at[h, zp], frecv.at[h, zp], me.plane(2 - h))

    def f_block(h, place):
        return (fu_ref, fd_ref)[h].at[rows_at((late * PLANE + place) * chunk, chunk), :]

    def late_copy(h):
        return remote(f_block(h, pq[1 + h]), rxl.at[h], lsend.at[h], lrecv.at[h], me.plane(1 + h))

    def block_of(a, size):
        return lambda zz: a.at[rows_at(zz * size, size), :]

    v_sum = LineSum(me, block_of(av, deep), rxv, *line[:4], add_rows)
    q_sum = LineSum(me, block_of(aq, deep), rxq, *line[4:8], add_rows)
    fa_sum = LineSum(me, lambda zz: kf.at[0, zz], rxfa, *line[8:12], add_rows)
    fb_sum = LineSum(me, lambda zz: kf.at[1, zz], rxfb, *line[12:16], add_rows)
    v_sum.begin(src=block_of(av_ref, deep))
    q_sum.begin(src=block_of(aq_ref, deep))
    for zp in (3, 0, 2, 1):
        for h in range(2):
            f_copy(h, zp).start()
    for h in range(2):
        late_copy(h).start()
    load = start(pltpu.make_async_copy(dh_ref, dh, lsem.at[0]))
    owns = [
        start(pltpu.make_async_copy(av_ref, av, lsem.at[7])),
        start(pltpu.make_async_copy(aq_ref, aq, lsem.at[8])),
    ]
    loads, at = [], 0
    for i, w in enumerate((wq_ref, wk_ref, wv_ref, wg_ref)):
        size = w.shape[1]
        loads.append(start(pltpu.make_async_copy(w, wh.at[:, at : at + size], lsem.at[1 + i])))
        at += size
    keeps = []
    for h in range(2):
        for i, zp in enumerate((3, 0, 2)):
            keeps.append(start(pltpu.make_async_copy(f1_ref.at[h, zp, 0], kf.at[h, zp], ksem.at[h, i])))
        keeps.append(start(pltpu.make_async_copy(f_block(h, p), kf.at[h, late], ksem.at[h, 3])))
    rest = [
        start(pltpu.make_async_copy(tok_ref, tok, lsem.at[5])),
        start(pltpu.make_async_copy(resid_ref, resid, lsem.at[6])),
    ]

    load.wait()
    plane = []

    def deal(i, chain, a):
        chain.arrive()
        total_rows(z, fin.at[i], a.at[rows_at(z * deep, deep), :], chain.rx)
        spread(i, fin.at[i])

    def spread(i, src):
        cols = pl.ds(i * values, values)
        for m in (1, 2, 3):
            plane.append(
                start(
                    remote(
                        src.at[rows_at(pq[m] * chunk, chunk), :], sums.at[p, :, cols],
                        psend.at[i, m], precv.at[i, m], me.plane(m),
                    )
                )
            )
        plane.append(
            start(
                pltpu.make_async_copy(
                    src.at[rows_at(p * chunk, chunk), :], sums.at[p, :, cols], psend.at[i, 0]
                )
            )
        )

    gate_load = start(pltpu.make_async_copy(gate_ref, fin.at[2], lsem.at[9]))
    for c in loads + owns + [gate_load]:
        c.wait()

    own_rows, their_rows = rows_at(f * rows, rows), rows_at((1 - f) * rows, rows)
    wide = width // 2
    ca, cb = pl.ds(0, wide), pl.ds(wide, wide)
    everything, whole = pl.ds(0, width), pl.ds(0, wide)
    first, sends = {}, {}

    def share_part(m):
        at_rows = rows_at(pq[m] * 2 * rows, 2 * rows)

        @pl.loop(0, width, step=256)
        def _(c):
            at = rows_at(c, 256)
            share[m, :, at] = nt(dh[at_rows, :], wh[at, :]).astype(BF16)

        first[m] = start(
            remote(share.at[m, their_rows], rx0.at[m], csend.at[m], crecv.at[m], me.partner())
        )

    def pass_on(m):
        first[m].wait_recv()
        add_into(rx0.at[m], everything, share.at[m, own_rows], everything)
        k = 0 if m == 3 else 1
        if m & 1:
            sends["a", k] = start(
                remote(rx0.at[m, :, ca], rx1a.at[k], xsend.at[k], xrecv.at[k], me.plane(1))
            )
        if m & 2:
            sends["b", k] = start(
                remote(rx0.at[m, :, cb], rx1b.at[k], xsend.at[2 + k], xrecv.at[2 + k], me.plane(2))
            )

    share_part(3)
    share_part(1)
    pass_on(3)
    v_sum.near(0)
    share_part(2)
    pass_on(1)
    share_part(0)
    pass_on(2)
    v_sum.near(1)
    pass_on(0)
    for c in keeps:
        c.wait()
    v_sum.far()
    q_sum.near(0)
    for ends, turns in (((3, 0), (3,)), ((2, 1), (2,))):
        for zp in ends:
            for h in range(2):
                f_copy(h, zp).wait_recv()
                add_rows(kf.at[h, zp], rf2.at[h, zp])
                if zp == late:
                    late_copy(h).wait_recv()
                    add_rows(kf.at[h, zp], rxl.at[h])
        for zz in turns:
            fa_sum.begin((zz,))
            fb_sum.begin((zz,))
    q_sum.near(1)
    q_sum.far()
    sends["a", 0].wait_recv()
    add_into(rx1a.at[0], whole, rx0.at[2], ca)
    s2a = start(remote(rx1a.at[0], rx2a, xsend.at[4], xrecv.at[4], me.plane(2)))
    sends["b", 0].wait_recv()
    add_into(rx1b.at[0], whole, rx0.at[1], cb)
    s2b = start(remote(rx1b.at[0], rx2b, xsend.at[5], xrecv.at[5], me.plane(1)))
    spread(2, fin.at[2])
    deal(0, v_sum, av)
    fa_sum.near(0)
    sends["a", 1].wait_recv()
    sends["b", 1].wait_recv()
    deal(1, q_sum, aq)
    fb_sum.near(0)
    s2a.wait_recv()
    s2b.wait_recv()
    for c in rest:
        c.wait()
    gains[...] = jnp.zeros_like(gains)
    gains[2:4, :] = second_ref[0:2, :]
    step = 32

    @pl.loop(0, rows, step=step)
    def _(r):
        at = rows_at(r, step)
        left = rx0[0, at, ca].astype(F32) + rx1a[1, at, :].astype(F32) + rx2a[at, :].astype(F32)
        right = rx0[0, at, cb].astype(F32) + rx1b[1, at, :].astype(F32) + rx2b[at, :].astype(F32)
        dx = jnp.concatenate([left, right], axis=1)
        v = tok[at, :].astype(F32)
        centered = v - jnp.mean(v, axis=1, keepdims=True)
        scale = lax.rsqrt(jnp.mean(centered * centered, axis=1, keepdims=True) + 1e-05)
        hat = centered * scale
        gains[0:1, :] += jnp.sum(dx * hat, axis=0, keepdims=True)
        gains[1:2, :] += jnp.sum(dx, axis=0, keepdims=True)
        g = dx * gain_ref[...]
        back = scale * (
            g - jnp.mean(g, axis=1, keepdims=True) - hat * jnp.mean(g * hat, axis=1, keepdims=True)
        )
        tok[at, :] = (back + resid[at, :]).astype(BF16)

    out_copy = start(pltpu.make_async_copy(tok, grad_out, lsem.at[0]))

    def gain_copies(r):
        base = (0, 3, 4)[r]
        return [
            remote(gains, grx.at[base + i], gsend.at[base + i], grecv.at[base + i], d)
            for i, d in enumerate(rounds[r])
        ]

    def gain_begin(r):
        for c in gain_copies(r):
            c.start()

    def gain_end(r):
        for c in gain_copies(r):
            c.wait()
        for i in range(len(rounds[r])):
            gains[...] += grx[(0, 3, 4)[r] + i]

    gain_begin(0)
    fa_sum.begin((1,))
    fb_sum.begin((1,))
    fa_sum.near(1)
    fa_sum.far()
    gain_end(0)
    gain_begin(1)
    fb_sum.near(1)
    gain_end(1)
    gain_begin(2)
    fb_sum.far()
    gain_end(2)
    fa_sum.arrive()
    total_rows(z, fout.at[0], kf.at[0, z], rxfa)
    fb_sum.arrive()
    total_rows(z, fout.at[1], kf.at[1, z], rxfb)
    for c in plane + [out_copy]:
        c.wait()
    for h in range(2):
        late_copy(h).wait_send()
    for chain in (v_sum, q_sum, fa_sum, fb_sum):
        chain.finish()
    for c in list(first.values()) + list(sends.values()) + [s2a, s2b]:
        c.wait_send()
    for zp in range(LINE):
        for h in range(2):
            f_copy(h, zp).wait_send()


def last_sums(dh, av, aq, wq, wk, wv, wg, f1, fu, fd, gate_fin, tokens, gain, resid, second, cid):
    width = av.shape[0]
    rows = tokens.shape[0]
    keys, values = wq.shape[1], wv.shape[1]
    assert 2 * keys == values
    chunk, deep = width // SPANS, width // LINE
    hidden = f1.shape[-1]
    return comm_call(
        last_kernel,
        [
            jax.ShapeDtypeStruct((rows, width), BF16),
            jax.ShapeDtypeStruct((8, width), F32),
            jax.ShapeDtypeStruct((2, chunk, hidden), BF16),
            jax.ShapeDtypeStruct((PLANE, chunk, 3 * values), BF16),
        ],
        [dh, av, aq, wq, wk, wv, wg, f1, fu, fd, gate_fin, tokens, gain[None], resid, second],
        [
            pltpu.VMEM((rows, width), BF16),
            pltpu.VMEM((rows, width), F32),
            pltpu.VMEM((2, chunk, hidden), BF16),
            pltpu.VMEM(dh.shape, BF16),
            pltpu.VMEM((width, dh.shape[1]), BF16),
            pltpu.VMEM((PLANE, 2 * rows, width), BF16),
            pltpu.VMEM((PLANE, rows, width), BF16),
            pltpu.VMEM((2, rows, width // 2), BF16),
            pltpu.VMEM((2, rows, width // 2), BF16),
            pltpu.VMEM((rows, width // 2), BF16),
            pltpu.VMEM((rows, width // 2), BF16),
            pltpu.VMEM((width, values), BF16),
            pltpu.VMEM((width, 2 * keys), BF16),
            pltpu.VMEM((LINE + 1, deep, values), BF16),
            pltpu.VMEM((LINE + 1, deep, 2 * keys), BF16),
            pltpu.VMEM((3, deep, values), BF16),
            pltpu.VMEM((2, LINE, chunk, hidden), BF16),
            pltpu.VMEM((2, LINE, chunk, hidden), BF16),
            pltpu.VMEM((LINE + 1, chunk, hidden), BF16),
            pltpu.VMEM((LINE + 1, chunk, hidden), BF16),
            pltpu.VMEM((7, 8, width), F32),
            DMA((10,)),
            DMA((2, 4)),
            DMA((2,)),
            DMA((2,)),
            DMA((2, LINE)),
            DMA((2, LINE)),
            DMA((4,)),
            DMA((4,)),
            DMA((6,)),
            DMA((6,)),
            DMA((7,)),
            DMA((7,)),
            DMA((3, PLANE)),
            DMA((3, PLANE)),
        ]
        + line_sems()
        + line_sems()
        + line_sems()
        + line_sems(),
        cid,
        in_specs=[ANY] * 12 + [VM, ANY, VM],
        out_specs=[ANY, VM, VM, ANY],
    )


def outputs_kernel(
    last, first, ffn, low_out, low_grad, gains, q, k, v, gate, out, up, down, block_out, grad_tokens, *vectors
):
    values = v.shape[1]
    keys = q.shape[1]
    v[...] = last[0, :, :values].astype(F32)
    q[...] = last[0, :, values : values + keys].astype(F32)
    k[...] = last[0, :, values + keys : 2 * values].astype(F32)
    gate[...] = last[0, :, 2 * values :].astype(F32)
    out[...] = first[0].astype(F32).T
    up[...] = ffn[0].astype(F32)
    down[...] = ffn[1].astype(F32).T
    block_out[...] = low_out[...]
    grad_tokens[...] = low_grad[...]
    for i, g in enumerate(vectors):
        g[...] = gains[i, :]


def outputs(last, first, ffn, low_out, low_grad, gains, keys):
    heads, chunk, values = first.shape
    hidden = ffn.shape[-1]
    rows, width = low_out.shape
    piece, slab = hidden // heads, rows // heads
    sd = jax.ShapeDtypeStruct
    by_column = [pl.BlockSpec((chunk, size), lambda i: (0, i)) for size in (keys, keys, values, values)]
    by_row = pl.BlockSpec((values, chunk), lambda i: (i, 0))
    low = pl.BlockSpec((slab, width), lambda i: (i, 0))
    sums = [pl.BlockSpec((1, chunk, a.shape[-1]), lambda i: (i, 0, 0)) for a in (last, first)]
    return pl.pallas_call(
        outputs_kernel,
        grid=(heads,),
        in_specs=[
            *sums,
            pl.BlockSpec((2, chunk, piece), lambda i: (0, 0, i)),
            low,
            low,
            pl.BlockSpec(gains.shape, lambda i: (0, 0)),
        ],
        out_specs=by_column
        + [
            by_row,
            pl.BlockSpec((chunk, piece), lambda i: (0, i)),
            pl.BlockSpec((piece, chunk), lambda i: (i, 0)),
            low,
            low,
        ]
        + [pl.BlockSpec((width,), lambda i: (0,))] * 4,
        out_shape=[
            sd((chunk, heads * keys), F32),
            sd((chunk, heads * keys), F32),
            sd((chunk, heads * values), F32),
            sd((chunk, heads * values), F32),
            sd((heads * values, chunk), F32),
            sd((chunk, hidden), F32),
            sd((hidden, chunk), F32),
            sd((rows, width), BF16),
            sd((rows, width), BF16),
        ]
        + [sd((width,), F32)] * 4,
    )(last, first, ffn, low_out, low_grad, gains)


def angle_tables(fine, half_width):
    frequency = 10000.0 ** (-np.linspace(0.0, 1.0, half_width))
    coarse = fine * np.arange(SEQUENCE_LENGTH // fine)[:, None] * frequency[None, :]
    near = np.arange(fine)[:, None] * frequency[None, :]
    return [np.asarray(f(a), np.float32) for a in (coarse, near) for f in (np.cos, np.sin)]


def shards(
    tokens,
    ln1_gain,
    ln1_bias,
    w_query,
    w_key,
    w_value,
    w_gate,
    w_out,
    decay_log,
    ln2_gain,
    ln2_bias,
    w_up,
    w_down,
    cotangent,
):
    row_count, width = tokens.shape
    span_rows = cotangent.shape[0]
    heads = decay_log.shape[1]
    repeats = lax.axis_size("seq") // SPANS
    peers = [[lo + SPANS * k for k in range(repeats)] for lo in range(SPANS)]
    narrow = width // (SPANS * repeats)

    def wide_in(w, axis):
        if repeats == 1:
            return w
        return lax.all_gather(w, "seq", axis_index_groups=peers, axis=axis, tiled=True)

    def narrow_out(g, axis):
        if repeats == 1:
            return g
        return lax.psum_scatter(
            g, "seq", scatter_dimension=axis, axis_index_groups=peers, tiled=True
        )

    def features_in(a):
        if repeats == 1:
            return a
        return a.reshape(a.shape[:-1] + (repeats, SPANS, narrow)).swapaxes(-3, -2).reshape(a.shape)

    def features_out(a):
        if repeats == 1:
            return a
        return a.reshape(a.shape[:-1] + (SPANS, repeats, narrow)).swapaxes(-3, -2).reshape(a.shape)

    spot = lax.axis_index("seq") % SPANS
    z, p = spot // PLANE, spot % PLANE
    group_rows = span_rows * PLANE
    blocks = group_rows // STRETCH

    tokens, cotangent, w_down = features_in(tokens), features_in(cotangent), features_in(w_down)
    w_up = features_in(w_up.T).T if repeats > 1 else w_up
    ln1_gain, ln1_bias = features_in(ln1_gain), features_in(ln1_bias)
    ln2_gain, ln2_bias = features_in(ln2_gain), features_in(ln2_bias)
    decays = jnp.pad(decay_log.T, ((0, 8 - heads), (0, 0)))
    (
        normed, q_rot, k_rot, value, gate_proj, retained, gated_low, prev_states,
        cosine, sine_part, ccol, crow, scalars, key_w, value_w, query_w, gate_w, out_w,
    ) = attention(
        tokens,
        ln1_gain,
        ln1_bias,
        decays,
        angle_tables(64, w_key.shape[1] // heads // 2),
        [
            wide_in(w_key, 0),
            wide_in(w_value, 0),
            wide_in(w_query, 0),
            wide_in(w_gate, 0),
            wide_in(w_out, 1),
        ],
        (False, False, False, False, True),
        0,
    )
    block_out, grad_resid, gains_second, grad_attn, grad_up, grad_down = ffn_part(
        gated_low,
        out_w,
        tokens,
        ln2_gain,
        ln2_bias,
        w_up,
        w_down,
        cotangent,
        2,
    )
    grad_heads, sums_first, gate_sum, ffn_first, grad_value_w, grad_qk_w = retention_back(
        grad_attn,
        out_w,
        gated_low,
        gate_proj,
        retained,
        q_rot,
        k_rot,
        value,
        prev_states,
        cosine,
        sine_part,
        ccol,
        crow,
        scalars,
        normed,
        grad_up,
        grad_down,
        7,
    )
    grad_tokens, gains, ffn_sum, sums_last = last_sums(
        grad_heads,
        grad_value_w,
        grad_qk_w,
        query_w,
        key_w,
        value_w,
        gate_w,
        ffn_first,
        grad_up,
        grad_down,
        gate_sum,
        tokens,
        ln1_gain,
        grad_resid,
        gains_second,
        8,
    )
    if repeats > 1:
        gains = lax.psum(gains, "seq", axis_index_groups=peers)

    *sums, block_out, grad_tokens, gain_one, bias_one, gain_two, bias_two = outputs(
        sums_last, sums_first, ffn_sum, block_out, grad_tokens, gains, key_w.shape[1]
    )
    gain_one, bias_one, gain_two, bias_two = map(features_out, (gain_one, bias_one, gain_two, bias_two))
    sum_query, sum_key, sum_value, sum_gate, sum_out, sum_up, sum_down = (
        narrow_out(g, axis) for g, axis in zip(sums, (0, 0, 0, 0, 1, 0, 1))
    )
    return (
        features_out(block_out),
        features_out(grad_tokens),
        gain_one,
        bias_one,
        sum_query,
        sum_key,
        sum_value,
        sum_gate,
        sum_out,
        gain_two,
        bias_two,
        sum_up,
        sum_down,
    )


def solution(mesh):
    return jax.shard_map(
        shards,
        mesh=mesh,
        in_specs=(
            P(("seq", "ffn"), None),
            P(),
            P(),
            P("seq", "ffn"),
            P("seq", "ffn"),
            P("seq", "ffn"),
            P("seq", "ffn"),
            P("ffn", "seq"),
            P("seq", "ffn"),
            P(),
            P(),
            P(None, "ffn"),
            P("ffn", None),
            P("seq", None),
        ),
        out_specs=(
            P(("seq", "ffn"), None),
            P(("seq", "ffn"), None),
            P(),
            P(),
            P("seq", "ffn"),
            P("seq", "ffn"),
            P("seq", "ffn"),
            P("seq", "ffn"),
            P("ffn", "seq"),
            P(),
            P(),
            P("seq", "ffn"),
            P("ffn", "seq"),
        ),
        check_vma=False,
    )
```
